32 devices in a mesh: space: 4 (over y, x), mode: 8 (over z, core).
Axes of the slice: x: 2, y: 2, z: 4, core: 2. Of those that a mesh axis runs over, the one named last changes fastest.
Arguments:
- distribution: float32 [8192, 1024], P('mode', 'space'), may hold values from -6 to 6
- scatter_matrix: bfloat16 [8192, 8192], P(None, 'mode'), as said below
- velocity: float32 [2, 8192], P(None, 'mode'), may hold values from -0.4 to 0.4
- capacity: float32 [8192], P('mode'), may hold values from 0.3 to 3
- cell_type: int32 [1024], P('space'), may hold values from 0 to 2
Outputs:
- updated: float32 [8192, 1024], P('mode', 'space')
- heat_flux: float32 [2, 1024], P(None, 'space')
The draws below stay inside these ranges and needn't reach their ends.
Inputs may be any that keep to these rules, and one draw needn't show every extreme that they name: scatter_matrix is symmetric.
All inputs are finite; a program needn't handle non-finite values.
Results may differ from the reference program's by a relative error of at most 0.0003.
Values sent between devices are 32-bit elements; how exact they have to be, the bound alone decides.
No kernel may reach another device: no remote copies, remote signals or barrier semaphores. Data moves between devices by JAX's collectives and lax.ppermute only.
A program may use at most 64 MiB of HBM per device.

```python
import math
import jax
import jax.numpy as jnp
from jax import lax

MODES = 8192
NY = 16
NX = 64
CELLS = 1024


def draw_scatter_matrix(key, part):
    first_key, second_key = jax.random.split(key, 2)
    raw = jax.random.normal(first_key, (MODES, MODES), jnp.float32)
    off_part = (raw + raw.T) * (0.2 / jnp.sqrt(2.0 * MODES))
    diag_rates = 0.5 + jnp.exp(jax.random.uniform(second_key, (MODES,), jnp.float32, -3.0, 0.0))
    rows_index = jnp.arange(MODES)[:, None]
    cols_index = jnp.arange(MODES)[None, :]
    matrix = jnp.where(rows_index == cols_index, diag_rates[:, None], off_part)
    return matrix.astype(jnp.bfloat16)


def touch_ends(values, key, smallest, largest):
    index_at = [jax.random.randint(jax.random.fold_in(key, axis), (), 0, length) for axis, length in enumerate(values.shape)]
    widest = values.shape.index(max(values.shape))
    neighbour = index_at[:widest] + [(index_at[widest] + 1) % values.shape[widest]] + index_at[widest + 1:]
    return values.at[tuple(index_at)].set(smallest).at[tuple(neighbour)].set(largest)


def block_scale(stream_key, dims, shards, least, largest):
    loudness = 1.0
    for position, parts in shards:
        steps = jax.random.uniform(jax.random.fold_in(jax.random.fold_in(stream_key, 6), position), (parts,), jnp.float32, least / len(shards), largest / len(shards))
        loudness = loudness * jnp.repeat(jnp.exp(steps), dims[position] // parts).reshape((-1,) + (1,) * (len(dims) - 1 - position))
    return loudness


def scatter_about(own_key, shape, scale, bound, cuts=(), dtype=jnp.bfloat16):
    loudness = block_scale(own_key, shape, cuts, -0.22, 0.18) if cuts else 1.0
    array = jax.random.normal(own_key, shape, jnp.float32) * scale * loudness
    return jnp.minimum(jnp.maximum(array, -bound), bound).astype(dtype)


def setup_inputs(seed: int = 0) -> dict:
    keys = jax.random.split(jax.random.key(seed), 6)
    distribution = scatter_about(keys[0], (MODES, CELLS), 1.0, 6.0, ((0, 8), (1, 4)), jnp.float32)
    scatter_matrix = draw_scatter_matrix(jax.random.fold_in(keys[5], 71), 0)
    velocity = jnp.clip(jax.random.uniform(keys[2], (2, MODES), jnp.float32, -0.4, 0.4) * block_scale(keys[2], (2, MODES), ((1, 8),), -0.4, 0.0), -0.4, 0.4)
    capacity = jnp.clip(jnp.exp(math.log(3.0) - 2.3025851 * jax.random.uniform(keys[3], (MODES,), jnp.float32) ** block_scale(keys[3], (MODES,), ((0, 8),), -0.2, 0.2)), 0.3, 3.0)
    cell_type = touch_ends(jax.random.randint(keys[4], (CELLS,), 0, 3), jax.random.fold_in(keys[4], 1), 0, 2).astype(jnp.int32)
    return dict(distribution=distribution, scatter_matrix=scatter_matrix, velocity=velocity, capacity=capacity, cell_type=cell_type)


relax_rate = 0.5
time_step = 0.5

def tendency(padded, collision, cell_kinds, velocity, capacity):
    padded_y = jnp.pad(padded, ((0, 0), (0, 0), (2, 2)))
    width = padded.shape[1] - 4
    centre = padded_y[:, 2:width + 2, 2:-2]
    west_one = padded_y[:, 1:width + 1, 2:-2]
    west_two = padded_y[:, 0:width, 2:-2]
    east_one = padded_y[:, 3:width + 3, 2:-2]
    east_two = padded_y[:, 4:width + 4, 2:-2]
    south_one = padded_y[:, 2:width + 2, 1:-3]
    south_two = padded_y[:, 2:width + 2, 0:-4]
    north_one = padded_y[:, 2:width + 2, 3:-1]
    north_two = padded_y[:, 2:width + 2, 4:]
    speed_x = velocity[0][:, None, None]
    speed_y = velocity[1][:, None, None]
    advection = jnp.maximum(speed_x, 0.0) * 0.5 * (3.0 * centre - 4.0 * west_one + west_two)
    advection = advection + jnp.minimum(speed_x, 0.0) * 0.5 * (-3.0 * centre + 4.0 * east_one - east_two)
    advection = advection + jnp.maximum(speed_y, 0.0) * 0.5 * (3.0 * centre - 4.0 * south_one + south_two)
    advection = advection + jnp.minimum(speed_y, 0.0) * 0.5 * (-3.0 * centre + 4.0 * north_one - north_two)
    contact = (cell_kinds > 0).astype(jnp.float32)
    reservoir = jnp.where(cell_kinds == 1, 1.0, -1.0).astype(jnp.float32)
    contact_term = relax_rate * contact[None] * (centre - reservoir[None] * capacity[:, None, None])
    return -advection - collision - contact_term

def reference(distribution, scatter_matrix, velocity, capacity, cell_type):
    total_modes = distribution.shape[0]
    field_now = distribution.reshape(total_modes, NX, NY)
    cell_kinds = cell_type.reshape(NX, NY)
    matrix_wide = scatter_matrix.astype(jnp.float32)

    def collide(values_in):
        summed = jnp.dot(matrix_wide, values_in.reshape(total_modes, -1), precision=lax.Precision.HIGHEST)
        return summed.reshape(total_modes, NX, NY)

    def extend(values_in):
        return jnp.pad(values_in, ((0, 0), (2, 2), (0, 0)))
    first_rate = tendency(extend(field_now), collide(field_now), cell_kinds, velocity, capacity)
    midpoint = field_now + time_step * first_rate
    second_rate = tendency(extend(midpoint), collide(midpoint), cell_kinds, velocity, capacity)
    updated = field_now + 0.5 * time_step * (first_rate + second_rate)
    updated = updated.reshape(total_modes, -1)
    weights = capacity[None, :] * velocity
    heat_flux = jnp.dot(weights, updated, precision=lax.Precision.HIGHEST) / jnp.sqrt(jnp.float32(total_modes))
    return (updated, heat_flux)
```

```python
import jax
import jax.numpy as jnp
from jax import lax
from jax.sharding import PartitionSpec as P

NY = 16


relax_rate = 0.5
time_step = 0.5


def halo_x(value, width):
    count, length = (lax.axis_size("space"), value.shape[1])
    up = [(i, (i + 1) % count) for i in range(count - 1)]
    down = [(j, i) for i, j in up]
    before = lax.ppermute(value[:, length - width :], "space", up)
    after = lax.ppermute(value[:, :width], "space", down)
    return before, after


def split_two(value):
    high = lax.reduce_precision(value, 8, 7)
    return jnp.concatenate(
        [high.astype(jnp.bfloat16), (value - high).astype(jnp.bfloat16)], axis=-1
    )


def dot_halves(matrix, value, contract):
    width = value.shape[1]
    both = lax.dot_general(
        matrix,
        split_two(value),
        (((contract,), (0,)), ((), ())),
        preferred_element_type=jnp.float32,
    )
    return both[:, :width] + both[:, width:]


def local_rate(flat, before, after, cell_type, velocity, capacity):
    cells = flat.shape[1]
    wide = jnp.concatenate([before, flat, after], axis=1)
    two = 2 * NY
    y = lax.broadcasted_iota(jnp.int32, (1, cells), 1) % NY

    def shifted(offset):
        return wide[:, two + offset : two + offset + cells]

    def shifted_y(offset):
        inside = (y + offset >= 0) & (y + offset < NY)
        return jnp.where(inside, shifted(offset), 0.0)

    def one_axis(speed, back_one, back_two, ahead_one, ahead_two):
        return jnp.maximum(speed, 0.0) * 0.5 * (
            3.0 * flat - 4.0 * back_one + back_two
        ) + jnp.minimum(speed, 0.0) * 0.5 * (-3.0 * flat + 4.0 * ahead_one - ahead_two)

    advection = one_axis(
        velocity[0][:, None], shifted(-NY), shifted(-two), shifted(NY), shifted(two)
    ) + one_axis(
        velocity[1][:, None], shifted_y(-1), shifted_y(-2), shifted_y(1), shifted_y(2)
    )
    contact = (cell_type > 0).astype(jnp.float32)
    reservoir = jnp.where(cell_type == 1, 1.0, -1.0).astype(jnp.float32)
    contact_term = relax_rate * contact[None] * (flat - reservoir[None] * capacity[:, None])
    return -advection - contact_term


def on_device(distribution, scatter_matrix, velocity, capacity, cell_type):
    local_cells = distribution.shape[1]
    total_modes = scatter_matrix.shape[0]
    half = local_cells // 2

    def by_gather(value):
        whole = lax.all_gather(value, "mode", axis=0, tiled=True)
        return dot_halves(scatter_matrix, whole, 0)

    def by_scatter(value):
        terms = dot_halves(scatter_matrix, value, 1)
        return lax.psum_scatter(terms, "mode", scatter_dimension=0, tiled=True)

    weights = capacity[None, :] * velocity
    all_weights = lax.all_gather(weights, "mode", axis=1, tiled=True)
    weights_scattered = dot_halves(scatter_matrix, all_weights.T, 0).T

    first_a = by_gather(distribution[:, :half])
    first_b = by_scatter(distribution[:, half:])
    before, after = halo_x(distribution, 2 * NY)
    still = local_rate(distribution, before, after, cell_type, velocity, capacity)
    rate_a = still[:, :half] - first_a
    rate_b = still[:, half:] - first_b
    mid_a = distribution[:, :half] + time_step * rate_a
    mid_b = distribution[:, half:] + time_step * rate_b
    second_a = by_scatter(mid_a)
    second_b = by_gather(mid_b)
    midpoint = jnp.concatenate([mid_a, mid_b], axis=1)
    before, after = halo_x(midpoint, 2 * NY)
    still_mid = local_rate(midpoint, before, after, cell_type, velocity, capacity)
    step = 0.5 * time_step
    most = distribution + step * (jnp.concatenate([rate_a, rate_b], axis=1) + still_mid)
    flux_part = (
        jnp.dot(weights, most, precision=lax.Precision.HIGHEST)
        - step * jnp.dot(weights_scattered, midpoint, precision=lax.Precision.HIGHEST)
    ) / jnp.sqrt(jnp.float32(total_modes))
    heat_flux = lax.all_gather(flux_part, "mode", axis=0).sum(0)
    updated = most - step * jnp.concatenate([second_a, second_b], axis=1)
    return (updated, heat_flux)


def solution(mesh):
    return jax.shard_map(
        on_device,
        mesh=mesh,
        in_specs=(P("mode", "space"), P(None, "mode"), P(None, "mode"), P("mode"), P("space")),
        out_specs=(P("mode", "space"), P(None, "space")),
        check_vma=False,
    )
```

```python
import functools

import numpy as np

import jax
import jax.numpy as jnp
from jax import lax
from jax.experimental import pallas as pl
from jax.experimental.pallas import tpu as pltpu
from jax.sharding import PartitionSpec as P

NY = 16
HALO = 2 * NY


relax_rate = 0.5
time_step = 0.5
VMEM_BYTES = 48 * 1024 * 1024


def halves(value):
    high = value.astype(jnp.bfloat16)
    low = (value - high.astype(jnp.float32)).astype(jnp.bfloat16)
    return high, low


def scatter_kernel(core_ref, mine_rows, other_rows, field, mine, other, parts):
    cells = field.shape[1]

    @pl.when(pl.program_id(0) == 0)
    def _():
        parts[...] = jnp.concatenate(halves(field[...]), axis=1)

    for rows, out in ((mine_rows, mine), (other_rows, other)):
        both = jnp.dot(rows[...], parts[...], preferred_element_type=jnp.float32)
        out[0] = both[:, :cells] + both[:, cells:]


def partial_products(matrix, field, core):
    total, modes = matrix.shape
    cells = field.shape[1]
    chips = total // (2 * modes)
    out = jax.ShapeDtypeStruct((chips, modes, cells), jnp.float32)
    out_spec = pl.BlockSpec((1, modes, cells), lambda t, core: (t, 0, 0))
    return pl.pallas_call(
        scatter_kernel,
        out_shape=(out, out),
        grid_spec=pltpu.PrefetchScalarGridSpec(
            num_scalar_prefetch=1,
            grid=(chips,),
            in_specs=[
                pl.BlockSpec((modes, modes), lambda t, core: (2 * t + core[0], 0)),
                pl.BlockSpec((modes, modes), lambda t, core: (2 * t + 1 - core[0], 0)),
                pl.BlockSpec((modes, cells), lambda t, core: (0, 0)),
            ],
            out_specs=(out_spec, out_spec),
            scratch_shapes=[pltpu.VMEM((modes, 2 * cells), jnp.bfloat16)],
        ),
        compiler_params=pltpu.CompilerParams(vmem_limit_bytes=VMEM_BYTES),
        cost_estimate=pl.CostEstimate(
            flops=4 * total * modes * cells,
            bytes_accessed=2 * total * modes + 4 * total * cells,
            transcendentals=0,
        ),
        name="partial_products",
    )(core, matrix, matrix, field)


def gather_kernel(scale, slots, order_ref, rows, base, *refs):
    fields, refs = refs[:slots], refs[slots:]
    if len(refs) == 4:
        weights, out, weights_out, total = refs
    else:
        (out, total), weights = refs, None
    step = pl.program_id(0)
    cells = out.shape[1]

    @pl.when(step == 0)
    def _():
        total[...] = jnp.zeros_like(total)

    for slot in range(slots):

        @pl.when(step == slot)
        def _(slot=slot):
            pieces = list(halves(fields[slot][...].T))
            if weights is not None:
                pieces += halves(weights[...])
            left = jnp.concatenate(pieces, axis=0)
            total[...] += jnp.dot(left, rows[...], preferred_element_type=jnp.float32)

    @pl.when(step == slots - 1)
    def _():
        result = total[:cells] + total[cells : 2 * cells]
        out[...] = base[...] - scale * result.T
        if weights is not None:
            weights_out[...] = total[2 * cells : 2 * cells + 8] + total[2 * cells + 8 :]


def whole_product(matrix, fields, order, base, scale, weights=None):
    total, modes = matrix.shape
    cells = base.shape[1]
    slots = len(fields)
    whole = pl.BlockSpec((modes, cells), lambda s, order: (0, 0))
    in_specs = [pl.BlockSpec((modes, modes), lambda s, order: (order[s], 0)), whole]
    in_specs += [whole] * slots
    out_shape = [jax.ShapeDtypeStruct((modes, cells), jnp.float32)]
    out_specs = [whole]
    operands = [matrix, base, *fields]
    rows = 2 * cells
    if weights is not None:
        in_specs.append(pl.BlockSpec((8, modes), lambda s, order: (0, order[s])))
        operands.append(weights)
        out_shape.append(jax.ShapeDtypeStruct((8, modes), jnp.float32))
        out_specs.append(pl.BlockSpec((8, modes), lambda s, order: (0, 0)))
        rows += 16
    return pl.pallas_call(
        functools.partial(gather_kernel, scale, slots),
        out_shape=out_shape,
        grid_spec=pltpu.PrefetchScalarGridSpec(
            num_scalar_prefetch=1,
            grid=(slots,),
            in_specs=in_specs,
            out_specs=out_specs,
            scratch_shapes=[pltpu.VMEM((rows, modes), jnp.float32)],
        ),
        compiler_params=pltpu.CompilerParams(vmem_limit_bytes=VMEM_BYTES),
        cost_estimate=pl.CostEstimate(
            flops=4 * total * modes * cells,
            bytes_accessed=2 * total * modes + 4 * total * cells,
            transcendentals=0,
        ),
        name="whole_product",
    )(order, *operands)


def still_rate(field, before, after, columns, kinds):
    cells = field.shape[1]
    wide = jnp.concatenate([before, field, after], axis=1)
    edge = before.shape[1]
    y = lax.broadcasted_iota(jnp.int32, (1, cells), 1) % NY

    def shifted(offset):
        return wide[:, edge + offset : edge + offset + cells]

    def shifted_y(offset):
        inside = (y + offset >= 0) & (y + offset < NY)
        return jnp.where(inside, shifted(offset), 0.0)

    def one_axis(speed, back_one, back_two, ahead_one, ahead_two):
        return jnp.maximum(speed, 0.0) * 0.5 * (
            3.0 * field - 4.0 * back_one + back_two
        ) + jnp.minimum(speed, 0.0) * 0.5 * (-3.0 * field + 4.0 * ahead_one - ahead_two)

    advection = one_axis(
        columns[:, 0:1], shifted(-NY), shifted(-2 * NY), shifted(NY), shifted(2 * NY)
    ) + one_axis(
        columns[:, 1:2], shifted_y(-1), shifted_y(-2), shifted_y(1), shifted_y(2)
    )
    contact = (kinds > 0).astype(jnp.float32)
    reservoir = jnp.where(kinds == 1, 1.0, -1.0).astype(jnp.float32)
    return -advection - relax_rate * contact * (field - reservoir * columns[:, 2:3])


def strips(before, after):
    rows = before.shape[1]
    pad = jnp.zeros((rows, 128 - HALO), jnp.float32)
    return (
        jnp.concatenate([pad, before[...].T], axis=1),
        jnp.concatenate([after[...].T, pad], axis=1),
    )


def first_kernel(field, before, after, table, kinds, base_a, base_b):
    value = field[...]
    half = base_a.shape[1]
    rate = still_rate(value, *strips(before, after), table[...].T, kinds[...])
    base = value + time_step * rate
    base_a[...] = base[:, :half]
    base_b[...] = base[:, half:]


def second_kernel(
    field, mid_a, mid_b, before, after, table, kinds, scattered, end_a, end_b, flux
):
    half = end_a.shape[1]
    mid = jnp.concatenate([mid_a[...], mid_b[...]], axis=1)
    columns = table[...].T
    rate = still_rate(mid, *strips(before, after), columns, kinds[...])
    step = 0.5 * time_step
    end = 0.5 * (field[...] + mid) + step * rate
    end_a[...] = end[:, :half]
    end_b[...] = end[:, half:]
    taken = scattered[...].T

    @pl.when(pl.program_id(0) == 0)
    def _():
        flux[...] = jnp.zeros_like(flux)

    for d in range(2):
        weight = columns[:, 3 + d : 4 + d]
        terms = weight * end - (step * taken[:, d : d + 1]) * mid
        flux[d : d + 1, :] += jnp.sum(terms, axis=0, keepdims=True)


def stencil_call(kernel, modes, cells, arrays, kinds_of, outs):
    block = min(modes, 256)
    specs = {
        "rows": lambda a: pl.BlockSpec((block, a.shape[1]), lambda i: (i, 0)),
        "columns": lambda a: pl.BlockSpec((a.shape[0], block), lambda i: (0, i)),
        "whole": lambda a: pl.BlockSpec(a.shape, lambda i: (0, 0)),
    }
    return pl.pallas_call(
        kernel,
        out_shape=[shape for shape, _ in outs],
        grid=(modes // block,),
        in_specs=[specs[kind](a) for a, kind in zip(arrays, kinds_of)],
        out_specs=[specs[kind](shape) for shape, kind in outs],
        compiler_params=pltpu.CompilerParams(vmem_limit_bytes=VMEM_BYTES),
        cost_estimate=pl.CostEstimate(
            flops=40 * modes * cells, bytes_accessed=12 * modes * cells, transcendentals=0
        ),
        name="stencil",
    )(*arrays)


def halo(leading, last):
    count = lax.axis_size("space")
    up = [(i, i + 1) for i in range(count - 1)]
    down = [(j, i) for i, j in up]
    before = lax.ppermute(last, "space", up)
    after = lax.ppermute(leading, "space", down)
    return before, after


def slot_sources(chips, place):
    found = []
    for step in range(chips - 1):
        if place >= step + 1:
            found.append((0, step, place - 1 - step))
        if place <= chips - 2 - step:
            found.append((1, step, place + 1 + step))
    return found


def block_order(chips):
    orders = []
    for device in range(2 * chips):
        order = []
        for core in (device % 2, 1 - device % 2):
            chip = device // 2
            place = chip if core == 0 else chips - 1 - chip
            sources = [place] + [q for _, _, q in slot_sources(chips, place)]
            blocks = [2 * (q if core == 0 else chips - 1 - q) + core for q in sources]
            order.append(blocks)
        orders.append(order[0] + order[1])
    return np.array(orders, np.int32)


class Line:
    def __init__(self):
        devices = lax.axis_size("mode")
        self.chips = devices // 2
        me = lax.axis_index("mode")
        self.core = me % 2
        self.chip = me // 2
        self.place = jnp.where(self.core == 0, self.chip, self.chips - 1 - self.chip)
        right = [[(2 * z + c, 2 * z + 2 + c) for z in range(self.chips - 1)] for c in (0, 1)]
        left = [[(j, i) for i, j in pairs] for pairs in right]
        self.streams = (right[0] + left[1], right[1] + left[0])
        self.pairs = [(i, i ^ 1) for i in range(devices)]
        self.order = jnp.asarray(block_order(self.chips))[me]

    def exchange(self, value):
        return lax.ppermute(value, "mode", self.pairs)

    def along(self, stream, value):
        return lax.ppermute(value, "mode", self.streams[stream])

    def chip_at(self, stream, place):
        turned = self.core == stream
        chip = jnp.where(turned, place, self.chips - 1 - place)
        return jnp.clip(chip, 0, self.chips - 1)

    def place_in(self, stream):
        return self.place if stream == 0 else self.chips - 1 - self.place

    def pick(self, arrived, slot):
        chosen = None
        for place in range(self.chips):
            stream, step, _ = slot_sources(self.chips, place)[slot]
            value = arrived[stream][step]
            chosen = value if chosen is None else jnp.where(self.place == place, value, chosen)
        return chosen

    def run(self, own, mine, other):
        theirs = self.exchange(other)

        def term(chip):
            return lax.dynamic_index_in_dim(mine, chip, 0, False) + lax.dynamic_index_in_dim(
                theirs, chip, 0, False
            )

        here, there = [own], [self.exchange(own)]
        arrived = ([], [])
        for step in range(self.chips):
            for stream in (0, 1):
                if step == 0:
                    payload = own
                else:
                    place = self.place_in(stream)
                    added = term(self.chip_at(stream, place + self.chips - step))
                    payload = arrived[stream][-1] + jnp.where(place < step, added, 0.0)
                arrived[stream].append(self.along(stream, payload))
            if step < self.chips - 1:
                block = self.pick(arrived, step)
                here.append(block)
                there.append(self.exchange(block))
        total = arrived[0][-1] + arrived[1][-1] + term(self.chip)
        return here + there, total

    def gather_rows(self, value):
        me = lax.axis_index("mode")
        bit = 1
        while bit < 2 * self.chips:
            pairs = [(i, i ^ bit) for i in range(2 * self.chips)]
            other = lax.ppermute(value, "mode", pairs)
            later = (me // bit) % 2 == 1
            value = jnp.concatenate(
                [jnp.where(later, other, value), jnp.where(later, value, other)], axis=1
            )
            bit *= 2
        return value

    def add_up(self, value):
        bit = 1
        while bit < 2 * self.chips:
            pairs = [(i, i ^ bit) for i in range(2 * self.chips)]
            value = value + lax.ppermute(value, "mode", pairs)
            bit *= 2
        return value


def on_device(distribution, scatter_matrix, velocity, capacity, cell_type):
    modes, cells = distribution.shape
    total_modes = scatter_matrix.shape[0]
    half = cells // 2
    line = Line()
    core = jnp.reshape(line.core, (1,)).astype(jnp.int32)
    weights = capacity[None, :] * velocity
    table = jnp.concatenate(
        [velocity, capacity[None, :], weights, jnp.zeros((3, modes), jnp.float32)], axis=0
    )
    kinds = cell_type[None, :]
    part = jax.ShapeDtypeStruct((modes, half), jnp.float32)

    own_a = distribution[:, :half]
    own_b = distribution[:, half:]
    mine, other = partial_products(scatter_matrix, own_b, core)
    before, after = halo(distribution[:, :HALO].T, distribution[:, -HALO:].T)
    all_weights = jnp.pad(line.gather_rows(weights), ((0, 6), (0, 0)))
    base_a, base_b = stencil_call(
        first_kernel,
        modes,
        cells,
        [distribution, before, after, table, kinds],
        ["rows", "columns", "columns", "columns", "whole"],
        [(part, "rows"), (part, "rows")],
    )
    blocks, sum_b = line.run(own_a, mine, other)
    mid_b = base_b - time_step * sum_b
    mid_a, scattered = whole_product(
        scatter_matrix, blocks, line.order, base_a, time_step, all_weights
    )

    step = 0.5 * time_step
    mine, other = partial_products(scatter_matrix, mid_a, core)
    before, after = halo(mid_a[:, :HALO].T, mid_b[:, -HALO:].T)
    end_a, end_b, flux = stencil_call(
        second_kernel,
        modes,
        cells,
        [distribution, mid_a, mid_b, before, after, table, kinds, scattered],
        ["rows", "rows", "rows", "columns", "columns", "columns", "whole", "columns"],
        [(part, "rows"), (part, "rows"), (jax.ShapeDtypeStruct((8, cells), jnp.float32), "whole")],
    )
    heat_flux = line.add_up(flux[:2]) / jnp.sqrt(jnp.float32(total_modes))
    blocks, sum_a = line.run(mid_b, mine, other)
    (last_b,) = whole_product(scatter_matrix, blocks, line.order, end_b, step)
    updated = jnp.concatenate([end_a - step * sum_a, last_b], axis=1)
    return (updated, heat_flux)


def solution(mesh):
    return jax.shard_map(
        on_device,
        mesh=mesh,
        in_specs=(P("mode", "space"), P(None, "mode"), P(None, "mode"), P("mode"), P("space")),
        out_specs=(P("mode", "space"), P(None, "space")),
        check_vma=False,
    )
```

```python
import functools

import numpy as np

import jax
import jax.numpy as jnp
from jax import lax
from jax.experimental import pallas as pl
from jax.experimental.pallas import tpu as pltpu
from jax.sharding import PartitionSpec as P

NY = 16
HALO = 2 * NY
LANES = 128


relax_rate = 0.5
time_step = 0.5

VMEM = pl.BlockSpec(memory_space=pltpu.VMEM)
SMEM = pl.BlockSpec(memory_space=pltpu.SMEM)
ANY = pl.BlockSpec(memory_space=pl.ANY)
HBM = pl.BlockSpec(memory_space=pltpu.HBM)


class Chain:
    def __init__(self):
        self.last = None

    def __call__(self, kernel, outs, arrays, info=None, places=None, scratch=(), out_specs=None):
        scalars = [] if info is None else [info]
        extra = [] if self.last is None else [self.last]
        skip = len(extra)
        first = len(scalars) + len(arrays)

        def body(*refs):
            kernel(*refs[:first], *refs[first + skip :])

        results = pl.pallas_call(
            body,
            out_shape=[jax.ShapeDtypeStruct(shape, jnp.float32) for shape in outs],
            in_specs=[SMEM] * len(scalars)
            + list(places or [VMEM] * len(arrays))
            + [ANY] * skip,
            out_specs=out_specs or [VMEM] * len(outs),
            scratch_shapes=list(scratch),
            compiler_params=pltpu.CompilerParams(vmem_limit_bytes=16 * 1024 * 1024),
            cost_estimate=pl.CostEstimate(flops=1024, bytes_accessed=1024, transcendentals=0),
            name=getattr(kernel, "func", kernel).__name__,
        )(*scalars, *arrays, *extra)
        self.last = results[0]
        return results


def halves(value):
    high = value.astype(jnp.bfloat16)
    low = (value - high.astype(jnp.float32)).astype(jnp.bfloat16)
    return high, low


def slot_products(at, column, info, matrix, field, mine, other):
    modes = matrix.shape[1]
    cells = mine.shape[1]
    parts = jnp.concatenate(halves(field[:, column : column + cells]), axis=1)
    for k, out in ((1, other), (0, mine)):
        start = pl.multiple_of(info[at + k] * modes, modes)
        both = jnp.dot(
            matrix[pl.ds(start, modes), :], parts, preferred_element_type=jnp.float32
        )
        out[...] = both[:, :cells] + both[:, cells:]


def two_blocks(at, first, last, scale, rows, info, matrix, *refs):
    modes = matrix.shape[1]
    blocks, refs = refs[:2], refs[2:]
    if not first:
        before, refs = refs[0], refs[1:]
    if last:
        base, refs = refs[0], refs[1:]
    total = None if first else before[...]
    for k, block in enumerate(blocks):
        pieces = list(halves(block[:modes].T))
        if rows:
            weights = [
                jnp.concatenate(
                    [
                        block[modes + i : modes + i + 1, :]
                        for i in range(d * modes // LANES, (d + 1) * modes // LANES)
                    ],
                    axis=1,
                )
                for d in range(2)
            ]
            weights.append(jnp.zeros((6, modes), jnp.float32))
            pieces += halves(jnp.concatenate(weights, axis=0))
        left = jnp.concatenate(pieces, axis=0)
        start = pl.multiple_of(info[at + k] * modes, modes)
        term = jnp.dot(left, matrix[pl.ds(start, modes), :], preferred_element_type=jnp.float32)
        total = term if total is None else total + term
    if not last:
        refs[0][...] = total
        return
    cells = base.shape[1]
    value = base[...] - scale * (total[:cells] + total[cells : 2 * cells]).T
    refs[0][...] = value
    if rows:
        refs[1][...] = value.T[:HALO]
        refs[2][...] = total[2 * cells : 2 * cells + 8] + total[2 * cells + 8 :]


def own_rows(distribution, velocity, capacity, out, sem):
    modes, cells = (velocity.shape[1], out.shape[1])
    copy = pltpu.make_async_copy(
        distribution.at[:, pl.ds(0, cells)], out.at[pl.ds(0, modes), :], sem
    )
    copy.start()
    per = modes // LANES
    for d in range(2):
        for i in range(per):
            lanes = slice(i * LANES, (i + 1) * LANES)
            out[modes + d * per + i : modes + d * per + i + 1, :] = (
                velocity[d : d + 1, lanes] * capacity[:, lanes]
            )
    for r in range(modes + 2 * per, out.shape[0]):
        out[r : r + 1, :] = jnp.zeros((1, LANES), jnp.float32)
    copy.wait()


def payload(at, slots, info, arrived, *refs):
    out = refs[-1]

    for k, slot in enumerate(slots):

        @pl.when(info[at] == slot)
        def _(k=k):
            mine, theirs = refs[2 * k], refs[2 * k + 1]
            modes = mine.shape[0]
            out[:modes] = arrived[:modes] + (mine[...] + theirs[...])
            if out.shape[0] > modes:
                out[modes:] = arrived[modes:]

    @pl.when(info[at] < 0)
    def _():
        out[...] = arrived[...]


def pick(at, info, *refs):
    out = refs[-1]
    for k, ref in enumerate(refs[:-1]):

        @pl.when(info[at] == k)
        def _(ref=ref):
            out[...] = ref[...]


def turn_sum(scale, one, two, mine, theirs, base, out, strip):
    modes = mine.shape[0]
    total = one[:modes] + two[:modes] + (mine[...] + theirs[...])
    value = base[...] - scale * total
    out[...] = value
    strip[...] = value.T[-HALO:]


def last_sum(scale, one, two, mine, theirs, base, other, out, value, sems):
    cells = base.shape[1]
    ahead = pltpu.make_async_copy(other, out.at[:, pl.ds(cells, cells)], sems.at[0])
    ahead.start()
    total = one[...] + two[...] + (mine[...] + theirs[...])
    value[...] = base[...] - scale * total
    copy = pltpu.make_async_copy(value, out.at[:, pl.ds(0, cells)], sems.at[1])
    copy.start()
    ahead.wait()
    copy.wait()


def strip_rows(distribution, leading, last):
    cells = distribution.shape[1]
    leading[...] = distribution[:, :LANES].T[:HALO]
    last[...] = distribution[:, cells - LANES :].T[-HALO:]


def still_rate(pieces, before, after, columns, kinds):
    lane = lax.broadcasted_iota(jnp.int32, (1, LANES), 1)
    y = lane % NY
    vx, vy, capacity = (columns[:, i : i + 1] for i in range(3))
    fore_x, back_x = 0.5 * jnp.maximum(vx, 0.0), 0.5 * jnp.minimum(vx, 0.0)
    fore_y, back_y = 0.5 * jnp.maximum(vy, 0.0), 0.5 * jnp.minimum(vy, 0.0)
    centre = 3.0 * (fore_x - back_x + fore_y - back_y)
    padded = [before, *pieces, after]
    rates = []
    for k, value in enumerate(pieces):
        def along_x(offset):
            near = pltpu.roll(value, -offset % LANES, 1)
            if offset < 0:
                return jnp.where(lane < -offset, pltpu.roll(padded[k], -offset, 1), near)
            return jnp.where(
                lane >= LANES - offset, pltpu.roll(padded[k + 2], LANES - offset, 1), near
            )

        def along_y(offset):
            inside = (y + offset >= 0) & (y + offset < NY)
            return jnp.where(inside, pltpu.roll(value, -offset % LANES, 1), 0.0)

        kind = kinds[:, k * LANES : (k + 1) * LANES]
        contact = jnp.where(kind > 0, relax_rate, 0.0)
        source = jnp.where(kind == 1, contact, -contact)
        rate = (
            source * capacity
            - (centre + contact) * value
            + fore_x * (4.0 * along_x(-NY) - along_x(-2 * NY))
            + back_x * (along_x(2 * NY) - 4.0 * along_x(NY))
            + fore_y * (4.0 * along_y(-1) - along_y(-2))
            + back_y * (along_y(2) - 4.0 * along_y(1))
        )
        rates.append(rate)
    return rates


def edges(before, after, rows):
    pad = jnp.zeros((rows.size, LANES - HALO), jnp.float32)
    return (
        jnp.concatenate([pad, before[:, rows].T], axis=1),
        jnp.concatenate([after[:, rows].T, pad], axis=1),
    )


def first_rest(field, before, after, table, kinds, base_a, base_b):
    modes, half = base_a.shape
    block = min(modes, LANES)

    def step(i, _):
        rows = pl.ds(pl.multiple_of(i * block, block), block)
        value = field[rows, :]
        pieces = [value[:, k : k + LANES] for k in range(0, 2 * half, LANES)]
        rates = still_rate(pieces, *edges(before, after, rows), table[:, rows].T, kinds[...])
        bases = [v + time_step * r for v, r in zip(pieces, rates)]
        middle = len(bases) // 2
        base_a[rows, :] = jnp.concatenate(bases[:middle], axis=1)
        base_b[rows, :] = jnp.concatenate(bases[middle:], axis=1)
        return 0

    lax.fori_loop(0, modes // block, step, 0)


def second_rest(
    field, mid_a, mid_b, before, after, table, kinds, scattered, end_a, end_b, flux
):
    modes, half = end_a.shape
    block = min(modes, LANES)
    step_size = 0.5 * time_step
    flux[...] = jnp.zeros_like(flux)

    def step(i, _):
        rows = pl.ds(pl.multiple_of(i * block, block), block)
        value = field[rows, :]
        mids = [
            mid[rows, k : k + LANES] for mid in (mid_a, mid_b) for k in range(0, half, LANES)
        ]
        columns = table[:, rows].T
        rates = still_rate(mids, *edges(before, after, rows), columns, kinds[...])
        taken = step_size * scattered[:, rows].T
        ends = []
        for k, (mid, rate) in enumerate(zip(mids, rates)):
            lanes = slice(k * LANES, (k + 1) * LANES)
            end = 0.5 * (value[:, lanes] + mid) + step_size * rate
            ends.append(end)
            for d in range(2):
                terms = columns[:, 3 + d : 4 + d] * end - taken[:, d : d + 1] * mid
                flux[d : d + 1, lanes] += jnp.sum(terms, axis=0, keepdims=True)
        middle = len(ends) // 2
        end_a[rows, :] = jnp.concatenate(ends[:middle], axis=1)
        end_b[rows, :] = jnp.concatenate(ends[middle:], axis=1)
        return 0

    lax.fori_loop(0, modes // block, step, 0)


def halo(leading, last):
    count = lax.axis_size("space")
    up = [(i, i + 1) for i in range(count - 1)]
    down = [(j, i) for i, j in up]
    before = lax.ppermute(last, "space", up)
    after = lax.ppermute(leading, "space", down)
    return before, after


def block_sources(chips, place):
    found = []
    for step in range(chips - 1):
        if place >= step + 1:
            found.append((0, step, place - 1 - step))
        if place <= chips - 2 - step:
            found.append((1, step, place + 1 + step))
    return found


def sum_targets(chips, chip):
    found = []
    for step in range(1, chips):
        far = chips - step
        found += [t for t in (chip + far, chip - far) if 0 <= t < chips]
    return found + [chip]


class Plan:
    def __init__(self, chips):
        rows = []
        self.choices = [
            sorted({block_sources(chips, p)[s][:2] for p in range(chips)})
            for s in range(chips - 1)
        ]
        self.slots = {}
        for device in range(2 * chips):
            chip, core = device // 2, device % 2
            place = chip if core == 0 else chips - 1 - chip
            blocks = []
            for c in (core, 1 - core):
                p = chip if c == 0 else chips - 1 - chip
                sources = [p] + [q for _, _, q in block_sources(chips, p)]
                blocks.append([2 * (q if c == 0 else chips - 1 - q) + c for q in sources])
            targets = sum_targets(chips, chip)
            row = [b for pair in zip(*blocks) for b in pair]
            row += [b for t in targets for b in (2 * t + core, 2 * t + 1 - core)]
            for stream in (0, 1):
                here = place if stream == 0 else chips - 1 - place
                for step in range(1, chips):
                    slot = -1
                    if here < step:
                        q = here + chips - step
                        slot = targets.index(q if core == stream else chips - 1 - q)
                        self.slots.setdefault((stream, step), set()).add(slot)
                    row.append(slot)
            own = [s[:2] for s in block_sources(chips, place)]
            row += [self.choices[s].index(own[s]) for s in range(chips - 1)]
            rows.append(row)
        self.table = np.array(rows, np.int32)
        self.block = lambda slot: 2 * slot
        self.target = lambda slot: 2 * chips + 2 * slot
        self.sent = lambda stream, step: 4 * chips + stream * (chips - 1) + step - 1
        self.picked = lambda slot: 4 * chips + 2 * (chips - 1) + slot


def on_device(distribution, scatter_matrix, velocity, capacity, cell_type):
    modes, cells = distribution.shape
    total_modes = scatter_matrix.shape[0]
    half = cells // 2
    extra = -(-2 * modes // LANES // 8) * 8
    step_size = 0.5 * time_step
    part = (modes, half)
    devices = lax.axis_size("mode")
    chips = devices // 2
    me = lax.axis_index("mode")
    plan = Plan(chips)
    info = jnp.asarray(plan.table)[me]
    call = Chain()
    right = [[(2 * z + c, 2 * z + 2 + c) for z in range(chips - 1)] for c in (0, 1)]
    left = [[(j, i) for i, j in pairs] for pairs in right]
    streams = (right[0] + left[1], right[1] + left[0])
    across = [(i, i ^ 1) for i in range(devices)]
    cap = capacity[None, :]
    table = jnp.concatenate(
        [velocity, cap, cap * velocity, jnp.zeros((3, modes), jnp.float32)], axis=0
    )
    kinds = cell_type[None, :]

    def exchange(value):
        return lax.ppermute(value, "mode", across)

    def along(stream, value):
        return lax.ppermute(value, "mode", streams[stream])

    class Round:
        def __init__(self, own, scale, rows):
            self.own, self.scale, self.rows = own, scale, rows
            self.arrived = [[along(stream, own)] for stream in (0, 1)]
            self.terms, self.blocks, self.total = [], [], None

        def add_terms(self, field, column):
            slot = len(self.terms)
            kernel = functools.partial(slot_products, plan.target(slot), column)
            mine, other = call(kernel, [part] * 2, [scatter_matrix, field], info)
            self.terms.append((mine, exchange(other)))

        def take_own(self):
            self.blocks.append((self.own, exchange(self.own)))

        def send(self, stream, step):
            slots = sorted(plan.slots[stream, step])
            arrived = self.arrived[stream][step - 1]
            kernel = functools.partial(payload, plan.sent(stream, step), slots)
            arrays = [arrived] + [a for s in slots for a in self.terms[s]]
            (value,) = call(kernel, [arrived.shape], arrays, info)
            self.arrived[stream].append(along(stream, value))

        def take(self, slot):
            arrays = [self.arrived[stream][step] for stream, step in plan.choices[slot - 1]]
            kernel = functools.partial(pick, plan.picked(slot - 1))
            (here,) = call(kernel, [arrays[0].shape], arrays, info)
            self.blocks.append((here, exchange(here)))

        def multiply(self, slot, base=None):
            first, last = slot == 0, base is not None
            kernel = functools.partial(
                two_blocks, plan.block(slot), first, last, self.scale, self.rows
            )
            arrays = [scatter_matrix, *self.blocks[slot]]
            arrays += [] if first else [self.total]
            arrays += [base] if last else []
            outs = [(2 * half + (16 if self.rows else 0), modes)]
            if last:
                outs = [part, (HALO, modes), (8, modes)] if self.rows else [part]
            results = call(kernel, outs, arrays, info)
            self.total = results[0]
            return results

        def ends(self):
            return [self.arrived[0][-1], self.arrived[1][-1], *self.terms[-1]]

    (own,) = call(
        own_rows,
        [(modes + extra, half)],
        [distribution, velocity, cap],
        places=[HBM, VMEM, VMEM],
        scratch=[pltpu.SemaphoreType.DMA(())],
    )
    one = Round(own, time_step, True)
    for slot in range(chips - 1):
        one.add_terms(distribution, half)
    one.take_own()
    for step in range(1, chips):
        if step == 1:
            one.take(step)
        for stream in (0, 1):
            one.send(stream, step)
        if step > 1:
            one.take(step)
        if step == 1:
            one.add_terms(distribution, half)
            strips = halo(*call(strip_rows, [(HALO, modes)] * 2, [distribution]))
        one.multiply(step - 1)
        if step == min(2, chips - 1):
            base_a, base_b = call(
                first_rest, [part] * 2, [distribution, *strips, table, kinds]
            )
    mid_a, leading, scattered = one.multiply(chips - 1, base_a)

    two = Round.__new__(Round)
    two.terms = []
    two.add_terms(mid_a, 0)
    mid_b, last = call(
        functools.partial(turn_sum, time_step), [part, (HALO, modes)], [*one.ends(), base_b]
    )
    terms = two.terms
    two = Round(mid_b, step_size, False)
    two.terms = terms
    for slot in range(1, chips - 1):
        two.add_terms(mid_a, 0)
    two.take_own()
    strips = halo(leading, last)
    for step in range(1, chips):
        if step == 1:
            two.take(step)
        for stream in (0, 1):
            two.send(stream, step)
        if step > 1:
            two.take(step)
        if step == 1:
            two.add_terms(mid_a, 0)
        two.multiply(step - 1)
        if step == min(2, chips - 1):
            end_a, end_b, flux = call(
                second_rest,
                [part, part, (8, cells)],
                [distribution, mid_a, mid_b, *strips, table, kinds, scattered],
            )
    flux = flux[:2]
    bit = 1
    while bit < devices:
        flux = flux + lax.ppermute(flux, "mode", [(i, i ^ bit) for i in range(devices)])
        bit *= 2
    heat_flux = flux / jnp.sqrt(jnp.float32(total_modes))
    (last_b,) = two.multiply(chips - 1, end_b)
    (updated,) = call(
        functools.partial(last_sum, step_size),
        [(modes, cells)],
        [*two.ends(), end_a, last_b],
        scratch=[pltpu.VMEM(part, jnp.float32), pltpu.SemaphoreType.DMA((2,))],
        out_specs=[HBM],
    )
    return (updated, heat_flux)


def solution(mesh):
    return jax.shard_map(
        on_device,
        mesh=mesh,
        in_specs=(P("mode", "space"), P(None, "mode"), P(None, "mode"), P("mode"), P("space")),
        out_specs=(P("mode", "space"), P(None, "space")),
        check_vma=False,
    )
```

```python
import functools

import numpy as np

import jax
import jax.numpy as jnp
from jax import lax
from jax.experimental import pallas as pl
from jax.experimental.pallas import tpu as pltpu
from jax.sharding import PartitionSpec as P

NY = 16
HALO = 2 * NY
LANES = 128
SMALL = 32


relax_rate = 0.5
time_step = 0.5

VMEM = pl.BlockSpec(memory_space=pltpu.VMEM)
ANY = pl.BlockSpec(memory_space=pl.ANY)
HBM = pl.BlockSpec(memory_space=pltpu.HBM)


class Chain:
    def __init__(self):
        self.last = None

    def __call__(self, kernel, outs, arrays, places=None, scratch=(), out_specs=None, room=16):
        extra = [] if self.last is None else [self.last]
        skip = len(extra)
        first = len(arrays)

        def body(*refs):
            kernel(*refs[:first], *refs[first + skip :])

        results = pl.pallas_call(
            body,
            out_shape=[
                jax.ShapeDtypeStruct(shape, jnp.float32) if isinstance(shape, tuple) else shape
                for shape in outs
            ],
            in_specs=list(places or [VMEM] * len(arrays)) + [ANY] * skip,
            out_specs=out_specs or [VMEM] * len(outs),
            scratch_shapes=list(scratch),
            compiler_params=pltpu.CompilerParams(vmem_limit_bytes=room * 1024 * 1024),
            cost_estimate=pl.CostEstimate(flops=1024, bytes_accessed=1024, transcendentals=0),
            name=getattr(kernel, "func", kernel).__name__,
        )(*arrays, *extra)
        self.last = results[0]
        return results


def halves(value):
    high = value.astype(jnp.bfloat16)
    low = (value - high.astype(jnp.float32)).astype(jnp.bfloat16)
    return high, low


def for_device(numbers):
    if len(set(numbers)) == 1:
        return numbers[0]
    me = lax.axis_index("mode")
    chosen = jnp.int32(numbers[0])
    for device, number in enumerate(numbers[1:], 1):
        chosen = jnp.where(me == device, jnp.int32(number), chosen)
    return chosen


def rows_of(matrix, block):
    modes = matrix.shape[1]
    return pl.ds(pl.multiple_of(block * modes, modes), modes)


def one_slot(blocks, matrix, parts, mine, other):
    cells = mine.shape[1]
    for block, out in zip(blocks, (mine, other)):
        both = jnp.dot(matrix[rows_of(matrix, block), :], parts, preferred_element_type=jnp.float32)
        out[...] = both[:, :cells] + both[:, cells:]


def slot_products(blocks, matrix, field, mine, other):
    blocks = [for_device(numbers) for numbers in blocks]
    parts = jnp.concatenate(halves(field[...]), axis=1)
    one_slot(blocks, matrix, parts, mine, other)


def load_and_products(blocks, column, matrix, distribution, *refs):
    slots = len(blocks)
    outs, (held, field, sems) = refs[: 2 * slots], refs[2 * slots :]
    cells = field.shape[1]
    start = pltpu.make_async_copy(
        distribution.at[:, pl.ds(column, cells)], field, sems.at[2 * slots]
    )
    start.start()
    blocks = [[for_device(numbers) for numbers in pair] for pair in blocks]
    copies = []
    for slot, pair in enumerate(blocks):
        for k, block in enumerate(pair):
            rows = rows_of(held, block)
            copies.append(
                pltpu.make_async_copy(
                    matrix.at[rows, :], held.at[rows, :], sems.at[2 * slot + k]
                )
            )
            copies[-1].start()
    start.wait()
    parts = jnp.concatenate(halves(field[...]), axis=1)
    for slot, pair in enumerate(blocks):
        for k in range(2):
            copies[2 * slot + k].wait()
        one_slot(pair, held, parts, outs[2 * slot], outs[2 * slot + 1])


def two_blocks(numbers, first, last, scale, rows, matrix, *refs):
    modes = matrix.shape[1]
    blocks, refs = refs[:2], refs[2:]
    if not first:
        before, refs = refs[0], refs[1:]
    if last:
        base, refs = refs[0], refs[1:]
    total = None if first else before[...]
    for k, block in enumerate(blocks):
        pieces = list(halves(block[:modes].T))
        if rows:
            weights = [
                jnp.concatenate(
                    [
                        block[modes + i : modes + i + 1, :]
                        for i in range(d * modes // LANES, (d + 1) * modes // LANES)
                    ],
                    axis=1,
                )
                for d in range(2)
            ]
            weights.append(jnp.zeros((6, modes), jnp.float32))
            pieces += halves(jnp.concatenate(weights, axis=0))
        left = jnp.concatenate(pieces, axis=0)
        there = rows_of(matrix, for_device(numbers[k]))
        term = jnp.dot(left, matrix[there, :], preferred_element_type=jnp.float32)
        total = term if total is None else total + term
    if not last:
        refs[0][...] = total
        return
    cells = base.shape[1]
    value = base[...] - scale * (total[:cells] + total[cells : 2 * cells]).T
    refs[0][...] = value
    if rows:
        refs[1][...] = value.T[:HALO]
        refs[2][...] = total[2 * cells : 2 * cells + 8] + total[2 * cells + 8 :]


def own_rows(distribution, velocity, capacity, out, speeds, weight, sems):
    modes, cells = (velocity.shape[1], out.shape[1])
    copies = [
        pltpu.make_async_copy(velocity, speeds, sems.at[0]),
        pltpu.make_async_copy(capacity, weight, sems.at[1]),
        pltpu.make_async_copy(
            distribution.at[:, pl.ds(0, cells)], out.at[pl.ds(0, modes), :], sems.at[2]
        ),
    ]
    for copy in copies:
        copy.start()
    for copy in copies[:2]:
        copy.wait()
    per = modes // LANES
    out[modes:] = jnp.zeros((out.shape[0] - modes, LANES), jnp.float32)
    for d in range(2):
        for i in range(per):
            lanes = slice(i * LANES, (i + 1) * LANES)
            out[modes + d * per + i : modes + d * per + i + 1, :] = (
                speeds[d : d + 1, lanes] * weight[:, lanes]
            )
    copies[2].wait()


def payload(numbers, slots, arrived, *refs):
    out = refs[-1]
    slot_here = for_device(numbers)

    for k, slot in enumerate(slots):

        @pl.when(slot_here == slot)
        def _(k=k):
            mine, theirs = refs[2 * k], refs[2 * k + 1]
            modes = mine.shape[0]
            out[:modes] = arrived[:modes] + (mine[...] + theirs[...])
            if out.shape[0] > modes:
                out[modes:] = arrived[modes:]

    @pl.when(slot_here < 0)
    def _():
        out[...] = arrived[...]


def pick(numbers, *refs):
    out = refs[-1]
    choice = for_device(numbers)
    for k, ref in enumerate(refs[:-1]):

        @pl.when(choice == k)
        def _(ref=ref):
            out[...] = ref[...]


def add(one, two, out):
    out[...] = one[...] + two[...]


def turn_sum(scale, one, two, mine, theirs, base, out, strip):
    modes = mine.shape[0]
    total = one[:modes] + two[:modes] + (mine[...] + theirs[...])
    value = base[...] - scale * total
    out[...] = value
    strip[...] = value.T[-HALO:]


def last_sum(scale, one, two, mine, theirs, base, other, out, value, sems):
    cells = base.shape[1]
    ahead = pltpu.make_async_copy(other, out.at[:, pl.ds(cells, cells)], sems.at[0])
    ahead.start()
    total = one[...] + two[...] + (mine[...] + theirs[...])
    value[...] = base[...] - scale * total
    copy = pltpu.make_async_copy(value, out.at[:, pl.ds(0, cells)], sems.at[1])
    copy.start()
    ahead.wait()
    copy.wait()


def strip_rows(distribution, leading, last):
    cells = distribution.shape[1]
    leading[...] = distribution[:, :LANES].T[:HALO]
    last[...] = distribution[:, cells - LANES :].T[-HALO:]


def strip_pairs(leading, last, out_even, out_odd):
    even = lax.axis_index("space") % 2 == 0

    @pl.when(even)
    def _():
        out_even[...] = last[...]
        out_odd[...] = leading[...]

    @pl.when(jnp.logical_not(even))
    def _():
        out_even[...] = leading[...]
        out_odd[...] = last[...]


def still_rate(pieces, before, after, columns, kinds):
    lane = lax.broadcasted_iota(jnp.int32, (1, LANES), 1)
    y = lane % NY
    vx, vy, capacity = (columns[:, i : i + 1] for i in range(3))
    fore_x, back_x = 0.5 * jnp.maximum(vx, 0.0), 0.5 * jnp.minimum(vx, 0.0)
    fore_y, back_y = 0.5 * jnp.maximum(vy, 0.0), 0.5 * jnp.minimum(vy, 0.0)
    centre = 3.0 * (fore_x - back_x + fore_y - back_y)
    padded = [before, *pieces, after]
    rates = []
    for k, value in enumerate(pieces):
        def along_x(offset):
            near = pltpu.roll(value, -offset % LANES, 1)
            if offset < 0:
                return jnp.where(lane < -offset, pltpu.roll(padded[k], -offset, 1), near)
            return jnp.where(
                lane >= LANES - offset, pltpu.roll(padded[k + 2], LANES - offset, 1), near
            )

        def along_y(offset):
            inside = (y + offset >= 0) & (y + offset < NY)
            return jnp.where(inside, pltpu.roll(value, -offset % LANES, 1), 0.0)

        kind = kinds[:, k * LANES : (k + 1) * LANES]
        contact = jnp.where(kind > 0, relax_rate, 0.0)
        source = jnp.where(kind == 1, contact, -contact)
        rate = (
            source * capacity
            - (centre + contact) * value
            + fore_x * (4.0 * along_x(-NY) - along_x(-2 * NY))
            + back_x * (along_x(2 * NY) - 4.0 * along_x(NY))
            + fore_y * (4.0 * along_y(-1) - along_y(-2))
            + back_y * (along_y(2) - 4.0 * along_y(1))
        )
        rates.append(rate)
    return rates


def edges(came_even, came_odd, rows):
    even = lax.axis_index("space") % 2 == 0
    from_even, from_odd = came_even[:, rows].T, came_odd[:, rows].T
    before = jnp.where(even, from_odd, from_even)
    after = jnp.where(even, from_even, from_odd)
    pad = jnp.zeros((before.shape[0], LANES - HALO), jnp.float32)
    return (
        jnp.concatenate([pad, before], axis=1),
        jnp.concatenate([after, pad], axis=1),
    )


def pieces_of(value):
    return [value[:, k : k + LANES] for k in range(0, value.shape[1], LANES)]


def first_rest(field, came_even, came_odd, table, kinds, base_a, base_b):
    modes, half = base_a.shape
    block = min(modes, LANES)
    small = min(block, SMALL)

    def step(i, _):
        start = pl.multiple_of(i * block, block)
        before, after = edges(came_even, came_odd, pl.ds(start, block))
        columns = table[:, pl.ds(start, block)].T
        for k in range(0, block, small):
            rows = pl.ds(pl.multiple_of(start + k, small), small)
            here = slice(k, k + small)
            pieces = pieces_of(field[rows, :])
            rates = still_rate(pieces, before[here], after[here], columns[here], kinds[...])
            middle = len(pieces) // 2
            for j, (piece, rate) in enumerate(zip(pieces, rates)):
                out, at = (base_a, j) if j < middle else (base_b, j - middle)
                out[rows, at * LANES : (at + 1) * LANES] = piece + time_step * rate
        return 0

    lax.fori_loop(0, modes // block, step, 0)


def second_rest(
    field, mid_a, mid_b, came_even, came_odd, table, kinds, scattered, end_a, end_b, flux
):
    modes, half = end_a.shape
    cells = field.shape[1]
    block = min(modes, LANES)
    small = min(block, SMALL)
    step_size = 0.5 * time_step

    def step(i, sums):
        start = pl.multiple_of(i * block, block)
        before, after = edges(came_even, came_odd, pl.ds(start, block))
        columns = table[:, pl.ds(start, block)].T
        taken = step_size * scattered[:, pl.ds(start, block)].T
        sums = list(sums)
        for k in range(0, block, small):
            rows = pl.ds(pl.multiple_of(start + k, small), small)
            here = slice(k, k + small)
            values = pieces_of(field[rows, :])
            mids = pieces_of(mid_a[rows, :]) + pieces_of(mid_b[rows, :])
            rates = still_rate(mids, before[here], after[here], columns[here], kinds[...])
            middle = len(mids) // 2
            for j, (value, mid, rate) in enumerate(zip(values, mids, rates)):
                out, at = (end_a, j) if j < middle else (end_b, j - middle)
                end = 0.5 * (value + mid) + step_size * rate
                out[rows, at * LANES : (at + 1) * LANES] = end
                for d in range(2):
                    terms = columns[here, 3 + d : 4 + d] * end - taken[here, d : d + 1] * mid
                    folded = sum(terms[r : r + 8] for r in range(0, small, 8))
                    sums[2 * j + d] = sums[2 * j + d] + folded
        return tuple(sums)

    zero = jnp.zeros((8, LANES), jnp.float32)
    sums = lax.fori_loop(0, modes // block, step, (zero,) * (2 * cells // LANES))
    for j in range(cells // LANES):
        for d in range(2):
            flux[d : d + 1, j * LANES : (j + 1) * LANES] = jnp.sum(
                sums[2 * j + d], axis=0, keepdims=True
            )


def paired(to_even, to_odd):
    count = lax.axis_size("space")
    came = []
    for first, value in enumerate((to_even, to_odd)):
        pairs = [(i, i + 1) for i in range(first, count - 1, 2)]
        came.append(lax.ppermute(value, "space", pairs + [(j, i) for i, j in pairs]))
    return came


class Plan:
    def __init__(self, chips):
        self.chips = chips
        self.devices = range(2 * chips)
        sources = [self.sources(d) for d in self.devices]
        targets = [self.targets(d // 2) for d in self.devices]
        self.blocks = [
            [
                [2 * sources[e][slot][2] + e % 2 for e in (d ^ other for d in self.devices)]
                for other in (0, 1)
            ]
            for slot in range(chips)
        ]
        self.rows = [
            [[2 * targets[d][slot] + (d % 2 ^ other) for d in self.devices] for other in (0, 1)]
            for slot in range(chips)
        ]
        self.choices = [
            sorted({sources[d][slot][:2] for d in self.devices}) for slot in range(chips)
        ]
        self.picked = [
            [self.choices[slot].index(sources[d][slot][:2]) for d in self.devices]
            for slot in range(chips)
        ]
        self.sent = {}
        for stream in (0, 1):
            for step in range(1, chips):
                numbers = []
                for d in self.devices:
                    way = self.way(d, stream)
                    place = d // 2 if way > 0 else chips - 1 - d // 2
                    target = d // 2 + way * (chips - step)
                    numbers.append(targets[d].index(target) if place < step else -1)
                self.sent[stream, step] = numbers
        self.pairs = []
        for stream in (0, 1):
            up = [
                (d, d + 2) for d in self.devices[:-2] if self.way(d, stream) > 0
            ]
            self.pairs.append(up + [(j, i) for i, j in up])

    def way(self, device, stream):
        return 1 if (device // 2 + device % 2 + stream) % 2 == 0 else -1

    def sources(self, device):
        found = [(-1, -1, device // 2)]
        for step in range(self.chips - 1):
            for stream in (step % 2, 1 - step % 2):
                chip = device // 2 + self.way(device, stream) * (step + 1)
                if 0 <= chip < self.chips:
                    found.append((stream, step, chip))
        return found

    def targets(self, chip):
        found = []
        for step in range(1, self.chips):
            far = self.chips - step
            found += [t for t in (chip + far, chip - far) if 0 <= t < self.chips]
        return found + [chip]


def on_device(distribution, scatter_matrix, velocity, capacity, cell_type):
    modes, cells = distribution.shape
    total_modes = scatter_matrix.shape[0]
    half = cells // 2
    extra = -(-2 * modes // LANES // 8) * 8
    step_size = 0.5 * time_step
    part = (modes, half)
    devices = lax.axis_size("mode")
    chips = devices // 2
    plan = Plan(chips)
    call = Chain()
    across = [(i, i ^ 1) for i in range(devices)]
    cap = capacity[None, :]
    table = jnp.concatenate(
        [velocity, cap, cap * velocity, jnp.zeros((3, modes), jnp.float32)], axis=0
    )
    kinds = cell_type[None, :]

    def exchange(value):
        return lax.ppermute(value, "mode", across)

    def along(stream, value):
        return lax.ppermute(value, "mode", plan.pairs[stream])

    class Round:
        def __init__(self, matrix, scale, rows):
            self.matrix, self.scale, self.rows = matrix, scale, rows
            self.terms, self.total = [], None

        def begin(self, own):
            self.own = own
            self.arrived = [[along(0, own)], [along(1, own)]]
            self.blocks = []

        def add_terms(self, field):
            kernel = functools.partial(slot_products, plan.rows[len(self.terms)])
            mine, other = call(kernel, [part] * 2, [self.matrix, field])
            self.terms.append((mine, exchange(other)))

        def take_own(self):
            self.blocks.append((self.own, exchange(self.own)))

        def send(self, step):
            sent = {}
            for stream in (step % 2, 1 - step % 2):
                numbers = plan.sent[stream, step]
                slots = sorted({n for n in numbers if n >= 0})
                arrived = self.arrived[1 - stream][step - 1]
                kernel = functools.partial(payload, numbers, slots)
                arrays = [arrived] + [a for s in slots for a in self.terms[s]]
                (value,) = call(kernel, [arrived.shape], arrays)
                sent[stream] = along(stream, value)
            for stream in (0, 1):
                self.arrived[stream].append(sent[stream])

        def take(self, slot):
            arrays = [self.arrived[stream][step] for stream, step in plan.choices[slot]]
            kernel = functools.partial(pick, plan.picked[slot])
            (here,) = call(kernel, [arrays[0].shape], arrays)
            self.blocks.append((here, exchange(here)))

        def multiply(self, slot, base=None):
            first, last = slot == 0, base is not None
            kernel = functools.partial(
                two_blocks, plan.blocks[slot], first, last, self.scale, self.rows
            )
            arrays = [self.matrix, *self.blocks[slot]]
            arrays += [] if first else [self.total]
            arrays += [base] if last else []
            outs = [(2 * half + (16 if self.rows else 0), modes)]
            if last:
                outs = [part, (HALO, modes), (8, modes)] if self.rows else [part]
            results = call(kernel, outs, arrays)
            self.total = results[0]
            return results

        def ends(self):
            return [self.arrived[0][-1], self.arrived[1][-1], *self.terms[-1]]

    (own,) = call(
        own_rows,
        [(modes + extra, half)],
        [distribution, velocity, cap],
        places=[HBM] * 3,
        scratch=[
            pltpu.VMEM((2, modes), jnp.float32),
            pltpu.VMEM((1, modes), jnp.float32),
            pltpu.SemaphoreType.DMA((3,)),
        ],
        room=56,
    )
    one = Round(None, time_step, True)
    one.begin(own)
    *terms, matrix = call(
        functools.partial(load_and_products, plan.rows, half),
        [part] * (2 * chips) + [jax.ShapeDtypeStruct(scatter_matrix.shape, jnp.bfloat16)],
        [scatter_matrix, distribution],
        places=[HBM] * 2,
        scratch=[
            pltpu.VMEM(part, jnp.float32),
            pltpu.SemaphoreType.DMA((2 * chips + 1,)),
        ],
        room=28,
    )
    one.matrix = matrix
    one.terms = [(terms[2 * s], exchange(terms[2 * s + 1])) for s in range(chips)]
    one.take_own()
    for step in range(1, chips):
        if step in (1, chips - 1):
            one.take(step)
        one.send(step)
        if step not in (1, chips - 1):
            one.take(step)
        if step == 1:
            strips = call(strip_rows, [(HALO, modes)] * 2, [distribution])
            strips = paired(*call(strip_pairs, [(HALO, modes)] * 2, strips))
        one.multiply(step - 1)
        if step == min(2, chips - 1):
            base_a, base_b = call(
                first_rest, [part] * 2, [distribution, *strips, table, kinds]
            )
    mid_a, leading, scattered = one.multiply(chips - 1, base_a)

    two = Round(matrix, step_size, False)
    two.add_terms(mid_a)
    mid_b, last = call(
        functools.partial(turn_sum, time_step), [part, (HALO, modes)], [*one.ends(), base_b]
    )
    two.begin(mid_b)
    for slot in range(1, chips - 1):
        two.add_terms(mid_a)
    two.take_own()
    strips = paired(*call(strip_pairs, [(HALO, modes)] * 2, [leading, last]))
    for step in range(1, chips):
        if step in (1, chips - 1):
            two.take(step)
        two.send(step)
        if step not in (1, chips - 1):
            two.take(step)
        if step == 1:
            two.add_terms(mid_a)
        two.multiply(step - 1)
        if step == 1:
            end_a, end_b, flux = call(
                second_rest,
                [part, part, (2, cells)],
                [distribution, mid_a, mid_b, *strips, table, kinds, scattered],
            )
        else:
            flux = sum_pairs(call, flux, devices, step - 1, chips - 1)
    heat_flux = flux / jnp.sqrt(jnp.float32(total_modes))
    (last_b,) = two.multiply(chips - 1, end_b)
    (updated,) = call(
        functools.partial(last_sum, step_size),
        [(modes, cells)],
        [*two.ends(), end_a, last_b],
        scratch=[pltpu.VMEM(part, jnp.float32), pltpu.SemaphoreType.DMA((2,))],
        out_specs=[HBM],
    )
    return (updated, heat_flux)


def sum_pairs(call, value, devices, turn, turns):
    bits = [1 << k for k in range(devices.bit_length() - 1)]
    share = -(-len(bits) // (turns - 1))
    for bit in bits[(turn - 1) * share : turn * share]:
        came = lax.ppermute(value, "mode", [(i, i ^ bit) for i in range(devices)])
        (value,) = call(add, [value.shape], [value, came])
    return value


def solution(mesh):
    return jax.shard_map(
        on_device,
        mesh=mesh,
        in_specs=(P("mode", "space"), P(None, "mode"), P(None, "mode"), P("mode"), P("space")),
        out_specs=(P("mode", "space"), P(None, "space")),
        check_vma=False,
    )
```

```python
import functools

import numpy as np

import jax
import jax.numpy as jnp
from jax import lax
from jax.experimental import pallas as pl
from jax.experimental.pallas import tpu as pltpu
from jax.sharding import PartitionSpec as P

NY = 16
HALO = 2 * NY
LANES = 128
BLOCK = 512


relax_rate = 0.5
time_step = 0.5

VMEM = pl.BlockSpec(memory_space=pltpu.VMEM)
ANY = pl.BlockSpec(memory_space=pl.ANY)
HBM = pl.BlockSpec(memory_space=pltpu.HBM)


class Chain:
    def __init__(self):
        self.last = None

    def __call__(self, kernel, outs, arrays, places=None, scratch=(), out_specs=None, room=16):
        extra = [] if self.last is None else [self.last]
        skip = len(extra)
        first = len(arrays)

        def body(*refs):
            kernel(*refs[:first], *refs[first + skip :])

        results = pl.pallas_call(
            body,
            out_shape=[
                jax.ShapeDtypeStruct(shape, jnp.float32) if isinstance(shape, tuple) else shape
                for shape in outs
            ],
            in_specs=list(places or [VMEM] * len(arrays)) + [ANY] * skip,
            out_specs=out_specs or [VMEM] * len(outs),
            scratch_shapes=list(scratch),
            compiler_params=pltpu.CompilerParams(vmem_limit_bytes=room * 1024 * 1024),
            cost_estimate=pl.CostEstimate(flops=1024, bytes_accessed=1024, transcendentals=0),
            name=getattr(kernel, "func", kernel).__name__,
        )(*arrays, *extra)
        self.last = results[0]
        return results


def halves(value):
    high = value.astype(jnp.bfloat16)
    low = (value - high.astype(jnp.float32)).astype(jnp.bfloat16)
    return high, low


def for_device(numbers):
    if len(set(numbers)) == 1:
        return numbers[0]
    me = lax.axis_index("mode")
    chosen = jnp.int32(numbers[0])
    for device, number in enumerate(numbers[1:], 1):
        chosen = jnp.where(me == device, jnp.int32(number), chosen)
    return chosen


def rows_of(matrix, block):
    modes = matrix.shape[1]
    return pl.ds(pl.multiple_of(block * modes, modes), modes)


def one_slot(blocks, matrix, parts, mine, other):
    cells = mine.shape[1]
    for block, out in zip(blocks, (mine, other)):
        both = jnp.dot(matrix[rows_of(matrix, block), :], parts, preferred_element_type=jnp.float32)
        out[...] = both[:, :cells] + both[:, cells:]


def slot_products(blocks, matrix, field, mine, other):
    blocks = [for_device(numbers) for numbers in blocks]
    parts = jnp.concatenate(halves(field[...]), axis=1)
    one_slot(blocks, matrix, parts, mine, other)


def load_and_products(blocks, column, matrix, distribution, *refs):
    slots = len(blocks)
    outs, (held, field, sems) = refs[: 2 * slots], refs[2 * slots :]
    cells = field.shape[1]
    start = pltpu.make_async_copy(
        distribution.at[:, pl.ds(column, cells)], field, sems.at[2 * slots]
    )
    start.start()
    blocks = [[for_device(numbers) for numbers in pair] for pair in blocks]
    copies = []
    for slot, pair in enumerate(blocks):
        for k, block in enumerate(pair):
            rows = rows_of(held, block)
            copies.append(
                pltpu.make_async_copy(
                    matrix.at[rows, :], held.at[rows, :], sems.at[2 * slot + k]
                )
            )
            copies[-1].start()
    start.wait()
    parts = jnp.concatenate(halves(field[...]), axis=1)
    for slot, pair in enumerate(blocks):
        for k in range(2):
            copies[2 * slot + k].wait()
        one_slot(pair, held, parts, outs[2 * slot], outs[2 * slot + 1])


def two_blocks(numbers, parts, first, last, scale, rows, matrix, *refs):
    modes = matrix.shape[1]
    blocks, refs = [[refs[0]], refs[1 : 1 + parts]], refs[1 + parts :]
    if not first:
        before, refs = refs[0], refs[1:]
    if last:
        base, refs = refs[0], refs[1:]
    total = None if first else before[...]
    for k, pieces in enumerate(blocks):
        block = jnp.concatenate([piece[...] for piece in pieces], axis=0)
        pieces = list(halves(block[:modes].T))
        if rows:
            weights = [
                jnp.concatenate(
                    [
                        block[modes + i : modes + i + 1, :]
                        for i in range(d * modes // LANES, (d + 1) * modes // LANES)
                    ],
                    axis=1,
                )
                for d in range(2)
            ]
            weights.append(jnp.zeros((6, modes), jnp.float32))
            pieces += halves(jnp.concatenate(weights, axis=0))
        left = jnp.concatenate(pieces, axis=0)
        there = rows_of(matrix, for_device(numbers[k]))
        term = jnp.dot(left, matrix[there, :], preferred_element_type=jnp.float32)
        total = term if total is None else total + term
    if not last:
        refs[0][...] = total
        return
    cells = base.shape[1]
    value = base[...] - scale * (total[:cells] + total[cells : 2 * cells]).T
    refs[0][...] = value
    if rows:
        refs[1][...] = value.T[:HALO]
        refs[2][...] = total[2 * cells : 2 * cells + 8] + total[2 * cells + 8 :]


def own_rows(distribution, velocity, capacity, out, speeds, weight, sems):
    modes, cells = (velocity.shape[1], out.shape[1])
    copies = [
        pltpu.make_async_copy(velocity, speeds, sems.at[0]),
        pltpu.make_async_copy(capacity, weight, sems.at[1]),
        pltpu.make_async_copy(
            distribution.at[:, pl.ds(0, cells)], out.at[pl.ds(0, modes), :], sems.at[2]
        ),
    ]
    for copy in copies:
        copy.start()
    for copy in copies[:2]:
        copy.wait()
    per = modes // LANES
    out[modes:] = jnp.zeros((out.shape[0] - modes, LANES), jnp.float32)
    for d in range(2):
        for i in range(per):
            lanes = slice(i * LANES, (i + 1) * LANES)
            out[modes + d * per + i : modes + d * per + i + 1, :] = (
                speeds[d : d + 1, lanes] * weight[:, lanes]
            )
    copies[2].wait()


def payload(numbers, slots, arrived, *refs):
    out = refs[-1]
    slot_here = for_device(numbers)

    for k, slot in enumerate(slots):

        @pl.when(slot_here == slot)
        def _(k=k):
            terms = refs[k]
            modes = terms.shape[0]
            out[:modes] = arrived[:modes] + terms[...]
            if out.shape[0] > modes:
                out[modes:] = arrived[modes:]

    @pl.when(slot_here < 0)
    def _():
        out[...] = arrived[...]


def pick(numbers, *refs):
    out = refs[-1]
    choice = for_device(numbers)
    for k, ref in enumerate(refs[:-1]):

        @pl.when(choice == k)
        def _(ref=ref):
            out[...] = ref[...]


def add(one, two, out):
    out[...] = one[...] + two[...]


def turn_sum(scale, one, two, terms, base, out, strip):
    modes = terms.shape[0]
    total = one[:modes] + two[:modes] + terms[...]
    value = base[...] - scale * total
    out[...] = value
    strip[...] = value.T[-HALO:]


def last_sum(scale, one, two, terms, base, other, out, value, sems):
    cells = base.shape[1]
    ahead = pltpu.make_async_copy(other, out.at[:, pl.ds(cells, cells)], sems.at[0])
    ahead.start()
    total = one[...] + two[...] + terms[...]
    value[...] = base[...] - scale * total
    copy = pltpu.make_async_copy(value, out.at[:, pl.ds(0, cells)], sems.at[1])
    copy.start()
    ahead.wait()
    copy.wait()


def strip_rows(distribution, leading, last):
    cells = distribution.shape[1]
    leading[...] = distribution[:, :LANES].T[:HALO]
    last[...] = distribution[:, cells - LANES :].T[-HALO:]


def strip_pairs(leading, last, out_even, out_odd):
    even = lax.axis_index("space") % 2 == 0

    @pl.when(even)
    def _():
        out_even[...] = last[...]
        out_odd[...] = leading[...]

    @pl.when(jnp.logical_not(even))
    def _():
        out_even[...] = leading[...]
        out_odd[...] = last[...]


def differences(cells):
    columns = cells // NY
    own, strip = np.zeros((cells, 4 * cells)), np.zeros((2 * HALO, 4 * cells))
    for x in range(columns):
        for y in range(NY):
            cell = x * NY + y
            for way in (-1, 1):
                for far, factor in enumerate((3.0, -4.0, 1.0)):
                    at_x, at_y = x + way * far, y + way * far
                    first = cell + (0 if way < 0 else cells)
                    factor = -way * factor
                    if at_x < 0:
                        strip[(at_x + 2) * NY + y, first] = factor
                    elif at_x >= columns:
                        strip[HALO + (at_x - columns) * NY + y, first] = factor
                    else:
                        own[at_x * NY + y, first] = factor
                    if 0 <= at_y < NY:
                        own[x * NY + at_y, first + 2 * cells] = factor
    return np.concatenate([own, own, strip, strip]).astype(jnp.bfloat16)


def strip_columns(came_even, came_odd):
    even = lax.axis_index("space") % 2 == 0
    before = jnp.where(even, came_odd[...], came_even[...])
    after = jnp.where(even, came_even[...], came_odd[...])
    parts = halves(jnp.concatenate([before, after], axis=0))
    return jnp.concatenate([p.astype(jnp.float32) for p in parts], axis=0).T.astype(jnp.bfloat16)


def still_rate(field, strip, operators, columns, kinds):
    cells = field.shape[1]
    left = jnp.concatenate([*halves(field), strip], axis=1)
    steps = jnp.dot(left, operators[...], preferred_element_type=jnp.float32)
    vx, vy, capacity = (columns[:, i : i + 1] for i in range(3))
    speeds = (jnp.maximum(vx, 0.0), jnp.minimum(vx, 0.0))
    speeds += (jnp.maximum(vy, 0.0), jnp.minimum(vy, 0.0))
    contact = jnp.where(kinds > 0, relax_rate, 0.0)
    source = jnp.where(kinds == 1, contact, -contact)
    rate = source * capacity - contact * field
    for k, speed in enumerate(speeds):
        rate = rate - (0.5 * speed) * steps[:, k * cells : (k + 1) * cells]
    return rate


def first_rest(field, came_even, came_odd, operators, table, kinds, base_a, base_b, strips):
    modes, half = base_a.shape
    block = min(modes, BLOCK)
    strips[...] = strip_columns(came_even, came_odd)

    def step(i, _):
        rows = pl.ds(pl.multiple_of(i * block, block), block)
        value = field[rows, :]
        rate = still_rate(value, strips[rows, :], operators, table[:, rows].T, kinds[...])
        base = value + time_step * rate
        base_a[rows, :] = base[:, :half]
        base_b[rows, :] = base[:, half:]
        return 0

    lax.fori_loop(0, modes // block, step, 0)


def second_rest(
    field,
    mid_a,
    mid_b,
    came_even,
    came_odd,
    operators,
    table,
    kinds,
    scattered,
    end_a,
    end_b,
    flux,
    strips,
):
    modes, half = end_a.shape
    block = min(modes, BLOCK)
    step_size = 0.5 * time_step
    strips[...] = strip_columns(came_even, came_odd)
    flux[...] = jnp.zeros_like(flux)

    def step(i, _):
        rows = pl.ds(pl.multiple_of(i * block, block), block)
        mid = jnp.concatenate([mid_a[rows, :], mid_b[rows, :]], axis=1)
        columns = table[:, rows].T
        taken = step_size * scattered[:, rows].T
        rate = still_rate(mid, strips[rows, :], operators, columns, kinds[...])
        end = 0.5 * (field[rows, :] + mid) + step_size * rate
        end_a[rows, :] = end[:, :half]
        end_b[rows, :] = end[:, half:]
        for d in range(2):
            terms = columns[:, 3 + d : 4 + d] * end - taken[:, d : d + 1] * mid
            flux[d : d + 1, :] += jnp.sum(terms, axis=0, keepdims=True)
        return 0

    lax.fori_loop(0, modes // block, step, 0)


def paired(to_even, to_odd):
    count = lax.axis_size("space")
    came = []
    for first, value in enumerate((to_even, to_odd)):
        pairs = [(i, i + 1) for i in range(first, count - 1, 2)]
        came.append(lax.ppermute(value, "space", pairs + [(j, i) for i, j in pairs]))
    return came


class Plan:
    def __init__(self, chips):
        self.chips = chips
        self.devices = range(2 * chips)
        sources = [self.sources(d) for d in self.devices]
        targets = [self.targets(d // 2) for d in self.devices]
        self.blocks = [
            [
                [2 * sources[e][slot][2] + e % 2 for e in (d ^ other for d in self.devices)]
                for other in (0, 1)
            ]
            for slot in range(chips)
        ]
        self.rows = [
            [[2 * targets[d][slot] + (d % 2 ^ other) for d in self.devices] for other in (0, 1)]
            for slot in range(chips)
        ]
        self.choices = [
            sorted({sources[d][slot][:2] for d in self.devices}) for slot in range(chips)
        ]
        self.picked = [
            [self.choices[slot].index(sources[d][slot][:2]) for d in self.devices]
            for slot in range(chips)
        ]
        self.sent = {}
        for stream in (0, 1):
            for step in range(1, chips):
                numbers = []
                for d in self.devices:
                    way = self.way(d, stream)
                    place = d // 2 if way > 0 else chips - 1 - d // 2
                    target = d // 2 + way * (chips - step)
                    numbers.append(targets[d].index(target) if place < step else -1)
                self.sent[stream, step] = numbers
        self.pairs = []
        for stream in (0, 1):
            up = [
                (d, d + 2) for d in self.devices[:-2] if self.way(d, stream) > 0
            ]
            self.pairs.append(up + [(j, i) for i, j in up])

    def way(self, device, stream):
        return 1 if (device // 2 + device % 2 + stream) % 2 == 0 else -1

    def sources(self, device):
        found = [(-1, -1, device // 2)]
        for step in range(self.chips - 1):
            for stream in (step % 2, 1 - step % 2):
                chip = device // 2 + self.way(device, stream) * (step + 1)
                if 0 <= chip < self.chips:
                    found.append((stream, step, chip))
        return found

    def targets(self, chip):
        found = []
        for step in range(1, self.chips):
            far = self.chips - step
            found += [t for t in (chip + far, chip - far) if 0 <= t < self.chips]
        return found + [chip]


def on_device(distribution, scatter_matrix, velocity, capacity, cell_type):
    modes, cells = distribution.shape
    total_modes = scatter_matrix.shape[0]
    half = cells // 2
    extra = -(-2 * modes // LANES // 8) * 8
    step_size = 0.5 * time_step
    part = (modes, half)
    devices = lax.axis_size("mode")
    chips = devices // 2
    plan = Plan(chips)
    call = Chain()
    across = [(i, i ^ 1) for i in range(devices)]
    cap = capacity[None, :]
    table = jnp.concatenate(
        [velocity, cap, cap * velocity, jnp.zeros((3, modes), jnp.float32)], axis=0
    )
    kinds = cell_type[None, :]

    def exchange(value):
        return lax.ppermute(value, "mode", across)

    def along(stream, value):
        return lax.ppermute(value, "mode", plan.pairs[stream])

    class Round:
        def __init__(self, matrix, scale, rows):
            self.matrix, self.scale, self.rows = matrix, scale, rows
            self.terms, self.total = [], None

        def begin(self, own):
            self.own = own
            self.arrived = [[along(0, own)], [along(1, own)]]
            self.blocks = []

        def add_terms(self, field):
            kernel = functools.partial(slot_products, plan.rows[len(self.terms)])
            mine, other = call(kernel, [part] * 2, [self.matrix, field])
            self.terms.append((mine, exchange(other)))

        def join_terms(self, *slots):
            for slot in slots:
                (self.terms[slot],) = call(add, [part], self.terms[slot])

        def take_own(self):
            self.blocks.append((self.own, exchange(self.own)))

        def send(self, step):
            sent = {}
            for stream in (step % 2, 1 - step % 2):
                numbers = plan.sent[stream, step]
                slots = sorted({n for n in numbers if n >= 0})
                for slot in slots:
                    if isinstance(self.terms[slot], tuple):
                        self.join_terms(slot)
                arrived = self.arrived[1 - stream][step - 1]
                kernel = functools.partial(payload, numbers, slots)
                arrays = [arrived] + [self.terms[s] for s in slots]
                (value,) = call(kernel, [arrived.shape], arrays)
                sent[stream] = along(stream, value)
            for stream in (0, 1):
                self.arrived[stream].append(sent[stream])

        def take(self, slot, parts=1):
            arrays = [self.arrived[stream][step] for stream, step in plan.choices[slot]]
            kernel = functools.partial(pick, plan.picked[slot])
            (here,) = call(kernel, [arrays[0].shape], arrays)
            cut = here.shape[0] // parts // 8 * 8
            ends = [cut * k for k in range(parts)] + [here.shape[0]]
            there = [exchange(here[i:j]) for i, j in zip(ends, ends[1:])]
            self.blocks.append((here, *there))

        def multiply(self, slot, base=None):
            first, last = slot == 0, base is not None
            blocks = self.blocks[slot]
            kernel = functools.partial(
                two_blocks, plan.blocks[slot], len(blocks) - 1, first, last, self.scale, self.rows
            )
            arrays = [self.matrix, *blocks]
            arrays += [] if first else [self.total]
            arrays += [base] if last else []
            outs = [(2 * half + (16 if self.rows else 0), modes)]
            if last:
                outs = [part, (HALO, modes), (8, modes)] if self.rows else [part]
            results = call(kernel, outs, arrays)
            self.total = results[0]
            return results

        def ends(self):
            return [self.arrived[0][-1], self.arrived[1][-1], self.terms[-1]]

    (own,) = call(
        own_rows,
        [(modes + extra, half)],
        [distribution, velocity, cap],
        places=[HBM] * 3,
        scratch=[
            pltpu.VMEM((2, modes), jnp.float32),
            pltpu.VMEM((1, modes), jnp.float32),
            pltpu.SemaphoreType.DMA((3,)),
        ],
        room=56,
    )
    one = Round(None, time_step, True)
    one.begin(own)
    *terms, matrix = call(
        functools.partial(load_and_products, plan.rows, half),
        [part] * (2 * chips) + [jax.ShapeDtypeStruct(scatter_matrix.shape, jnp.bfloat16)],
        [scatter_matrix, distribution],
        places=[HBM] * 2,
        scratch=[
            pltpu.VMEM(part, jnp.float32),
            pltpu.SemaphoreType.DMA((2 * chips + 1,)),
        ],
        room=28,
    )
    one.matrix = matrix
    one.terms = [(terms[2 * s], exchange(terms[2 * s + 1])) for s in range(chips)]
    one.take_own()
    operators = jnp.asarray(differences(cells))
    aside = [pltpu.VMEM((modes, 4 * HALO), jnp.bfloat16)]
    strips = None
    for step in range(1, chips):
        if step == 1:
            one.take(1)
        one.send(step)
        if step == 1:
            one.join_terms(*(s for s in range(chips) if isinstance(one.terms[s], tuple)))
            strips = call(strip_rows, [(HALO, modes)] * 2, [distribution])
            strips = paired(*call(strip_pairs, [(HALO, modes)] * 2, strips))
        else:
            one.take(step, 2 if step == chips - 1 else 1)
        one.multiply(step - 1)
        if step == min(2, chips - 1):
            base_a, base_b = call(
                first_rest,
                [part] * 2,
                [distribution, *strips, operators, table, kinds],
                scratch=aside,
            )
    mid_a, leading, scattered = one.multiply(chips - 1, base_a)

    two = Round(matrix, step_size, False)
    two.add_terms(mid_a)
    mid_b, last = call(
        functools.partial(turn_sum, time_step), [part, (HALO, modes)], [*one.ends(), base_b]
    )
    two.begin(mid_b)
    two.join_terms(0)
    for slot in range(1, chips - 1):
        two.add_terms(mid_a)
    two.take_own()
    strips = call(strip_pairs, [(HALO, modes)] * 2, [leading, last])
    strips = paired(*strips)
    adding = None
    for step in range(1, chips):
        if adding is not None:
            adding.next()
        two.send(step)
        if step == 1:
            two.join_terms(*(s for s in range(1, chips - 1) if isinstance(two.terms[s], tuple)))
        two.take(step, 2 if step == chips - 1 else 1)
        if step == 1:
            two.add_terms(mid_a)
        two.multiply(step - 1)
        if step == 1:
            end_a, end_b, flux = call(
                second_rest,
                [part, part, (2, cells)],
                [distribution, mid_a, mid_b, *strips, operators, table, kinds, scattered],
                scratch=aside,
            )
            adding = Adding(call, flux, devices)
    (last_b,) = two.multiply(chips - 1, end_b)
    heat_flux = adding.finish() / jnp.sqrt(jnp.float32(total_modes))
    if isinstance(two.terms[-1], tuple):
        two.join_terms(chips - 1)
    (updated,) = call(
        functools.partial(last_sum, step_size),
        [(modes, cells)],
        [*two.ends(), end_a, last_b],
        scratch=[pltpu.VMEM(part, jnp.float32), pltpu.SemaphoreType.DMA((2,))],
        out_specs=[HBM],
    )
    return (updated, heat_flux)


class Adding:
    def __init__(self, call, value, devices):
        self.call, self.value, self.devices, self.bit = call, value, devices, 1

    def next(self):
        if self.bit < self.devices:
            pairs = [(i, i ^ self.bit) for i in range(self.devices)]
            came = lax.ppermute(self.value, "mode", pairs)
            (self.value,) = self.call(add, [self.value.shape], [self.value, came])
            self.bit *= 2

    def finish(self):
        while self.bit < self.devices:
            self.next()
        return self.value


def solution(mesh):
    return jax.shard_map(
        on_device,
        mesh=mesh,
        in_specs=(P("mode", "space"), P(None, "mode"), P(None, "mode"), P("mode"), P("space")),
        out_specs=(P("mode", "space"), P(None, "space")),
        check_vma=False,
    )
```

```python
import functools
import math

import numpy as np

import jax
import jax.numpy as jnp
from jax import lax
from jax.experimental import pallas as pl
from jax.experimental.pallas import tpu as pltpu
from jax.sharding import PartitionSpec as P

NY = 16
HALO = 2 * NY
LANES = 128
BLOCK = 512


relax_rate = 0.5
time_step = 0.5

VMEM = pl.BlockSpec(memory_space=pltpu.VMEM)
ANY = pl.BlockSpec(memory_space=pl.ANY)
HBM = pl.BlockSpec(memory_space=pltpu.HBM)


class Chain:
    def __init__(self):
        self.last = None

    def __call__(self, kernel, outs, arrays, places=None, scratch=(), out_specs=None, room=16):
        extra = [] if self.last is None else [self.last]
        skip = len(extra)
        first = len(arrays)

        def body(*refs):
            kernel(*refs[:first], *refs[first + skip :])

        results = pl.pallas_call(
            body,
            out_shape=[
                jax.ShapeDtypeStruct(shape, jnp.float32) if isinstance(shape, tuple) else shape
                for shape in outs
            ],
            in_specs=list(places or [VMEM] * len(arrays)) + [ANY] * skip,
            out_specs=out_specs or [VMEM] * len(outs),
            scratch_shapes=list(scratch),
            compiler_params=pltpu.CompilerParams(vmem_limit_bytes=room * 1024 * 1024),
            cost_estimate=pl.CostEstimate(flops=1024, bytes_accessed=1024, transcendentals=0),
            name=getattr(kernel, "func", kernel).__name__,
        )(*arrays, *extra)
        self.last = results[-1]
        return results


def halves(value):
    high = value.astype(jnp.bfloat16)
    low = (value - high.astype(jnp.float32)).astype(jnp.bfloat16)
    return high, low


def for_device(numbers):
    if len(set(numbers)) == 1:
        return numbers[0]
    me = lax.axis_index("mode")
    chosen = jnp.int32(numbers[0])
    for device, number in enumerate(numbers[1:], 1):
        chosen = jnp.where(me == device, jnp.int32(number), chosen)
    return chosen


def rows_of(matrix, block):
    modes = matrix.shape[1]
    return pl.ds(pl.multiple_of(block * modes, modes), modes)


def one_slot(blocks, matrix, parts, mine, other):
    cells = mine.shape[1]
    for block, out in zip(blocks, (mine, other)):
        both = jnp.dot(matrix[rows_of(matrix, block), :], parts, preferred_element_type=jnp.float32)
        out[...] = both[:, :cells] + both[:, cells:]


def slot_products(blocks, matrix, field, mine, other):
    blocks = [for_device(numbers) for numbers in blocks]
    parts = jnp.concatenate(halves(field[...]), axis=1)
    one_slot(blocks, matrix, parts, mine, other)


def load_and_products(blocks, column, matrix, distribution, *refs):
    slots = len(blocks)
    outs, (held, field, sems) = refs[: 2 * slots], refs[2 * slots :]
    cells = field.shape[1]
    start = pltpu.make_async_copy(
        distribution.at[:, pl.ds(column, cells)], field, sems.at[2 * slots]
    )
    start.start()
    blocks = [[for_device(numbers) for numbers in pair] for pair in blocks]
    copies = []
    for slot, pair in enumerate(blocks):
        for k, block in enumerate(pair):
            rows = rows_of(held, block)
            copies.append(
                pltpu.make_async_copy(
                    matrix.at[rows, :], held.at[rows, :], sems.at[2 * slot + k]
                )
            )
            copies[-1].start()
    start.wait()
    parts = jnp.concatenate(halves(field[...]), axis=1)
    for slot, pair in enumerate(blocks):
        for k in range(2):
            copies[2 * slot + k].wait()
        one_slot(pair, held, parts, outs[2 * slot], outs[2 * slot + 1])


def two_blocks(numbers, parts, first, last, scale, rows, matrix, *refs):
    modes = matrix.shape[1]
    blocks, refs = [[refs[0]], refs[1 : 1 + parts]], refs[1 + parts :]
    if not first:
        before, refs = refs[0], refs[1:]
    if last:
        base, refs = refs[0], refs[1:]
    total = None if first else before[...]
    for k, pieces in enumerate(blocks):
        block = jnp.concatenate([piece[...] for piece in pieces], axis=0)
        pieces = list(halves(block[:modes].T))
        if rows:
            weights = [
                jnp.concatenate(
                    [
                        block[modes + i : modes + i + 1, :]
                        for i in range(d * modes // LANES, (d + 1) * modes // LANES)
                    ],
                    axis=1,
                )
                for d in range(2)
            ]
            weights.append(jnp.zeros((6, modes), jnp.float32))
            pieces += halves(jnp.concatenate(weights, axis=0))
        left = jnp.concatenate(pieces, axis=0)
        there = rows_of(matrix, for_device(numbers[k]))
        term = jnp.dot(left, matrix[there, :], preferred_element_type=jnp.float32)
        total = term if total is None else total + term
    if not last:
        refs[0][...] = total
        return
    cells = base.shape[1]
    value = base[...] - scale * (total[:cells] + total[cells : 2 * cells]).T
    refs[0][...] = value
    if rows:
        refs[1][...] = value.T[:HALO]
        refs[2][...] = total[2 * cells : 2 * cells + 8] + total[2 * cells + 8 :]


def own_rows(distribution, velocity, capacity, out, token, speeds, weight, rows, sems):
    modes, cells = velocity.shape[1], out.shape[1]
    field = pltpu.make_async_copy(
        distribution.at[:, pl.ds(0, cells)], out.at[pl.ds(0, modes), :], sems.at[0]
    )
    field.start()
    copies = [
        pltpu.make_async_copy(velocity, speeds, sems.at[1]),
        pltpu.make_async_copy(capacity, weight, sems.at[2]),
    ]
    for copy in copies:
        copy.start()
    token[...] = jnp.zeros_like(token)
    rows[...] = jnp.zeros_like(rows)
    for copy in copies:
        copy.wait()
    per = modes // LANES
    for d in range(2):
        for i in range(per):
            lanes = slice(i * LANES, (i + 1) * LANES)
            rows[d * per + i : d * per + i + 1, :] = speeds[d : d + 1, lanes] * weight[:, lanes]
    extra = pltpu.make_async_copy(
        rows, out.at[pl.ds(modes, rows.shape[0]), :], sems.at[3]
    )
    extra.start()
    field.wait()
    extra.wait()


def payload(numbers, slots, arrived, *refs):
    out = refs[-1]
    slot_here = for_device(numbers)

    for k, slot in enumerate(slots):

        @pl.when(slot_here == slot)
        def _(k=k):
            terms = refs[k]
            modes = terms.shape[0]
            out[:modes] = arrived[:modes] + terms[...]
            if out.shape[0] > modes:
                out[modes:] = arrived[modes:]

    @pl.when(slot_here < 0)
    def _():
        out[...] = arrived[...]


def pick(numbers, *refs):
    out = refs[-1]
    choice = for_device(numbers)
    for k, ref in enumerate(refs[:-1]):

        @pl.when(choice == k)
        def _(ref=ref):
            out[...] = ref[...]


def add(one, two, out):
    out[...] = one[...] + two[...]


def add_all(*refs):
    out, token = refs[-2:]
    total = refs[0][...]
    for ref in refs[1:-2]:
        total = total + ref[...]
    out[...] = total
    token[...] = jnp.zeros_like(token)


def take_off(scale, arrived, terms, base, out):
    modes = terms.shape[0]
    out[...] = base[...] - scale * (arrived[:modes] + terms[...])


def turn_sum(scale, arrived, base, out, strip):
    modes = base.shape[0]
    value = base[...] - scale * arrived[:modes]
    out[...] = value
    strip[...] = value.T[-HALO:]


def last_sum(scale, arrived, base, other, out, value, sems):
    cells = base.shape[1]
    ahead = pltpu.make_async_copy(other, out.at[:, pl.ds(cells, cells)], sems.at[0])
    ahead.start()
    value[...] = base[...] - scale * arrived[...]
    copy = pltpu.make_async_copy(value, out.at[:, pl.ds(0, cells)], sems.at[1])
    copy.start()
    ahead.wait()
    copy.wait()


def strip_rows(distribution, leading, last):
    cells = distribution.shape[1]
    leading[...] = distribution[:, :LANES].T[:HALO]
    last[...] = distribution[:, cells - LANES :].T[-HALO:]


def strip_pairs(leading, last, out_even, out_odd):
    even = lax.axis_index("space") % 2 == 0

    @pl.when(even)
    def _():
        out_even[...] = last[...]
        out_odd[...] = leading[...]

    @pl.when(jnp.logical_not(even))
    def _():
        out_even[...] = leading[...]
        out_odd[...] = last[...]


def differences(cells):
    columns = cells // NY
    own, strip = np.zeros((cells, 4 * cells)), np.zeros((2 * HALO, 4 * cells))
    for x in range(columns):
        for y in range(NY):
            cell = x * NY + y
            for way in (-1, 1):
                for far, factor in enumerate((3.0, -4.0, 1.0)):
                    at_x, at_y = x + way * far, y + way * far
                    first = cell + (0 if way < 0 else cells)
                    factor = -way * factor
                    if at_x < 0:
                        strip[(at_x + 2) * NY + y, first] = factor
                    elif at_x >= columns:
                        strip[HALO + (at_x - columns) * NY + y, first] = factor
                    else:
                        own[at_x * NY + y, first] = factor
                    if 0 <= at_y < NY:
                        own[x * NY + at_y, first + 2 * cells] = factor
    return np.concatenate([own, own, strip, strip]).astype(jnp.bfloat16)


def strip_columns(came_even, came_odd):
    even = lax.axis_index("space") % 2 == 0
    before = jnp.where(even, came_odd[...], came_even[...])
    after = jnp.where(even, came_even[...], came_odd[...])
    parts = halves(jnp.concatenate([before, after], axis=0))
    return jnp.concatenate([p.astype(jnp.float32) for p in parts], axis=0).T.astype(jnp.bfloat16)


def still_rate(field, strip, operators, columns, kinds):
    cells = field.shape[1]
    left = jnp.concatenate([*halves(field), strip], axis=1)
    steps = jnp.dot(left, operators[...], preferred_element_type=jnp.float32)
    vx, vy, capacity = (columns[:, i : i + 1] for i in range(3))
    speeds = (jnp.maximum(vx, 0.0), jnp.minimum(vx, 0.0))
    speeds += (jnp.maximum(vy, 0.0), jnp.minimum(vy, 0.0))
    contact = jnp.where(kinds > 0, relax_rate, 0.0)
    source = jnp.where(kinds == 1, contact, -contact)
    rate = source * capacity - contact * field
    for k, speed in enumerate(speeds):
        rate = rate - (0.5 * speed) * steps[:, k * cells : (k + 1) * cells]
    return rate


def first_rest(field, came_even, came_odd, operators, table, kinds, base_a, base_b, strips):
    modes, half = base_a.shape
    block = min(modes, BLOCK)
    strips[...] = strip_columns(came_even, came_odd)

    def step(i, _):
        rows = pl.ds(pl.multiple_of(i * block, block), block)
        value = field[rows, :]
        rate = still_rate(value, strips[rows, :], operators, table[:, rows].T, kinds[...])
        base = value + time_step * rate
        base_a[rows, :] = base[:, :half]
        base_b[rows, :] = base[:, half:]
        return 0

    lax.fori_loop(0, modes // block, step, 0)


def second_rest(
    flux_scale,
    field,
    mid_a,
    mid_b,
    came_even,
    came_odd,
    operators,
    table,
    kinds,
    scattered,
    end_a,
    end_b,
    flux,
    strips,
):
    modes, half = end_a.shape
    block = min(modes, BLOCK)
    step_size = 0.5 * time_step
    strips[...] = strip_columns(came_even, came_odd)
    flux[...] = jnp.zeros_like(flux)

    def step(i, _):
        rows = pl.ds(pl.multiple_of(i * block, block), block)
        mid = jnp.concatenate([mid_a[rows, :], mid_b[rows, :]], axis=1)
        columns = table[:, rows].T
        taken = step_size * scattered[:, rows].T
        rate = still_rate(mid, strips[rows, :], operators, columns, kinds[...])
        end = 0.5 * (field[rows, :] + mid) + step_size * rate
        end_a[rows, :] = end[:, :half]
        end_b[rows, :] = end[:, half:]
        for d in range(2):
            terms = columns[:, 3 + d : 4 + d] * end - taken[:, d : d + 1] * mid
            flux[d : d + 1, :] += flux_scale * jnp.sum(terms, axis=0, keepdims=True)
        return 0

    lax.fori_loop(0, modes // block, step, 0)


def paired(to_even, to_odd):
    count = lax.axis_size("space")
    came = []
    for first, value in enumerate((to_even, to_odd)):
        pairs = [(i, i + 1) for i in range(first, count - 1, 2)]
        came.append(lax.ppermute(value, "space", pairs + [(j, i) for i, j in pairs]))
    return came


class Plan:
    def __init__(self, chips):
        self.chips = chips
        self.devices = range(2 * chips)
        sources = [self.sources(d) for d in self.devices]
        targets = [self.targets(d // 2) for d in self.devices]
        self.blocks = [
            [
                [2 * sources[e][slot][2] + e % 2 for e in (d ^ other for d in self.devices)]
                for other in (0, 1)
            ]
            for slot in range(chips)
        ]
        self.rows = [
            [[2 * targets[d][slot] + (d % 2 ^ other) for d in self.devices] for other in (0, 1)]
            for slot in range(chips)
        ]
        self.choices = [
            sorted({sources[d][slot][:2] for d in self.devices}) for slot in range(chips)
        ]
        self.picked = [
            [self.choices[slot].index(sources[d][slot][:2]) for d in self.devices]
            for slot in range(chips)
        ]
        self.sent = {}
        for stream in (0, 1):
            for step in range(1, chips):
                numbers = []
                for d in self.devices:
                    way = self.way(d, stream)
                    place = d // 2 if way > 0 else chips - 1 - d // 2
                    target = d // 2 + way * (chips - step)
                    numbers.append(targets[d].index(target) if place < step else -1)
                self.sent[stream, step] = numbers
        self.pairs = []
        for stream in (0, 1):
            up = [
                (d, d + 2) for d in self.devices[:-2] if self.way(d, stream) > 0
            ]
            self.pairs.append(up + [(j, i) for i, j in up])

    def way(self, device, stream):
        return 1 if (device // 2 + device % 2 + stream) % 2 == 0 else -1

    def sources(self, device):
        found = [(-1, -1, device // 2)]
        for step in range(self.chips - 1):
            for stream in (step % 2, 1 - step % 2):
                chip = device // 2 + self.way(device, stream) * (step + 1)
                if 0 <= chip < self.chips:
                    found.append((stream, step, chip))
        return found

    def targets(self, chip):
        found = []
        for step in range(1, self.chips):
            far = self.chips - step
            found += [t for t in (chip + far, chip - far) if 0 <= t < self.chips]
        return found + [chip]


def on_device(distribution, scatter_matrix, velocity, capacity, cell_type):
    modes, cells = distribution.shape
    total_modes = scatter_matrix.shape[0]
    half = cells // 2
    extra = -(-2 * modes // LANES // 8) * 8
    step_size = 0.5 * time_step
    part = (modes, half)
    devices = lax.axis_size("mode")
    chips = devices // 2
    plan = Plan(chips)
    call = Chain()
    across = [(i, i ^ 1) for i in range(devices)]
    cap = capacity[None, :]
    table = jnp.concatenate(
        [velocity, cap, cap * velocity, jnp.zeros((3, modes), jnp.float32)], axis=0
    )
    kinds = cell_type[None, :]

    def exchange(value):
        return lax.ppermute(value, "mode", across)

    def along(stream, value):
        return lax.ppermute(value, "mode", plan.pairs[stream])

    class Round:
        def __init__(self, matrix, scale, rows):
            self.matrix, self.scale, self.rows = matrix, scale, rows
            self.terms, self.total = [], None

        def begin(self, own):
            self.own = own
            self.arrived = [[along(0, own)], [along(1, own)]]
            self.blocks = []

        def add_terms(self, field):
            kernel = functools.partial(slot_products, plan.rows[len(self.terms)])
            mine, other = call(kernel, [part] * 2, [self.matrix, field])
            self.terms.append((mine, exchange(other)))

        def join_terms(self, *slots):
            for slot in slots:
                (self.terms[slot],) = call(add, [part], self.terms[slot])

        def take_own(self):
            self.blocks.append((self.own, exchange(self.own)))

        def send(self, step, between=None):
            sent = {}
            for stream in (step % 2, 1 - step % 2):
                if between is not None and sent:
                    between()
                numbers = plan.sent[stream, step]
                slots = sorted({n for n in numbers if n >= 0})
                for slot in slots:
                    if isinstance(self.terms[slot], tuple):
                        self.join_terms(slot)
                arrived = self.arrived[1 - stream][step - 1]
                kernel = functools.partial(payload, numbers, slots)
                arrays = [arrived] + [self.terms[s] for s in slots]
                (value,) = call(kernel, [arrived.shape], arrays)
                sent[stream] = along(stream, value)
            for stream in (0, 1):
                self.arrived[stream].append(sent[stream])

        def take(self, slot, parts=1):
            arrays = [self.arrived[stream][step] for stream, step in plan.choices[slot]]
            kernel = functools.partial(pick, plan.picked[slot])
            (here,) = call(kernel, [arrays[0].shape], arrays)
            cut = here.shape[0] // parts // 8 * 8
            ends = [cut * k for k in range(parts)] + [here.shape[0]]
            there = [exchange(here[i:j]) for i, j in zip(ends, ends[1:])]
            self.blocks.append((here, *there))

        def multiply(self, slot, base=None):
            first, last = slot == 0, base is not None
            blocks = self.blocks[slot]
            kernel = functools.partial(
                two_blocks, plan.blocks[slot], len(blocks) - 1, first, last, self.scale, self.rows
            )
            arrays = [self.matrix, *blocks]
            arrays += [] if first else [self.total]
            arrays += [base] if last else []
            outs = [(2 * half + (16 if self.rows else 0), modes)]
            if last:
                outs = [part, (HALO, modes), (8, modes)] if self.rows else [part]
            results = call(kernel, outs, arrays)
            self.total = results[0]
            return results

        def ends(self, base):
            first = (chips - 1) % 2
            kernel = functools.partial(take_off, self.scale)
            (rest,) = call(kernel, [part], [self.arrived[first][-1], self.terms[-1], base])
            return [self.arrived[1 - first][-1], rest]

    own, _ = call(
        own_rows,
        [(modes + extra, half), (8, LANES)],
        [distribution, velocity, cap],
        places=[HBM] * 3,
        scratch=[
            pltpu.VMEM((2, modes), jnp.float32),
            pltpu.VMEM((1, modes), jnp.float32),
            pltpu.VMEM((extra, LANES), jnp.float32),
            pltpu.SemaphoreType.DMA((4,)),
        ],
        out_specs=[HBM, VMEM],
        room=56,
    )
    one = Round(None, time_step, True)
    one.begin(own)
    *terms, matrix = call(
        functools.partial(load_and_products, plan.rows, half),
        [part] * (2 * chips) + [jax.ShapeDtypeStruct(scatter_matrix.shape, jnp.bfloat16)],
        [scatter_matrix, distribution],
        places=[HBM] * 2,
        scratch=[
            pltpu.VMEM(part, jnp.float32),
            pltpu.SemaphoreType.DMA((2 * chips + 1,)),
        ],
        room=28,
    )
    one.matrix = matrix
    one.terms = [(terms[2 * s], exchange(terms[2 * s + 1])) for s in range(chips)]
    one.take_own()
    operators = jnp.asarray(differences(cells))
    aside = [pltpu.VMEM((modes, 4 * HALO), jnp.bfloat16)]
    strips = None
    for step in range(1, chips):
        if step == 1:
            one.take(1)
        one.send(step)
        if step == 1:
            one.join_terms(*(s for s in range(chips) if isinstance(one.terms[s], tuple)))
            strips = call(strip_rows, [(HALO, modes)] * 2, [distribution])
            strips = paired(*call(strip_pairs, [(HALO, modes)] * 2, strips))
        else:
            one.take(step, 2 if step == chips - 1 else 1)
        one.multiply(step - 1)
        if step == min(2, chips - 1):
            base_a, base_b = call(
                first_rest,
                [part] * 2,
                [distribution, *strips, operators, table, kinds],
                scratch=aside,
            )
    mid_a, leading, scattered = one.multiply(chips - 1, base_a)

    two = Round(matrix, step_size, False)
    two.add_terms(mid_a)
    mid_b, last = call(
        functools.partial(turn_sum, time_step), [part, (HALO, modes)], one.ends(base_b)
    )
    two.begin(mid_b)
    two.join_terms(0)
    for slot in range(1, chips - 1):
        two.add_terms(mid_a)
    two.take_own()
    strips = call(strip_pairs, [(HALO, modes)] * 2, [leading, last])
    strips = paired(*strips)
    flux = None
    for step in range(1, chips):
        if step == 1:
            two.send(step)
            two.join_terms(*(s for s in range(1, chips - 1) if isinstance(two.terms[s], tuple)))
        elif step == 2:
            two.send(step, lambda: flux.over(1))
        elif step == chips - 1:
            two.send(step, lambda: flux.over(*range(2, devices, 2)))
        else:
            two.send(step)
        if step == 2 and isinstance(two.terms[-1], tuple):
            two.join_terms(chips - 1)
        two.take(step, 2 if step >= chips - 2 else 1)
        if step == 1:
            two.add_terms(mid_a)
        if step < chips - 1:
            two.multiply(step - 1)
        if step == chips - 2:
            two.multiply(step)
        if step == 1:
            end_a, end_b, part_flux = call(
                functools.partial(second_rest, 1.0 / math.sqrt(total_modes)),
                [part, part, (2, cells)],
                [distribution, mid_a, mid_b, *strips, operators, table, kinds, scattered],
                scratch=aside,
            )
            flux = Flux(call, part_flux, devices)
    (last_b,) = two.multiply(chips - 1, end_b)
    heat_flux = flux.value
    if isinstance(two.terms[-1], tuple):
        two.join_terms(chips - 1)
    (updated,) = call(
        functools.partial(last_sum, step_size),
        [(modes, cells)],
        [*two.ends(end_a), last_b],
        scratch=[pltpu.VMEM(part, jnp.float32), pltpu.SemaphoreType.DMA((2,))],
        out_specs=[HBM],
    )
    return (updated, heat_flux)


class Flux:
    def __init__(self, call, value, devices):
        self.call, self.value, self.devices = call, value, devices

    def over(self, *bits):
        came = [
            lax.ppermute(self.value, "mode", [(i, i ^ bit) for i in range(self.devices)])
            for bit in bits
        ]
        self.value, _ = self.call(add_all, [self.value.shape, (8, LANES)], [self.value, *came])


def solution(mesh):
    return jax.shard_map(
        on_device,
        mesh=mesh,
        in_specs=(P("mode", "space"), P(None, "mode"), P(None, "mode"), P("mode"), P("space")),
        out_specs=(P("mode", "space"), P(None, "space")),
        check_vma=False,
    )
```

```python
import functools
import math

import numpy as np

import jax
import jax.numpy as jnp
from jax import lax
from jax.experimental import pallas as pl
from jax.experimental.pallas import tpu as pltpu
from jax.sharding import PartitionSpec as P

NY = 16
HALO = 2 * NY
LANES = 128
BLOCK = 512


relax_rate = 0.5
time_step = 0.5

VMEM = pl.BlockSpec(memory_space=pltpu.VMEM)
ANY = pl.BlockSpec(memory_space=pl.ANY)
HBM = pl.BlockSpec(memory_space=pltpu.HBM)


class Chain:
    def __init__(self):
        self.last = None

    def __call__(self, kernel, outs, arrays, places=None, scratch=(), out_specs=None, room=16):
        extra = [] if self.last is None else [self.last]
        skip = len(extra)
        first = len(arrays)

        def body(*refs):
            kernel(*refs[:first], *refs[first + skip :])

        results = pl.pallas_call(
            body,
            out_shape=[
                jax.ShapeDtypeStruct(shape, jnp.float32) if isinstance(shape, tuple) else shape
                for shape in outs
            ],
            in_specs=list(places or [VMEM] * len(arrays)) + [ANY] * skip,
            out_specs=out_specs or [VMEM] * len(outs),
            scratch_shapes=list(scratch),
            compiler_params=pltpu.CompilerParams(vmem_limit_bytes=room * 1024 * 1024),
            cost_estimate=pl.CostEstimate(flops=1024, bytes_accessed=1024, transcendentals=0),
            name=getattr(kernel, "func", kernel).__name__,
        )(*arrays, *extra)
        self.last = results[-1]
        return results


def halves(value):
    high = value.astype(jnp.bfloat16)
    low = (value - high.astype(jnp.float32)).astype(jnp.bfloat16)
    return high, low


def for_device(numbers):
    if len(set(numbers)) == 1:
        return numbers[0]
    me = lax.axis_index("mode")
    chosen = jnp.int32(numbers[0])
    for device, number in enumerate(numbers[1:], 1):
        chosen = jnp.where(me == device, jnp.int32(number), chosen)
    return chosen


def rows_of(matrix, block):
    modes = matrix.shape[1]
    return pl.ds(pl.multiple_of(block * modes, modes), modes)


def one_slot(blocks, matrix, parts, mine, other):
    cells = mine.shape[1]
    for block, out in zip(blocks, (mine, other)):
        both = jnp.dot(matrix[rows_of(matrix, block), :], parts, preferred_element_type=jnp.float32)
        out[...] = both[:, :cells] + both[:, cells:]


def slot_products(blocks, matrix, field, mine, other):
    blocks = [for_device(numbers) for numbers in blocks]
    parts = jnp.concatenate(halves(field[...]), axis=1)
    one_slot(blocks, matrix, parts, mine, other)


def load_and_products(blocks, column, matrix, distribution, *refs):
    slots = len(blocks)
    outs, (held, field, sems) = refs[: 2 * slots], refs[2 * slots :]
    cells = field.shape[1]
    start = pltpu.make_async_copy(
        distribution.at[:, pl.ds(column, cells)], field, sems.at[2 * slots]
    )
    start.start()
    blocks = [[for_device(numbers) for numbers in pair] for pair in blocks]
    copies = []
    for slot, pair in enumerate(blocks):
        for k, block in enumerate(pair):
            rows = rows_of(held, block)
            copies.append(
                pltpu.make_async_copy(
                    matrix.at[rows, :], held.at[rows, :], sems.at[2 * slot + k]
                )
            )
            copies[-1].start()
    start.wait()
    parts = jnp.concatenate(halves(field[...]), axis=1)
    for slot, pair in enumerate(blocks):
        for k in range(2):
            copies[2 * slot + k].wait()
        one_slot(pair, held, parts, outs[2 * slot], outs[2 * slot + 1])


def two_blocks(numbers, parts, first, last, scale, rows, matrix, *refs):
    modes = matrix.shape[1]
    blocks, refs = [[refs[0]], refs[1 : 1 + parts]], refs[1 + parts :]
    if not first:
        before, refs = refs[0], refs[1:]
    if last:
        base, refs = refs[0], refs[1:]
    total = None if first else before[...]
    for k, pieces in enumerate(blocks):
        block = jnp.concatenate([piece[...] for piece in pieces], axis=0)
        pieces = list(halves(block[:modes].T))
        if rows:
            weights = [
                jnp.concatenate(
                    [
                        block[modes + i : modes + i + 1, :]
                        for i in range(d * modes // LANES, (d + 1) * modes // LANES)
                    ],
                    axis=1,
                )
                for d in range(2)
            ]
            weights.append(jnp.zeros((6, modes), jnp.float32))
            pieces += halves(jnp.concatenate(weights, axis=0))
        left = jnp.concatenate(pieces, axis=0)
        there = rows_of(matrix, for_device(numbers[k]))
        term = jnp.dot(left, matrix[there, :], preferred_element_type=jnp.float32)
        total = term if total is None else total + term
    if not last:
        refs[0][...] = total
        return
    cells = base.shape[1]
    value = base[...] - scale * (total[:cells] + total[cells : 2 * cells]).T
    refs[0][...] = value
    if rows:
        refs[1][...] = value.T[:HALO]
        refs[2][...] = total[2 * cells : 2 * cells + 8] + total[2 * cells + 8 :]


def own_rows(distribution, velocity, capacity, out, token, speeds, weight, sems):
    modes, cells = velocity.shape[1], out.shape[1]
    copies = [
        pltpu.make_async_copy(velocity, speeds, sems.at[0]),
        pltpu.make_async_copy(capacity, weight, sems.at[1]),
        pltpu.make_async_copy(
            distribution.at[:, pl.ds(0, cells)], out.at[pl.ds(0, modes), :], sems.at[2]
        ),
    ]
    for copy in copies:
        copy.start()
    token[...] = jnp.zeros_like(token)
    for copy in copies[:2]:
        copy.wait()
    per = modes // LANES
    out[modes:] = jnp.zeros((out.shape[0] - modes, LANES), jnp.float32)
    for d in range(2):
        for i in range(per):
            lanes = slice(i * LANES, (i + 1) * LANES)
            out[modes + d * per + i : modes + d * per + i + 1, :] = (
                speeds[d : d + 1, lanes] * weight[:, lanes]
            )
    copies[2].wait()


def payload(numbers, slots, arrived, *refs):
    out = refs[-1]
    slot_here = for_device(numbers)

    for k, slot in enumerate(slots):

        @pl.when(slot_here == slot)
        def _(k=k):
            terms = refs[k]
            modes = terms.shape[0]
            out[:modes] = arrived[:modes] + terms[...]
            if out.shape[0] > modes:
                out[modes:] = arrived[modes:]

    @pl.when(slot_here < 0)
    def _():
        out[...] = arrived[...]


def pick(numbers, *refs):
    out = refs[-1]
    choice = for_device(numbers)
    for k, ref in enumerate(refs[:-1]):

        @pl.when(choice == k)
        def _(ref=ref):
            out[...] = ref[...]


def add(one, *refs):
    out, first = refs[-1], 0
    for piece in refs[:-1]:
        rows = slice(first, first + piece.shape[0])
        out[rows] = one[rows] + piece[...]
        first += piece.shape[0]


def add_all(*refs):
    out, token = refs[-2:]
    total = refs[0][...]
    for ref in refs[1:-2]:
        total = total + ref[...]
    out[...] = total
    token[...] = jnp.zeros_like(token)


def take_off(scale, arrived, terms, base, out):
    modes = terms.shape[0]
    out[...] = base[...] - scale * (arrived[:modes] + terms[...])


def turn_sum(scale, arrived, base, out, strip):
    modes = base.shape[0]
    value = base[...] - scale * arrived[:modes]
    out[...] = value
    strip[...] = value.T[-HALO:]


def last_sum(scale, arrived, base, other, out, value, sems):
    cells = base.shape[1]
    ahead = pltpu.make_async_copy(other, out.at[:, pl.ds(cells, cells)], sems.at[0])
    ahead.start()
    value[...] = base[...] - scale * arrived[...]
    copy = pltpu.make_async_copy(value, out.at[:, pl.ds(0, cells)], sems.at[1])
    copy.start()
    ahead.wait()
    copy.wait()


def strip_rows(distribution, leading, last):
    cells = distribution.shape[1]
    leading[...] = distribution[:, :LANES].T[:HALO]
    last[...] = distribution[:, cells - LANES :].T[-HALO:]


def strip_pairs(leading, last, out_even, out_odd):
    even = lax.axis_index("space") % 2 == 0

    @pl.when(even)
    def _():
        out_even[...] = last[...]
        out_odd[...] = leading[...]

    @pl.when(jnp.logical_not(even))
    def _():
        out_even[...] = leading[...]
        out_odd[...] = last[...]


def differences(cells):
    columns = cells // NY
    own, strip = np.zeros((cells, 4 * cells)), np.zeros((2 * HALO, 4 * cells))
    for x in range(columns):
        for y in range(NY):
            cell = x * NY + y
            for way in (-1, 1):
                for far, factor in enumerate((3.0, -4.0, 1.0)):
                    at_x, at_y = x + way * far, y + way * far
                    first = cell + (0 if way < 0 else cells)
                    factor = -way * factor
                    if at_x < 0:
                        strip[(at_x + 2) * NY + y, first] = factor
                    elif at_x >= columns:
                        strip[HALO + (at_x - columns) * NY + y, first] = factor
                    else:
                        own[at_x * NY + y, first] = factor
                    if 0 <= at_y < NY:
                        own[x * NY + at_y, first + 2 * cells] = factor
    return np.concatenate([own, own, strip, strip]).astype(jnp.bfloat16)


def strip_columns(came_even, came_odd):
    even = lax.axis_index("space") % 2 == 0
    before = jnp.where(even, came_odd[...], came_even[...])
    after = jnp.where(even, came_even[...], came_odd[...])
    parts = halves(jnp.concatenate([before, after], axis=0))
    return jnp.concatenate([p.astype(jnp.float32) for p in parts], axis=0).T.astype(jnp.bfloat16)


def still_rate(field, strip, operators, columns, kinds):
    cells = field.shape[1]
    left = jnp.concatenate([*halves(field), strip], axis=1)
    steps = jnp.dot(left, operators[...], preferred_element_type=jnp.float32)
    vx, vy, capacity = (columns[:, i : i + 1] for i in range(3))
    speeds = (jnp.maximum(vx, 0.0), jnp.minimum(vx, 0.0))
    speeds += (jnp.maximum(vy, 0.0), jnp.minimum(vy, 0.0))
    contact = jnp.where(kinds > 0, relax_rate, 0.0)
    source = jnp.where(kinds == 1, contact, -contact)
    rate = source * capacity - contact * field
    for k, speed in enumerate(speeds):
        rate = rate - (0.5 * speed) * steps[:, k * cells : (k + 1) * cells]
    return rate


def first_rest(field, came_even, came_odd, operators, table, kinds, base_a, base_b, strips):
    modes, half = base_a.shape
    block = min(modes, BLOCK)
    strips[...] = strip_columns(came_even, came_odd)

    def step(i, _):
        rows = pl.ds(pl.multiple_of(i * block, block), block)
        value = field[rows, :]
        rate = still_rate(value, strips[rows, :], operators, table[:, rows].T, kinds[...])
        base = value + time_step * rate
        base_a[rows, :] = base[:, :half]
        base_b[rows, :] = base[:, half:]
        return 0

    lax.fori_loop(0, modes // block, step, 0)


def second_rest(
    flux_scale,
    field,
    mid_a,
    mid_b,
    came_even,
    came_odd,
    operators,
    table,
    kinds,
    scattered,
    end_a,
    end_b,
    flux,
    strips,
):
    modes, half = end_a.shape
    block = min(modes, BLOCK)
    step_size = 0.5 * time_step
    strips[...] = strip_columns(came_even, came_odd)
    flux[...] = jnp.zeros_like(flux)

    def step(i, _):
        rows = pl.ds(pl.multiple_of(i * block, block), block)
        mid = jnp.concatenate([mid_a[rows, :], mid_b[rows, :]], axis=1)
        columns = table[:, rows].T
        taken = step_size * scattered[:, rows].T
        rate = still_rate(mid, strips[rows, :], operators, columns, kinds[...])
        end = 0.5 * (field[rows, :] + mid) + step_size * rate
        end_a[rows, :] = end[:, :half]
        end_b[rows, :] = end[:, half:]
        for d in range(2):
            terms = columns[:, 3 + d : 4 + d] * end - taken[:, d : d + 1] * mid
            flux[d : d + 1, :] += flux_scale * jnp.sum(terms, axis=0, keepdims=True)
        return 0

    lax.fori_loop(0, modes // block, step, 0)


def paired(to_even, to_odd):
    count = lax.axis_size("space")
    came = []
    for first, value in enumerate((to_even, to_odd)):
        pairs = [(i, i + 1) for i in range(first, count - 1, 2)]
        came.append(lax.ppermute(value, "space", pairs + [(j, i) for i, j in pairs]))
    return came


class Plan:
    def __init__(self, chips):
        self.chips = chips
        self.devices = range(2 * chips)
        sources = [self.sources(d) for d in self.devices]
        targets = [self.targets(d // 2) for d in self.devices]
        self.blocks = [
            [
                [2 * sources[e][slot][2] + e % 2 for e in (d ^ other for d in self.devices)]
                for other in (0, 1)
            ]
            for slot in range(chips)
        ]
        self.rows = [
            [[2 * targets[d][slot] + (d % 2 ^ other) for d in self.devices] for other in (0, 1)]
            for slot in range(chips)
        ]
        self.choices = [
            sorted({sources[d][slot][:2] for d in self.devices}) for slot in range(chips)
        ]
        self.picked = [
            [self.choices[slot].index(sources[d][slot][:2]) for d in self.devices]
            for slot in range(chips)
        ]
        self.sent = {}
        for stream in (0, 1):
            for step in range(1, chips):
                numbers = []
                for d in self.devices:
                    way = self.way(d, stream)
                    place = d // 2 if way > 0 else chips - 1 - d // 2
                    target = d // 2 + way * (chips - step)
                    numbers.append(targets[d].index(target) if place < step else -1)
                self.sent[stream, step] = numbers
        self.pairs = []
        for stream in (0, 1):
            up = [
                (d, d + 2) for d in self.devices[:-2] if self.way(d, stream) > 0
            ]
            self.pairs.append(up + [(j, i) for i, j in up])

    def way(self, device, stream):
        return 1 if (device // 2 + device % 2 + stream) % 2 == 0 else -1

    def sources(self, device):
        found = [(-1, -1, device // 2)]
        for step in range(self.chips - 1):
            for stream in (step % 2, 1 - step % 2):
                chip = device // 2 + self.way(device, stream) * (step + 1)
                if 0 <= chip < self.chips:
                    found.append((stream, step, chip))
        return found

    def targets(self, chip):
        found = []
        for step in range(1, self.chips):
            far = self.chips - step
            found += [t for t in (chip + far, chip - far) if 0 <= t < self.chips]
        return found + [chip]


def on_device(distribution, scatter_matrix, velocity, capacity, cell_type):
    modes, cells = distribution.shape
    total_modes = scatter_matrix.shape[0]
    half = cells // 2
    extra = -(-2 * modes // LANES // 8) * 8
    step_size = 0.5 * time_step
    part = (modes, half)
    devices = lax.axis_size("mode")
    chips = devices // 2
    plan = Plan(chips)
    call = Chain()
    across = [(i, i ^ 1) for i in range(devices)]
    cap = capacity[None, :]
    table = jnp.concatenate(
        [velocity, cap, cap * velocity, jnp.zeros((3, modes), jnp.float32)], axis=0
    )
    kinds = cell_type[None, :]

    def exchange(value, parts=1):
        cut = value.shape[0] // parts // 8 * 8
        ends = [cut * k for k in range(parts)] + [value.shape[0]]
        return [lax.ppermute(value[i:j], "mode", across) for i, j in zip(ends, ends[1:])]

    def along(stream, value):
        return lax.ppermute(value, "mode", plan.pairs[stream])

    class Round:
        def __init__(self, matrix, scale, rows):
            self.matrix, self.scale, self.rows = matrix, scale, rows
            self.terms, self.total = [], None

        def begin(self, own):
            self.own = own
            self.arrived = [[along(0, own)], [along(1, own)]]
            self.blocks = []

        def add_terms(self, field, parts=1):
            kernel = functools.partial(slot_products, plan.rows[len(self.terms)])
            mine, other = call(kernel, [part] * 2, [self.matrix, field])
            self.terms.append((mine, *exchange(other, parts)))

        def join_terms(self, *slots):
            for slot in slots:
                (self.terms[slot],) = call(add, [part], self.terms[slot])

        def take_own(self):
            self.blocks.append((self.own, *exchange(self.own)))

        def send(self, step, between=None):
            sent = {}
            for stream in (step % 2, 1 - step % 2):
                if between is not None and sent:
                    between()
                numbers = plan.sent[stream, step]
                slots = sorted({n for n in numbers if n >= 0})
                for slot in slots:
                    if isinstance(self.terms[slot], tuple):
                        self.join_terms(slot)
                arrived = self.arrived[1 - stream][step - 1]
                kernel = functools.partial(payload, numbers, slots)
                arrays = [arrived] + [self.terms[s] for s in slots]
                (value,) = call(kernel, [arrived.shape], arrays)
                sent[stream] = along(stream, value)
            for stream in (0, 1):
                self.arrived[stream].append(sent[stream])

        def take(self, slot, parts=1):
            arrays = [self.arrived[stream][step] for stream, step in plan.choices[slot]]
            kernel = functools.partial(pick, plan.picked[slot])
            (here,) = call(kernel, [arrays[0].shape], arrays)
            self.blocks.append((here, *exchange(here, parts)))

        def multiply(self, slot, base=None):
            first, last = slot == 0, base is not None
            blocks = self.blocks[slot]
            kernel = functools.partial(
                two_blocks, plan.blocks[slot], len(blocks) - 1, first, last, self.scale, self.rows
            )
            arrays = [self.matrix, *blocks]
            arrays += [] if first else [self.total]
            arrays += [base] if last else []
            outs = [(2 * half + (16 if self.rows else 0), modes)]
            if last:
                outs = [part, (HALO, modes), (8, modes)] if self.rows else [part]
            results = call(kernel, outs, arrays)
            self.total = results[0]
            return results

        def first_end(self, base):
            kernel = functools.partial(take_off, self.scale)
            arrived = self.arrived[(chips - 1) % 2][-1]
            (self.rest,) = call(kernel, [part], [arrived, self.terms[-1], base])

        def ends(self):
            return [self.arrived[chips % 2][-1], self.rest]

    own, _ = call(
        own_rows,
        [(modes + extra, half), (8, LANES)],
        [distribution, velocity, cap],
        places=[HBM] * 3,
        scratch=[
            pltpu.VMEM((2, modes), jnp.float32),
            pltpu.VMEM((1, modes), jnp.float32),
            pltpu.SemaphoreType.DMA((3,)),
        ],
        room=56,
    )
    one = Round(None, time_step, True)
    one.begin(own)
    *terms, matrix = call(
        functools.partial(load_and_products, plan.rows, half),
        [part] * (2 * chips) + [jax.ShapeDtypeStruct(scatter_matrix.shape, jnp.bfloat16)],
        [scatter_matrix, distribution],
        places=[HBM] * 2,
        scratch=[
            pltpu.VMEM(part, jnp.float32),
            pltpu.SemaphoreType.DMA((2 * chips + 1,)),
        ],
        room=28,
    )
    one.matrix = matrix
    one.terms = [(terms[2 * s], *exchange(terms[2 * s + 1])) for s in range(chips)]
    one.take_own()
    operators = jnp.asarray(differences(cells))
    aside = [pltpu.VMEM((modes, 4 * HALO), jnp.bfloat16)]
    strips = None
    for step in range(1, chips):
        if step == 1:
            one.take(1)
        one.send(step)
        if step == 1:
            one.join_terms(*(s for s in range(chips) if isinstance(one.terms[s], tuple)))
            strips = call(strip_rows, [(HALO, modes)] * 2, [distribution])
            strips = paired(*call(strip_pairs, [(HALO, modes)] * 2, strips))
        else:
            one.take(step, 2 if step == chips - 1 else 1)
        one.multiply(step - 1)
        if step == min(2, chips - 1):
            base_a, base_b = call(
                first_rest,
                [part] * 2,
                [distribution, *strips, operators, table, kinds],
                scratch=aside,
            )
    mid_a, leading, scattered = one.multiply(chips - 1, base_a)

    two = Round(matrix, step_size, False)
    one.first_end(base_b)
    two.add_terms(mid_a, 1)
    mid_b, last = call(
        functools.partial(turn_sum, time_step), [part, (HALO, modes)], one.ends()
    )
    two.begin(mid_b)
    for slot in range(1, chips - 1):
        two.add_terms(mid_a)
    two.join_terms(0)
    two.take_own()
    strips = call(strip_pairs, [(HALO, modes)] * 2, [leading, last])
    strips = paired(*strips)
    flux = None
    for step in range(1, chips):
        if step == 1:
            two.send(step)
            two.join_terms(*(s for s in range(1, chips - 1) if isinstance(two.terms[s], tuple)))
        elif step == 2:
            two.send(step, lambda: flux.over(1))
        elif step == chips - 1:
            two.send(step, lambda: flux.over(*range(2, devices, 2)))
        else:
            two.send(step)
        if step == 2 and isinstance(two.terms[-1], tuple):
            two.join_terms(chips - 1)
        two.take(step, 2 if step >= chips - 2 else 1)
        if step == 1:
            two.add_terms(mid_a)
        if step < chips - 1:
            two.multiply(step - 1)
        if step == chips - 2:
            two.multiply(step)
        if step == 1:
            end_a, end_b, part_flux = call(
                functools.partial(second_rest, 1.0 / math.sqrt(total_modes)),
                [part, part, (2, cells)],
                [distribution, mid_a, mid_b, *strips, operators, table, kinds, scattered],
                scratch=aside,
            )
            flux = Flux(call, part_flux, devices)
    (last_b,) = two.multiply(chips - 1, end_b)
    heat_flux = flux.value
    if isinstance(two.terms[-1], tuple):
        two.join_terms(chips - 1)
    two.first_end(end_a)
    (updated,) = call(
        functools.partial(last_sum, step_size),
        [(modes, cells)],
        [*two.ends(), last_b],
        scratch=[pltpu.VMEM(part, jnp.float32), pltpu.SemaphoreType.DMA((2,))],
        out_specs=[HBM],
    )
    return (updated, heat_flux)


class Flux:
    def __init__(self, call, value, devices):
        self.call, self.value, self.devices = call, value, devices

    def over(self, *bits):
        came = [
            lax.ppermute(self.value, "mode", [(i, i ^ bit) for i in range(self.devices)])
            for bit in bits
        ]
        self.value, _ = self.call(add_all, [self.value.shape, (8, LANES)], [self.value, *came])


def solution(mesh):
    return jax.shard_map(
        on_device,
        mesh=mesh,
        in_specs=(P("mode", "space"), P(None, "mode"), P(None, "mode"), P("mode"), P("space")),
        out_specs=(P("mode", "space"), P(None, "space")),
        check_vma=False,
    )
```

```python
import functools
import math

import numpy as np

import jax
import jax.numpy as jnp
from jax import lax
from jax.experimental import pallas as pl
from jax.experimental.pallas import tpu as pltpu
from jax.sharding import PartitionSpec as P

NY = 16
HALO = 2 * NY
LANES = 128
BLOCK = 512


relax_rate = 0.5
time_step = 0.5

VMEM = pl.BlockSpec(memory_space=pltpu.VMEM)
ANY = pl.BlockSpec(memory_space=pl.ANY)
HBM = pl.BlockSpec(memory_space=pltpu.HBM)


class Chain:
    def __init__(self):
        self.last = None

    def __call__(self, kernel, outs, arrays, places=None, scratch=(), out_specs=None, room=16):
        extra = [] if self.last is None else [self.last]
        skip = len(extra)
        first = len(arrays)

        def body(*refs):
            kernel(*refs[:first], *refs[first + skip :])

        results = pl.pallas_call(
            body,
            out_shape=[
                jax.ShapeDtypeStruct(shape, jnp.float32) if isinstance(shape, tuple) else shape
                for shape in outs
            ],
            in_specs=list(places or [VMEM] * len(arrays)) + [ANY] * skip,
            out_specs=out_specs or [VMEM] * len(outs),
            scratch_shapes=list(scratch),
            compiler_params=pltpu.CompilerParams(vmem_limit_bytes=room * 1024 * 1024),
            cost_estimate=pl.CostEstimate(flops=1024, bytes_accessed=1024, transcendentals=0),
            name=getattr(kernel, "func", kernel).__name__,
        )(*arrays, *extra)
        self.last = results[-1]
        return results


def halves(value):
    high = value.astype(jnp.bfloat16)
    low = (value - high.astype(jnp.float32)).astype(jnp.bfloat16)
    return high, low


def for_device(numbers):
    if len(set(numbers)) == 1:
        return numbers[0]
    me = lax.axis_index("mode")
    chosen = jnp.int32(numbers[0])
    for device, number in enumerate(numbers[1:], 1):
        chosen = jnp.where(me == device, jnp.int32(number), chosen)
    return chosen


def rows_of(matrix, block):
    modes = matrix.shape[1]
    return pl.ds(pl.multiple_of(block * modes, modes), modes)


def one_slot(blocks, matrix, parts, mine, other):
    cells = mine.shape[1]
    for block, out in zip(blocks, (mine, other)):
        both = jnp.dot(matrix[rows_of(matrix, block), :], parts, preferred_element_type=jnp.float32)
        out[...] = both[:, :cells] + both[:, cells:]


def slot_products(blocks, matrix, field, mine, other):
    blocks = [for_device(numbers) for numbers in blocks]
    parts = jnp.concatenate(halves(field[...]), axis=1)
    one_slot(blocks, matrix, parts, mine, other)


def load_and_products(blocks, column, matrix, distribution, *refs):
    slots = len(blocks)
    outs, (held, field, sems) = refs[: 2 * slots], refs[2 * slots :]
    cells = field.shape[1]
    start = pltpu.make_async_copy(
        distribution.at[:, pl.ds(column, cells)], field, sems.at[2 * slots]
    )
    start.start()
    blocks = [[for_device(numbers) for numbers in pair] for pair in blocks]
    copies = []
    for slot, pair in enumerate(blocks):
        for k, block in enumerate(pair):
            rows = rows_of(held, block)
            copies.append(
                pltpu.make_async_copy(
                    matrix.at[rows, :], held.at[rows, :], sems.at[2 * slot + k]
                )
            )
            copies[-1].start()
    start.wait()
    parts = jnp.concatenate(halves(field[...]), axis=1)
    for slot, pair in enumerate(blocks):
        for k in range(2):
            copies[2 * slot + k].wait()
        one_slot(pair, held, parts, outs[2 * slot], outs[2 * slot + 1])


def two_blocks(numbers, parts, first, last, scale, rows, matrix, *refs):
    modes = matrix.shape[1]
    blocks, refs = [[refs[0]], refs[1 : 1 + parts]], refs[1 + parts :]
    if not first:
        before, refs = refs[0], refs[1:]
    if last:
        base, refs = refs[0], refs[1:]
    total = None if first else before[...]
    for k, pieces in enumerate(blocks):
        block = jnp.concatenate([piece[...] for piece in pieces], axis=0)
        pieces = list(halves(block[:modes].T))
        if rows:
            weights = [
                jnp.concatenate(
                    [
                        block[modes + i : modes + i + 1, :]
                        for i in range(d * modes // LANES, (d + 1) * modes // LANES)
                    ],
                    axis=1,
                )
                for d in range(2)
            ]
            weights.append(jnp.zeros((6, modes), jnp.float32))
            pieces += halves(jnp.concatenate(weights, axis=0))
        left = jnp.concatenate(pieces, axis=0)
        there = rows_of(matrix, for_device(numbers[k]))
        term = jnp.dot(left, matrix[there, :], preferred_element_type=jnp.float32)
        total = term if total is None else total + term
    if not last:
        refs[0][...] = total
        return
    cells = base.shape[1]
    value = base[...] - scale * (total[:cells] + total[cells : 2 * cells]).T
    refs[0][...] = value
    if rows:
        refs[1][...] = value.T[:HALO]
        refs[2][...] = total[2 * cells : 2 * cells + 8] + total[2 * cells + 8 :]


def own_rows(distribution, velocity, capacity, out, token, speeds, weight, sems):
    modes, cells = velocity.shape[1], out.shape[1]
    copies = [
        pltpu.make_async_copy(velocity, speeds, sems.at[0]),
        pltpu.make_async_copy(capacity, weight, sems.at[1]),
        pltpu.make_async_copy(
            distribution.at[:, pl.ds(0, cells)], out.at[pl.ds(0, modes), :], sems.at[2]
        ),
    ]
    for copy in copies:
        copy.start()
    token[...] = jnp.zeros_like(token)
    for copy in copies[:2]:
        copy.wait()
    per = modes // LANES
    out[modes:] = jnp.zeros((out.shape[0] - modes, LANES), jnp.float32)
    for d in range(2):
        for i in range(per):
            lanes = slice(i * LANES, (i + 1) * LANES)
            out[modes + d * per + i : modes + d * per + i + 1, :] = (
                speeds[d : d + 1, lanes] * weight[:, lanes]
            )
    copies[2].wait()


def payload(numbers, slots, arrived, *refs):
    out = refs[-1]
    slot_here = for_device(numbers)

    for k, slot in enumerate(slots):

        @pl.when(slot_here == slot)
        def _(k=k):
            terms = refs[k]
            modes = terms.shape[0]
            out[:modes] = arrived[:modes] + terms[...]
            if out.shape[0] > modes:
                out[modes:] = arrived[modes:]

    @pl.when(slot_here < 0)
    def _():
        out[...] = arrived[...]


def pick(numbers, *refs):
    out = refs[-1]
    choice = for_device(numbers)
    for k, ref in enumerate(refs[:-1]):

        @pl.when(choice == k)
        def _(ref=ref):
            out[...] = ref[...]


def add(one, *refs):
    out, first = refs[-1], 0
    for piece in refs[:-1]:
        rows = slice(first, first + piece.shape[0])
        out[rows] = one[rows] + piece[...]
        first += piece.shape[0]


def add_all(*refs):
    out, token = refs[-2:]
    total = refs[0][...]
    for ref in refs[1:-2]:
        total = total + ref[...]
    out[...] = total
    token[...] = jnp.zeros_like(token)


def take_off(scale, arrived, terms, base, out):
    modes = terms.shape[0]
    out[...] = base[...] - scale * (arrived[:modes] + terms[...])


def turn_sum(scale, arrived, base, out, strip):
    modes = base.shape[0]
    value = base[...] - scale * arrived[:modes]
    out[...] = value
    strip[...] = value.T[-HALO:]


def last_sum(scale, arrived, base, other, out, value, sems):
    cells = base.shape[1]
    ahead = pltpu.make_async_copy(other, out.at[:, pl.ds(cells, cells)], sems.at[0])
    ahead.start()
    value[...] = base[...] - scale * arrived[...]
    copy = pltpu.make_async_copy(value, out.at[:, pl.ds(0, cells)], sems.at[1])
    copy.start()
    ahead.wait()
    copy.wait()


def strip_rows(distribution, leading, last):
    cells = distribution.shape[1]
    leading[...] = distribution[:, :LANES].T[:HALO]
    last[...] = distribution[:, cells - LANES :].T[-HALO:]


def strip_pairs(leading, last, out_even, out_odd):
    even = lax.axis_index("space") % 2 == 0

    @pl.when(even)
    def _():
        out_even[...] = last[...]
        out_odd[...] = leading[...]

    @pl.when(jnp.logical_not(even))
    def _():
        out_even[...] = leading[...]
        out_odd[...] = last[...]


def differences(cells):
    columns = cells // NY
    own, strip = np.zeros((cells, 4 * cells)), np.zeros((2 * HALO, 4 * cells))
    for x in range(columns):
        for y in range(NY):
            cell = x * NY + y
            for way in (-1, 1):
                for far, factor in enumerate((3.0, -4.0, 1.0)):
                    at_x, at_y = x + way * far, y + way * far
                    first = cell + (0 if way < 0 else cells)
                    factor = -way * factor
                    if at_x < 0:
                        strip[(at_x + 2) * NY + y, first] = factor
                    elif at_x >= columns:
                        strip[HALO + (at_x - columns) * NY + y, first] = factor
                    else:
                        own[at_x * NY + y, first] = factor
                    if 0 <= at_y < NY:
                        own[x * NY + at_y, first + 2 * cells] = factor
    return np.concatenate([own, own, strip, strip]).astype(jnp.bfloat16)


def strip_columns(came_even, came_odd, out):
    even = lax.axis_index("space") % 2 == 0
    before = jnp.where(even, came_odd[...], came_even[...])
    after = jnp.where(even, came_even[...], came_odd[...])
    parts = halves(jnp.concatenate([before, after], axis=0))
    rows = jnp.concatenate([p.astype(jnp.float32) for p in parts], axis=0)
    out[...] = rows.T.astype(jnp.bfloat16)


def still_rate(field, strip, operators, columns, kinds):
    cells = field.shape[1]
    left = jnp.concatenate([*halves(field), strip], axis=1)
    steps = jnp.dot(left, operators[...], preferred_element_type=jnp.float32)
    vx, vy, capacity = (columns[:, i : i + 1] for i in range(3))
    speeds = (jnp.maximum(vx, 0.0), jnp.minimum(vx, 0.0))
    speeds += (jnp.maximum(vy, 0.0), jnp.minimum(vy, 0.0))
    contact = jnp.where(kinds > 0, relax_rate, 0.0)
    source = jnp.where(kinds == 1, contact, -contact)
    rate = source * capacity - contact * field
    for k, speed in enumerate(speeds):
        rate = rate - (0.5 * speed) * steps[:, k * cells : (k + 1) * cells]
    return rate


def first_rest(field, strips, operators, table, kinds, base_a, base_b):
    modes, half = base_a.shape
    block = min(modes, BLOCK)

    def step(i, _):
        rows = pl.ds(pl.multiple_of(i * block, block), block)
        value = field[rows, :]
        rate = still_rate(value, strips[rows, :], operators, table[:, rows].T, kinds[...])
        base = value + time_step * rate
        base_a[rows, :] = base[:, :half]
        base_b[rows, :] = base[:, half:]
        return 0

    lax.fori_loop(0, modes // block, step, 0)


def second_rest(
    flux_scale,
    field,
    mid_a,
    mid_b,
    strips,
    operators,
    table,
    kinds,
    scattered,
    end_a,
    end_b,
    flux,
):
    modes, half = end_a.shape
    block = min(modes, BLOCK)
    step_size = 0.5 * time_step
    flux[...] = jnp.zeros_like(flux)

    def step(i, _):
        rows = pl.ds(pl.multiple_of(i * block, block), block)
        mid = jnp.concatenate([mid_a[rows, :], mid_b[rows, :]], axis=1)
        columns = table[:, rows].T
        taken = step_size * scattered[:, rows].T
        rate = still_rate(mid, strips[rows, :], operators, columns, kinds[...])
        end = 0.5 * (field[rows, :] + mid) + step_size * rate
        end_a[rows, :] = end[:, :half]
        end_b[rows, :] = end[:, half:]
        for d in range(2):
            terms = columns[:, 3 + d : 4 + d] * end - taken[:, d : d + 1] * mid
            flux[d : d + 1, :] += flux_scale * jnp.sum(terms, axis=0, keepdims=True)
        return 0

    lax.fori_loop(0, modes // block, step, 0)


def paired(to_even, to_odd):
    count = lax.axis_size("space")
    came = []
    for first, value in enumerate((to_even, to_odd)):
        pairs = [(i, i + 1) for i in range(first, count - 1, 2)]
        came.append(lax.ppermute(value, "space", pairs + [(j, i) for i, j in pairs]))
    return came


class Plan:
    def __init__(self, chips):
        self.chips = chips
        self.devices = range(2 * chips)
        sources = [self.sources(d) for d in self.devices]
        targets = [self.targets(d // 2) for d in self.devices]
        self.blocks = [
            [
                [2 * sources[e][slot][2] + e % 2 for e in (d ^ other for d in self.devices)]
                for other in (0, 1)
            ]
            for slot in range(chips)
        ]
        self.rows = [
            [[2 * targets[d][slot] + (d % 2 ^ other) for d in self.devices] for other in (0, 1)]
            for slot in range(chips)
        ]
        self.choices = [
            sorted({sources[d][slot][:2] for d in self.devices}) for slot in range(chips)
        ]
        self.picked = [
            [self.choices[slot].index(sources[d][slot][:2]) for d in self.devices]
            for slot in range(chips)
        ]
        self.sent = {}
        for stream in (0, 1):
            for step in range(1, chips):
                numbers = []
                for d in self.devices:
                    way = self.way(d, stream)
                    place = d // 2 if way > 0 else chips - 1 - d // 2
                    target = d // 2 + way * (chips - step)
                    numbers.append(targets[d].index(target) if place < step else -1)
                self.sent[stream, step] = numbers
        self.pairs = []
        for stream in (0, 1):
            up = [
                (d, d + 2) for d in self.devices[:-2] if self.way(d, stream) > 0
            ]
            self.pairs.append(up + [(j, i) for i, j in up])

    def way(self, device, stream):
        return 1 if (device // 2 + device % 2 + stream) % 2 == 0 else -1

    def sources(self, device):
        found = [(-1, -1, device // 2)]
        for step in range(self.chips - 1):
            for stream in (step % 2, 1 - step % 2):
                chip = device // 2 + self.way(device, stream) * (step + 1)
                if 0 <= chip < self.chips:
                    found.append((stream, step, chip))
        return found

    def targets(self, chip):
        found = []
        for step in range(1, self.chips):
            far = self.chips - step
            found += [t for t in (chip + far, chip - far) if 0 <= t < self.chips]
        return found + [chip]


def on_device(distribution, scatter_matrix, velocity, capacity, cell_type):
    modes, cells = distribution.shape
    total_modes = scatter_matrix.shape[0]
    half = cells // 2
    extra = -(-2 * modes // LANES // 8) * 8
    step_size = 0.5 * time_step
    part = (modes, half)
    devices = lax.axis_size("mode")
    chips = devices // 2
    plan = Plan(chips)
    call = Chain()
    across = [(i, i ^ 1) for i in range(devices)]
    cap = capacity[None, :]
    table = jnp.concatenate(
        [velocity, cap, cap * velocity, jnp.zeros((3, modes), jnp.float32)], axis=0
    )
    kinds = cell_type[None, :]

    def exchange(value, parts=1):
        cut = value.shape[0] // parts // 8 * 8
        ends = [cut * k for k in range(parts)] + [value.shape[0]]
        return [lax.ppermute(value[i:j], "mode", across) for i, j in zip(ends, ends[1:])]

    def along(stream, value):
        return lax.ppermute(value, "mode", plan.pairs[stream])

    class Round:
        def __init__(self, matrix, scale, rows):
            self.matrix, self.scale, self.rows = matrix, scale, rows
            self.terms, self.total = [], None

        def begin(self, own):
            self.own = own
            self.arrived = [[along(0, own)], [along(1, own)]]
            self.blocks = []

        def add_terms(self, field, parts=1):
            kernel = functools.partial(slot_products, plan.rows[len(self.terms)])
            mine, other = call(kernel, [part] * 2, [self.matrix, field])
            self.terms.append((mine, *exchange(other, parts)))

        def join_terms(self, *slots):
            for slot in slots:
                (self.terms[slot],) = call(add, [part], self.terms[slot])

        def take_own(self):
            self.blocks.append((self.own, *exchange(self.own)))

        def send(self, step, between=None):
            sent = {}
            for stream in (step % 2, 1 - step % 2):
                if between is not None and sent:
                    between()
                numbers = plan.sent[stream, step]
                slots = sorted({n for n in numbers if n >= 0})
                for slot in slots:
                    if isinstance(self.terms[slot], tuple):
                        self.join_terms(slot)
                arrived = self.arrived[1 - stream][step - 1]
                kernel = functools.partial(payload, numbers, slots)
                arrays = [arrived] + [self.terms[s] for s in slots]
                (value,) = call(kernel, [arrived.shape], arrays)
                sent[stream] = along(stream, value)
            for stream in (0, 1):
                self.arrived[stream].append(sent[stream])

        def take(self, slot, parts=1):
            arrays = [self.arrived[stream][step] for stream, step in plan.choices[slot]]
            kernel = functools.partial(pick, plan.picked[slot])
            (here,) = call(kernel, [arrays[0].shape], arrays)
            self.blocks.append((here, *exchange(here, parts)))

        def multiply(self, slot, base=None):
            first, last = slot == 0, base is not None
            blocks = self.blocks[slot]
            kernel = functools.partial(
                two_blocks, plan.blocks[slot], len(blocks) - 1, first, last, self.scale, self.rows
            )
            arrays = [self.matrix, *blocks]
            arrays += [] if first else [self.total]
            arrays += [base] if last else []
            outs = [(2 * half + (16 if self.rows else 0), modes)]
            if last:
                outs = [part, (HALO, modes), (8, modes)] if self.rows else [part]
            results = call(kernel, outs, arrays)
            self.total = results[0]
            return results

        def first_end(self, base):
            kernel = functools.partial(take_off, self.scale)
            arrived = self.arrived[(chips - 1) % 2][-1]
            (self.rest,) = call(kernel, [part], [arrived, self.terms[-1], base])

        def ends(self):
            return [self.arrived[chips % 2][-1], self.rest]

    own, _ = call(
        own_rows,
        [(modes + extra, half), (8, LANES)],
        [distribution, velocity, cap],
        places=[HBM] * 3,
        scratch=[
            pltpu.VMEM((2, modes), jnp.float32),
            pltpu.VMEM((1, modes), jnp.float32),
            pltpu.SemaphoreType.DMA((3,)),
        ],
        room=56,
    )
    one = Round(None, time_step, True)
    one.begin(own)
    *terms, matrix = call(
        functools.partial(load_and_products, plan.rows, half),
        [part] * (2 * chips) + [jax.ShapeDtypeStruct(scatter_matrix.shape, jnp.bfloat16)],
        [scatter_matrix, distribution],
        places=[HBM] * 2,
        scratch=[
            pltpu.VMEM(part, jnp.float32),
            pltpu.SemaphoreType.DMA((2 * chips + 1,)),
        ],
        room=28,
    )
    one.matrix = matrix
    one.terms = [(terms[2 * s], *exchange(terms[2 * s + 1])) for s in range(chips)]
    one.take_own()
    operators = jnp.asarray(differences(cells))
    strips = None

    def unpack():
        nonlocal strips
        shape = jax.ShapeDtypeStruct((modes, 4 * HALO), jnp.bfloat16)
        (strips,) = call(strip_columns, [shape], strips)

    for step in range(1, chips):
        if step == 1:
            one.take(1)
        one.send(step, unpack if step == 2 else None)
        if step == 1:
            one.join_terms(*(s for s in range(chips) if isinstance(one.terms[s], tuple)))
            strips = call(strip_rows, [(HALO, modes)] * 2, [distribution])
            strips = paired(*call(strip_pairs, [(HALO, modes)] * 2, strips))
        else:
            one.take(step, 2 if step == chips - 1 else 1)
        one.multiply(step - 1)
        if step == min(2, chips - 1):
            base_a, base_b = call(
                first_rest,
                [part] * 2,
                [distribution, strips, operators, table, kinds],
            )
    mid_a, leading, scattered = one.multiply(chips - 1, base_a)

    two = Round(matrix, step_size, False)
    two.add_terms(mid_a, 1)
    one.first_end(base_b)
    mid_b, last = call(
        functools.partial(turn_sum, time_step), [part, (HALO, modes)], one.ends()
    )
    two.begin(mid_b)
    two.add_terms(mid_a)
    two.add_terms(mid_a)
    two.join_terms(0)
    strips = paired(*call(strip_pairs, [(HALO, modes)] * 2, [leading, last]))
    flux = None
    for step in range(1, chips):
        if step == 1:
            two.send(step, unpack)
            two.take_own()
            two.join_terms(1, 2)
        elif step == 2:
            two.send(step, lambda: flux.over(1))
            two.join_terms(*range(3, chips))
        elif step == chips - 1:
            two.send(step, lambda: flux.over(*range(2, devices, 2)))
        else:
            two.send(step)
        two.take(step, 2 if step >= chips - 2 else 1)
        if step == 1:
            for slot in range(3, chips):
                two.add_terms(mid_a)
        if step < chips - 1:
            two.multiply(step - 1)
        if step == chips - 2:
            two.multiply(step)
        if step == 1:
            end_a, end_b, part_flux = call(
                functools.partial(second_rest, 1.0 / math.sqrt(total_modes)),
                [part, part, (2, cells)],
                [distribution, mid_a, mid_b, strips, operators, table, kinds, scattered],
            )
            flux = Flux(call, part_flux, devices)
    (last_b,) = two.multiply(chips - 1, end_b)
    heat_flux = flux.value
    two.first_end(end_a)
    (updated,) = call(
        functools.partial(last_sum, step_size),
        [(modes, cells)],
        [*two.ends(), last_b],
        scratch=[pltpu.VMEM(part, jnp.float32), pltpu.SemaphoreType.DMA((2,))],
        out_specs=[HBM],
    )
    return (updated, heat_flux)


class Flux:
    def __init__(self, call, value, devices):
        self.call, self.value, self.devices = call, value, devices

    def over(self, *bits):
        came = [
            lax.ppermute(self.value, "mode", [(i, i ^ bit) for i in range(self.devices)])
            for bit in bits
        ]
        self.value, _ = self.call(add_all, [self.value.shape, (8, LANES)], [self.value, *came])


def solution(mesh):
    return jax.shard_map(
        on_device,
        mesh=mesh,
        in_specs=(P("mode", "space"), P(None, "mode"), P(None, "mode"), P("mode"), P("space")),
        out_specs=(P("mode", "space"), P(None, "space")),
        check_vma=False,
    )
```

```python
import functools
import math

import numpy as np

import jax
import jax.numpy as jnp
from jax import lax
from jax.experimental import pallas as pl
from jax.experimental.pallas import tpu as pltpu
from jax.sharding import PartitionSpec as P

NY = 16
HALO = 2 * NY
LANES = 128
BLOCK = 512


relax_rate = 0.5
time_step = 0.5

VMEM = pl.BlockSpec(memory_space=pltpu.VMEM)
ANY = pl.BlockSpec(memory_space=pl.ANY)
HBM = pl.BlockSpec(memory_space=pltpu.HBM)


class Chain:
    def __init__(self):
        self.last = None

    def __call__(self, kernel, outs, arrays, places=None, scratch=(), out_specs=None, room=16):
        extra = [] if self.last is None else [self.last]
        skip = len(extra)
        first = len(arrays)

        def body(*refs):
            kernel(*refs[:first], *refs[first + skip :])

        results = pl.pallas_call(
            body,
            out_shape=[
                jax.ShapeDtypeStruct(shape, jnp.float32) if isinstance(shape, tuple) else shape
                for shape in outs
            ],
            in_specs=list(places or [VMEM] * len(arrays)) + [ANY] * skip,
            out_specs=out_specs or [VMEM] * len(outs),
            scratch_shapes=list(scratch),
            compiler_params=pltpu.CompilerParams(vmem_limit_bytes=room * 1024 * 1024),
            cost_estimate=pl.CostEstimate(flops=1024, bytes_accessed=1024, transcendentals=0),
            name=getattr(kernel, "func", kernel).__name__,
        )(*arrays, *extra)
        self.last = results[-1]
        return results


def halves(value):
    high = value.astype(jnp.bfloat16)
    low = (value - high.astype(jnp.float32)).astype(jnp.bfloat16)
    return high, low


def for_device(numbers):
    if len(set(numbers)) == 1:
        return numbers[0]
    me = lax.axis_index("mode")
    chosen = jnp.int32(numbers[0])
    for device, number in enumerate(numbers[1:], 1):
        chosen = jnp.where(me == device, jnp.int32(number), chosen)
    return chosen


def rows_of(matrix, block):
    modes = matrix.shape[1]
    return pl.ds(pl.multiple_of(block * modes, modes), modes)


def one_slot(blocks, matrix, parts, mine, other):
    cells = mine.shape[1]
    for block, out in zip(blocks, (mine, other)):
        both = jnp.dot(matrix[rows_of(matrix, block), :], parts, preferred_element_type=jnp.float32)
        out[...] = both[:, :cells] + both[:, cells:]


def slot_products(blocks, matrix, field, mine, other):
    blocks = [for_device(numbers) for numbers in blocks]
    parts = jnp.concatenate(halves(field[...]), axis=1)
    one_slot(blocks, matrix, parts, mine, other)


def load_and_products(blocks, column, matrix, distribution, *refs):
    slots = len(blocks)
    outs, (held, field, sems) = refs[: 2 * slots], refs[2 * slots :]
    cells = field.shape[1]
    start = pltpu.make_async_copy(
        distribution.at[:, pl.ds(column, cells)], field, sems.at[2 * slots]
    )
    start.start()
    blocks = [[for_device(numbers) for numbers in pair] for pair in blocks]
    copies = []
    for slot, pair in enumerate(blocks):
        for k, block in enumerate(pair):
            rows = rows_of(held, block)
            copies.append(
                pltpu.make_async_copy(
                    matrix.at[rows, :], held.at[rows, :], sems.at[2 * slot + k]
                )
            )
            copies[-1].start()
    start.wait()
    parts = jnp.concatenate(halves(field[...]), axis=1)
    for slot, pair in enumerate(blocks):
        for k in range(2):
            copies[2 * slot + k].wait()
        one_slot(pair, held, parts, outs[2 * slot], outs[2 * slot + 1])


def two_blocks(numbers, parts, first, last, scale, rows, matrix, *refs):
    modes = matrix.shape[1]
    blocks, refs = [[refs[0]], refs[1 : 1 + parts]], refs[1 + parts :]
    if not first:
        before, refs = refs[0], refs[1:]
    if last:
        base, refs = refs[0], refs[1:]
    total = None if first else before[...]
    for k, pieces in enumerate(blocks):
        block = jnp.concatenate([piece[...] for piece in pieces], axis=0)
        pieces = list(halves(block[:modes].T))
        if rows:
            weights = [
                jnp.concatenate(
                    [
                        block[modes + i : modes + i + 1, :]
                        for i in range(d * modes // LANES, (d + 1) * modes // LANES)
                    ],
                    axis=1,
                )
                for d in range(2)
            ]
            weights.append(jnp.zeros((6, modes), jnp.float32))
            pieces += halves(jnp.concatenate(weights, axis=0))
        left = jnp.concatenate(pieces, axis=0)
        there = rows_of(matrix, for_device(numbers[k]))
        term = jnp.dot(left, matrix[there, :], preferred_element_type=jnp.float32)
        total = term if total is None else total + term
    if not last:
        refs[0][...] = total
        return
    cells = base.shape[1]
    value = base[...] - scale * (total[:cells] + total[cells : 2 * cells]).T
    refs[0][...] = value
    if rows:
        refs[1][...] = value.T[:HALO]
        refs[2][...] = total[2 * cells : 2 * cells + 8] + total[2 * cells + 8 :]


def own_rows(distribution, velocity, capacity, out, token, speeds, weight, sems):
    modes, cells = velocity.shape[1], out.shape[1]
    copies = [
        pltpu.make_async_copy(velocity, speeds, sems.at[0]),
        pltpu.make_async_copy(capacity, weight, sems.at[1]),
        pltpu.make_async_copy(
            distribution.at[:, pl.ds(0, cells)], out.at[pl.ds(0, modes), :], sems.at[2]
        ),
    ]
    for copy in copies:
        copy.start()
    token[...] = jnp.zeros_like(token)
    for copy in copies[:2]:
        copy.wait()
    per = modes // LANES
    out[modes:] = jnp.zeros((out.shape[0] - modes, LANES), jnp.float32)
    for d in range(2):
        for i in range(per):
            lanes = slice(i * LANES, (i + 1) * LANES)
            out[modes + d * per + i : modes + d * per + i + 1, :] = (
                speeds[d : d + 1, lanes] * weight[:, lanes]
            )
    copies[2].wait()


def payload(numbers, slots, arrived, *refs):
    out = refs[-1]
    slot_here = for_device(numbers)

    for k, slot in enumerate(slots):

        @pl.when(slot_here == slot)
        def _(k=k):
            terms = refs[k]
            modes = terms.shape[0]
            out[:modes] = arrived[:modes] + terms[...]
            if out.shape[0] > modes:
                out[modes:] = arrived[modes:]

    @pl.when(slot_here < 0)
    def _():
        out[...] = arrived[...]


def pick(numbers, *refs):
    out = refs[-1]
    choice = for_device(numbers)
    for k, ref in enumerate(refs[:-1]):

        @pl.when(choice == k)
        def _(ref=ref):
            out[...] = ref[...]


def add(one, *refs):
    out, first = refs[-1], 0
    for piece in refs[:-1]:
        rows = slice(first, first + piece.shape[0])
        out[rows] = one[rows] + piece[...]
        first += piece.shape[0]


def pass_on(value, out):
    out[...] = value[...]


def add_all(*refs):
    out, token = refs[-2:]
    total = refs[0][...]
    for ref in refs[1:-2]:
        total = total + ref[...]
    out[...] = total
    token[...] = jnp.zeros_like(token)


def take_off(scale, arrived, terms, base, out):
    modes = terms.shape[0]
    out[...] = base[...] - scale * (arrived[:modes] + terms[...])


def turn_sum(scale, arrived, base, out, strip):
    modes = base.shape[0]
    value = base[...] - scale * arrived[:modes]
    out[...] = value
    strip[...] = value.T[-HALO:]


def last_sum(scale, arrived, base, other, out, value, sems):
    cells = base.shape[1]
    ahead = pltpu.make_async_copy(other, out.at[:, pl.ds(cells, cells)], sems.at[0])
    ahead.start()
    value[...] = base[...] - scale * arrived[...]
    copy = pltpu.make_async_copy(value, out.at[:, pl.ds(0, cells)], sems.at[1])
    copy.start()
    ahead.wait()
    copy.wait()


def strip_rows(distribution, leading, last):
    cells = distribution.shape[1]
    leading[...] = distribution[:, :LANES].T[:HALO]
    last[...] = distribution[:, cells - LANES :].T[-HALO:]


def strip_pairs(leading, last, out_even, out_odd):
    even = lax.axis_index("space") % 2 == 0

    @pl.when(even)
    def _():
        out_even[...] = last[...]
        out_odd[...] = leading[...]

    @pl.when(jnp.logical_not(even))
    def _():
        out_even[...] = leading[...]
        out_odd[...] = last[...]


def differences(cells):
    columns = cells // NY
    own, strip = np.zeros((cells, 4 * cells)), np.zeros((2 * HALO, 4 * cells))
    for x in range(columns):
        for y in range(NY):
            cell = x * NY + y
            for way in (-1, 1):
                for far, factor in enumerate((3.0, -4.0, 1.0)):
                    at_x, at_y = x + way * far, y + way * far
                    first = cell + (0 if way < 0 else cells)
                    factor = -way * factor
                    if at_x < 0:
                        strip[(at_x + 2) * NY + y, first] = factor
                    elif at_x >= columns:
                        strip[HALO + (at_x - columns) * NY + y, first] = factor
                    else:
                        own[at_x * NY + y, first] = factor
                    if 0 <= at_y < NY:
                        own[x * NY + at_y, first + 2 * cells] = factor
    return np.concatenate([own, own, strip, strip]).astype(jnp.bfloat16)


def strip_columns(came_even, came_odd, out):
    even = lax.axis_index("space") % 2 == 0
    before = jnp.where(even, came_odd[...], came_even[...])
    after = jnp.where(even, came_even[...], came_odd[...])
    parts = halves(jnp.concatenate([before, after], axis=0))
    rows = jnp.concatenate([p.astype(jnp.float32) for p in parts], axis=0)
    out[...] = rows.T.astype(jnp.bfloat16)


def still_rate(field, strip, operators, columns, kinds):
    cells = field.shape[1]
    left = jnp.concatenate([*halves(field), strip], axis=1)
    steps = jnp.dot(left, operators[...], preferred_element_type=jnp.float32)
    vx, vy, capacity = (columns[:, i : i + 1] for i in range(3))
    speeds = (jnp.maximum(vx, 0.0), jnp.minimum(vx, 0.0))
    speeds += (jnp.maximum(vy, 0.0), jnp.minimum(vy, 0.0))
    contact = jnp.where(kinds > 0, relax_rate, 0.0)
    source = jnp.where(kinds == 1, contact, -contact)
    rate = source * capacity - contact * field
    for k, speed in enumerate(speeds):
        rate = rate - (0.5 * speed) * steps[:, k * cells : (k + 1) * cells]
    return rate


def first_rest(field, strips, operators, table, kinds, base_a, base_b):
    modes, half = base_a.shape
    block = min(modes, BLOCK)

    def step(i, _):
        rows = pl.ds(pl.multiple_of(i * block, block), block)
        value = field[rows, :]
        rate = still_rate(value, strips[rows, :], operators, table[:, rows].T, kinds[...])
        base = value + time_step * rate
        base_a[rows, :] = base[:, :half]
        base_b[rows, :] = base[:, half:]
        return 0

    lax.fori_loop(0, modes // block, step, 0)


def second_rest(
    flux_scale,
    field,
    mid_a,
    mid_b,
    strips,
    operators,
    table,
    kinds,
    scattered,
    end_a,
    end_b,
    flux,
):
    modes, half = end_a.shape
    block = min(modes, BLOCK)
    step_size = 0.5 * time_step
    flux[...] = jnp.zeros_like(flux)

    def step(i, _):
        rows = pl.ds(pl.multiple_of(i * block, block), block)
        mid = jnp.concatenate([mid_a[rows, :], mid_b[rows, :]], axis=1)
        columns = table[:, rows].T
        taken = step_size * scattered[:, rows].T
        rate = still_rate(mid, strips[rows, :], operators, columns, kinds[...])
        end = 0.5 * (field[rows, :] + mid) + step_size * rate
        end_a[rows, :] = end[:, :half]
        end_b[rows, :] = end[:, half:]
        for d in range(2):
            terms = columns[:, 3 + d : 4 + d] * end - taken[:, d : d + 1] * mid
            flux[d : d + 1, :] += flux_scale * jnp.sum(terms, axis=0, keepdims=True)
        return 0

    lax.fori_loop(0, modes // block, step, 0)


def paired(to_even, to_odd):
    count = lax.axis_size("space")
    came = []
    for first, value in enumerate((to_even, to_odd)):
        pairs = [(i, i + 1) for i in range(first, count - 1, 2)]
        came.append(lax.ppermute(value, "space", pairs + [(j, i) for i, j in pairs]))
    return came


class Plan:
    def __init__(self, chips):
        self.chips = chips
        self.devices = range(2 * chips)
        sources = [self.sources(d) for d in self.devices]
        targets = [self.targets(d // 2) for d in self.devices]
        self.blocks = [
            [
                [2 * sources[e][slot][2] + e % 2 for e in (d ^ other for d in self.devices)]
                for other in (0, 1)
            ]
            for slot in range(chips)
        ]
        self.rows = [
            [[2 * targets[d][slot] + (d % 2 ^ other) for d in self.devices] for other in (0, 1)]
            for slot in range(chips)
        ]
        self.choices = [
            sorted({sources[d][slot][:2] for d in self.devices}) for slot in range(chips)
        ]
        self.picked = [
            [self.choices[slot].index(sources[d][slot][:2]) for d in self.devices]
            for slot in range(chips)
        ]
        self.sent = {}
        for stream in (0, 1):
            for step in range(1, chips):
                numbers = []
                for d in self.devices:
                    way = self.way(d, stream)
                    place = d // 2 if way > 0 else chips - 1 - d // 2
                    target = d // 2 + way * (chips - step)
                    numbers.append(targets[d].index(target) if place < step else -1)
                self.sent[stream, step] = numbers
        self.pairs = []
        for stream in (0, 1):
            up = [
                (d, d + 2) for d in self.devices[:-2] if self.way(d, stream) > 0
            ]
            self.pairs.append(up + [(j, i) for i, j in up])

    def way(self, device, stream):
        return 1 if (device // 2 + device % 2 + stream) % 2 == 0 else -1

    def sources(self, device):
        found = [(-1, -1, device // 2)]
        for step in range(self.chips - 1):
            for stream in (step % 2, 1 - step % 2):
                chip = device // 2 + self.way(device, stream) * (step + 1)
                if 0 <= chip < self.chips:
                    found.append((stream, step, chip))
        return found

    def targets(self, chip):
        found = []
        for step in range(1, self.chips):
            far = self.chips - step
            found += [t for t in (chip + far, chip - far) if 0 <= t < self.chips]
        return found + [chip]


def on_device(distribution, scatter_matrix, velocity, capacity, cell_type):
    modes, cells = distribution.shape
    total_modes = scatter_matrix.shape[0]
    half = cells // 2
    extra = -(-2 * modes // LANES // 8) * 8
    step_size = 0.5 * time_step
    part = (modes, half)
    devices = lax.axis_size("mode")
    chips = devices // 2
    plan = Plan(chips)
    call = Chain()
    across = [(i, i ^ 1) for i in range(devices)]
    cap = capacity[None, :]
    table = jnp.concatenate(
        [velocity, cap, cap * velocity, jnp.zeros((3, modes), jnp.float32)], axis=0
    )
    kinds = cell_type[None, :]

    def exchange(value, parts=1):
        cut = value.shape[0] // parts // 8 * 8
        ends = [cut * k for k in range(parts)] + [value.shape[0]]
        return [lax.ppermute(value[i:j], "mode", across) for i, j in zip(ends, ends[1:])]

    def along(stream, value):
        return lax.ppermute(value, "mode", plan.pairs[stream])

    class Round:
        def __init__(self, matrix, scale, rows):
            self.matrix, self.scale, self.rows = matrix, scale, rows
            self.terms, self.total = [], None

        def begin(self, own):
            self.own = own
            self.arrived = [[along(0, own)], [along(1, own)]]
            self.blocks = []

        def add_terms(self, field, parts=1):
            kernel = functools.partial(slot_products, plan.rows[len(self.terms)])
            mine, other = call(kernel, [part] * 2, [self.matrix, field])
            self.terms.append((mine, *exchange(other, parts)))

        def join_terms(self, *slots):
            for slot in slots:
                (self.terms[slot],) = call(add, [part], self.terms[slot])

        def take_own(self, later=False):
            own = call(pass_on, [self.own.shape], [self.own])[0] if later else self.own
            self.blocks.append((self.own, *exchange(own)))

        def send(self, step, between=None):
            sent = {}
            for stream in (step % 2, 1 - step % 2):
                if between is not None and sent:
                    between()
                numbers = plan.sent[stream, step]
                slots = sorted({n for n in numbers if n >= 0})
                for slot in slots:
                    if isinstance(self.terms[slot], tuple):
                        self.join_terms(slot)
                arrived = self.arrived[1 - stream][step - 1]
                kernel = functools.partial(payload, numbers, slots)
                arrays = [arrived] + [self.terms[s] for s in slots]
                (value,) = call(kernel, [arrived.shape], arrays)
                sent[stream] = along(stream, value)
            for stream in (0, 1):
                self.arrived[stream].append(sent[stream])

        def take(self, slot, parts=1):
            arrays = [self.arrived[stream][step] for stream, step in plan.choices[slot]]
            kernel = functools.partial(pick, plan.picked[slot])
            (here,) = call(kernel, [arrays[0].shape], arrays)
            self.blocks.append((here, *exchange(here, parts)))

        def multiply(self, slot, base=None):
            first, last = slot == 0, base is not None
            blocks = self.blocks[slot]
            kernel = functools.partial(
                two_blocks, plan.blocks[slot], len(blocks) - 1, first, last, self.scale, self.rows
            )
            arrays = [self.matrix, *blocks]
            arrays += [] if first else [self.total]
            arrays += [base] if last else []
            outs = [(2 * half + (16 if self.rows else 0), modes)]
            if last:
                outs = [part, (HALO, modes), (8, modes)] if self.rows else [part]
            results = call(kernel, outs, arrays)
            self.total = results[0]
            return results

        def first_end(self, base):
            kernel = functools.partial(take_off, self.scale)
            arrived = self.arrived[(chips - 1) % 2][-1]
            (self.rest,) = call(kernel, [part], [arrived, self.terms[-1], base])

        def ends(self):
            return [self.arrived[chips % 2][-1], self.rest]

    own, _ = call(
        own_rows,
        [(modes + extra, half), (8, LANES)],
        [distribution, velocity, cap],
        places=[HBM] * 3,
        scratch=[
            pltpu.VMEM((2, modes), jnp.float32),
            pltpu.VMEM((1, modes), jnp.float32),
            pltpu.SemaphoreType.DMA((3,)),
        ],
        room=56,
    )
    one = Round(None, time_step, True)
    one.begin(own)
    *terms, matrix = call(
        functools.partial(load_and_products, plan.rows, half),
        [part] * (2 * chips) + [jax.ShapeDtypeStruct(scatter_matrix.shape, jnp.bfloat16)],
        [scatter_matrix, distribution],
        places=[HBM] * 2,
        scratch=[
            pltpu.VMEM(part, jnp.float32),
            pltpu.SemaphoreType.DMA((2 * chips + 1,)),
        ],
        room=28,
    )
    one.matrix = matrix
    one.terms = [(terms[2 * s], *exchange(terms[2 * s + 1])) for s in range(chips)]
    one.take_own()
    operators = jnp.asarray(differences(cells))
    strips = None

    def unpack():
        nonlocal strips
        shape = jax.ShapeDtypeStruct((modes, 4 * HALO), jnp.bfloat16)
        (strips,) = call(strip_columns, [shape], strips)

    for step in range(1, chips):
        if step == 1:
            one.take(1)
        one.send(step, unpack if step == 2 else None)
        if step == 1:
            one.join_terms(*(s for s in range(chips) if isinstance(one.terms[s], tuple)))
            strips = call(strip_rows, [(HALO, modes)] * 2, [distribution])
            strips = paired(*call(strip_pairs, [(HALO, modes)] * 2, strips))
        else:
            one.take(step, 2 if step == chips - 1 else 1)
        one.multiply(step - 1)
        if step == min(2, chips - 1):
            base_a, base_b = call(
                first_rest,
                [part] * 2,
                [distribution, strips, operators, table, kinds],
            )
    mid_a, leading, scattered = one.multiply(chips - 1, base_a)

    two = Round(matrix, step_size, False)
    two.add_terms(mid_a, 1)
    one.first_end(base_b)
    mid_b, last = call(
        functools.partial(turn_sum, time_step), [part, (HALO, modes)], one.ends()
    )
    two.begin(mid_b)
    two.add_terms(mid_a)
    two.join_terms(0)
    strips = paired(*call(strip_pairs, [(HALO, modes)] * 2, [leading, last]))
    flux = None
    for step in range(1, chips):
        if step == 1:
            two.send(step, unpack)
            two.take_own()
            two.join_terms(1)
        elif step == 2:
            two.send(step, lambda: flux.over(1))
            two.join_terms(*range(2, chips))
        elif step == chips - 1:
            two.send(step, lambda: flux.over(*range(2, devices, 2)))
        else:
            two.send(step)
        two.take(step, 2 if step >= chips - 2 else 1)
        if step == 1:
            for slot in range(2, chips):
                two.add_terms(mid_a)
        if step == 2:
            two.multiply(0)
        if 1 < step < chips - 1:
            two.multiply(step - 1)
        if step == chips - 2:
            two.multiply(step)
        if step == 1:
            end_a, end_b, part_flux = call(
                functools.partial(second_rest, 1.0 / math.sqrt(total_modes)),
                [part, part, (2, cells)],
                [distribution, mid_a, mid_b, strips, operators, table, kinds, scattered],
            )
            flux = Flux(call, part_flux, devices)
    (last_b,) = two.multiply(chips - 1, end_b)
    heat_flux = flux.value
    two.first_end(end_a)
    (updated,) = call(
        functools.partial(last_sum, step_size),
        [(modes, cells)],
        [*two.ends(), last_b],
        scratch=[pltpu.VMEM(part, jnp.float32), pltpu.SemaphoreType.DMA((2,))],
        out_specs=[HBM],
    )
    return (updated, heat_flux)


class Flux:
    def __init__(self, call, value, devices):
        self.call, self.value, self.devices = call, value, devices

    def over(self, *bits):
        came = [
            lax.ppermute(self.value, "mode", [(i, i ^ bit) for i in range(self.devices)])
            for bit in bits
        ]
        self.value, _ = self.call(add_all, [self.value.shape, (8, LANES)], [self.value, *came])


def solution(mesh):
    return jax.shard_map(
        on_device,
        mesh=mesh,
        in_specs=(P("mode", "space"), P(None, "mode"), P(None, "mode"), P("mode"), P("space")),
        out_specs=(P("mode", "space"), P(None, "space")),
        check_vma=False,
    )
```

```python
import functools
import math

import numpy as np

import jax
import jax.numpy as jnp
from jax import lax
from jax.experimental import pallas as pl
from jax.experimental.pallas import tpu as pltpu
from jax.sharding import PartitionSpec as P

NY = 16
HALO = 2 * NY
LANES = 128
BLOCK = 512


relax_rate = 0.5
time_step = 0.5

VMEM = pl.BlockSpec(memory_space=pltpu.VMEM)
ANY = pl.BlockSpec(memory_space=pl.ANY)
HBM = pl.BlockSpec(memory_space=pltpu.HBM)


class Chain:
    def __init__(self):
        self.last = None

    def __call__(self, kernel, outs, arrays, places=None, scratch=(), out_specs=None, room=16):
        extra = [] if self.last is None else [self.last]
        skip = len(extra)
        first = len(arrays)

        def body(*refs):
            kernel(*refs[:first], *refs[first + skip :])

        results = pl.pallas_call(
            body,
            out_shape=[
                jax.ShapeDtypeStruct(shape, jnp.float32) if isinstance(shape, tuple) else shape
                for shape in outs
            ],
            in_specs=list(places or [VMEM] * len(arrays)) + [ANY] * skip,
            out_specs=out_specs or [VMEM] * len(outs),
            scratch_shapes=list(scratch),
            compiler_params=pltpu.CompilerParams(vmem_limit_bytes=room * 1024 * 1024),
            cost_estimate=pl.CostEstimate(flops=1024, bytes_accessed=1024, transcendentals=0),
            name=getattr(kernel, "func", kernel).__name__,
        )(*arrays, *extra)
        self.last = results[-1]
        return results


def halves(value):
    high = value.astype(jnp.bfloat16)
    low = (value - high.astype(jnp.float32)).astype(jnp.bfloat16)
    return high, low


def for_device(numbers):
    if len(set(numbers)) == 1:
        return numbers[0]
    me = lax.axis_index("mode")
    chosen = jnp.int32(numbers[0])
    for device, number in enumerate(numbers[1:], 1):
        chosen = jnp.where(me == device, jnp.int32(number), chosen)
    return chosen


def rows_of(matrix, block):
    modes = matrix.shape[1]
    return pl.ds(pl.multiple_of(block * modes, modes), modes)


def one_slot(blocks, matrix, parts, mine, other):
    cells = mine.shape[1]
    for block, out in zip(blocks, (mine, other)):
        both = jnp.dot(matrix[rows_of(matrix, block), :], parts, preferred_element_type=jnp.float32)
        out[...] = both[:, :cells] + both[:, cells:]


def slot_products(blocks, matrix, field, mine, other):
    blocks = [for_device(numbers) for numbers in blocks]
    parts = jnp.concatenate(halves(field[...]), axis=1)
    one_slot(blocks, matrix, parts, mine, other)


def load_and_products(blocks, column, matrix, distribution, *refs):
    slots = len(blocks)
    outs, (held, field, sems) = refs[: 2 * slots], refs[2 * slots :]
    cells = field.shape[1]
    start = pltpu.make_async_copy(
        distribution.at[:, pl.ds(column, cells)], field, sems.at[2 * slots]
    )
    start.start()
    blocks = [[for_device(numbers) for numbers in pair] for pair in blocks]
    copies = []
    for slot, pair in enumerate(blocks):
        for k, block in enumerate(pair):
            rows = rows_of(held, block)
            copies.append(
                pltpu.make_async_copy(
                    matrix.at[rows, :], held.at[rows, :], sems.at[2 * slot + k]
                )
            )
            copies[-1].start()
    start.wait()
    parts = jnp.concatenate(halves(field[...]), axis=1)
    for slot, pair in enumerate(blocks):
        for k in range(2):
            copies[2 * slot + k].wait()
        one_slot(pair, held, parts, outs[2 * slot], outs[2 * slot + 1])


def two_blocks(numbers, parts, first, last, scale, rows, matrix, *refs):
    modes = matrix.shape[1]
    blocks, refs = [[refs[0]], refs[1 : 1 + parts]], refs[1 + parts :]
    if not first:
        before, refs = refs[0], refs[1:]
    if last:
        base, refs = refs[0], refs[1:]
    total = None if first else before[...]
    for k, pieces in enumerate(blocks):
        block = jnp.concatenate([piece[...] for piece in pieces], axis=0)
        pieces = list(halves(block[:modes].T))
        if rows:
            weights = [
                jnp.concatenate(
                    [
                        block[modes + i : modes + i + 1, :]
                        for i in range(d * modes // LANES, (d + 1) * modes // LANES)
                    ],
                    axis=1,
                )
                for d in range(2)
            ]
            weights.append(jnp.zeros((6, modes), jnp.float32))
            pieces += halves(jnp.concatenate(weights, axis=0))
        left = jnp.concatenate(pieces, axis=0)
        there = rows_of(matrix, for_device(numbers[k]))
        term = jnp.dot(left, matrix[there, :], preferred_element_type=jnp.float32)
        total = term if total is None else total + term
    if not last:
        refs[0][...] = total
        return
    cells = base.shape[1]
    value = base[...] - scale * (total[:cells] + total[cells : 2 * cells]).T
    refs[0][...] = value
    if rows:
        refs[1][...] = value.T[:HALO]
        refs[2][...] = total[2 * cells : 2 * cells + 8] + total[2 * cells + 8 :]


def own_rows(distribution, velocity, capacity, out, token, speeds, weight, sems):
    modes, cells = velocity.shape[1], out.shape[1]
    copies = [
        pltpu.make_async_copy(velocity, speeds, sems.at[0]),
        pltpu.make_async_copy(capacity, weight, sems.at[1]),
        pltpu.make_async_copy(
            distribution.at[:, pl.ds(0, cells)], out.at[pl.ds(0, modes), :], sems.at[2]
        ),
    ]
    for copy in copies:
        copy.start()
    token[...] = jnp.zeros_like(token)
    for copy in copies[:2]:
        copy.wait()
    per = modes // LANES
    out[modes:] = jnp.zeros((out.shape[0] - modes, LANES), jnp.float32)
    for d in range(2):
        for i in range(per):
            lanes = slice(i * LANES, (i + 1) * LANES)
            out[modes + d * per + i : modes + d * per + i + 1, :] = (
                speeds[d : d + 1, lanes] * weight[:, lanes]
            )
    copies[2].wait()


def payload(numbers, slots, arrived, *refs):
    out = refs[-1]
    slot_here = for_device(numbers)

    for k, slot in enumerate(slots):

        @pl.when(slot_here == slot)
        def _(k=k):
            terms = refs[k]
            modes = terms.shape[0]
            out[:modes] = arrived[:modes] + terms[...]
            if out.shape[0] > modes:
                out[modes:] = arrived[modes:]

    @pl.when(slot_here < 0)
    def _():
        out[...] = arrived[...]


def pick(numbers, *refs):
    out = refs[-1]
    choice = for_device(numbers)
    for k, ref in enumerate(refs[:-1]):

        @pl.when(choice == k)
        def _(ref=ref):
            out[...] = ref[...]


def add(one, *refs):
    out, first = refs[-1], 0
    for piece in refs[:-1]:
        rows = slice(first, first + piece.shape[0])
        out[rows] = one[rows] + piece[...]
        first += piece.shape[0]


def pass_on(value, out):
    out[...] = value[...]


def add_all(*refs):
    out, token = refs[-2:]
    total = refs[0][...]
    for ref in refs[1:-2]:
        total = total + ref[...]
    out[...] = total
    token[...] = jnp.zeros_like(token)


def take_off(scale, arrived, terms, base, out):
    modes = terms.shape[0]
    out[...] = base[...] - scale * (arrived[:modes] + terms[...])


def turn_sum(scale, arrived, base, out, strip):
    modes = base.shape[0]
    value = base[...] - scale * arrived[:modes]
    out[...] = value
    strip[...] = value.T[-HALO:]


def last_sum(scale, arrived, base, other, out, value, sems):
    cells = base.shape[1]
    ahead = pltpu.make_async_copy(other, out.at[:, pl.ds(cells, cells)], sems.at[0])
    ahead.start()
    value[...] = base[...] - scale * arrived[...]
    copy = pltpu.make_async_copy(value, out.at[:, pl.ds(0, cells)], sems.at[1])
    copy.start()
    ahead.wait()
    copy.wait()


def strip_rows(distribution, leading, last):
    cells = distribution.shape[1]
    leading[...] = distribution[:, :LANES].T[:HALO]
    last[...] = distribution[:, cells - LANES :].T[-HALO:]


def strip_pairs(leading, last, out_even, out_odd):
    even = lax.axis_index("space") % 2 == 0

    @pl.when(even)
    def _():
        out_even[...] = last[...]
        out_odd[...] = leading[...]

    @pl.when(jnp.logical_not(even))
    def _():
        out_even[...] = leading[...]
        out_odd[...] = last[...]


def differences(cells):
    columns = cells // NY
    own, strip = np.zeros((cells, 4 * cells)), np.zeros((2 * HALO, 4 * cells))
    for x in range(columns):
        for y in range(NY):
            cell = x * NY + y
            for way in (-1, 1):
                for far, factor in enumerate((3.0, -4.0, 1.0)):
                    at_x, at_y = x + way * far, y + way * far
                    first = cell + (0 if way < 0 else cells)
                    factor = -way * factor
                    if at_x < 0:
                        strip[(at_x + 2) * NY + y, first] = factor
                    elif at_x >= columns:
                        strip[HALO + (at_x - columns) * NY + y, first] = factor
                    else:
                        own[at_x * NY + y, first] = factor
                    if 0 <= at_y < NY:
                        own[x * NY + at_y, first + 2 * cells] = factor
    return np.concatenate([own, own, strip, strip]).astype(jnp.bfloat16)


def strip_columns(came_even, came_odd, out):
    even = lax.axis_index("space") % 2 == 0
    before = jnp.where(even, came_odd[...], came_even[...])
    after = jnp.where(even, came_even[...], came_odd[...])
    parts = halves(jnp.concatenate([before, after], axis=0))
    rows = jnp.concatenate([p.astype(jnp.float32) for p in parts], axis=0)
    out[...] = rows.T.astype(jnp.bfloat16)


def still_rate(field, strip, operators, columns, kinds):
    cells = field.shape[1]
    left = jnp.concatenate([*halves(field), strip], axis=1)
    steps = jnp.dot(left, operators[...], preferred_element_type=jnp.float32)
    vx, vy, capacity = (columns[:, i : i + 1] for i in range(3))
    speeds = (jnp.maximum(vx, 0.0), jnp.minimum(vx, 0.0))
    speeds += (jnp.maximum(vy, 0.0), jnp.minimum(vy, 0.0))
    contact = jnp.where(kinds > 0, relax_rate, 0.0)
    source = jnp.where(kinds == 1, contact, -contact)
    rate = source * capacity - contact * field
    for k, speed in enumerate(speeds):
        rate = rate - (0.5 * speed) * steps[:, k * cells : (k + 1) * cells]
    return rate


def first_rest(field, strips, operators, table, kinds, base_a, base_b):
    modes, half = base_a.shape
    block = min(modes, BLOCK)

    def step(i, _):
        rows = pl.ds(pl.multiple_of(i * block, block), block)
        value = field[rows, :]
        rate = still_rate(value, strips[rows, :], operators, table[:, rows].T, kinds[...])
        base = value + time_step * rate
        base_a[rows, :] = base[:, :half]
        base_b[rows, :] = base[:, half:]
        return 0

    lax.fori_loop(0, modes // block, step, 0)


def second_rest(
    flux_scale,
    field,
    mid_a,
    mid_b,
    strips,
    operators,
    table,
    kinds,
    scattered,
    end_a,
    end_b,
    flux,
):
    modes, half = end_a.shape
    block = min(modes, BLOCK)
    step_size = 0.5 * time_step
    flux[...] = jnp.zeros_like(flux)

    def step(i, _):
        rows = pl.ds(pl.multiple_of(i * block, block), block)
        mid = jnp.concatenate([mid_a[rows, :], mid_b[rows, :]], axis=1)
        columns = table[:, rows].T
        taken = step_size * scattered[:, rows].T
        rate = still_rate(mid, strips[rows, :], operators, columns, kinds[...])
        end = 0.5 * (field[rows, :] + mid) + step_size * rate
        end_a[rows, :] = end[:, :half]
        end_b[rows, :] = end[:, half:]
        for d in range(2):
            terms = columns[:, 3 + d : 4 + d] * end - taken[:, d : d + 1] * mid
            flux[d : d + 1, :] += flux_scale * jnp.sum(terms, axis=0, keepdims=True)
        return 0

    lax.fori_loop(0, modes // block, step, 0)


def paired(to_even, to_odd):
    count = lax.axis_size("space")
    came = []
    for first, value in enumerate((to_even, to_odd)):
        pairs = [(i, i + 1) for i in range(first, count - 1, 2)]
        came.append(lax.ppermute(value, "space", pairs + [(j, i) for i, j in pairs]))
    return came


class Plan:
    def __init__(self, chips):
        self.chips = chips
        self.devices = range(2 * chips)
        sources = [self.sources(d) for d in self.devices]
        targets = [self.targets(d // 2) for d in self.devices]
        self.blocks = [
            [
                [2 * sources[e][slot][2] + e % 2 for e in (d ^ other for d in self.devices)]
                for other in (0, 1)
            ]
            for slot in range(chips)
        ]
        self.rows = [
            [[2 * targets[d][slot] + (d % 2 ^ other) for d in self.devices] for other in (0, 1)]
            for slot in range(chips)
        ]
        self.choices = [
            sorted({sources[d][slot][:2] for d in self.devices}) for slot in range(chips)
        ]
        self.picked = [
            [self.choices[slot].index(sources[d][slot][:2]) for d in self.devices]
            for slot in range(chips)
        ]
        self.sent = {}
        for stream in (0, 1):
            for step in range(1, chips):
                numbers = []
                for d in self.devices:
                    way = self.way(d, stream)
                    place = d // 2 if way > 0 else chips - 1 - d // 2
                    target = d // 2 + way * (chips - step)
                    numbers.append(targets[d].index(target) if place < step else -1)
                self.sent[stream, step] = numbers
        self.pairs = []
        for stream in (0, 1):
            up = [
                (d, d + 2) for d in self.devices[:-2] if self.way(d, stream) > 0
            ]
            self.pairs.append(up + [(j, i) for i, j in up])

    def way(self, device, stream):
        return 1 if (device // 2 + device % 2 + stream) % 2 == 0 else -1

    def sources(self, device):
        found = [(-1, -1, device // 2)]
        for step in range(self.chips - 1):
            for stream in (step % 2, 1 - step % 2):
                chip = device // 2 + self.way(device, stream) * (step + 1)
                if 0 <= chip < self.chips:
                    found.append((stream, step, chip))
        return found

    def targets(self, chip):
        found = []
        for step in range(1, self.chips):
            far = self.chips - step
            found += [t for t in (chip + far, chip - far) if 0 <= t < self.chips]
        return found + [chip]


def on_device(distribution, scatter_matrix, velocity, capacity, cell_type):
    modes, cells = distribution.shape
    total_modes = scatter_matrix.shape[0]
    half = cells // 2
    extra = -(-2 * modes // LANES // 8) * 8
    step_size = 0.5 * time_step
    part = (modes, half)
    devices = lax.axis_size("mode")
    chips = devices // 2
    plan = Plan(chips)
    call = Chain()
    across = [(i, i ^ 1) for i in range(devices)]
    cap = capacity[None, :]
    table = jnp.concatenate(
        [velocity, cap, cap * velocity, jnp.zeros((3, modes), jnp.float32)], axis=0
    )
    kinds = cell_type[None, :]

    def exchange(value, parts=1):
        cut = value.shape[0] // parts // 8 * 8
        ends = [cut * k for k in range(parts)] + [value.shape[0]]
        return [lax.ppermute(value[i:j], "mode", across) for i, j in zip(ends, ends[1:])]

    def along(stream, value):
        return lax.ppermute(value, "mode", plan.pairs[stream])

    class Round:
        def __init__(self, matrix, scale, rows):
            self.matrix, self.scale, self.rows = matrix, scale, rows
            self.terms, self.total = [], None

        def begin(self, own):
            self.own = own
            self.arrived = [[along(0, own)], [along(1, own)]]
            self.blocks = []

        def add_terms(self, field, parts=1):
            kernel = functools.partial(slot_products, plan.rows[len(self.terms)])
            mine, other = call(kernel, [part] * 2, [self.matrix, field])
            self.terms.append((mine, *exchange(other, parts)))

        def join_terms(self, *slots):
            for slot in slots:
                (self.terms[slot],) = call(add, [part], self.terms[slot])

        def take_own(self, later=False):
            own = call(pass_on, [self.own.shape], [self.own])[0] if later else self.own
            self.blocks.append((self.own, *exchange(own)))

        def send(self, step, between=None):
            sent = {}
            for stream in (step % 2, 1 - step % 2):
                if between is not None and sent:
                    between()
                numbers = plan.sent[stream, step]
                slots = sorted({n for n in numbers if n >= 0})
                for slot in slots:
                    if isinstance(self.terms[slot], tuple):
                        self.join_terms(slot)
                arrived = self.arrived[1 - stream][step - 1]
                kernel = functools.partial(payload, numbers, slots)
                arrays = [arrived] + [self.terms[s] for s in slots]
                (value,) = call(kernel, [arrived.shape], arrays)
                sent[stream] = along(stream, value)
            for stream in (0, 1):
                self.arrived[stream].append(sent[stream])

        def take(self, slot, parts=1):
            arrays = [self.arrived[stream][step] for stream, step in plan.choices[slot]]
            kernel = functools.partial(pick, plan.picked[slot])
            (here,) = call(kernel, [arrays[0].shape], arrays)
            self.blocks.append((here, *exchange(here, parts)))

        def hold(self, *slots):
            for slot in slots:
                here, there = self.blocks[slot]
                (there,) = call(pass_on, [there.shape], [there])
                self.blocks[slot] = (here, there)

        def multiply(self, slot, base=None, first=None):
            first, last = slot == 0 if first is None else first, base is not None
            blocks = self.blocks[slot]
            kernel = functools.partial(
                two_blocks, plan.blocks[slot], len(blocks) - 1, first, last, self.scale, self.rows
            )
            arrays = [self.matrix, *blocks]
            arrays += [] if first else [self.total]
            arrays += [base] if last else []
            outs = [(2 * half + (16 if self.rows else 0), modes)]
            if last:
                outs = [part, (HALO, modes), (8, modes)] if self.rows else [part]
            results = call(kernel, outs, arrays)
            self.total = results[0]
            return results

        def first_end(self, base):
            kernel = functools.partial(take_off, self.scale)
            arrived = self.arrived[(chips - 1) % 2][-1]
            (self.rest,) = call(kernel, [part], [arrived, self.terms[-1], base])

        def ends(self):
            return [self.arrived[chips % 2][-1], self.rest]

    own, _ = call(
        own_rows,
        [(modes + extra, half), (8, LANES)],
        [distribution, velocity, cap],
        places=[HBM] * 3,
        scratch=[
            pltpu.VMEM((2, modes), jnp.float32),
            pltpu.VMEM((1, modes), jnp.float32),
            pltpu.SemaphoreType.DMA((3,)),
        ],
        room=56,
    )
    one = Round(None, time_step, True)
    one.begin(own)
    *terms, matrix = call(
        functools.partial(load_and_products, plan.rows, half),
        [part] * (2 * chips) + [jax.ShapeDtypeStruct(scatter_matrix.shape, jnp.bfloat16)],
        [scatter_matrix, distribution],
        places=[HBM] * 2,
        scratch=[
            pltpu.VMEM(part, jnp.float32),
            pltpu.SemaphoreType.DMA((2 * chips + 1,)),
        ],
        room=28,
    )
    one.matrix = matrix
    one.terms = [(terms[2 * s], *exchange(terms[2 * s + 1])) for s in range(chips)]
    one.take_own()
    operators = jnp.asarray(differences(cells))
    strips = None

    def unpack():
        nonlocal strips
        shape = jax.ShapeDtypeStruct((modes, 4 * HALO), jnp.bfloat16)
        (strips,) = call(strip_columns, [shape], strips)

    for step in range(1, chips):
        if step == 1:
            one.take(1)
        one.send(step, unpack if step == 2 else None)
        if step == 1:
            one.join_terms(*(s for s in range(chips) if isinstance(one.terms[s], tuple)))
            strips = call(strip_rows, [(HALO, modes)] * 2, [distribution])
            strips = paired(*call(strip_pairs, [(HALO, modes)] * 2, strips))
        else:
            one.take(step, 2 if step == chips - 1 else 1)
        one.multiply(step - 1)
        if step == min(2, chips - 1):
            base_a, base_b = call(
                first_rest,
                [part] * 2,
                [distribution, strips, operators, table, kinds],
            )
    mid_a, leading, scattered = one.multiply(chips - 1, base_a)

    two = Round(matrix, step_size, False)
    two.add_terms(mid_a, 1)
    one.first_end(base_b)
    mid_b, last = call(
        functools.partial(turn_sum, time_step), [part, (HALO, modes)], one.ends()
    )
    two.begin(mid_b)
    two.add_terms(mid_a)
    two.join_terms(0)
    strips = paired(*call(strip_pairs, [(HALO, modes)] * 2, [leading, last]))
    flux = None
    for step in range(1, chips):
        if step == 1:
            two.send(step, unpack)
            two.take_own()
            two.join_terms(1)
        elif step == 2:
            two.send(step, lambda: flux.over(1))
            two.join_terms(*range(2, chips))
        elif step == chips - 1:
            two.send(step, lambda: flux.over(*range(2, devices, 2)))
        else:
            two.send(step)
        two.take(step, 2 if step >= chips - 2 else 1)
        if step == 1:
            for slot in range(2, chips):
                two.add_terms(mid_a)
        if 1 < step < chips - 1:
            two.hold(*range(step) if step == 2 else (step - 1,))
        if step == chips - 2:
            two.multiply(step, first=True)
        if step == chips - 1:
            for slot in range(chips - 2):
                two.multiply(slot, first=False)
        if step == 1:
            end_a, end_b, part_flux = call(
                functools.partial(second_rest, 1.0 / math.sqrt(total_modes)),
                [part, part, (2, cells)],
                [distribution, mid_a, mid_b, strips, operators, table, kinds, scattered],
            )
            flux = Flux(call, part_flux, devices)
    (last_b,) = two.multiply(chips - 1, end_b)
    heat_flux = flux.value
    two.first_end(end_a)
    (updated,) = call(
        functools.partial(last_sum, step_size),
        [(modes, cells)],
        [*two.ends(), last_b],
        scratch=[pltpu.VMEM(part, jnp.float32), pltpu.SemaphoreType.DMA((2,))],
        out_specs=[HBM],
    )
    return (updated, heat_flux)


class Flux:
    def __init__(self, call, value, devices):
        self.call, self.value, self.devices = call, value, devices

    def over(self, *bits):
        came = [
            lax.ppermute(self.value, "mode", [(i, i ^ bit) for i in range(self.devices)])
            for bit in bits
        ]
        self.value, _ = self.call(add_all, [self.value.shape, (8, LANES)], [self.value, *came])


def solution(mesh):
    return jax.shard_map(
        on_device,
        mesh=mesh,
        in_specs=(P("mode", "space"), P(None, "mode"), P(None, "mode"), P("mode"), P("space")),
        out_specs=(P("mode", "space"), P(None, "space")),
        check_vma=False,
    )
```

```python
import functools
import math

import numpy as np

import jax
import jax.numpy as jnp
from jax import lax
from jax.experimental import pallas as pl
from jax.experimental.pallas import tpu as pltpu
from jax.sharding import PartitionSpec as P

NY = 16
HALO = 2 * NY
LANES = 128
BLOCK = 512


relax_rate = 0.5
time_step = 0.5

VMEM = pl.BlockSpec(memory_space=pltpu.VMEM)
ANY = pl.BlockSpec(memory_space=pl.ANY)
HBM = pl.BlockSpec(memory_space=pltpu.HBM)


class Chain:
    def __init__(self):
        self.last = None

    def __call__(self, kernel, outs, arrays, places=None, scratch=(), out_specs=None, room=16):
        extra = [] if self.last is None else [self.last]
        skip = len(extra)
        first = len(arrays)

        def body(*refs):
            kernel(*refs[:first], *refs[first + skip :])

        results = pl.pallas_call(
            body,
            out_shape=[
                jax.ShapeDtypeStruct(shape, jnp.float32) if isinstance(shape, tuple) else shape
                for shape in outs
            ],
            in_specs=list(places or [VMEM] * len(arrays)) + [ANY] * skip,
            out_specs=out_specs or [VMEM] * len(outs),
            scratch_shapes=list(scratch),
            compiler_params=pltpu.CompilerParams(vmem_limit_bytes=room * 1024 * 1024),
            cost_estimate=pl.CostEstimate(flops=1024, bytes_accessed=1024, transcendentals=0),
            name=getattr(kernel, "func", kernel).__name__,
        )(*arrays, *extra)
        self.last = results[-1]
        return results


def halves(value):
    high = value.astype(jnp.bfloat16)
    low = (value - high.astype(jnp.float32)).astype(jnp.bfloat16)
    return high, low


def for_device(numbers):
    if len(set(numbers)) == 1:
        return numbers[0]
    me = lax.axis_index("mode")
    chosen = jnp.int32(numbers[0])
    for device, number in enumerate(numbers[1:], 1):
        chosen = jnp.where(me == device, jnp.int32(number), chosen)
    return chosen


def rows_of(matrix, block):
    modes = matrix.shape[1]
    return pl.ds(pl.multiple_of(block * modes, modes), modes)


def one_slot(blocks, matrix, parts, mine, other):
    cells = mine.shape[1]
    for block, out in zip(blocks, (mine, other)):
        both = jnp.dot(matrix[rows_of(matrix, block), :], parts, preferred_element_type=jnp.float32)
        out[...] = both[:, :cells] + both[:, cells:]


def slot_products(blocks, matrix, field, mine, other):
    blocks = [for_device(numbers) for numbers in blocks]
    parts = jnp.concatenate(halves(field[...]), axis=1)
    one_slot(blocks, matrix, parts, mine, other)


def load_and_products(blocks, column, matrix, distribution, *refs):
    slots = len(blocks)
    outs, (held, field, sems) = refs[: 2 * slots], refs[2 * slots :]
    cells = field.shape[1]
    start = pltpu.make_async_copy(
        distribution.at[:, pl.ds(column, cells)], field, sems.at[2 * slots]
    )
    start.start()
    blocks = [[for_device(numbers) for numbers in pair] for pair in blocks]
    copies = []
    for slot, pair in enumerate(blocks):
        for k, block in enumerate(pair):
            rows = rows_of(held, block)
            copies.append(
                pltpu.make_async_copy(
                    matrix.at[rows, :], held.at[rows, :], sems.at[2 * slot + k]
                )
            )
            copies[-1].start()
    start.wait()
    parts = jnp.concatenate(halves(field[...]), axis=1)
    for slot, pair in enumerate(blocks):
        for k in range(2):
            copies[2 * slot + k].wait()
        one_slot(pair, held, parts, outs[2 * slot], outs[2 * slot + 1])


def whole_product(scale, rows, matrix, gathered, base, *refs):
    outs, (held, sems) = refs[:-2], refs[-2:]
    modes, cells = base.shape
    copies = []
    for k in range(gathered.shape[0]):
        copies.append(pltpu.make_async_copy(gathered.at[k], held.at[k], sems.at[k]))
        copies[-1].start()
    total = None
    for k, copy in enumerate(copies):
        copy.wait()
        pieces = list(halves(held[k, :modes].T))
        if rows:
            per = modes // LANES
            weights = [
                jnp.concatenate(
                    [held[k, modes + i : modes + i + 1, :] for i in range(d * per, (d + 1) * per)],
                    axis=1,
                )
                for d in range(2)
            ]
            weights.append(jnp.zeros((6, modes), jnp.float32))
            pieces += halves(jnp.concatenate(weights, axis=0))
        left = jnp.concatenate(pieces, axis=0)
        block = matrix[k * modes : (k + 1) * modes, :]
        term = jnp.dot(left, block, preferred_element_type=jnp.float32)
        total = term if total is None else total + term
    value = base[...] - scale * (total[:cells] + total[cells : 2 * cells]).T
    outs[0][...] = value
    if rows:
        outs[1][...] = value.T[:HALO]
        outs[2][...] = total[2 * cells : 2 * cells + 8] + total[2 * cells + 8 :]


def own_rows(distribution, velocity, capacity, out, token, speeds, weight, sems):
    modes, cells = velocity.shape[1], out.shape[1]
    copies = [
        pltpu.make_async_copy(velocity, speeds, sems.at[0]),
        pltpu.make_async_copy(capacity, weight, sems.at[1]),
        pltpu.make_async_copy(
            distribution.at[:, pl.ds(0, cells)], out.at[pl.ds(0, modes), :], sems.at[2]
        ),
    ]
    for copy in copies:
        copy.start()
    token[...] = jnp.zeros_like(token)
    for copy in copies[:2]:
        copy.wait()
    per = modes // LANES
    out[modes:] = jnp.zeros((out.shape[0] - modes, LANES), jnp.float32)
    for d in range(2):
        for i in range(per):
            lanes = slice(i * LANES, (i + 1) * LANES)
            out[modes + d * per + i : modes + d * per + i + 1, :] = (
                speeds[d : d + 1, lanes] * weight[:, lanes]
            )
    copies[2].wait()


def payload(numbers, slots, *refs):
    *arrived, out = (refs[0], refs[-1]) if len(refs) > len(slots) + 1 else (refs[-1],)
    terms = refs[len(arrived) : -1]
    slot_here = for_device(numbers)
    for k, slot in enumerate(slots):

        @pl.when(slot_here == slot)
        def _(k=k):
            out[...] = arrived[0][...] + terms[k][...] if arrived else terms[k][...]


def add(one, *refs):
    out, first = refs[-1], 0
    for piece in refs[:-1]:
        rows = slice(first, first + piece.shape[0])
        out[rows] = one[rows] + piece[...]
        first += piece.shape[0]


def add_all(*refs):
    out, token = refs[-2:]
    total = refs[0][...]
    for ref in refs[1:-2]:
        total = total + ref[...]
    out[...] = total
    token[...] = jnp.zeros_like(token)


def take_off(scale, arrived, terms, base, out):
    modes = terms.shape[0]
    out[...] = base[...] - scale * (arrived[:modes] + terms[...])


def turn_sum(scale, arrived, base, out, strip):
    modes = base.shape[0]
    value = base[...] - scale * arrived[:modes]
    out[...] = value
    strip[...] = value.T[-HALO:]


def last_sum(scale, arrived, base, other, out, value, sems):
    cells = base.shape[1]
    ahead = pltpu.make_async_copy(other, out.at[:, pl.ds(cells, cells)], sems.at[0])
    ahead.start()
    value[...] = base[...] - scale * arrived[...]
    copy = pltpu.make_async_copy(value, out.at[:, pl.ds(0, cells)], sems.at[1])
    copy.start()
    ahead.wait()
    copy.wait()


def strip_rows(distribution, leading, last):
    cells = distribution.shape[1]
    leading[...] = distribution[:, :LANES].T[:HALO]
    last[...] = distribution[:, cells - LANES :].T[-HALO:]


def strip_pairs(leading, last, out_even, out_odd):
    even = lax.axis_index("space") % 2 == 0

    @pl.when(even)
    def _():
        out_even[...] = last[...]
        out_odd[...] = leading[...]

    @pl.when(jnp.logical_not(even))
    def _():
        out_even[...] = leading[...]
        out_odd[...] = last[...]


def differences(cells):
    columns = cells // NY
    own, strip = np.zeros((cells, 4 * cells)), np.zeros((2 * HALO, 4 * cells))
    for x in range(columns):
        for y in range(NY):
            cell = x * NY + y
            for way in (-1, 1):
                for far, factor in enumerate((3.0, -4.0, 1.0)):
                    at_x, at_y = x + way * far, y + way * far
                    first = cell + (0 if way < 0 else cells)
                    factor = -way * factor
                    if at_x < 0:
                        strip[(at_x + 2) * NY + y, first] = factor
                    elif at_x >= columns:
                        strip[HALO + (at_x - columns) * NY + y, first] = factor
                    else:
                        own[at_x * NY + y, first] = factor
                    if 0 <= at_y < NY:
                        own[x * NY + at_y, first + 2 * cells] = factor
    return np.concatenate([own, own, strip, strip]).astype(jnp.bfloat16)


def strip_columns(came_even, came_odd, out):
    even = lax.axis_index("space") % 2 == 0
    before = jnp.where(even, came_odd[...], came_even[...])
    after = jnp.where(even, came_even[...], came_odd[...])
    parts = halves(jnp.concatenate([before, after], axis=0))
    rows = jnp.concatenate([p.astype(jnp.float32) for p in parts], axis=0)
    out[...] = rows.T.astype(jnp.bfloat16)


def still_rate(field, strip, operators, columns, kinds):
    cells = field.shape[1]
    left = jnp.concatenate([*halves(field), strip], axis=1)
    steps = jnp.dot(left, operators[...], preferred_element_type=jnp.float32)
    vx, vy, capacity = (columns[:, i : i + 1] for i in range(3))
    speeds = (jnp.maximum(vx, 0.0), jnp.minimum(vx, 0.0))
    speeds += (jnp.maximum(vy, 0.0), jnp.minimum(vy, 0.0))
    contact = jnp.where(kinds > 0, relax_rate, 0.0)
    source = jnp.where(kinds == 1, contact, -contact)
    rate = source * capacity - contact * field
    for k, speed in enumerate(speeds):
        rate = rate - (0.5 * speed) * steps[:, k * cells : (k + 1) * cells]
    return rate


def first_rest(field, strips, operators, table, kinds, base_a, base_b):
    modes, half = base_a.shape
    block = min(modes, BLOCK)

    def step(i, _):
        rows = pl.ds(pl.multiple_of(i * block, block), block)
        value = field[rows, :]
        rate = still_rate(value, strips[rows, :], operators, table[:, rows].T, kinds[...])
        base = value + time_step * rate
        base_a[rows, :] = base[:, :half]
        base_b[rows, :] = base[:, half:]
        return 0

    lax.fori_loop(0, modes // block, step, 0)


def second_rest(
    flux_scale,
    field,
    mid_a,
    mid_b,
    strips,
    operators,
    table,
    kinds,
    scattered,
    end_a,
    end_b,
    flux,
):
    modes, half = end_a.shape
    block = min(modes, BLOCK)
    step_size = 0.5 * time_step
    flux[...] = jnp.zeros_like(flux)

    def step(i, _):
        rows = pl.ds(pl.multiple_of(i * block, block), block)
        mid = jnp.concatenate([mid_a[rows, :], mid_b[rows, :]], axis=1)
        columns = table[:, rows].T
        taken = step_size * scattered[:, rows].T
        rate = still_rate(mid, strips[rows, :], operators, columns, kinds[...])
        end = 0.5 * (field[rows, :] + mid) + step_size * rate
        end_a[rows, :] = end[:, :half]
        end_b[rows, :] = end[:, half:]
        for d in range(2):
            terms = columns[:, 3 + d : 4 + d] * end - taken[:, d : d + 1] * mid
            flux[d : d + 1, :] += flux_scale * jnp.sum(terms, axis=0, keepdims=True)
        return 0

    lax.fori_loop(0, modes // block, step, 0)


def paired(to_even, to_odd):
    count = lax.axis_size("space")
    came = []
    for first, value in enumerate((to_even, to_odd)):
        pairs = [(i, i + 1) for i in range(first, count - 1, 2)]
        came.append(lax.ppermute(value, "space", pairs + [(j, i) for i, j in pairs]))
    return came


class Plan:
    def __init__(self, chips):
        self.chips = chips
        self.devices = range(2 * chips)
        targets = [self.targets(d // 2) for d in self.devices]
        self.rows = [
            [[2 * targets[d][slot] + (d % 2 ^ other) for d in self.devices] for other in (0, 1)]
            for slot in range(chips)
        ]
        self.sent, self.pairs = {}, {}
        for stream in (0, 1):
            for step in range(1, chips):
                numbers, pairs = [], []
                for d in self.devices:
                    way = self.way(d, stream)
                    place = d // 2 if way > 0 else chips - 1 - d // 2
                    sends = place < step
                    target = d // 2 + way * (chips - step)
                    numbers.append(targets[d].index(target) if sends else -1)
                    if sends:
                        pairs.append((d, d + 2 * way))
                self.sent[stream, step], self.pairs[stream, step] = numbers, pairs

    def way(self, device, stream):
        return 1 if (device // 2 + device % 2 + stream) % 2 == 0 else -1

    def targets(self, chip):
        found = []
        for step in range(1, self.chips):
            far = self.chips - step
            found += [t for t in (chip + far, chip - far) if 0 <= t < self.chips]
        return found + [chip]


def on_device(distribution, scatter_matrix, velocity, capacity, cell_type):
    modes, cells = distribution.shape
    total_modes = scatter_matrix.shape[0]
    half = cells // 2
    extra = -(-2 * modes // LANES // 8) * 8
    step_size = 0.5 * time_step
    part = (modes, half)
    devices = lax.axis_size("mode")
    chips = devices // 2
    plan = Plan(chips)
    call = Chain()
    across = [(i, i ^ 1) for i in range(devices)]
    cap = capacity[None, :]
    table = jnp.concatenate(
        [velocity, cap, cap * velocity, jnp.zeros((3, modes), jnp.float32)], axis=0
    )
    kinds = cell_type[None, :]

    def exchange(value, parts=1):
        cut = value.shape[0] // parts // 8 * 8
        ends = [cut * k for k in range(parts)] + [value.shape[0]]
        return [lax.ppermute(value[i:j], "mode", across) for i, j in zip(ends, ends[1:])]

    class Sums:
        def __init__(self, scale):
            self.scale, self.terms, self.arrived = scale, [], [[None], [None]]

        def add_terms(self, field):
            kernel = functools.partial(slot_products, plan.rows[len(self.terms)])
            mine, other = call(kernel, [part] * 2, [matrix, field])
            self.terms.append((mine, *exchange(other)))

        def join_terms(self, *slots):
            for slot in slots:
                (self.terms[slot],) = call(add, [part], self.terms[slot])

        def send(self, step, between=None):
            sent = {}
            for stream in (step % 2, 1 - step % 2):
                if between is not None and sent:
                    between()
                numbers = plan.sent[stream, step]
                slots = sorted({n for n in numbers if n >= 0})
                arrived = self.arrived[1 - stream][step - 1]
                arrays = [] if arrived is None else [arrived]
                if step == 1:
                    value = self.terms[0]
                else:
                    kernel = functools.partial(payload, numbers, slots)
                    (value,) = call(kernel, [part], arrays + [self.terms[s] for s in slots])
                sent[stream] = lax.ppermute(value, "mode", plan.pairs[stream, step])
            for stream in (0, 1):
                self.arrived[stream].append(sent[stream])

        def first_end(self, base):
            kernel = functools.partial(take_off, self.scale)
            arrived = self.arrived[(chips - 1) % 2][-1]
            (self.rest,) = call(kernel, [part], [arrived, self.terms[-1], base])

        def ends(self):
            return [self.arrived[chips % 2][-1], self.rest]

    def product(gathered, base, scale, rows):
        kernel = functools.partial(whole_product, scale, rows)
        outs = [part, (HALO, modes), (8, modes)] if rows else [part]
        return call(
            kernel,
            outs,
            [matrix, gathered, base],
            places=[VMEM, HBM, VMEM],
            scratch=[
                pltpu.VMEM(gathered.shape, jnp.float32),
                pltpu.SemaphoreType.DMA((devices,)),
            ],
            room=24,
        )

    own, _ = call(
        own_rows,
        [(modes + extra, half), (8, LANES)],
        [distribution, velocity, cap],
        places=[HBM] * 3,
        scratch=[
            pltpu.VMEM((2, modes), jnp.float32),
            pltpu.VMEM((1, modes), jnp.float32),
            pltpu.SemaphoreType.DMA((3,)),
        ],
        room=56,
    )
    gathered = lax.all_gather(own, "mode")
    *terms, matrix = call(
        functools.partial(load_and_products, plan.rows, half),
        [part] * (2 * chips) + [jax.ShapeDtypeStruct(scatter_matrix.shape, jnp.bfloat16)],
        [scatter_matrix, distribution],
        places=[HBM] * 2,
        scratch=[
            pltpu.VMEM(part, jnp.float32),
            pltpu.SemaphoreType.DMA((2 * chips + 1,)),
        ],
        room=28,
    )
    operators = jnp.asarray(differences(cells))
    strips = None

    def unpack():
        nonlocal strips
        shape = jax.ShapeDtypeStruct((modes, 4 * HALO), jnp.bfloat16)
        (strips,) = call(strip_columns, [shape], strips)

    one = Sums(time_step)
    one.terms = [(terms[2 * s], *exchange(terms[2 * s + 1])) for s in range(chips)]
    one.join_terms(0)
    one.send(1)
    one.join_terms(*range(1, chips))
    strips = call(strip_rows, [(HALO, modes)] * 2, [distribution])
    strips = paired(*call(strip_pairs, [(HALO, modes)] * 2, strips))
    for step in range(2, chips):
        one.send(step, unpack if step == 2 else None)
        if step == 2:
            base_a, base_b = call(
                first_rest, [part] * 2, [distribution, strips, operators, table, kinds]
            )
    one.first_end(base_b)
    mid_b, last = call(
        functools.partial(turn_sum, time_step), [part, (HALO, modes)], one.ends()
    )
    gathered_mid = lax.all_gather(mid_b, "mode")
    mid_a, leading, scattered = product(gathered, base_a, time_step, True)

    two = Sums(step_size)
    two.add_terms(mid_a)
    two.add_terms(mid_a)
    two.join_terms(0)
    two.send(1)
    strips = paired(*call(strip_pairs, [(HALO, modes)] * 2, [leading, last]))
    for slot in range(2, chips):
        two.add_terms(mid_a)
    two.join_terms(*range(1, chips))
    flux = None
    for step in range(2, chips):
        if step == 2:
            two.send(step, unpack)
            end_a, end_b, part_flux = call(
                functools.partial(second_rest, 1.0 / math.sqrt(total_modes)),
                [part, part, (2, cells)],
                [distribution, mid_a, mid_b, strips, operators, table, kinds, scattered],
            )
            flux = Flux(call, part_flux, devices)
            flux.over(1)
        else:
            two.send(step)
    flux.over(*range(2, devices, 2))
    heat_flux = flux.value
    two.first_end(end_a)
    (last_b,) = product(gathered_mid, end_b, step_size, False)
    (updated,) = call(
        functools.partial(last_sum, step_size),
        [(modes, cells)],
        [*two.ends(), last_b],
        scratch=[pltpu.VMEM(part, jnp.float32), pltpu.SemaphoreType.DMA((2,))],
        out_specs=[HBM],
    )
    return (updated, heat_flux)


class Flux:
    def __init__(self, call, value, devices):
        self.call, self.value, self.devices = call, value, devices

    def over(self, *bits):
        came = [
            lax.ppermute(self.value, "mode", [(i, i ^ bit) for i in range(self.devices)])
            for bit in bits
        ]
        self.value, _ = self.call(add_all, [self.value.shape, (8, LANES)], [self.value, *came])


def solution(mesh):
    return jax.shard_map(
        on_device,
        mesh=mesh,
        in_specs=(P("mode", "space"), P(None, "mode"), P(None, "mode"), P("mode"), P("space")),
        out_specs=(P("mode", "space"), P(None, "space")),
        check_vma=False,
    )
```

```python
import functools
import math

import numpy as np

import jax
import jax.numpy as jnp
from jax import lax
from jax.experimental import pallas as pl
from jax.experimental.pallas import tpu as pltpu
from jax.sharding import PartitionSpec as P

NY = 16
HALO = 2 * NY
LANES = 128
BLOCK = 512
PIECES = 4


relax_rate = 0.5
time_step = 0.5

VMEM = pl.BlockSpec(memory_space=pltpu.VMEM)
ANY = pl.BlockSpec(memory_space=pl.ANY)
HBM = pl.BlockSpec(memory_space=pltpu.HBM)


class Chain:
    def __init__(self):
        self.last = None

    def __call__(self, kernel, outs, arrays, places=None, scratch=(), out_specs=None, room=16):
        extra = [] if self.last is None else [self.last]
        skip = len(extra)
        first = len(arrays)

        def body(*refs):
            kernel(*refs[:first], *refs[first + skip :])

        results = pl.pallas_call(
            body,
            out_shape=[
                jax.ShapeDtypeStruct(shape, jnp.float32) if isinstance(shape, tuple) else shape
                for shape in outs
            ],
            in_specs=list(places or [VMEM] * len(arrays)) + [ANY] * skip,
            out_specs=out_specs or [VMEM] * len(outs),
            scratch_shapes=list(scratch),
            compiler_params=pltpu.CompilerParams(vmem_limit_bytes=room * 1024 * 1024),
            cost_estimate=pl.CostEstimate(flops=1024, bytes_accessed=1024, transcendentals=0),
            name=getattr(kernel, "func", kernel).__name__,
        )(*arrays, *extra)
        self.last = results[-1]
        return results


def halves(value):
    high = value.astype(jnp.bfloat16)
    low = (value - high.astype(jnp.float32)).astype(jnp.bfloat16)
    return high, low


def for_device(numbers):
    if len(set(numbers)) == 1:
        return numbers[0]
    me = lax.axis_index("mode")
    chosen = jnp.int32(numbers[0])
    for device, number in enumerate(numbers[1:], 1):
        chosen = jnp.where(me == device, jnp.int32(number), chosen)
    return chosen


def rows_of(matrix, block):
    modes = matrix.shape[1]
    return pl.ds(pl.multiple_of(block * modes, modes), modes)


def one_slot(blocks, matrix, parts, mine, other):
    cells = mine.shape[1]
    for block, out in zip(blocks, (mine, other)):
        both = jnp.dot(matrix[rows_of(matrix, block), :], parts, preferred_element_type=jnp.float32)
        out[...] = both[:, :cells] + both[:, cells:]


def slot_products(blocks, matrix, field, mine, other):
    blocks = [for_device(numbers) for numbers in blocks]
    parts = jnp.concatenate(halves(field[...]), axis=1)
    one_slot(blocks, matrix, parts, mine, other)


def load_and_products(blocks, column, matrix, distribution, *refs):
    slots = len(blocks)
    outs, (held, field, sems) = refs[: 2 * slots], refs[2 * slots :]
    cells = field.shape[1]
    start = pltpu.make_async_copy(
        distribution.at[:, pl.ds(column, cells)], field, sems.at[2 * slots]
    )
    start.start()
    blocks = [[for_device(numbers) for numbers in pair] for pair in blocks]
    copies = []
    for slot, pair in enumerate(blocks):
        for k, block in enumerate(pair):
            rows = rows_of(held, block)
            copies.append(
                pltpu.make_async_copy(
                    matrix.at[rows, :], held.at[rows, :], sems.at[2 * slot + k]
                )
            )
            copies[-1].start()
    start.wait()
    parts = jnp.concatenate(halves(field[...]), axis=1)
    for slot, pair in enumerate(blocks):
        for k in range(2):
            copies[2 * slot + k].wait()
        one_slot(pair, held, parts, outs[2 * slot], outs[2 * slot + 1])


def two_blocks(numbers, parts, first, last, scale, rows, matrix, *refs):
    modes = matrix.shape[1]
    blocks, refs = [[refs[0]], refs[1 : 1 + parts]], refs[1 + parts :]
    if not first:
        before, refs = refs[0], refs[1:]
    if last:
        base, refs = refs[0], refs[1:]
    total = None if first else before[...]
    for k, pieces in enumerate(blocks):
        block = jnp.concatenate([piece[...] for piece in pieces], axis=0)
        pieces = list(halves(block[:modes].T))
        if rows:
            weights = [
                jnp.concatenate(
                    [
                        block[modes + i : modes + i + 1, :]
                        for i in range(d * modes // LANES, (d + 1) * modes // LANES)
                    ],
                    axis=1,
                )
                for d in range(2)
            ]
            weights.append(jnp.zeros((6, modes), jnp.float32))
            pieces += halves(jnp.concatenate(weights, axis=0))
        left = jnp.concatenate(pieces, axis=0)
        there = rows_of(matrix, for_device(numbers[k]))
        term = jnp.dot(left, matrix[there, :], preferred_element_type=jnp.float32)
        total = term if total is None else total + term
    if not last:
        refs[0][...] = total
        return
    cells = base.shape[1]
    value = base[...] - scale * (total[:cells] + total[cells : 2 * cells]).T
    refs[0][...] = value
    if rows:
        refs[1][...] = value.T[:HALO]
        refs[2][...] = total[2 * cells : 2 * cells + 8] + total[2 * cells + 8 :]


def own_rows(distribution, velocity, capacity, out, token, field, speeds, weight, extra, sems):
    modes, cells = field.shape
    pieces = [pl.ds(r, modes // PIECES) for r in range(0, modes, modes // PIECES)]
    copies = [
        pltpu.make_async_copy(velocity, speeds, sems.at[0]),
        pltpu.make_async_copy(capacity, weight, sems.at[1]),
    ]
    copies += [
        pltpu.make_async_copy(
            distribution.at[rows, pl.ds(0, cells)], field.at[rows, :], sems.at[2 + k]
        )
        for k, rows in enumerate(pieces)
    ]
    for copy in copies:
        copy.start()
    token[...] = jnp.zeros_like(token)
    extra[...] = jnp.zeros_like(extra)
    for copy in copies[:2]:
        copy.wait()
    per = modes // LANES
    for d in range(2):
        for i in range(per):
            lanes = slice(i * LANES, (i + 1) * LANES)
            extra[d * per + i : d * per + i + 1, :] = speeds[d : d + 1, lanes] * weight[:, lanes]
    onward = [
        pltpu.make_async_copy(extra, out.at[pl.ds(modes, extra.shape[0]), :], sems.at[0])
    ]
    onward[0].start()
    for k, rows in enumerate(pieces):
        copies[2 + k].wait()
        onward.append(
            pltpu.make_async_copy(field.at[rows, :], out.at[rows, :], sems.at[2 + PIECES + k])
        )
        onward[-1].start()
    for copy in onward:
        copy.wait()


def payload(numbers, slots, arrived, *refs):
    out = refs[-1]
    slot_here = for_device(numbers)

    for k, slot in enumerate(slots):

        @pl.when(slot_here == slot)
        def _(k=k):
            terms = refs[k]
            modes = terms.shape[0]
            out[:modes] = arrived[:modes] + terms[...]
            if out.shape[0] > modes:
                out[modes:] = arrived[modes:]

    @pl.when(slot_here < 0)
    def _():
        out[...] = arrived[: out.shape[0]]


def pick(numbers, *refs):
    out = refs[-1]
    choice = for_device(numbers)
    for k, ref in enumerate(refs[:-1]):

        @pl.when(choice == k)
        def _(ref=ref):
            out[...] = ref[...]


def add(one, *refs):
    out, first = refs[-1], 0
    for piece in refs[:-1]:
        rows = slice(first, first + piece.shape[0])
        out[rows] = one[rows] + piece[...]
        first += piece.shape[0]


def pass_on(value, out):
    out[...] = value[...]


def add_all(*refs):
    out, token = refs[-2:]
    total = refs[0][...]
    for ref in refs[1:-2]:
        total = total + ref[...]
    out[...] = total
    token[...] = jnp.zeros_like(token)


def take_off(scale, arrived, terms, base, out):
    modes = terms.shape[0]
    out[...] = base[...] - scale * (arrived[:modes] + terms[...])


def turn_sum(scale, arrived, base, out, strip):
    modes = base.shape[0]
    value = base[...] - scale * arrived[:modes]
    out[...] = value
    strip[...] = value.T[-HALO:]


def last_sum(scale, arrived, base, other, out, value, sems):
    modes, cells = base.shape
    copies = [pltpu.make_async_copy(other, out.at[:, pl.ds(cells, cells)], sems.at[0])]
    copies[0].start()
    for k in range(PIECES):
        rows = pl.ds(k * modes // PIECES, modes // PIECES)
        value[rows, :] = base[rows, :] - scale * arrived[rows, :]
        copies.append(
            pltpu.make_async_copy(
                value.at[rows, :], out.at[rows, pl.ds(0, cells)], sems.at[1 + k]
            )
        )
        copies[-1].start()
    for copy in copies:
        copy.wait()


def strip_rows(distribution, leading, last):
    cells = distribution.shape[1]
    leading[...] = distribution[:, :LANES].T[:HALO]
    last[...] = distribution[:, cells - LANES :].T[-HALO:]


def strip_pairs(leading, last, out_even, out_odd):
    even = lax.axis_index("space") % 2 == 0

    @pl.when(even)
    def _():
        out_even[...] = last[...]
        out_odd[...] = leading[...]

    @pl.when(jnp.logical_not(even))
    def _():
        out_even[...] = leading[...]
        out_odd[...] = last[...]


def differences(cells):
    columns = cells // NY
    own, strip = np.zeros((cells, 4 * cells)), np.zeros((2 * HALO, 4 * cells))
    for x in range(columns):
        for y in range(NY):
            cell = x * NY + y
            for way in (-1, 1):
                for far, factor in enumerate((3.0, -4.0, 1.0)):
                    at_x, at_y = x + way * far, y + way * far
                    first = cell + (0 if way < 0 else cells)
                    factor = -way * factor
                    if at_x < 0:
                        strip[(at_x + 2) * NY + y, first] = factor
                    elif at_x >= columns:
                        strip[HALO + (at_x - columns) * NY + y, first] = factor
                    else:
                        own[at_x * NY + y, first] = factor
                    if 0 <= at_y < NY:
                        own[x * NY + at_y, first + 2 * cells] = factor
    return np.concatenate([own, own, strip, strip]).astype(jnp.bfloat16)


def strip_columns(came_even, came_odd, out):
    even = lax.axis_index("space") % 2 == 0
    before = jnp.where(even, came_odd[...], came_even[...])
    after = jnp.where(even, came_even[...], came_odd[...])
    parts = halves(jnp.concatenate([before, after], axis=0))
    rows = jnp.concatenate([p.astype(jnp.float32) for p in parts], axis=0)
    out[...] = rows.T.astype(jnp.bfloat16)


def still_rate(field, strip, operators, columns, kinds):
    cells = field.shape[1]
    left = jnp.concatenate([*halves(field), strip], axis=1)
    steps = jnp.dot(left, operators[...], preferred_element_type=jnp.float32)
    vx, vy, capacity = (columns[:, i : i + 1] for i in range(3))
    speeds = (jnp.maximum(vx, 0.0), jnp.minimum(vx, 0.0))
    speeds += (jnp.maximum(vy, 0.0), jnp.minimum(vy, 0.0))
    contact = jnp.where(kinds > 0, relax_rate, 0.0)
    source = jnp.where(kinds == 1, contact, -contact)
    rate = source * capacity - contact * field
    for k, speed in enumerate(speeds):
        rate = rate - (0.5 * speed) * steps[:, k * cells : (k + 1) * cells]
    return rate


def first_rest(field, strips, operators, table, kinds, base_a, base_b):
    modes, half = base_a.shape
    block = min(modes, BLOCK)

    def step(i, _):
        rows = pl.ds(pl.multiple_of(i * block, block), block)
        value = field[rows, :]
        rate = still_rate(value, strips[rows, :], operators, table[:, rows].T, kinds[...])
        base = value + time_step * rate
        base_a[rows, :] = base[:, :half]
        base_b[rows, :] = base[:, half:]
        return 0

    lax.fori_loop(0, modes // block, step, 0)


def second_rest(
    flux_scale,
    field,
    mid_a,
    mid_b,
    strips,
    operators,
    table,
    kinds,
    scattered,
    end_a,
    end_b,
    flux,
):
    modes, half = end_a.shape
    block = min(modes, BLOCK)
    step_size = 0.5 * time_step
    flux[...] = jnp.zeros_like(flux)

    def step(i, _):
        rows = pl.ds(pl.multiple_of(i * block, block), block)
        mid = jnp.concatenate([mid_a[rows, :], mid_b[rows, :]], axis=1)
        columns = table[:, rows].T
        taken = step_size * scattered[:, rows].T
        rate = still_rate(mid, strips[rows, :], operators, columns, kinds[...])
        end = 0.5 * (field[rows, :] + mid) + step_size * rate
        end_a[rows, :] = end[:, :half]
        end_b[rows, :] = end[:, half:]
        for d in range(2):
            terms = columns[:, 3 + d : 4 + d] * end - taken[:, d : d + 1] * mid
            flux[d : d + 1, :] += flux_scale * jnp.sum(terms, axis=0, keepdims=True)
        return 0

    lax.fori_loop(0, modes // block, step, 0)


def paired(to_even, to_odd):
    count = lax.axis_size("space")
    came = []
    for first, value in enumerate((to_even, to_odd)):
        pairs = [(i, i + 1) for i in range(first, count - 1, 2)]
        came.append(lax.ppermute(value, "space", pairs + [(j, i) for i, j in pairs]))
    return came


class Plan:
    def __init__(self, chips):
        self.chips = chips
        self.devices = range(2 * chips)
        sources = [self.sources(d) for d in self.devices]
        targets = [self.targets(d // 2) for d in self.devices]
        self.blocks = [
            [
                [2 * sources[e][slot][2] + e % 2 for e in (d ^ other for d in self.devices)]
                for other in (0, 1)
            ]
            for slot in range(chips)
        ]
        self.rows = [
            [[2 * targets[d][slot] + (d % 2 ^ other) for d in self.devices] for other in (0, 1)]
            for slot in range(chips)
        ]
        self.choices = [
            sorted({sources[d][slot][:2] for d in self.devices}) for slot in range(chips)
        ]
        self.picked = [
            [self.choices[slot].index(sources[d][slot][:2]) for d in self.devices]
            for slot in range(chips)
        ]
        self.sent = {}
        for stream in (0, 1):
            for step in range(1, chips):
                numbers = []
                for d in self.devices:
                    way = self.way(d, stream)
                    place = d // 2 if way > 0 else chips - 1 - d // 2
                    target = d // 2 + way * (chips - step)
                    numbers.append(targets[d].index(target) if place < step else -1)
                self.sent[stream, step] = numbers
        self.pairs = []
        for stream in (0, 1):
            up = [
                (d, d + 2) for d in self.devices[:-2] if self.way(d, stream) > 0
            ]
            self.pairs.append(up + [(j, i) for i, j in up])

    def way(self, device, stream):
        return 1 if (device // 2 + device % 2 + stream) % 2 == 0 else -1

    def sources(self, device):
        found = [(-1, -1, device // 2)]
        for step in range(self.chips - 1):
            for stream in (step % 2, 1 - step % 2):
                chip = device // 2 + self.way(device, stream) * (step + 1)
                if 0 <= chip < self.chips:
                    found.append((stream, step, chip))
        return found

    def targets(self, chip):
        found = []
        for step in range(1, self.chips):
            far = self.chips - step
            found += [t for t in (chip + far, chip - far) if 0 <= t < self.chips]
        return found + [chip]


def on_device(distribution, scatter_matrix, velocity, capacity, cell_type):
    modes, cells = distribution.shape
    total_modes = scatter_matrix.shape[0]
    half = cells // 2
    extra = -(-2 * modes // LANES // 8) * 8
    step_size = 0.5 * time_step
    part = (modes, half)
    devices = lax.axis_size("mode")
    chips = devices // 2
    plan = Plan(chips)
    call = Chain()
    across = [(i, i ^ 1) for i in range(devices)]
    cap = capacity[None, :]
    table = jnp.concatenate(
        [velocity, cap, cap * velocity, jnp.zeros((3, modes), jnp.float32)], axis=0
    )
    kinds = cell_type[None, :]

    def exchange(value, parts=1):
        cut = value.shape[0] // parts // 8 * 8
        ends = [cut * k for k in range(parts)] + [value.shape[0]]
        return [lax.ppermute(value[i:j], "mode", across) for i, j in zip(ends, ends[1:])]

    def along(stream, value):
        return lax.ppermute(value, "mode", plan.pairs[stream])

    class Round:
        def __init__(self, matrix, scale, rows):
            self.matrix, self.scale, self.rows = matrix, scale, rows
            self.terms, self.total = [], None

        def begin(self, own):
            self.own = own
            self.arrived = [[along(0, own)], [along(1, own)]]
            self.blocks = []

        def add_terms(self, field, parts=1):
            kernel = functools.partial(slot_products, plan.rows[len(self.terms)])
            mine, other = call(kernel, [part] * 2, [self.matrix, field])
            self.terms.append((mine, *exchange(other, parts)))

        def join_terms(self, *slots):
            for slot in slots:
                (self.terms[slot],) = call(add, [part], self.terms[slot])

        def take_own(self, later=False):
            own = call(pass_on, [self.own.shape], [self.own])[0] if later else self.own
            self.blocks.append((self.own, *exchange(own)))

        def send(self, step, between=None):
            sent = {}
            for stream in (step % 2, 1 - step % 2):
                if between is not None and sent:
                    between()
                numbers = plan.sent[stream, step]
                slots = sorted({n for n in numbers if n >= 0})
                for slot in slots:
                    if isinstance(self.terms[slot], tuple):
                        self.join_terms(slot)
                arrived = self.arrived[1 - stream][step - 1]
                kernel = functools.partial(payload, numbers, slots)
                arrays = [arrived] + [self.terms[s] for s in slots]
                shape = part if step == chips - 1 else arrived.shape
                (value,) = call(kernel, [shape], arrays)
                sent[stream] = along(stream, value)
            for stream in (0, 1):
                self.arrived[stream].append(sent[stream])

        def take(self, slot, parts=1):
            arrays = [self.arrived[stream][step] for stream, step in plan.choices[slot]]
            kernel = functools.partial(pick, plan.picked[slot])
            (here,) = call(kernel, [arrays[0].shape], arrays)
            self.blocks.append((here, *exchange(here, parts)))

        def hold(self, *slots):
            for slot in slots:
                here, there = self.blocks[slot]
                (there,) = call(pass_on, [there.shape], [there])
                self.blocks[slot] = (here, there)

        def multiply(self, slot, base=None, first=None):
            first, last = slot == 0 if first is None else first, base is not None
            blocks = self.blocks[slot]
            kernel = functools.partial(
                two_blocks, plan.blocks[slot], len(blocks) - 1, first, last, self.scale, self.rows
            )
            arrays = [self.matrix, *blocks]
            arrays += [] if first else [self.total]
            arrays += [base] if last else []
            outs = [(2 * half + (16 if self.rows else 0), modes)]
            if last:
                outs = [part, (HALO, modes), (8, modes)] if self.rows else [part]
            results = call(kernel, outs, arrays)
            self.total = results[0]
            return results

        def first_end(self, base):
            kernel = functools.partial(take_off, self.scale)
            arrived = self.arrived[(chips - 1) % 2][-1]
            (self.rest,) = call(kernel, [part], [arrived, self.terms[-1], base])

        def ends(self):
            return [self.arrived[chips % 2][-1], self.rest]

    own, _ = call(
        own_rows,
        [(modes + extra, half), (8, LANES)],
        [distribution, velocity, cap],
        places=[HBM] * 3,
        scratch=[
            pltpu.VMEM(part, jnp.float32),
            pltpu.VMEM((2, modes), jnp.float32),
            pltpu.VMEM((1, modes), jnp.float32),
            pltpu.VMEM((extra, LANES), jnp.float32),
            pltpu.SemaphoreType.DMA((2 + 2 * PIECES,)),
        ],
        out_specs=[HBM, VMEM],
        room=56,
    )
    one = Round(None, time_step, True)
    one.begin(own)
    *terms, matrix = call(
        functools.partial(load_and_products, plan.rows, half),
        [part] * (2 * chips) + [jax.ShapeDtypeStruct(scatter_matrix.shape, jnp.bfloat16)],
        [scatter_matrix, distribution],
        places=[HBM] * 2,
        scratch=[
            pltpu.VMEM(part, jnp.float32),
            pltpu.SemaphoreType.DMA((2 * chips + 1,)),
        ],
        room=28,
    )
    one.matrix = matrix
    one.terms = [(terms[2 * s], *exchange(terms[2 * s + 1])) for s in range(chips)]
    one.take_own()
    operators = jnp.asarray(differences(cells))
    strips = None

    def unpack():
        nonlocal strips
        shape = jax.ShapeDtypeStruct((modes, 4 * HALO), jnp.bfloat16)
        (strips,) = call(strip_columns, [shape], strips)

    for step in range(1, chips):
        if step == 1:
            one.take(1)
        one.send(step, unpack if step == 2 else None)
        if step == 1:
            one.join_terms(*(s for s in range(chips) if isinstance(one.terms[s], tuple)))
            strips = call(strip_rows, [(HALO, modes)] * 2, [distribution])
            strips = paired(*call(strip_pairs, [(HALO, modes)] * 2, strips))
        else:
            one.take(step, 2 if step == chips - 1 else 1)
        if step == 2:
            one.multiply(0)
        if step > 1:
            one.multiply(step - 1)
        if step == min(2, chips - 1):
            base_a, base_b = call(
                first_rest,
                [part] * 2,
                [distribution, strips, operators, table, kinds],
            )
    mid_a, leading, scattered = one.multiply(chips - 1, base_a)

    two = Round(matrix, step_size, False)
    two.add_terms(mid_a, 1)
    one.first_end(base_b)
    mid_b, last = call(
        functools.partial(turn_sum, time_step), [part, (HALO, modes)], one.ends()
    )
    two.begin(mid_b)
    two.add_terms(mid_a)
    two.join_terms(0)
    strips = paired(*call(strip_pairs, [(HALO, modes)] * 2, [leading, last]))
    flux = None
    for step in range(1, chips):
        if step == 1:
            two.send(step, unpack)
            two.take_own()
            two.join_terms(1)
        elif step == 2:
            two.send(step, lambda: flux.over(1))
            two.join_terms(*range(2, chips))
        elif step == chips - 1:
            two.send(step, lambda: flux.over(*range(2, devices, 2)))
        else:
            two.send(step)
        two.take(step, 2 if step >= chips - 2 else 1)
        if step == 1:
            for slot in range(2, chips):
                two.add_terms(mid_a)
        if 1 < step < chips - 1:
            two.hold(*range(step) if step == 2 else (step - 1,))
        if step == chips - 2:
            two.multiply(step, first=True)
        if step == chips - 1:
            for slot in range(chips - 2):
                two.multiply(slot, first=False)
        if step == 1:
            end_a, end_b, part_flux = call(
                functools.partial(second_rest, 1.0 / math.sqrt(total_modes)),
                [part, part, (2, cells)],
                [distribution, mid_a, mid_b, strips, operators, table, kinds, scattered],
            )
            flux = Flux(call, part_flux, devices)
    (last_b,) = two.multiply(chips - 1, end_b)
    heat_flux = flux.value
    two.first_end(end_a)
    (updated,) = call(
        functools.partial(last_sum, step_size),
        [(modes, cells)],
        [*two.ends(), last_b],
        scratch=[pltpu.VMEM(part, jnp.float32), pltpu.SemaphoreType.DMA((1 + PIECES,))],
        out_specs=[HBM],
    )
    return (updated, heat_flux)


class Flux:
    def __init__(self, call, value, devices):
        self.call, self.value, self.devices = call, value, devices

    def over(self, *bits):
        came = [
            lax.ppermute(self.value, "mode", [(i, i ^ bit) for i in range(self.devices)])
            for bit in bits
        ]
        self.value, _ = self.call(add_all, [self.value.shape, (8, LANES)], [self.value, *came])


def solution(mesh):
    return jax.shard_map(
        on_device,
        mesh=mesh,
        in_specs=(P("mode", "space"), P(None, "mode"), P(None, "mode"), P("mode"), P("space")),
        out_specs=(P("mode", "space"), P(None, "space")),
        check_vma=False,
    )
```

```python
import functools
import math

import numpy as np

import jax
import jax.numpy as jnp
from jax import lax
from jax.experimental import pallas as pl
from jax.experimental.pallas import tpu as pltpu
from jax.sharding import PartitionSpec as P

NY = 16
HALO = 2 * NY
LANES = 128
BLOCK = 512


relax_rate = 0.5
time_step = 0.5

VMEM = pl.BlockSpec(memory_space=pltpu.VMEM)
ANY = pl.BlockSpec(memory_space=pl.ANY)
HBM = pl.BlockSpec(memory_space=pltpu.HBM)


class Chain:
    def __init__(self):
        self.last = None

    def __call__(self, kernel, outs, arrays, places=None, scratch=(), out_specs=None, room=16):
        extra = [] if self.last is None else [self.last]
        skip = len(extra)
        first = len(arrays)

        def body(*refs):
            kernel(*refs[:first], *refs[first + skip :])

        results = pl.pallas_call(
            body,
            out_shape=[
                jax.ShapeDtypeStruct(shape, jnp.float32) if isinstance(shape, tuple) else shape
                for shape in outs
            ],
            in_specs=list(places or [VMEM] * len(arrays)) + [ANY] * skip,
            out_specs=out_specs or [VMEM] * len(outs),
            scratch_shapes=list(scratch),
            compiler_params=pltpu.CompilerParams(vmem_limit_bytes=room * 1024 * 1024),
            cost_estimate=pl.CostEstimate(flops=1024, bytes_accessed=1024, transcendentals=0),
            name=getattr(kernel, "func", kernel).__name__,
        )(*arrays, *extra)
        self.last = results[-1]
        return results


def halves(value):
    high = value.astype(jnp.bfloat16)
    low = (value - high.astype(jnp.float32)).astype(jnp.bfloat16)
    return high, low


def for_device(numbers):
    if len(set(numbers)) == 1:
        return numbers[0]
    me = lax.axis_index("mode")
    chosen = jnp.int32(numbers[0])
    for device, number in enumerate(numbers[1:], 1):
        chosen = jnp.where(me == device, jnp.int32(number), chosen)
    return chosen


def rows_of(matrix, block):
    modes = matrix.shape[1]
    return pl.ds(pl.multiple_of(block * modes, modes), modes)


def one_slot(blocks, matrix, parts, mine, other):
    cells = mine.shape[1]
    for block, out in zip(blocks, (mine, other)):
        both = jnp.dot(matrix[rows_of(matrix, block), :], parts, preferred_element_type=jnp.float32)
        out[...] = both[:, :cells] + both[:, cells:]


def slot_products(blocks, matrix, field, mine, other):
    blocks = [for_device(numbers) for numbers in blocks]
    parts = jnp.concatenate(halves(field[...]), axis=1)
    one_slot(blocks, matrix, parts, mine, other)


def load_and_products(blocks, column, matrix, distribution, *refs):
    slots = len(blocks)
    outs, (held, field, sems) = refs[: 2 * slots], refs[2 * slots :]
    cells = field.shape[1]
    start = pltpu.make_async_copy(
        distribution.at[:, pl.ds(column, cells)], field, sems.at[2 * slots]
    )
    start.start()
    blocks = [[for_device(numbers) for numbers in pair] for pair in blocks]
    copies = []
    for slot, pair in enumerate(blocks):
        for k, block in enumerate(pair):
            rows = rows_of(held, block)
            copies.append(
                pltpu.make_async_copy(
                    matrix.at[rows, :], held.at[rows, :], sems.at[2 * slot + k]
                )
            )
            copies[-1].start()
    start.wait()
    parts = jnp.concatenate(halves(field[...]), axis=1)
    for slot, pair in enumerate(blocks):
        for k in range(2):
            copies[2 * slot + k].wait()
        one_slot(pair, held, parts, outs[2 * slot], outs[2 * slot + 1])


def two_blocks(numbers, parts, first, last, scale, rows, matrix, *refs):
    modes = matrix.shape[1]
    blocks, refs = [[refs[0]], refs[1 : 1 + parts]], refs[1 + parts :]
    if not first:
        before, refs = refs[0], refs[1:]
    if last:
        base, refs = refs[0], refs[1:]
    total = None if first else before[...]
    for k, pieces in enumerate(blocks):
        block = jnp.concatenate([piece[...] for piece in pieces], axis=0)
        pieces = list(halves(block[:modes].T))
        if rows:
            weights = [
                jnp.concatenate(
                    [
                        block[modes + i : modes + i + 1, :]
                        for i in range(d * modes // LANES, (d + 1) * modes // LANES)
                    ],
                    axis=1,
                )
                for d in range(2)
            ]
            weights.append(jnp.zeros((6, modes), jnp.float32))
            pieces += halves(jnp.concatenate(weights, axis=0))
        left = jnp.concatenate(pieces, axis=0)
        there = rows_of(matrix, for_device(numbers[k]))
        term = jnp.dot(left, matrix[there, :], preferred_element_type=jnp.float32)
        total = term if total is None else total + term
    if not last:
        refs[0][...] = total
        return
    cells = base.shape[1]
    value = base[...] - scale * (total[:cells] + total[cells : 2 * cells]).T
    refs[0][...] = value
    if rows:
        refs[1][...] = value.T[:HALO]
        refs[2][...] = total[2 * cells : 2 * cells + 8] + total[2 * cells + 8 :]


def own_rows(distribution, velocity, capacity, out, token, speeds, weight, sems):
    modes, cells = velocity.shape[1], out.shape[1]
    copies = [
        pltpu.make_async_copy(velocity, speeds, sems.at[0]),
        pltpu.make_async_copy(capacity, weight, sems.at[1]),
        pltpu.make_async_copy(
            distribution.at[:, pl.ds(0, cells)], out.at[pl.ds(0, modes), :], sems.at[2]
        ),
    ]
    for copy in copies:
        copy.start()
    token[...] = jnp.zeros_like(token)
    for copy in copies[:2]:
        copy.wait()
    per = modes // LANES
    out[modes:] = jnp.zeros((out.shape[0] - modes, LANES), jnp.float32)
    for d in range(2):
        for i in range(per):
            lanes = slice(i * LANES, (i + 1) * LANES)
            out[modes + d * per + i : modes + d * per + i + 1, :] = (
                speeds[d : d + 1, lanes] * weight[:, lanes]
            )
    copies[2].wait()


def payload(numbers, slots, arrived, *refs):
    out = refs[-1]
    slot_here = for_device(numbers)

    for k, slot in enumerate(slots):

        @pl.when(slot_here == slot)
        def _(k=k):
            terms = refs[k]
            modes = terms.shape[0]
            out[:modes] = arrived[:modes] + terms[...]
            if out.shape[0] > modes:
                out[modes:] = arrived[modes:]

    @pl.when(slot_here < 0)
    def _():
        out[...] = arrived[...]


def pick(numbers, *refs):
    out = refs[-1]
    choice = for_device(numbers)
    for k, ref in enumerate(refs[:-1]):

        @pl.when(choice == k)
        def _(ref=ref):
            out[...] = ref[...]


def add(one, *refs):
    out, first = refs[-1], 0
    for piece in refs[:-1]:
        rows = slice(first, first + piece.shape[0])
        out[rows] = one[rows] + piece[...]
        first += piece.shape[0]


def pass_on(value, out):
    out[...] = value[...]


def add_all(*refs):
    out, token = refs[-2:]
    total = refs[0][...]
    for ref in refs[1:-2]:
        total = total + ref[...]
    out[...] = total
    token[...] = jnp.zeros_like(token)


def take_off(scale, arrived, terms, base, out):
    modes = terms.shape[0]
    out[...] = base[...] - scale * (arrived[:modes] + terms[...])


def turn_sum(scale, arrived, base, out, strip):
    modes = base.shape[0]
    value = base[...] - scale * arrived[:modes]
    out[...] = value
    strip[...] = value.T[-HALO:]


def last_sum(scale, arrived, base, other, out, value, sems):
    cells = base.shape[1]
    ahead = pltpu.make_async_copy(other, out.at[:, pl.ds(cells, cells)], sems.at[0])
    ahead.start()
    value[...] = base[...] - scale * arrived[...]
    copy = pltpu.make_async_copy(value, out.at[:, pl.ds(0, cells)], sems.at[1])
    copy.start()
    ahead.wait()
    copy.wait()


def strip_rows(distribution, leading, last):
    cells = distribution.shape[1]
    leading[...] = distribution[:, :LANES].T[:HALO]
    last[...] = distribution[:, cells - LANES :].T[-HALO:]


def strip_pairs(leading, last, out_even, out_odd):
    even = lax.axis_index("space") % 2 == 0

    @pl.when(even)
    def _():
        out_even[...] = last[...]
        out_odd[...] = leading[...]

    @pl.when(jnp.logical_not(even))
    def _():
        out_even[...] = leading[...]
        out_odd[...] = last[...]


def differences(cells):
    columns = cells // NY
    own, strip = np.zeros((cells, 4 * cells)), np.zeros((2 * HALO, 4 * cells))
    for x in range(columns):
        for y in range(NY):
            cell = x * NY + y
            for way in (-1, 1):
                for far, factor in enumerate((3.0, -4.0, 1.0)):
                    at_x, at_y = x + way * far, y + way * far
                    first = cell + (0 if way < 0 else cells)
                    factor = -way * factor
                    if at_x < 0:
                        strip[(at_x + 2) * NY + y, first] = factor
                    elif at_x >= columns:
                        strip[HALO + (at_x - columns) * NY + y, first] = factor
                    else:
                        own[at_x * NY + y, first] = factor
                    if 0 <= at_y < NY:
                        own[x * NY + at_y, first + 2 * cells] = factor
    return np.concatenate([own, own, strip, strip]).astype(jnp.bfloat16)


def strip_columns(came_even, came_odd, out):
    even = lax.axis_index("space") % 2 == 0
    before = jnp.where(even, came_odd[...], came_even[...])
    after = jnp.where(even, came_even[...], came_odd[...])
    parts = halves(jnp.concatenate([before, after], axis=0))
    rows = jnp.concatenate([p.astype(jnp.float32) for p in parts], axis=0)
    out[...] = rows.T.astype(jnp.bfloat16)


def still_rate(field, strip, operators, columns, kinds):
    cells = field.shape[1]
    left = jnp.concatenate([*halves(field), strip], axis=1)
    steps = jnp.dot(left, operators[...], preferred_element_type=jnp.float32)
    vx, vy, capacity = (columns[:, i : i + 1] for i in range(3))
    speeds = (jnp.maximum(vx, 0.0), jnp.minimum(vx, 0.0))
    speeds += (jnp.maximum(vy, 0.0), jnp.minimum(vy, 0.0))
    contact = jnp.where(kinds > 0, relax_rate, 0.0)
    source = jnp.where(kinds == 1, contact, -contact)
    rate = source * capacity - contact * field
    for k, speed in enumerate(speeds):
        rate = rate - (0.5 * speed) * steps[:, k * cells : (k + 1) * cells]
    return rate


def first_rest(field, strips, operators, table, kinds, base_a, base_b):
    modes, half = base_a.shape
    block = min(modes, BLOCK)

    def step(i, _):
        rows = pl.ds(pl.multiple_of(i * block, block), block)
        value = field[rows, :]
        rate = still_rate(value, strips[rows, :], operators, table[:, rows].T, kinds[...])
        base = value + time_step * rate
        base_a[rows, :] = base[:, :half]
        base_b[rows, :] = base[:, half:]
        return 0

    lax.fori_loop(0, modes // block, step, 0)


def second_rest(
    flux_scale,
    field,
    mid_a,
    mid_b,
    strips,
    operators,
    table,
    kinds,
    scattered,
    end_a,
    end_b,
    flux,
):
    modes, half = end_a.shape
    block = min(modes, BLOCK)
    step_size = 0.5 * time_step
    flux[...] = jnp.zeros_like(flux)

    def step(i, _):
        rows = pl.ds(pl.multiple_of(i * block, block), block)
        mid = jnp.concatenate([mid_a[rows, :], mid_b[rows, :]], axis=1)
        columns = table[:, rows].T
        taken = step_size * scattered[:, rows].T
        rate = still_rate(mid, strips[rows, :], operators, columns, kinds[...])
        end = 0.5 * (field[rows, :] + mid) + step_size * rate
        end_a[rows, :] = end[:, :half]
        end_b[rows, :] = end[:, half:]
        for d in range(2):
            terms = columns[:, 3 + d : 4 + d] * end - taken[:, d : d + 1] * mid
            flux[d : d + 1, :] += flux_scale * jnp.sum(terms, axis=0, keepdims=True)
        return 0

    lax.fori_loop(0, modes // block, step, 0)


def paired(to_even, to_odd):
    count = lax.axis_size("space")
    came = []
    for first, value in enumerate((to_even, to_odd)):
        pairs = [(i, i + 1) for i in range(first, count - 1, 2)]
        came.append(lax.ppermute(value, "space", pairs + [(j, i) for i, j in pairs]))
    return came


class Plan:
    def __init__(self, chips):
        self.chips = chips
        self.devices = range(2 * chips)
        sources = [self.sources(d) for d in self.devices]
        targets = [self.targets(d // 2) for d in self.devices]
        self.blocks = [
            [
                [2 * sources[e][slot][2] + e % 2 for e in (d ^ other for d in self.devices)]
                for other in (0, 1)
            ]
            for slot in range(chips)
        ]
        self.rows = [
            [[2 * targets[d][slot] + (d % 2 ^ other) for d in self.devices] for other in (0, 1)]
            for slot in range(chips)
        ]
        self.choices = [
            sorted({sources[d][slot][:2] for d in self.devices}) for slot in range(chips)
        ]
        self.picked = [
            [self.choices[slot].index(sources[d][slot][:2]) for d in self.devices]
            for slot in range(chips)
        ]
        self.sent = {}
        for stream in (0, 1):
            for step in range(1, chips):
                numbers = []
                for d in self.devices:
                    way = self.way(d, stream)
                    place = d // 2 if way > 0 else chips - 1 - d // 2
                    target = d // 2 + way * (chips - step)
                    numbers.append(targets[d].index(target) if place < step else -1)
                self.sent[stream, step] = numbers
        self.pairs = []
        for stream in (0, 1):
            up = [
                (d, d + 2) for d in self.devices[:-2] if self.way(d, stream) > 0
            ]
            self.pairs.append(up + [(j, i) for i, j in up])

    def way(self, device, stream):
        return 1 if (device // 2 + device % 2 + stream) % 2 == 0 else -1

    def sources(self, device):
        found = [(-1, -1, device // 2)]
        for step in range(self.chips - 1):
            for stream in (step % 2, 1 - step % 2):
                chip = device // 2 + self.way(device, stream) * (step + 1)
                if 0 <= chip < self.chips:
                    found.append((stream, step, chip))
        return found

    def targets(self, chip):
        found = []
        for step in range(1, self.chips):
            far = self.chips - step
            found += [t for t in (chip + far, chip - far) if 0 <= t < self.chips]
        return found + [chip]


def on_device(distribution, scatter_matrix, velocity, capacity, cell_type):
    modes, cells = distribution.shape
    total_modes = scatter_matrix.shape[0]
    half = cells // 2
    extra = -(-2 * modes // LANES // 8) * 8
    step_size = 0.5 * time_step
    part = (modes, half)
    devices = lax.axis_size("mode")
    chips = devices // 2
    plan = Plan(chips)
    call = Chain()
    across = [(i, i ^ 1) for i in range(devices)]
    cap = capacity[None, :]
    table = jnp.concatenate(
        [velocity, cap, cap * velocity, jnp.zeros((3, modes), jnp.float32)], axis=0
    )
    kinds = cell_type[None, :]

    def exchange(value, parts=1):
        cut = value.shape[0] // parts // 8 * 8
        ends = [cut * k for k in range(parts)] + [value.shape[0]]
        return [lax.ppermute(value[i:j], "mode", across) for i, j in zip(ends, ends[1:])]

    def along(stream, value):
        return lax.ppermute(value, "mode", plan.pairs[stream])

    class Round:
        def __init__(self, matrix, scale, rows):
            self.matrix, self.scale, self.rows = matrix, scale, rows
            self.terms, self.total = [], None

        def begin(self, own):
            self.own = own
            self.arrived = [[along(0, own)], [along(1, own)]]
            self.blocks = []

        def add_terms(self, field, parts=1):
            kernel = functools.partial(slot_products, plan.rows[len(self.terms)])
            mine, other = call(kernel, [part] * 2, [self.matrix, field])
            self.terms.append((mine, *exchange(other, parts)))

        def join_terms(self, *slots):
            for slot in slots:
                (self.terms[slot],) = call(add, [part], self.terms[slot])

        def take_own(self, later=False):
            own = call(pass_on, [self.own.shape], [self.own])[0] if later else self.own
            self.blocks.append((self.own, *exchange(own)))

        def send(self, step, between=None):
            sent = {}
            for stream in (step % 2, 1 - step % 2):
                if between is not None and sent:
                    between()
                numbers = plan.sent[stream, step]
                slots = sorted({n for n in numbers if n >= 0})
                for slot in slots:
                    if isinstance(self.terms[slot], tuple):
                        self.join_terms(slot)
                arrived = self.arrived[1 - stream][step - 1]
                kernel = functools.partial(payload, numbers, slots)
                arrays = [arrived] + [self.terms[s] for s in slots]
                (value,) = call(kernel, [arrived.shape], arrays)
                sent[stream] = along(stream, value)
            for stream in (0, 1):
                self.arrived[stream].append(sent[stream])

        def take(self, slot, parts=1):
            arrays = [self.arrived[stream][step] for stream, step in plan.choices[slot]]
            kernel = functools.partial(pick, plan.picked[slot])
            (here,) = call(kernel, [arrays[0].shape], arrays)
            self.blocks.append((here, *exchange(here, parts)))

        def hold(self, *slots):
            for slot in slots:
                here, there = self.blocks[slot]
                (there,) = call(pass_on, [there.shape], [there])
                self.blocks[slot] = (here, there)

        def multiply(self, slot, base=None, first=None):
            first, last = slot == 0 if first is None else first, base is not None
            blocks = self.blocks[slot]
            kernel = functools.partial(
                two_blocks, plan.blocks[slot], len(blocks) - 1, first, last, self.scale, self.rows
            )
            arrays = [self.matrix, *blocks]
            arrays += [] if first else [self.total]
            arrays += [base] if last else []
            outs = [(2 * half + (16 if self.rows else 0), modes)]
            if last:
                outs = [part, (HALO, modes), (8, modes)] if self.rows else [part]
            results = call(kernel, outs, arrays)
            self.total = results[0]
            return results

        def first_end(self, base):
            kernel = functools.partial(take_off, self.scale)
            arrived = self.arrived[(chips - 1) % 2][-1]
            (self.rest,) = call(kernel, [part], [arrived, self.terms[-1], base])

        def ends(self):
            return [self.arrived[chips % 2][-1], self.rest]

    own, _ = call(
        own_rows,
        [(modes + extra, half), (8, LANES)],
        [distribution, velocity, cap],
        places=[HBM] * 3,
        scratch=[
            pltpu.VMEM((2, modes), jnp.float32),
            pltpu.VMEM((1, modes), jnp.float32),
            pltpu.SemaphoreType.DMA((3,)),
        ],
        room=56,
    )
    one = Round(None, time_step, True)
    one.begin(own)
    *terms, matrix = call(
        functools.partial(load_and_products, plan.rows, half),
        [part] * (2 * chips) + [jax.ShapeDtypeStruct(scatter_matrix.shape, jnp.bfloat16)],
        [scatter_matrix, distribution],
        places=[HBM] * 2,
        scratch=[
            pltpu.VMEM(part, jnp.float32),
            pltpu.SemaphoreType.DMA((2 * chips + 1,)),
        ],
        room=28,
    )
    one.matrix = matrix
    one.terms = [(terms[2 * s], *exchange(terms[2 * s + 1])) for s in range(chips)]
    one.take_own()
    operators = jnp.asarray(differences(cells))
    strips = None

    def unpack():
        nonlocal strips
        shape = jax.ShapeDtypeStruct((modes, 4 * HALO), jnp.bfloat16)
        (strips,) = call(strip_columns, [shape], strips)

    for step in range(1, chips):
        if step == 1:
            one.take(1)
        one.send(step, unpack if step == 2 else None)
        if step == 1:
            one.join_terms(*(s for s in range(chips) if isinstance(one.terms[s], tuple)))
            strips = call(strip_rows, [(HALO, modes)] * 2, [distribution])
            strips = paired(*call(strip_pairs, [(HALO, modes)] * 2, strips))
        else:
            one.take(step, 2 if step == chips - 1 else 1)
        one.multiply(step - 1)
        if step == min(2, chips - 1):
            base_a, base_b = call(
                first_rest,
                [part] * 2,
                [distribution, strips, operators, table, kinds],
            )
    mid_a, leading, scattered = one.multiply(chips - 1, base_a)

    two = Round(matrix, step_size, False)
    two.add_terms(mid_a)
    two.add_terms(mid_a)
    one.first_end(base_b)
    mid_b, last = call(
        functools.partial(turn_sum, time_step), [part, (HALO, modes)], one.ends()
    )
    two.begin(mid_b)
    two.join_terms(0, 1)
    two.take_own()
    strips = paired(*call(strip_pairs, [(HALO, modes)] * 2, [leading, last]))
    flux = None
    for step in range(1, chips):
        if step == 1:
            two.send(step, unpack)
            two.hold(0)
        elif step == 2:
            two.send(step)
            two.join_terms(*range(2, chips))
        elif step == chips - 1:
            two.send(step, lambda: flux.over(*range(2, devices, 2)))
        else:
            two.send(step)
        two.take(step, 2 if step >= chips - 2 else 1)
        if step == 1:
            for slot in range(2, chips):
                two.add_terms(mid_a)
        if 1 < step < chips - 1:
            two.hold(step - 1)
        if step == chips - 2:
            two.multiply(step, first=True)
        if step == chips - 1:
            for slot in range(chips - 2):
                two.multiply(slot, first=False)
        if step == 1:
            end_a, end_b, part_flux = call(
                functools.partial(second_rest, 1.0 / math.sqrt(total_modes)),
                [part, part, (2, cells)],
                [distribution, mid_a, mid_b, strips, operators, table, kinds, scattered],
            )
            flux = Flux(call, part_flux, devices)
    flux.over(1)
    (last_b,) = two.multiply(chips - 1, end_b)
    heat_flux = flux.value
    two.first_end(end_a)
    (updated,) = call(
        functools.partial(last_sum, step_size),
        [(modes, cells)],
        [*two.ends(), last_b],
        scratch=[pltpu.VMEM(part, jnp.float32), pltpu.SemaphoreType.DMA((2,))],
        out_specs=[HBM],
    )
    return (updated, heat_flux)


class Flux:
    def __init__(self, call, value, devices):
        self.call, self.value, self.devices = call, value, devices

    def over(self, *bits):
        came = [
            lax.ppermute(self.value, "mode", [(i, i ^ bit) for i in range(self.devices)])
            for bit in bits
        ]
        self.value, _ = self.call(add_all, [self.value.shape, (8, LANES)], [self.value, *came])


def solution(mesh):
    return jax.shard_map(
        on_device,
        mesh=mesh,
        in_specs=(P("mode", "space"), P(None, "mode"), P(None, "mode"), P("mode"), P("space")),
        out_specs=(P("mode", "space"), P(None, "space")),
        check_vma=False,
    )
```

```python
import functools
import math

import numpy as np

import jax
import jax.numpy as jnp
from jax import lax
from jax.experimental import pallas as pl
from jax.experimental.pallas import tpu as pltpu
from jax.sharding import PartitionSpec as P

NY = 16
HALO = 2 * NY
LANES = 128
BLOCK = 512


relax_rate = 0.5
time_step = 0.5

VMEM = pl.BlockSpec(memory_space=pltpu.VMEM)
ANY = pl.BlockSpec(memory_space=pl.ANY)
HBM = pl.BlockSpec(memory_space=pltpu.HBM)


class Chain:
    def __init__(self):
        self.last = None

    def __call__(self, kernel, outs, arrays, places=None, scratch=(), out_specs=None, room=16):
        extra = [] if self.last is None else [self.last]
        skip = len(extra)
        first = len(arrays)

        def body(*refs):
            kernel(*refs[:first], *refs[first + skip :])

        results = pl.pallas_call(
            body,
            out_shape=[
                jax.ShapeDtypeStruct(shape, jnp.float32) if isinstance(shape, tuple) else shape
                for shape in outs
            ],
            in_specs=list(places or [VMEM] * len(arrays)) + [ANY] * skip,
            out_specs=out_specs or [VMEM] * len(outs),
            scratch_shapes=list(scratch),
            compiler_params=pltpu.CompilerParams(vmem_limit_bytes=room * 1024 * 1024),
            cost_estimate=pl.CostEstimate(flops=1024, bytes_accessed=1024, transcendentals=0),
            name=getattr(kernel, "func", kernel).__name__,
        )(*arrays, *extra)
        self.last = results[-1]
        return results


def halves(value):
    high = value.astype(jnp.bfloat16)
    low = (value - high.astype(jnp.float32)).astype(jnp.bfloat16)
    return high, low


def for_device(numbers):
    if len(set(numbers)) == 1:
        return numbers[0]
    me = lax.axis_index("mode")
    chosen = jnp.int32(numbers[0])
    for device, number in enumerate(numbers[1:], 1):
        chosen = jnp.where(me == device, jnp.int32(number), chosen)
    return chosen


def rows_of(matrix, block):
    modes = matrix.shape[1]
    return pl.ds(pl.multiple_of(block * modes, modes), modes)


def one_slot(blocks, matrix, parts, mine, other):
    cells = mine.shape[1]
    for block, out in zip(blocks, (mine, other)):
        both = jnp.dot(matrix[rows_of(matrix, block), :], parts, preferred_element_type=jnp.float32)
        out[...] = both[:, :cells] + both[:, cells:]


def slot_products(blocks, column, matrix, field, mine, other):
    blocks = [for_device(numbers) for numbers in blocks]
    parts = jnp.concatenate(halves(field[:, column : column + mine.shape[1]]), axis=1)
    one_slot(blocks, matrix, parts, mine, other)


def load_and_products(blocks, column, matrix, distribution, *refs):
    slots = len(blocks) - 1
    outs, (held, field, sems) = refs[: 2 * slots], refs[2 * slots :]
    cells = field.shape[1]
    start = pltpu.make_async_copy(distribution.at[:, pl.ds(column, cells)], field, sems.at[0])
    start.start()
    blocks = [[for_device(numbers) for numbers in pair] for pair in blocks]
    copies = []
    for block in (block for pair in blocks for block in pair):
        rows = rows_of(held, block)
        copies.append(
            pltpu.make_async_copy(matrix.at[rows, :], held.at[rows, :], sems.at[1 + len(copies)])
        )
        copies[-1].start()
    start.wait()
    parts = jnp.concatenate(halves(field[...]), axis=1)
    for slot, pair in enumerate(blocks[:-1]):
        for copy in copies[2 * slot : 2 * slot + 2]:
            copy.wait()
        one_slot(pair, held, parts, outs[2 * slot], outs[2 * slot + 1])
    for copy in copies[2 * slots :]:
        copy.wait()


def two_blocks(numbers, parts, first, last, scale, rows, matrix, *refs):
    modes = matrix.shape[1]
    blocks, refs = [[refs[0]], refs[1 : 1 + parts]], refs[1 + parts :]
    if not first:
        before, refs = refs[0], refs[1:]
    if last:
        base, refs = refs[0], refs[1:]
    total = None if first else before[...]
    for k, pieces in enumerate(blocks):
        block = jnp.concatenate([piece[...] for piece in pieces], axis=0)
        pieces = list(halves(block[:modes].T))
        if rows:
            weights = [
                jnp.concatenate(
                    [
                        block[modes + i : modes + i + 1, :]
                        for i in range(d * modes // LANES, (d + 1) * modes // LANES)
                    ],
                    axis=1,
                )
                for d in range(2)
            ]
            weights.append(jnp.zeros((6, modes), jnp.float32))
            pieces += halves(jnp.concatenate(weights, axis=0))
        left = jnp.concatenate(pieces, axis=0)
        there = rows_of(matrix, for_device(numbers[k]))
        term = jnp.dot(left, matrix[there, :], preferred_element_type=jnp.float32)
        total = term if total is None else total + term
    if not last:
        refs[0][...] = total
        return
    cells = base.shape[1]
    value = base[...] - scale * (total[:cells] + total[cells : 2 * cells]).T
    refs[0][...] = value
    if rows:
        refs[1][...] = value.T[:HALO]
        refs[2][...] = total[2 * cells : 2 * cells + 8] + total[2 * cells + 8 :]


def own_rows(distribution, velocity, capacity, out, token, speeds, weight, sems):
    modes, cells = velocity.shape[1], out.shape[1]
    copies = [
        pltpu.make_async_copy(velocity, speeds, sems.at[0]),
        pltpu.make_async_copy(capacity, weight, sems.at[1]),
        pltpu.make_async_copy(
            distribution.at[:, pl.ds(0, cells)], out.at[pl.ds(0, modes), :], sems.at[2]
        ),
    ]
    for copy in copies:
        copy.start()
    token[...] = jnp.zeros_like(token)
    for copy in copies[:2]:
        copy.wait()
    per = modes // LANES
    out[modes:] = jnp.zeros((out.shape[0] - modes, LANES), jnp.float32)
    for d in range(2):
        for i in range(per):
            lanes = slice(i * LANES, (i + 1) * LANES)
            out[modes + d * per + i : modes + d * per + i + 1, :] = (
                speeds[d : d + 1, lanes] * weight[:, lanes]
            )
    copies[2].wait()


def payload(numbers, slots, arrived, *refs):
    out = refs[-1]
    slot_here = for_device(numbers)

    for k, slot in enumerate(slots):

        @pl.when(slot_here == slot)
        def _(k=k):
            terms = refs[k]
            modes = terms.shape[0]
            out[:modes] = arrived[:modes] + terms[...]
            if out.shape[0] > modes:
                out[modes:] = arrived[modes:]

    @pl.when(slot_here < 0)
    def _():
        out[...] = arrived[...]


def pick(numbers, *refs):
    out = refs[-1]
    choice = for_device(numbers)
    for k, ref in enumerate(refs[:-1]):

        @pl.when(choice == k)
        def _(ref=ref):
            out[...] = ref[...]


def add(one, *refs):
    out, first = refs[-1], 0
    for piece in refs[:-1]:
        rows = slice(first, first + piece.shape[0])
        out[rows] = one[rows] + piece[...]
        first += piece.shape[0]


def pass_on(value, out):
    out[...] = value[...]


def add_all(*refs):
    out, token = refs[-2:]
    total = refs[0][...]
    for ref in refs[1:-2]:
        total = total + ref[...]
    out[...] = total
    token[...] = jnp.zeros_like(token)


def take_off(scale, arrived, terms, base, out):
    modes = terms.shape[0]
    out[...] = base[...] - scale * (arrived[:modes] + terms[...])


def turn_sum(scale, arrived, base, out, strip):
    modes = base.shape[0]
    value = base[...] - scale * arrived[:modes]
    out[...] = value
    strip[...] = value.T[-HALO:]


def last_sum(scale, arrived, base, other, out, value, sems):
    cells = base.shape[1]
    ahead = pltpu.make_async_copy(other, out.at[:, pl.ds(cells, cells)], sems.at[0])
    ahead.start()
    value[...] = base[...] - scale * arrived[...]
    copy = pltpu.make_async_copy(value, out.at[:, pl.ds(0, cells)], sems.at[1])
    copy.start()
    ahead.wait()
    copy.wait()


def strip_rows(distribution, leading, last):
    cells = distribution.shape[1]
    leading[...] = distribution[:, :LANES].T[:HALO]
    last[...] = distribution[:, cells - LANES :].T[-HALO:]


def strip_pairs(leading, last, out_even, out_odd):
    even = lax.axis_index("space") % 2 == 0

    @pl.when(even)
    def _():
        out_even[...] = last[...]
        out_odd[...] = leading[...]

    @pl.when(jnp.logical_not(even))
    def _():
        out_even[...] = leading[...]
        out_odd[...] = last[...]


def differences(cells):
    columns = cells // NY
    own, strip = np.zeros((cells, 4 * cells)), np.zeros((2 * HALO, 4 * cells))
    for x in range(columns):
        for y in range(NY):
            cell = x * NY + y
            for way in (-1, 1):
                for far, factor in enumerate((3.0, -4.0, 1.0)):
                    at_x, at_y = x + way * far, y + way * far
                    first = cell + (0 if way < 0 else cells)
                    factor = -way * factor
                    if at_x < 0:
                        strip[(at_x + 2) * NY + y, first] = factor
                    elif at_x >= columns:
                        strip[HALO + (at_x - columns) * NY + y, first] = factor
                    else:
                        own[at_x * NY + y, first] = factor
                    if 0 <= at_y < NY:
                        own[x * NY + at_y, first + 2 * cells] = factor
    return np.concatenate([own, own, strip, strip]).astype(jnp.bfloat16)


def strip_columns(came_even, came_odd, out):
    even = lax.axis_index("space") % 2 == 0
    before = jnp.where(even, came_odd[...], came_even[...])
    after = jnp.where(even, came_even[...], came_odd[...])
    parts = halves(jnp.concatenate([before, after], axis=0))
    rows = jnp.concatenate([p.astype(jnp.float32) for p in parts], axis=0)
    out[...] = rows.T.astype(jnp.bfloat16)


def still_rate(field, strip, operators, columns, kinds):
    cells = field.shape[1]
    left = jnp.concatenate([*halves(field), strip], axis=1)
    steps = jnp.dot(left, operators[...], preferred_element_type=jnp.float32)
    vx, vy, capacity = (columns[:, i : i + 1] for i in range(3))
    speeds = (jnp.maximum(vx, 0.0), jnp.minimum(vx, 0.0))
    speeds += (jnp.maximum(vy, 0.0), jnp.minimum(vy, 0.0))
    contact = jnp.where(kinds > 0, relax_rate, 0.0)
    source = jnp.where(kinds == 1, contact, -contact)
    rate = source * capacity - contact * field
    for k, speed in enumerate(speeds):
        rate = rate - (0.5 * speed) * steps[:, k * cells : (k + 1) * cells]
    return rate


def first_rest(field, strips, operators, table, kinds, base_a, base_b):
    modes, half = base_a.shape
    block = min(modes, BLOCK)

    def step(i, _):
        rows = pl.ds(pl.multiple_of(i * block, block), block)
        value = field[rows, :]
        rate = still_rate(value, strips[rows, :], operators, table[:, rows].T, kinds[...])
        base = value + time_step * rate
        base_a[rows, :] = base[:, :half]
        base_b[rows, :] = base[:, half:]
        return 0

    lax.fori_loop(0, modes // block, step, 0)


def second_rest(
    flux_scale,
    field,
    mid_a,
    mid_b,
    strips,
    operators,
    table,
    kinds,
    scattered,
    end_a,
    end_b,
    flux,
):
    modes, half = end_a.shape
    block = min(modes, BLOCK)
    step_size = 0.5 * time_step
    flux[...] = jnp.zeros_like(flux)

    def step(i, _):
        rows = pl.ds(pl.multiple_of(i * block, block), block)
        mid = jnp.concatenate([mid_a[rows, :], mid_b[rows, :]], axis=1)
        columns = table[:, rows].T
        taken = step_size * scattered[:, rows].T
        rate = still_rate(mid, strips[rows, :], operators, columns, kinds[...])
        end = 0.5 * (field[rows, :] + mid) + step_size * rate
        end_a[rows, :] = end[:, :half]
        end_b[rows, :] = end[:, half:]
        for d in range(2):
            terms = columns[:, 3 + d : 4 + d] * end - taken[:, d : d + 1] * mid
            flux[d : d + 1, :] += flux_scale * jnp.sum(terms, axis=0, keepdims=True)
        return 0

    lax.fori_loop(0, modes // block, step, 0)


def paired(to_even, to_odd):
    count = lax.axis_size("space")
    came = []
    for first, value in enumerate((to_even, to_odd)):
        pairs = [(i, i + 1) for i in range(first, count - 1, 2)]
        came.append(lax.ppermute(value, "space", pairs + [(j, i) for i, j in pairs]))
    return came


class Plan:
    def __init__(self, chips):
        self.chips = chips
        self.devices = range(2 * chips)
        sources = [self.sources(d) for d in self.devices]
        targets = [self.targets(d // 2) for d in self.devices]
        self.blocks = [
            [
                [2 * sources[e][slot][2] + e % 2 for e in (d ^ other for d in self.devices)]
                for other in (0, 1)
            ]
            for slot in range(chips)
        ]
        self.rows = [
            [[2 * targets[d][slot] + (d % 2 ^ other) for d in self.devices] for other in (0, 1)]
            for slot in range(chips)
        ]
        self.choices = [
            sorted({sources[d][slot][:2] for d in self.devices}) for slot in range(chips)
        ]
        self.picked = [
            [self.choices[slot].index(sources[d][slot][:2]) for d in self.devices]
            for slot in range(chips)
        ]
        self.sent = {}
        for stream in (0, 1):
            for step in range(1, chips):
                numbers = []
                for d in self.devices:
                    way = self.way(d, stream)
                    place = d // 2 if way > 0 else chips - 1 - d // 2
                    target = d // 2 + way * (chips - step)
                    numbers.append(targets[d].index(target) if place < step else -1)
                self.sent[stream, step] = numbers
        self.pairs = []
        for stream in (0, 1):
            up = [
                (d, d + 2) for d in self.devices[:-2] if self.way(d, stream) > 0
            ]
            self.pairs.append(up + [(j, i) for i, j in up])

    def way(self, device, stream):
        return 1 if (device // 2 + device % 2 + stream) % 2 == 0 else -1

    def sources(self, device):
        found = [(-1, -1, device // 2)]
        for step in range(self.chips - 1):
            for stream in (step % 2, 1 - step % 2):
                chip = device // 2 + self.way(device, stream) * (step + 1)
                if 0 <= chip < self.chips:
                    found.append((stream, step, chip))
        return found

    def targets(self, chip):
        found = []
        for step in range(1, self.chips):
            far = self.chips - step
            found += [t for t in (chip + far, chip - far) if 0 <= t < self.chips]
        return found + [chip]


def on_device(distribution, scatter_matrix, velocity, capacity, cell_type):
    modes, cells = distribution.shape
    total_modes = scatter_matrix.shape[0]
    half = cells // 2
    extra = -(-2 * modes // LANES // 8) * 8
    step_size = 0.5 * time_step
    part = (modes, half)
    devices = lax.axis_size("mode")
    chips = devices // 2
    plan = Plan(chips)
    call = Chain()
    across = [(i, i ^ 1) for i in range(devices)]
    cap = capacity[None, :]
    table = jnp.concatenate(
        [velocity, cap, cap * velocity, jnp.zeros((3, modes), jnp.float32)], axis=0
    )
    kinds = cell_type[None, :]

    def exchange(value, parts=1):
        cut = value.shape[0] // parts // 8 * 8
        ends = [cut * k for k in range(parts)] + [value.shape[0]]
        return [lax.ppermute(value[i:j], "mode", across) for i, j in zip(ends, ends[1:])]

    def along(stream, value):
        return lax.ppermute(value, "mode", plan.pairs[stream])

    class Round:
        def __init__(self, matrix, scale, rows):
            self.matrix, self.scale, self.rows = matrix, scale, rows
            self.terms, self.total = [], None

        def begin(self, own):
            self.own = own
            self.arrived = [[along(0, own)], [along(1, own)]]
            self.blocks = []

        def add_terms(self, field, column=0):
            kernel = functools.partial(slot_products, plan.rows[len(self.terms)], column)
            mine, other = call(kernel, [part] * 2, [self.matrix, field])
            self.terms.append((mine, *exchange(other)))

        def join_terms(self, *slots):
            for slot in slots:
                (self.terms[slot],) = call(add, [part], self.terms[slot])

        def take_own(self, later=False):
            own = call(pass_on, [self.own.shape], [self.own])[0] if later else self.own
            self.blocks.append((self.own, *exchange(own)))

        def send(self, step, between=None):
            sent = {}
            for stream in (step % 2, 1 - step % 2):
                if between is not None and sent:
                    between()
                numbers = plan.sent[stream, step]
                slots = sorted({n for n in numbers if n >= 0})
                for slot in slots:
                    if isinstance(self.terms[slot], tuple):
                        self.join_terms(slot)
                arrived = self.arrived[1 - stream][step - 1]
                kernel = functools.partial(payload, numbers, slots)
                arrays = [arrived] + [self.terms[s] for s in slots]
                (value,) = call(kernel, [arrived.shape], arrays)
                sent[stream] = along(stream, value)
            for stream in (0, 1):
                self.arrived[stream].append(sent[stream])

        def take(self, slot, parts=1):
            arrays = [self.arrived[stream][step] for stream, step in plan.choices[slot]]
            kernel = functools.partial(pick, plan.picked[slot])
            (here,) = call(kernel, [arrays[0].shape], arrays)
            self.blocks.append((here, *exchange(here, parts)))

        def hold(self, *slots):
            for slot in slots:
                here, there = self.blocks[slot]
                (there,) = call(pass_on, [there.shape], [there])
                self.blocks[slot] = (here, there)

        def multiply(self, slot, base=None, first=None):
            first, last = slot == 0 if first is None else first, base is not None
            blocks = self.blocks[slot]
            kernel = functools.partial(
                two_blocks, plan.blocks[slot], len(blocks) - 1, first, last, self.scale, self.rows
            )
            arrays = [self.matrix, *blocks]
            arrays += [] if first else [self.total]
            arrays += [base] if last else []
            outs = [(2 * half + (16 if self.rows else 0), modes)]
            if last:
                outs = [part, (HALO, modes), (8, modes)] if self.rows else [part]
            results = call(kernel, outs, arrays)
            self.total = results[0]
            return results

        def first_end(self, base):
            kernel = functools.partial(take_off, self.scale)
            arrived = self.arrived[(chips - 1) % 2][-1]
            (self.rest,) = call(kernel, [part], [arrived, self.terms[-1], base])

        def ends(self):
            return [self.arrived[chips % 2][-1], self.rest]

    own, _ = call(
        own_rows,
        [(modes + extra, half), (8, LANES)],
        [distribution, velocity, cap],
        places=[HBM] * 3,
        scratch=[
            pltpu.VMEM((2, modes), jnp.float32),
            pltpu.VMEM((1, modes), jnp.float32),
            pltpu.SemaphoreType.DMA((3,)),
        ],
        room=56,
    )
    one = Round(None, time_step, True)
    one.begin(own)
    *terms, matrix = call(
        functools.partial(load_and_products, plan.rows, half),
        [part] * (2 * chips - 2) + [jax.ShapeDtypeStruct(scatter_matrix.shape, jnp.bfloat16)],
        [scatter_matrix, distribution],
        places=[HBM] * 2,
        scratch=[
            pltpu.VMEM(part, jnp.float32),
            pltpu.SemaphoreType.DMA((2 * chips + 1,)),
        ],
        room=28,
    )
    one.matrix = matrix
    one.terms = [(terms[2 * s], *exchange(terms[2 * s + 1])) for s in range(chips - 1)]
    one.take_own()
    operators = jnp.asarray(differences(cells))
    strips = None

    def unpack():
        nonlocal strips
        shape = jax.ShapeDtypeStruct((modes, 4 * HALO), jnp.bfloat16)
        (strips,) = call(strip_columns, [shape], strips)

    for step in range(1, chips):
        if step == 1:
            one.take(1)
        one.send(step, unpack if step == 2 else None)
        if step == 1:
            one.join_terms(*(s for s in range(chips - 1) if isinstance(one.terms[s], tuple)))
            strips = call(strip_rows, [(HALO, modes)] * 2, [distribution])
            strips = paired(*call(strip_pairs, [(HALO, modes)] * 2, strips))
        else:
            one.take(step, 2 if step == chips - 1 else 1)
        if step == 2:
            one.add_terms(distribution, half)
        if step == chips - 1:
            one.join_terms(chips - 1)
        one.multiply(step - 1)
        if step == min(2, chips - 1):
            base_a, base_b = call(
                first_rest,
                [part] * 2,
                [distribution, strips, operators, table, kinds],
            )
    mid_a, leading, scattered = one.multiply(chips - 1, base_a)

    two = Round(matrix, step_size, False)
    two.add_terms(mid_a)
    two.add_terms(mid_a)
    one.first_end(base_b)
    mid_b, last = call(
        functools.partial(turn_sum, time_step), [part, (HALO, modes)], one.ends()
    )
    two.begin(mid_b)
    two.join_terms(0, 1)
    two.take_own()
    strips = paired(*call(strip_pairs, [(HALO, modes)] * 2, [leading, last]))
    flux = None
    for step in range(1, chips):
        if step == 1:
            two.send(step, unpack)
            two.hold(0)
        elif step == 2:
            two.send(step)
            two.join_terms(*range(2, chips))
        elif step == chips - 1:
            two.send(step, lambda: flux.over(*range(2, devices, 2)))
        else:
            two.send(step)
        two.take(step, 2 if step >= chips - 2 else 1)
        if step == 1:
            for slot in range(2, chips):
                two.add_terms(mid_a)
        if 1 < step < chips - 1:
            two.hold(step - 1)
        if step == chips - 2:
            two.multiply(step, first=True)
        if step == chips - 1:
            for slot in range(chips - 2):
                two.multiply(slot, first=False)
        if step == 1:
            end_a, end_b, part_flux = call(
                functools.partial(second_rest, 1.0 / math.sqrt(total_modes)),
                [part, part, (2, cells)],
                [distribution, mid_a, mid_b, strips, operators, table, kinds, scattered],
            )
            flux = Flux(call, part_flux, devices)
    flux.over(1)
    (last_b,) = two.multiply(chips - 1, end_b)
    heat_flux = flux.value
    two.first_end(end_a)
    (updated,) = call(
        functools.partial(last_sum, step_size),
        [(modes, cells)],
        [*two.ends(), last_b],
        scratch=[pltpu.VMEM(part, jnp.float32), pltpu.SemaphoreType.DMA((2,))],
        out_specs=[HBM],
    )
    return (updated, heat_flux)


class Flux:
    def __init__(self, call, value, devices):
        self.call, self.value, self.devices = call, value, devices

    def over(self, *bits):
        came = [
            lax.ppermute(self.value, "mode", [(i, i ^ bit) for i in range(self.devices)])
            for bit in bits
        ]
        self.value, _ = self.call(add_all, [self.value.shape, (8, LANES)], [self.value, *came])


def solution(mesh):
    return jax.shard_map(
        on_device,
        mesh=mesh,
        in_specs=(P("mode", "space"), P(None, "mode"), P(None, "mode"), P("mode"), P("space")),
        out_specs=(P("mode", "space"), P(None, "space")),
        check_vma=False,
    )
```

```python
import functools
import math

import numpy as np

import jax
import jax.numpy as jnp
from jax import lax
from jax.experimental import pallas as pl
from jax.experimental.pallas import tpu as pltpu
from jax.sharding import PartitionSpec as P

NY = 16
HALO = 2 * NY
LANES = 128
BLOCK = 512


relax_rate = 0.5
time_step = 0.5

VMEM = pl.BlockSpec(memory_space=pltpu.VMEM)
ANY = pl.BlockSpec(memory_space=pl.ANY)
HBM = pl.BlockSpec(memory_space=pltpu.HBM)


class Chain:
    def __init__(self):
        self.last = None

    def __call__(self, kernel, outs, arrays, places=None, scratch=(), out_specs=None, room=16):
        extra = [] if self.last is None else [self.last]
        skip = len(extra)
        first = len(arrays)

        def body(*refs):
            kernel(*refs[:first], *refs[first + skip :])

        results = pl.pallas_call(
            body,
            out_shape=[
                jax.ShapeDtypeStruct(shape, jnp.float32) if isinstance(shape, tuple) else shape
                for shape in outs
            ],
            in_specs=list(places or [VMEM] * len(arrays)) + [ANY] * skip,
            out_specs=out_specs or [VMEM] * len(outs),
            scratch_shapes=list(scratch),
            compiler_params=pltpu.CompilerParams(vmem_limit_bytes=room * 1024 * 1024),
            cost_estimate=pl.CostEstimate(flops=1024, bytes_accessed=1024, transcendentals=0),
            name=getattr(kernel, "func", kernel).__name__,
        )(*arrays, *extra)
        self.last = results[-1]
        return results


def halves(value):
    high = value.astype(jnp.bfloat16)
    low = (value - high.astype(jnp.float32)).astype(jnp.bfloat16)
    return high, low


def for_device(numbers):
    if len(set(numbers)) == 1:
        return numbers[0]
    me = lax.axis_index("mode")
    chosen = jnp.int32(numbers[0])
    for device, number in enumerate(numbers[1:], 1):
        chosen = jnp.where(me == device, jnp.int32(number), chosen)
    return chosen


def rows_of(matrix, block):
    modes = matrix.shape[1]
    return pl.ds(pl.multiple_of(block * modes, modes), modes)


def one_slot(blocks, matrix, parts, mine, other):
    cells = mine.shape[1]
    for block, out in zip(blocks, (mine, other)):
        both = jnp.dot(matrix[rows_of(matrix, block), :], parts, preferred_element_type=jnp.float32)
        out[...] = both[:, :cells] + both[:, cells:]


def slot_products(blocks, column, matrix, field, mine, other):
    blocks = [for_device(numbers) for numbers in blocks]
    parts = jnp.concatenate(halves(field[:, column : column + mine.shape[1]]), axis=1)
    one_slot(blocks, matrix, parts, mine, other)


def load_and_products(blocks, column, matrix, distribution, *refs):
    slots = len(blocks) - 1
    outs, (held, field, sems) = refs[: 2 * slots], refs[2 * slots :]
    cells = field.shape[1]
    start = pltpu.make_async_copy(distribution.at[:, pl.ds(column, cells)], field, sems.at[0])
    start.start()
    blocks = [[for_device(numbers) for numbers in pair] for pair in blocks]
    copies = []
    for block in (block for pair in blocks for block in pair):
        rows = rows_of(held, block)
        copies.append(
            pltpu.make_async_copy(matrix.at[rows, :], held.at[rows, :], sems.at[1 + len(copies)])
        )
        copies[-1].start()
    start.wait()
    parts = jnp.concatenate(halves(field[...]), axis=1)
    for slot, pair in enumerate(blocks[:-1]):
        for copy in copies[2 * slot : 2 * slot + 2]:
            copy.wait()
        one_slot(pair, held, parts, outs[2 * slot], outs[2 * slot + 1])
    for copy in copies[2 * slots :]:
        copy.wait()


def two_blocks(numbers, parts, first, last, scale, rows, matrix, *refs):
    modes = matrix.shape[1]
    blocks, refs = [[refs[0]], refs[1 : 1 + parts]], refs[1 + parts :]
    if not first:
        before, refs = refs[0], refs[1:]
    if last:
        base, refs = refs[0], refs[1:]
    total = None if first else before[...]
    for k, pieces in enumerate(blocks):
        block = jnp.concatenate([piece[...] for piece in pieces], axis=0)
        pieces = list(halves(block[:modes].T))
        if rows:
            weights = [
                jnp.concatenate(
                    [
                        block[modes + i : modes + i + 1, :]
                        for i in range(d * modes // LANES, (d + 1) * modes // LANES)
                    ],
                    axis=1,
                )
                for d in range(2)
            ]
            weights.append(jnp.zeros((6, modes), jnp.float32))
            pieces += halves(jnp.concatenate(weights, axis=0))
        left = jnp.concatenate(pieces, axis=0)
        there = rows_of(matrix, for_device(numbers[k]))
        term = jnp.dot(left, matrix[there, :], preferred_element_type=jnp.float32)
        total = term if total is None else total + term
    if not last:
        refs[0][...] = total
        return
    cells = base.shape[1]
    value = base[...] - scale * (total[:cells] + total[cells : 2 * cells]).T
    refs[0][...] = value
    if rows:
        refs[1][...] = value.T[:HALO]
        refs[2][...] = total[2 * cells : 2 * cells + 8] + total[2 * cells + 8 :]


def own_rows(distribution, velocity, capacity, out, token, speeds, weight, sems):
    modes, cells = velocity.shape[1], out.shape[1]
    copies = [
        pltpu.make_async_copy(velocity, speeds, sems.at[0]),
        pltpu.make_async_copy(capacity, weight, sems.at[1]),
        pltpu.make_async_copy(
            distribution.at[:, pl.ds(0, cells)], out.at[pl.ds(0, modes), :], sems.at[2]
        ),
    ]
    for copy in copies:
        copy.start()
    token[...] = jnp.zeros_like(token)
    for copy in copies[:2]:
        copy.wait()
    per = modes // LANES
    out[modes:] = jnp.zeros((out.shape[0] - modes, LANES), jnp.float32)
    for d in range(2):
        for i in range(per):
            lanes = slice(i * LANES, (i + 1) * LANES)
            out[modes + d * per + i : modes + d * per + i + 1, :] = (
                speeds[d : d + 1, lanes] * weight[:, lanes]
            )
    copies[2].wait()


def payload(numbers, slots, arrived, *refs):
    out = refs[-1]
    slot_here = for_device(numbers)

    for k, slot in enumerate(slots):

        @pl.when(slot_here == slot)
        def _(k=k):
            terms = refs[k]
            modes = terms.shape[0]
            out[:modes] = arrived[:modes] + terms[...]
            if out.shape[0] > modes:
                out[modes:] = arrived[modes:]

    @pl.when(slot_here < 0)
    def _():
        out[...] = arrived[...]


def pick(numbers, *refs):
    out = refs[-1]
    choice = for_device(numbers)
    for k, ref in enumerate(refs[:-1]):

        @pl.when(choice == k)
        def _(ref=ref):
            out[...] = ref[...]


def add(one, *refs):
    out, first = refs[-1], 0
    for piece in refs[:-1]:
        rows = slice(first, first + piece.shape[0])
        out[rows] = one[rows] + piece[...]
        first += piece.shape[0]


def pass_on(value, out):
    out[...] = value[...]


def add_all(*refs):
    out, token = refs[-2:]
    total = refs[0][...]
    for ref in refs[1:-2]:
        total = total + ref[...]
    out[...] = total
    token[...] = jnp.zeros_like(token)


def take_off(scale, arrived, terms, base, out):
    modes = terms.shape[0]
    out[...] = base[...] - scale * (arrived[:modes] + terms[...])


def turn_sum(scale, arrived, base, out, strip):
    modes = base.shape[0]
    value = base[...] - scale * arrived[:modes]
    out[...] = value
    strip[...] = value.T[-HALO:]


def last_sum(scale, arrived, base, other, out, value, sems):
    cells = base.shape[1]
    ahead = pltpu.make_async_copy(other, out.at[:, pl.ds(cells, cells)], sems.at[0])
    ahead.start()
    value[...] = base[...] - scale * arrived[...]
    copy = pltpu.make_async_copy(value, out.at[:, pl.ds(0, cells)], sems.at[1])
    copy.start()
    ahead.wait()
    copy.wait()


def strip_rows(distribution, leading, last):
    cells = distribution.shape[1]
    leading[...] = distribution[:, :LANES].T[:HALO]
    last[...] = distribution[:, cells - LANES :].T[-HALO:]


def strip_pairs(leading, last, out_even, out_odd):
    even = lax.axis_index("space") % 2 == 0

    @pl.when(even)
    def _():
        out_even[...] = last[...]
        out_odd[...] = leading[...]

    @pl.when(jnp.logical_not(even))
    def _():
        out_even[...] = leading[...]
        out_odd[...] = last[...]


def differences(cells):
    columns = cells // NY
    own, strip = np.zeros((cells, 4 * cells)), np.zeros((2 * HALO, 4 * cells))
    for x in range(columns):
        for y in range(NY):
            cell = x * NY + y
            for way in (-1, 1):
                for far, factor in enumerate((3.0, -4.0, 1.0)):
                    at_x, at_y = x + way * far, y + way * far
                    first = cell + (0 if way < 0 else cells)
                    factor = -way * factor
                    if at_x < 0:
                        strip[(at_x + 2) * NY + y, first] = factor
                    elif at_x >= columns:
                        strip[HALO + (at_x - columns) * NY + y, first] = factor
                    else:
                        own[at_x * NY + y, first] = factor
                    if 0 <= at_y < NY:
                        own[x * NY + at_y, first + 2 * cells] = factor
    return np.concatenate([own, own, strip, strip]).astype(jnp.bfloat16)


def strip_columns(came_even, came_odd, out):
    even = lax.axis_index("space") % 2 == 0
    before = jnp.where(even, came_odd[...], came_even[...])
    after = jnp.where(even, came_even[...], came_odd[...])
    parts = halves(jnp.concatenate([before, after], axis=0))
    rows = jnp.concatenate([p.astype(jnp.float32) for p in parts], axis=0)
    out[...] = rows.T.astype(jnp.bfloat16)


def still_rate(field, strip, operators, columns, kinds):
    cells = field.shape[1]
    left = jnp.concatenate([*halves(field), strip], axis=1)
    steps = jnp.dot(left, operators[...], preferred_element_type=jnp.float32)
    vx, vy, capacity = (columns[:, i : i + 1] for i in range(3))
    speeds = (jnp.maximum(vx, 0.0), jnp.minimum(vx, 0.0))
    speeds += (jnp.maximum(vy, 0.0), jnp.minimum(vy, 0.0))
    contact = jnp.where(kinds > 0, relax_rate, 0.0)
    source = jnp.where(kinds == 1, contact, -contact)
    rate = source * capacity - contact * field
    for k, speed in enumerate(speeds):
        rate = rate - (0.5 * speed) * steps[:, k * cells : (k + 1) * cells]
    return rate


def first_rest(field, strips, operators, table, kinds, base_a, base_b):
    modes, half = base_a.shape
    block = min(modes, BLOCK)

    def step(i, _):
        rows = pl.ds(pl.multiple_of(i * block, block), block)
        value = field[rows, :]
        rate = still_rate(value, strips[rows, :], operators, table[:, rows].T, kinds[...])
        base = value + time_step * rate
        base_a[rows, :] = base[:, :half]
        base_b[rows, :] = base[:, half:]
        return 0

    lax.fori_loop(0, modes // block, step, 0)


def second_rest(
    flux_scale,
    field,
    mid_a,
    mid_b,
    strips,
    operators,
    table,
    kinds,
    scattered,
    end_a,
    end_b,
    flux,
):
    modes, half = end_a.shape
    block = min(modes, BLOCK)
    step_size = 0.5 * time_step
    flux[...] = jnp.zeros_like(flux)

    def step(i, _):
        rows = pl.ds(pl.multiple_of(i * block, block), block)
        mid = jnp.concatenate([mid_a[rows, :], mid_b[rows, :]], axis=1)
        columns = table[:, rows].T
        taken = step_size * scattered[:, rows].T
        rate = still_rate(mid, strips[rows, :], operators, columns, kinds[...])
        end = 0.5 * (field[rows, :] + mid) + step_size * rate
        end_a[rows, :] = end[:, :half]
        end_b[rows, :] = end[:, half:]
        for d in range(2):
            terms = columns[:, 3 + d : 4 + d] * end - taken[:, d : d + 1] * mid
            flux[d : d + 1, :] += flux_scale * jnp.sum(terms, axis=0, keepdims=True)
        return 0

    lax.fori_loop(0, modes // block, step, 0)


def paired(to_even, to_odd):
    count = lax.axis_size("space")
    came = []
    for first, value in enumerate((to_even, to_odd)):
        pairs = [(i, i + 1) for i in range(first, count - 1, 2)]
        came.append(lax.ppermute(value, "space", pairs + [(j, i) for i, j in pairs]))
    return came


class Plan:
    def __init__(self, chips):
        self.chips = chips
        self.devices = range(2 * chips)
        sources = [self.sources(d) for d in self.devices]
        targets = [self.targets(d // 2) for d in self.devices]
        self.blocks = [
            [
                [2 * sources[e][slot][2] + e % 2 for e in (d ^ other for d in self.devices)]
                for other in (0, 1)
            ]
            for slot in range(chips)
        ]
        self.rows = [
            [[2 * targets[d][slot] + (d % 2 ^ other) for d in self.devices] for other in (0, 1)]
            for slot in range(chips)
        ]
        self.choices = [
            sorted({sources[d][slot][:2] for d in self.devices}) for slot in range(chips)
        ]
        self.picked = [
            [self.choices[slot].index(sources[d][slot][:2]) for d in self.devices]
            for slot in range(chips)
        ]
        self.sent = {}
        for stream in (0, 1):
            for step in range(1, chips):
                numbers = []
                for d in self.devices:
                    way = self.way(d, stream)
                    place = d // 2 if way > 0 else chips - 1 - d // 2
                    target = d // 2 + way * (chips - step)
                    numbers.append(targets[d].index(target) if place < step else -1)
                self.sent[stream, step] = numbers
        self.pairs = []
        for stream in (0, 1):
            up = [
                (d, d + 2) for d in self.devices[:-2] if self.way(d, stream) > 0
            ]
            self.pairs.append(up + [(j, i) for i, j in up])

    def way(self, device, stream):
        return 1 if (device // 2 + device % 2 + stream) % 2 == 0 else -1

    def sources(self, device):
        found = [(-1, -1, device // 2)]
        for step in range(self.chips - 1):
            for stream in (step % 2, 1 - step % 2):
                chip = device // 2 + self.way(device, stream) * (step + 1)
                if 0 <= chip < self.chips:
                    found.append((stream, step, chip))
        return found

    def targets(self, chip):
        found = []
        for step in range(1, self.chips):
            far = self.chips - step
            found += [t for t in (chip + far, chip - far) if 0 <= t < self.chips]
        return found + [chip]


def on_device(distribution, scatter_matrix, velocity, capacity, cell_type):
    modes, cells = distribution.shape
    total_modes = scatter_matrix.shape[0]
    half = cells // 2
    extra = -(-2 * modes // LANES // 8) * 8
    step_size = 0.5 * time_step
    part = (modes, half)
    devices = lax.axis_size("mode")
    chips = devices // 2
    plan = Plan(chips)
    call = Chain()
    across = [(i, i ^ 1) for i in range(devices)]
    cap = capacity[None, :]
    table = jnp.concatenate(
        [velocity, cap, cap * velocity, jnp.zeros((3, modes), jnp.float32)], axis=0
    )
    kinds = cell_type[None, :]

    def exchange(value, parts=1):
        cut = value.shape[0] // parts // 8 * 8
        ends = [cut * k for k in range(parts)] + [value.shape[0]]
        return [lax.ppermute(value[i:j], "mode", across) for i, j in zip(ends, ends[1:])]

    def along(stream, value):
        return lax.ppermute(value, "mode", plan.pairs[stream])

    class Round:
        def __init__(self, matrix, scale, rows):
            self.matrix, self.scale, self.rows = matrix, scale, rows
            self.terms, self.total = [], None

        def begin(self, own):
            self.own = own
            self.arrived = [[along(0, own)], [along(1, own)]]
            self.blocks = []

        def add_terms(self, field, column=0):
            kernel = functools.partial(slot_products, plan.rows[len(self.terms)], column)
            mine, other = call(kernel, [part] * 2, [self.matrix, field])
            self.terms.append((mine, *exchange(other)))

        def join_terms(self, *slots):
            for slot in slots:
                (self.terms[slot],) = call(add, [part], self.terms[slot])

        def take_own(self, later=False):
            own = call(pass_on, [self.own.shape], [self.own])[0] if later else self.own
            self.blocks.append((self.own, *exchange(own)))

        def send(self, step, between=None):
            sent = {}
            for stream in (step % 2, 1 - step % 2):
                if between is not None and sent:
                    between()
                numbers = plan.sent[stream, step]
                slots = sorted({n for n in numbers if n >= 0})
                for slot in slots:
                    if isinstance(self.terms[slot], tuple):
                        self.join_terms(slot)
                arrived = self.arrived[1 - stream][step - 1]
                kernel = functools.partial(payload, numbers, slots)
                arrays = [arrived] + [self.terms[s] for s in slots]
                (value,) = call(kernel, [arrived.shape], arrays)
                sent[stream] = along(stream, value)
            for stream in (0, 1):
                self.arrived[stream].append(sent[stream])

        def take(self, slot, parts=1):
            arrays = [self.arrived[stream][step] for stream, step in plan.choices[slot]]
            kernel = functools.partial(pick, plan.picked[slot])
            (here,) = call(kernel, [arrays[0].shape], arrays)
            self.blocks.append((here, *exchange(here, parts)))

        def hold(self, *slots):
            for slot in slots:
                here, there = self.blocks[slot]
                (there,) = call(pass_on, [there.shape], [there])
                self.blocks[slot] = (here, there)

        def multiply(self, slot, base=None, first=None):
            first, last = slot == 0 if first is None else first, base is not None
            blocks = self.blocks[slot]
            kernel = functools.partial(
                two_blocks, plan.blocks[slot], len(blocks) - 1, first, last, self.scale, self.rows
            )
            arrays = [self.matrix, *blocks]
            arrays += [] if first else [self.total]
            arrays += [base] if last else []
            outs = [(2 * half + (16 if self.rows else 0), modes)]
            if last:
                outs = [part, (HALO, modes), (8, modes)] if self.rows else [part]
            results = call(kernel, outs, arrays)
            self.total = results[0]
            return results

        def first_end(self, base):
            kernel = functools.partial(take_off, self.scale)
            arrived = self.arrived[(chips - 1) % 2][-1]
            (self.rest,) = call(kernel, [part], [arrived, self.terms[-1], base])

        def ends(self):
            return [self.arrived[chips % 2][-1], self.rest]

    own, _ = call(
        own_rows,
        [(modes + extra, half), (8, LANES)],
        [distribution, velocity, cap],
        places=[HBM] * 3,
        scratch=[
            pltpu.VMEM((2, modes), jnp.float32),
            pltpu.VMEM((1, modes), jnp.float32),
            pltpu.SemaphoreType.DMA((3,)),
        ],
        room=56,
    )
    one = Round(None, time_step, True)
    one.begin(own)
    *terms, matrix = call(
        functools.partial(load_and_products, plan.rows, half),
        [part] * (2 * chips - 2) + [jax.ShapeDtypeStruct(scatter_matrix.shape, jnp.bfloat16)],
        [scatter_matrix, distribution],
        places=[HBM] * 2,
        scratch=[
            pltpu.VMEM(part, jnp.float32),
            pltpu.SemaphoreType.DMA((2 * chips + 1,)),
        ],
        room=28,
    )
    one.matrix = matrix
    one.terms = [
        (terms[2 * s], *exchange(terms[2 * s + 1], 1 if s == 0 else 1)) for s in range(chips - 1)
    ]
    one.take_own()
    operators = jnp.asarray(differences(cells))
    strips = None

    def unpack():
        nonlocal strips
        shape = jax.ShapeDtypeStruct((modes, 4 * HALO), jnp.bfloat16)
        (strips,) = call(strip_columns, [shape], strips)

    for step in range(1, chips):
        one.send(step, unpack if step == 2 else None)
        if step == 1:
            one.take(1)
            one.join_terms(*(s for s in range(chips - 1) if isinstance(one.terms[s], tuple)))
            strips = call(strip_rows, [(HALO, modes)] * 2, [distribution])
            strips = paired(*call(strip_pairs, [(HALO, modes)] * 2, strips))
        else:
            one.take(step, 2 if step == chips - 1 else 1)
        if step == 2:
            one.add_terms(distribution, half)
        if step == chips - 1:
            one.join_terms(chips - 1)
        one.multiply(step - 1)
        if step == min(2, chips - 1):
            base_a, base_b = call(
                first_rest,
                [part] * 2,
                [distribution, strips, operators, table, kinds],
            )
    mid_a, leading, scattered = one.multiply(chips - 1, base_a)

    two = Round(matrix, step_size, False)
    two.add_terms(mid_a)
    two.add_terms(mid_a)
    one.first_end(base_b)
    mid_b, last = call(
        functools.partial(turn_sum, time_step), [part, (HALO, modes)], one.ends()
    )
    two.begin(mid_b)
    two.join_terms(0, 1)
    two.take_own()
    strips = paired(*call(strip_pairs, [(HALO, modes)] * 2, [leading, last]))
    flux = None
    for step in range(1, chips):
        if step == 1:
            two.send(step, unpack)
            two.hold(0)
        elif step == 2:
            two.send(step)
            two.join_terms(*range(2, chips))
        elif step == chips - 1:
            two.send(step, lambda: flux.over(*range(2, devices, 2)))
        else:
            two.send(step)
        two.take(step, 2 if step >= chips - 2 else 1)
        if step == 1:
            for slot in range(2, chips):
                two.add_terms(mid_a)
        if 1 < step < chips - 1:
            two.hold(step - 1)
        if step == chips - 2:
            two.multiply(step, first=True)
        if step == chips - 1:
            for slot in range(chips - 2):
                two.multiply(slot, first=False)
        if step == 1:
            end_a, end_b, part_flux = call(
                functools.partial(second_rest, 1.0 / math.sqrt(total_modes)),
                [part, part, (2, cells)],
                [distribution, mid_a, mid_b, strips, operators, table, kinds, scattered],
            )
            flux = Flux(call, part_flux, devices)
    flux.over(1)
    (last_b,) = two.multiply(chips - 1, end_b)
    heat_flux = flux.value
    two.first_end(end_a)
    (updated,) = call(
        functools.partial(last_sum, step_size),
        [(modes, cells)],
        [*two.ends(), last_b],
        scratch=[pltpu.VMEM(part, jnp.float32), pltpu.SemaphoreType.DMA((2,))],
        out_specs=[HBM],
    )
    return (updated, heat_flux)


class Flux:
    def __init__(self, call, value, devices):
        self.call, self.value, self.devices = call, value, devices

    def over(self, *bits):
        came = [
            lax.ppermute(self.value, "mode", [(i, i ^ bit) for i in range(self.devices)])
            for bit in bits
        ]
        self.value, _ = self.call(add_all, [self.value.shape, (8, LANES)], [self.value, *came])


def solution(mesh):
    return jax.shard_map(
        on_device,
        mesh=mesh,
        in_specs=(P("mode", "space"), P(None, "mode"), P(None, "mode"), P("mode"), P("space")),
        out_specs=(P("mode", "space"), P(None, "space")),
        check_vma=False,
    )
```

```python
import functools
import math

import numpy as np

import jax
import jax.numpy as jnp
from jax import lax
from jax.experimental import pallas as pl
from jax.experimental.pallas import tpu as pltpu
from jax.sharding import PartitionSpec as P

NY = 16
HALO = 2 * NY
LANES = 128
BLOCK = 512


relax_rate = 0.5
time_step = 0.5

VMEM = pl.BlockSpec(memory_space=pltpu.VMEM)
ANY = pl.BlockSpec(memory_space=pl.ANY)
HBM = pl.BlockSpec(memory_space=pltpu.HBM)


class Chain:
    def __init__(self):
        self.last = None

    def __call__(self, kernel, outs, arrays, places=None, scratch=(), out_specs=None, room=16):
        extra = [] if self.last is None else [self.last]
        skip = len(extra)
        first = len(arrays)

        def body(*refs):
            kernel(*refs[:first], *refs[first + skip :])

        results = pl.pallas_call(
            body,
            out_shape=[
                jax.ShapeDtypeStruct(shape, jnp.float32) if isinstance(shape, tuple) else shape
                for shape in outs
            ],
            in_specs=list(places or [VMEM] * len(arrays)) + [ANY] * skip,
            out_specs=out_specs or [VMEM] * len(outs),
            scratch_shapes=list(scratch),
            compiler_params=pltpu.CompilerParams(vmem_limit_bytes=room * 1024 * 1024),
            cost_estimate=pl.CostEstimate(flops=1024, bytes_accessed=1024, transcendentals=0),
            name=getattr(kernel, "func", kernel).__name__,
        )(*arrays, *extra)
        self.last = results[-1]
        return results


def halves(value):
    high = value.astype(jnp.bfloat16)
    low = (value - high.astype(jnp.float32)).astype(jnp.bfloat16)
    return high, low


def for_device(numbers):
    if len(set(numbers)) == 1:
        return numbers[0]
    me = lax.axis_index("mode")
    chosen = jnp.int32(numbers[0])
    for device, number in enumerate(numbers[1:], 1):
        chosen = jnp.where(me == device, jnp.int32(number), chosen)
    return chosen


def rows_of(matrix, block):
    modes = matrix.shape[1]
    return pl.ds(pl.multiple_of(block * modes, modes), modes)


def one_slot(blocks, matrix, parts, mine, other):
    cells = mine.shape[1]
    for block, out in zip(blocks, (mine, other)):
        both = jnp.dot(matrix[rows_of(matrix, block), :], parts, preferred_element_type=jnp.float32)
        out[...] = both[:, :cells] + both[:, cells:]


def slot_products(blocks, column, matrix, field, mine, other):
    blocks = [for_device(numbers) for numbers in blocks]
    parts = jnp.concatenate(halves(field[:, column : column + mine.shape[1]]), axis=1)
    one_slot(blocks, matrix, parts, mine, other)


def load_and_products(blocks, column, matrix, distribution, *refs):
    slots = len(blocks) - 1
    outs, (held, field, sems) = refs[: 2 * slots], refs[2 * slots :]
    cells = field.shape[1]
    start = pltpu.make_async_copy(distribution.at[:, pl.ds(column, cells)], field, sems.at[0])
    start.start()
    blocks = [[for_device(numbers) for numbers in pair] for pair in blocks]
    copies = []
    for block in (block for pair in blocks for block in pair):
        rows = rows_of(held, block)
        copies.append(
            pltpu.make_async_copy(matrix.at[rows, :], held.at[rows, :], sems.at[1 + len(copies)])
        )
        copies[-1].start()
    start.wait()
    parts = jnp.concatenate(halves(field[...]), axis=1)
    for slot, pair in enumerate(blocks[:-1]):
        for copy in copies[2 * slot : 2 * slot + 2]:
            copy.wait()
        one_slot(pair, held, parts, outs[2 * slot], outs[2 * slot + 1])
    for copy in copies[2 * slots :]:
        copy.wait()


def two_blocks(numbers, parts, first, last, scale, rows, matrix, *refs):
    modes = matrix.shape[1]
    blocks, refs = [[refs[0]], refs[1 : 1 + parts]], refs[1 + parts :]
    if not first:
        before, refs = refs[0], refs[1:]
    if last:
        base, refs = refs[0], refs[1:]
    total = None if first else before[...]
    for k, pieces in enumerate(blocks):
        block = jnp.concatenate([piece[...] for piece in pieces], axis=0)
        pieces = list(halves(block[:modes].T))
        if rows:
            weights = [
                jnp.concatenate(
                    [
                        block[modes + i : modes + i + 1, :]
                        for i in range(d * modes // LANES, (d + 1) * modes // LANES)
                    ],
                    axis=1,
                )
                for d in range(2)
            ]
            weights.append(jnp.zeros((6, modes), jnp.float32))
            pieces += halves(jnp.concatenate(weights, axis=0))
        left = jnp.concatenate(pieces, axis=0)
        there = rows_of(matrix, for_device(numbers[k]))
        term = jnp.dot(left, matrix[there, :], preferred_element_type=jnp.float32)
        total = term if total is None else total + term
    if not last:
        refs[0][...] = total
        return
    cells = base.shape[1]
    value = base[...] - scale * (total[:cells] + total[cells : 2 * cells]).T
    refs[0][...] = value
    if rows:
        refs[1][...] = value.T[:HALO]
        refs[2][...] = total[2 * cells : 2 * cells + 8] + total[2 * cells + 8 :]


def own_rows(distribution, velocity, capacity, out, token, speeds, weight, sems):
    modes, cells = velocity.shape[1], out.shape[1]
    copies = [
        pltpu.make_async_copy(velocity, speeds, sems.at[0]),
        pltpu.make_async_copy(capacity, weight, sems.at[1]),
        pltpu.make_async_copy(
            distribution.at[:, pl.ds(0, cells)], out.at[pl.ds(0, modes), :], sems.at[2]
        ),
    ]
    for copy in copies:
        copy.start()
    token[...] = jnp.zeros_like(token)
    for copy in copies[:2]:
        copy.wait()
    per = modes // LANES
    out[modes:] = jnp.zeros((out.shape[0] - modes, LANES), jnp.float32)
    for d in range(2):
        for i in range(per):
            lanes = slice(i * LANES, (i + 1) * LANES)
            out[modes + d * per + i : modes + d * per + i + 1, :] = (
                speeds[d : d + 1, lanes] * weight[:, lanes]
            )
    copies[2].wait()


def payload(numbers, slots, arrived, *refs):
    out = refs[-1]
    slot_here = for_device(numbers)

    for k, slot in enumerate(slots):

        @pl.when(slot_here == slot)
        def _(k=k):
            terms = refs[k]
            modes = terms.shape[0]
            out[:modes] = arrived[:modes] + terms[...]
            if out.shape[0] > modes:
                out[modes:] = arrived[modes:]

    @pl.when(slot_here < 0)
    def _():
        out[...] = arrived[...]


def pick(numbers, *refs):
    out = refs[-1]
    choice = for_device(numbers)
    for k, ref in enumerate(refs[:-1]):

        @pl.when(choice == k)
        def _(ref=ref):
            out[...] = ref[...]


def add(one, *refs):
    out, first = refs[-1], 0
    for piece in refs[:-1]:
        rows = slice(first, first + piece.shape[0])
        out[rows] = one[rows] + piece[...]
        first += piece.shape[0]


def pass_on(value, out):
    out[...] = value[...]


def add_all(*refs):
    out, token = refs[-2:]
    total = refs[0][...]
    for ref in refs[1:-2]:
        total = total + ref[...]
    out[...] = total
    token[...] = jnp.zeros_like(token)


def take_off(scale, arrived, terms, base, out):
    modes = terms.shape[0]
    out[...] = base[...] - scale * (arrived[:modes] + terms[...])


def turn_sum(scale, arrived, base, out, strip):
    modes = base.shape[0]
    value = base[...] - scale * arrived[:modes]
    out[...] = value
    strip[...] = value.T[-HALO:]


def last_sum(scale, arrived, base, other, out, value, sems):
    cells = base.shape[1]
    ahead = pltpu.make_async_copy(other, out.at[:, pl.ds(cells, cells)], sems.at[0])
    ahead.start()
    value[...] = base[...] - scale * arrived[...]
    copy = pltpu.make_async_copy(value, out.at[:, pl.ds(0, cells)], sems.at[1])
    copy.start()
    ahead.wait()
    copy.wait()


def strip_rows(distribution, leading, last):
    cells = distribution.shape[1]
    leading[...] = distribution[:, :LANES].T[:HALO]
    last[...] = distribution[:, cells - LANES :].T[-HALO:]


def strip_pairs(leading, last, out_even, out_odd):
    even = lax.axis_index("space") % 2 == 0

    @pl.when(even)
    def _():
        out_even[...] = last[...]
        out_odd[...] = leading[...]

    @pl.when(jnp.logical_not(even))
    def _():
        out_even[...] = leading[...]
        out_odd[...] = last[...]


def differences(cells):
    columns = cells // NY
    own, strip = np.zeros((cells, 4 * cells)), np.zeros((2 * HALO, 4 * cells))
    for x in range(columns):
        for y in range(NY):
            cell = x * NY + y
            for way in (-1, 1):
                for far, factor in enumerate((3.0, -4.0, 1.0)):
                    at_x, at_y = x + way * far, y + way * far
                    first = cell + (0 if way < 0 else cells)
                    factor = -way * factor
                    if at_x < 0:
                        strip[(at_x + 2) * NY + y, first] = factor
                    elif at_x >= columns:
                        strip[HALO + (at_x - columns) * NY + y, first] = factor
                    else:
                        own[at_x * NY + y, first] = factor
                    if 0 <= at_y < NY:
                        own[x * NY + at_y, first + 2 * cells] = factor
    return np.concatenate([own, own, strip, strip]).astype(jnp.bfloat16)


def strip_columns(came_even, came_odd, out):
    even = lax.axis_index("space") % 2 == 0
    before = jnp.where(even, came_odd[...], came_even[...])
    after = jnp.where(even, came_even[...], came_odd[...])
    parts = halves(jnp.concatenate([before, after], axis=0))
    rows = jnp.concatenate([p.astype(jnp.float32) for p in parts], axis=0)
    out[...] = rows.T.astype(jnp.bfloat16)


def still_rate(field, strip, operators, columns, kinds):
    cells = field.shape[1]
    left = jnp.concatenate([*halves(field), strip], axis=1)
    steps = jnp.dot(left, operators[...], preferred_element_type=jnp.float32)
    vx, vy, capacity = (columns[:, i : i + 1] for i in range(3))
    speeds = (jnp.maximum(vx, 0.0), jnp.minimum(vx, 0.0))
    speeds += (jnp.maximum(vy, 0.0), jnp.minimum(vy, 0.0))
    contact = jnp.where(kinds > 0, relax_rate, 0.0)
    source = jnp.where(kinds == 1, contact, -contact)
    rate = source * capacity - contact * field
    for k, speed in enumerate(speeds):
        rate = rate - (0.5 * speed) * steps[:, k * cells : (k + 1) * cells]
    return rate


def first_rest(field, strips, operators, table, kinds, base_a, base_b):
    modes, half = base_a.shape
    block = min(modes, BLOCK)

    def step(i, _):
        rows = pl.ds(pl.multiple_of(i * block, block), block)
        value = field[rows, :]
        rate = still_rate(value, strips[rows, :], operators, table[:, rows].T, kinds[...])
        base = value + time_step * rate
        base_a[rows, :] = base[:, :half]
        base_b[rows, :] = base[:, half:]
        return 0

    lax.fori_loop(0, modes // block, step, 0)


def second_rest(
    flux_scale,
    field,
    mid_a,
    mid_b,
    strips,
    operators,
    table,
    kinds,
    scattered,
    end_a,
    end_b,
    flux,
):
    modes, half = end_a.shape
    block = min(modes, BLOCK)
    step_size = 0.5 * time_step
    flux[...] = jnp.zeros_like(flux)

    def step(i, _):
        rows = pl.ds(pl.multiple_of(i * block, block), block)
        mid = jnp.concatenate([mid_a[rows, :], mid_b[rows, :]], axis=1)
        columns = table[:, rows].T
        taken = step_size * scattered[:, rows].T
        rate = still_rate(mid, strips[rows, :], operators, columns, kinds[...])
        end = 0.5 * (field[rows, :] + mid) + step_size * rate
        end_a[rows, :] = end[:, :half]
        end_b[rows, :] = end[:, half:]
        for d in range(2):
            terms = columns[:, 3 + d : 4 + d] * end - taken[:, d : d + 1] * mid
            flux[d : d + 1, :] += flux_scale * jnp.sum(terms, axis=0, keepdims=True)
        return 0

    lax.fori_loop(0, modes // block, step, 0)


def paired(to_even, to_odd):
    count = lax.axis_size("space")
    came = []
    for first, value in enumerate((to_even, to_odd)):
        pairs = [(i, i + 1) for i in range(first, count - 1, 2)]
        came.append(lax.ppermute(value, "space", pairs + [(j, i) for i, j in pairs]))
    return came


class Plan:
    def __init__(self, chips):
        self.chips = chips
        self.devices = range(2 * chips)
        sources = [self.sources(d) for d in self.devices]
        targets = [self.targets(d // 2) for d in self.devices]
        self.blocks = [
            [
                [2 * sources[e][slot][2] + e % 2 for e in (d ^ other for d in self.devices)]
                for other in (0, 1)
            ]
            for slot in range(chips)
        ]
        self.rows = [
            [[2 * targets[d][slot] + (d % 2 ^ other) for d in self.devices] for other in (0, 1)]
            for slot in range(chips)
        ]
        self.choices = [
            sorted({sources[d][slot][:2] for d in self.devices}) for slot in range(chips)
        ]
        self.picked = [
            [self.choices[slot].index(sources[d][slot][:2]) for d in self.devices]
            for slot in range(chips)
        ]
        self.sent = {}
        for stream in (0, 1):
            for step in range(1, chips):
                numbers = []
                for d in self.devices:
                    way = self.way(d, stream)
                    place = d // 2 if way > 0 else chips - 1 - d // 2
                    target = d // 2 + way * (chips - step)
                    numbers.append(targets[d].index(target) if place < step else -1)
                self.sent[stream, step] = numbers
        self.pairs = []
        for stream in (0, 1):
            up = [
                (d, d + 2) for d in self.devices[:-2] if self.way(d, stream) > 0
            ]
            self.pairs.append(up + [(j, i) for i, j in up])

    def way(self, device, stream):
        return 1 if (device // 2 + device % 2 + stream) % 2 == 0 else -1

    def sources(self, device):
        found = [(-1, -1, device // 2)]
        for step in range(self.chips - 1):
            for stream in (step % 2, 1 - step % 2):
                chip = device // 2 + self.way(device, stream) * (step + 1)
                if 0 <= chip < self.chips:
                    found.append((stream, step, chip))
        return found

    def targets(self, chip):
        found = []
        for step in range(1, self.chips):
            far = self.chips - step
            found += [t for t in (chip + far, chip - far) if 0 <= t < self.chips]
        return found + [chip]


def on_device(distribution, scatter_matrix, velocity, capacity, cell_type):
    modes, cells = distribution.shape
    total_modes = scatter_matrix.shape[0]
    half = cells // 2
    extra = -(-2 * modes // LANES // 8) * 8
    step_size = 0.5 * time_step
    part = (modes, half)
    devices = lax.axis_size("mode")
    chips = devices // 2
    plan = Plan(chips)
    call = Chain()
    across = [(i, i ^ 1) for i in range(devices)]
    cap = capacity[None, :]
    table = jnp.concatenate(
        [velocity, cap, cap * velocity, jnp.zeros((3, modes), jnp.float32)], axis=0
    )
    kinds = cell_type[None, :]

    def exchange(value, parts=1):
        cut = value.shape[0] // parts // 8 * 8
        ends = [cut * k for k in range(parts)] + [value.shape[0]]
        return [lax.ppermute(value[i:j], "mode", across) for i, j in zip(ends, ends[1:])]

    def along(stream, value):
        return lax.ppermute(value, "mode", plan.pairs[stream])

    class Round:
        def __init__(self, matrix, scale, rows):
            self.matrix, self.scale, self.rows = matrix, scale, rows
            self.terms, self.total = [], None

        def begin(self, own):
            self.own = own
            self.arrived = [[along(0, own)], [along(1, own)]]
            self.blocks = []

        def add_terms(self, field, column=0):
            kernel = functools.partial(slot_products, plan.rows[len(self.terms)], column)
            mine, other = call(kernel, [part] * 2, [self.matrix, field])
            self.terms.append((mine, *exchange(other)))

        def join_terms(self, *slots):
            for slot in slots:
                (self.terms[slot],) = call(add, [part], self.terms[slot])

        def take_own(self, later=False):
            own = call(pass_on, [self.own.shape], [self.own])[0] if later else self.own
            self.blocks.append((self.own, *exchange(own)))

        def send(self, step, between=None):
            sent = {}
            for stream in (step % 2, 1 - step % 2):
                if between is not None and sent:
                    between()
                numbers = plan.sent[stream, step]
                slots = sorted({n for n in numbers if n >= 0})
                for slot in slots:
                    if isinstance(self.terms[slot], tuple):
                        self.join_terms(slot)
                arrived = self.arrived[1 - stream][step - 1]
                kernel = functools.partial(payload, numbers, slots)
                arrays = [arrived] + [self.terms[s] for s in slots]
                (value,) = call(kernel, [arrived.shape], arrays)
                sent[stream] = along(stream, value)
            for stream in (0, 1):
                self.arrived[stream].append(sent[stream])

        def take(self, slot, parts=1):
            arrays = [self.arrived[stream][step] for stream, step in plan.choices[slot]]
            kernel = functools.partial(pick, plan.picked[slot])
            (here,) = call(kernel, [arrays[0].shape], arrays)
            self.blocks.append((here, *exchange(here, parts)))

        def hold(self, *slots):
            for slot in slots:
                here, there = self.blocks[slot]
                (there,) = call(pass_on, [there.shape], [there])
                self.blocks[slot] = (here, there)

        def multiply(self, slot, base=None, first=None):
            first, last = slot == 0 if first is None else first, base is not None
            blocks = self.blocks[slot]
            kernel = functools.partial(
                two_blocks, plan.blocks[slot], len(blocks) - 1, first, last, self.scale, self.rows
            )
            arrays = [self.matrix, *blocks]
            arrays += [] if first else [self.total]
            arrays += [base] if last else []
            outs = [(2 * half + (16 if self.rows else 0), modes)]
            if last:
                outs = [part, (HALO, modes), (8, modes)] if self.rows else [part]
            results = call(kernel, outs, arrays)
            self.total = results[0]
            return results

        def first_end(self, base):
            kernel = functools.partial(take_off, self.scale)
            arrived = self.arrived[(chips - 1) % 2][-1]
            (self.rest,) = call(kernel, [part], [arrived, self.terms[-1], base])

        def ends(self):
            return [self.arrived[chips % 2][-1], self.rest]

    own, _ = call(
        own_rows,
        [(modes + extra, half), (8, LANES)],
        [distribution, velocity, cap],
        places=[HBM] * 3,
        scratch=[
            pltpu.VMEM((2, modes), jnp.float32),
            pltpu.VMEM((1, modes), jnp.float32),
            pltpu.SemaphoreType.DMA((3,)),
        ],
        room=56,
    )
    one = Round(None, time_step, True)
    one.begin(own)
    *terms, matrix = call(
        functools.partial(load_and_products, plan.rows, half),
        [part] * (2 * chips - 2) + [jax.ShapeDtypeStruct(scatter_matrix.shape, jnp.bfloat16)],
        [scatter_matrix, distribution],
        places=[HBM] * 2,
        scratch=[
            pltpu.VMEM(part, jnp.float32),
            pltpu.SemaphoreType.DMA((2 * chips + 1,)),
        ],
        room=28,
    )
    one.matrix = matrix
    one.terms = [(terms[2 * s], *exchange(terms[2 * s + 1])) for s in range(chips - 1)]
    one.take_own()
    operators = jnp.asarray(differences(cells))
    strips = None

    def unpack():
        nonlocal strips
        shape = jax.ShapeDtypeStruct((modes, 4 * HALO), jnp.bfloat16)
        (strips,) = call(strip_columns, [shape], strips)

    for step in range(1, chips):
        if step == 1:
            one.take(1)
        one.send(step, unpack if step == 2 else None)
        if step == 1:
            one.join_terms(*(s for s in range(chips - 1) if isinstance(one.terms[s], tuple)))
            strips = call(strip_rows, [(HALO, modes)] * 2, [distribution])
            strips = paired(*call(strip_pairs, [(HALO, modes)] * 2, strips))
        else:
            one.take(step, 2 if step == chips - 1 else 1)
        if step == 2:
            one.add_terms(distribution, half)
        if step == chips - 1:
            one.join_terms(chips - 1)
        one.multiply(step - 1)
        if step == min(2, chips - 1):
            base_a, base_b = call(
                first_rest,
                [part] * 2,
                [distribution, strips, operators, table, kinds],
            )
    mid_a, leading, scattered = one.multiply(chips - 1, base_a)

    two = Round(matrix, step_size, False)
    two.add_terms(mid_a)
    one.first_end(base_b)
    mid_b, last = call(
        functools.partial(turn_sum, time_step), [part, (HALO, modes)], one.ends()
    )
    two.begin(mid_b)
    two.add_terms(mid_a)
    two.join_terms(0)
    strips = paired(*call(strip_pairs, [(HALO, modes)] * 2, [leading, last]))
    flux = None
    for step in range(1, chips):
        if step == 1:
            two.send(step, unpack)
            two.take_own()
            two.join_terms(1)
        elif step == 2:
            two.send(step, lambda: flux.over(1))
            two.join_terms(*range(2, chips))
        elif step == chips - 1:
            two.send(step, lambda: flux.over(*range(2, devices, 2)))
        else:
            two.send(step)
        two.take(step, 2 if step >= chips - 2 else 1)
        if step == 1:
            for slot in range(2, chips):
                two.add_terms(mid_a)
        if 1 < step < chips - 1:
            two.hold(*range(step) if step == 2 else (step - 1,))
        if step == chips - 2:
            two.multiply(step, first=True)
        if step == chips - 1:
            for slot in range(chips - 2):
                two.multiply(slot, first=False)
        if step == 1:
            end_a, end_b, part_flux = call(
                functools.partial(second_rest, 1.0 / math.sqrt(total_modes)),
                [part, part, (2, cells)],
                [distribution, mid_a, mid_b, strips, operators, table, kinds, scattered],
            )
            flux = Flux(call, part_flux, devices)
    (last_b,) = two.multiply(chips - 1, end_b)
    heat_flux = flux.value
    two.first_end(end_a)
    (updated,) = call(
        functools.partial(last_sum, step_size),
        [(modes, cells)],
        [*two.ends(), last_b],
        scratch=[pltpu.VMEM(part, jnp.float32), pltpu.SemaphoreType.DMA((2,))],
        out_specs=[HBM],
    )
    return (updated, heat_flux)


class Flux:
    def __init__(self, call, value, devices):
        self.call, self.value, self.devices = call, value, devices

    def over(self, *bits):
        came = [
            lax.ppermute(self.value, "mode", [(i, i ^ bit) for i in range(self.devices)])
            for bit in bits
        ]
        self.value, _ = self.call(add_all, [self.value.shape, (8, LANES)], [self.value, *came])


def solution(mesh):
    return jax.shard_map(
        on_device,
        mesh=mesh,
        in_specs=(P("mode", "space"), P(None, "mode"), P(None, "mode"), P("mode"), P("space")),
        out_specs=(P("mode", "space"), P(None, "space")),
        check_vma=False,
    )
```

```python
import functools
import math

import numpy as np

import jax
import jax.numpy as jnp
from jax import lax
from jax.experimental import pallas as pl
from jax.experimental.pallas import tpu as pltpu
from jax.sharding import PartitionSpec as P

NY = 16
HALO = 2 * NY
LANES = 128
BLOCK = 512


relax_rate = 0.5
time_step = 0.5

VMEM = pl.BlockSpec(memory_space=pltpu.VMEM)
ANY = pl.BlockSpec(memory_space=pl.ANY)
HBM = pl.BlockSpec(memory_space=pltpu.HBM)


class Chain:
    def __init__(self):
        self.last = None

    def __call__(self, kernel, outs, arrays, places=None, scratch=(), out_specs=None, room=16):
        extra = [] if self.last is None else [self.last]
        skip = len(extra)
        first = len(arrays)

        def body(*refs):
            kernel(*refs[:first], *refs[first + skip :])

        results = pl.pallas_call(
            body,
            out_shape=[
                jax.ShapeDtypeStruct(shape, jnp.float32) if isinstance(shape, tuple) else shape
                for shape in outs
            ],
            in_specs=list(places or [VMEM] * len(arrays)) + [ANY] * skip,
            out_specs=out_specs or [VMEM] * len(outs),
            scratch_shapes=list(scratch),
            compiler_params=pltpu.CompilerParams(vmem_limit_bytes=room * 1024 * 1024),
            cost_estimate=pl.CostEstimate(flops=1024, bytes_accessed=1024, transcendentals=0),
            name=getattr(kernel, "func", kernel).__name__,
        )(*arrays, *extra)
        self.last = results[-1]
        return results


def halves(value):
    high = value.astype(jnp.bfloat16)
    low = (value - high.astype(jnp.float32)).astype(jnp.bfloat16)
    return high, low


def for_device(numbers):
    if len(set(numbers)) == 1:
        return numbers[0]
    me = lax.axis_index("mode")
    chosen = jnp.int32(numbers[0])
    for device, number in enumerate(numbers[1:], 1):
        chosen = jnp.where(me == device, jnp.int32(number), chosen)
    return chosen


def rows_of(matrix, block):
    modes = matrix.shape[1]
    return pl.ds(pl.multiple_of(block * modes, modes), modes)


def one_slot(blocks, matrix, parts, mine, other):
    cells = mine.shape[1]
    for block, out in zip(blocks, (mine, other)):
        both = jnp.dot(matrix[rows_of(matrix, block), :], parts, preferred_element_type=jnp.float32)
        out[...] = both[:, :cells] + both[:, cells:]


def slot_products(blocks, column, matrix, field, mine, other):
    blocks = [for_device(numbers) for numbers in blocks]
    parts = jnp.concatenate(halves(field[:, column : column + mine.shape[1]]), axis=1)
    one_slot(blocks, matrix, parts, mine, other)


def load_and_products(blocks, column, matrix, distribution, *refs):
    slots = len(blocks) - 1
    outs, (held, field, sems) = refs[: 2 * slots], refs[2 * slots :]
    cells = field.shape[1]
    start = pltpu.make_async_copy(distribution.at[:, pl.ds(column, cells)], field, sems.at[0])
    start.start()
    blocks = [[for_device(numbers) for numbers in pair] for pair in blocks]
    copies = []
    for block in (block for pair in blocks for block in pair):
        rows = rows_of(held, block)
        copies.append(
            pltpu.make_async_copy(matrix.at[rows, :], held.at[rows, :], sems.at[1 + len(copies)])
        )
        copies[-1].start()
    start.wait()
    parts = jnp.concatenate(halves(field[...]), axis=1)
    for slot, pair in enumerate(blocks[:-1]):
        for copy in copies[2 * slot : 2 * slot + 2]:
            copy.wait()
        one_slot(pair, held, parts, outs[2 * slot], outs[2 * slot + 1])
    for copy in copies[2 * slots :]:
        copy.wait()


def two_blocks(numbers, parts, first, last, scale, rows, matrix, *refs):
    modes = matrix.shape[1]
    blocks, refs = [[refs[0]], refs[1 : 1 + parts]], refs[1 + parts :]
    if not first:
        before, refs = refs[0], refs[1:]
    if last:
        base, refs = refs[0], refs[1:]
    total = None if first else before[...]
    for k, pieces in enumerate(blocks):
        block = jnp.concatenate([piece[...] for piece in pieces], axis=0)
        pieces = list(halves(block[:modes].T))
        if rows:
            weights = [
                jnp.concatenate(
                    [
                        block[modes + i : modes + i + 1, :]
                        for i in range(d * modes // LANES, (d + 1) * modes // LANES)
                    ],
                    axis=1,
                )
                for d in range(2)
            ]
            weights.append(jnp.zeros((6, modes), jnp.float32))
            pieces += halves(jnp.concatenate(weights, axis=0))
        left = jnp.concatenate(pieces, axis=0)
        there = rows_of(matrix, for_device(numbers[k]))
        term = jnp.dot(left, matrix[there, :], preferred_element_type=jnp.float32)
        total = term if total is None else total + term
    if not last:
        refs[0][...] = total
        return
    cells = base.shape[1]
    value = base[...] - scale * (total[:cells] + total[cells : 2 * cells]).T
    refs[0][...] = value
    if rows:
        refs[1][...] = value.T[:HALO]
        refs[2][...] = total[2 * cells : 2 * cells + 8] + total[2 * cells + 8 :]


def own_rows(distribution, velocity, capacity, out, token, speeds, weight, sems):
    modes, cells = velocity.shape[1], out.shape[1]
    copies = [
        pltpu.make_async_copy(velocity, speeds, sems.at[0]),
        pltpu.make_async_copy(capacity, weight, sems.at[1]),
        pltpu.make_async_copy(
            distribution.at[:, pl.ds(0, cells)], out.at[pl.ds(0, modes), :], sems.at[2]
        ),
    ]
    for copy in copies:
        copy.start()
    token[...] = jnp.zeros_like(token)
    for copy in copies[:2]:
        copy.wait()
    per = modes // LANES
    out[modes:] = jnp.zeros((out.shape[0] - modes, LANES), jnp.float32)
    for d in range(2):
        for i in range(per):
            lanes = slice(i * LANES, (i + 1) * LANES)
            out[modes + d * per + i : modes + d * per + i + 1, :] = (
                speeds[d : d + 1, lanes] * weight[:, lanes]
            )
    copies[2].wait()


def payload(numbers, slots, arrived, *refs):
    out = refs[-1]
    slot_here = for_device(numbers)

    for k, slot in enumerate(slots):

        @pl.when(slot_here == slot)
        def _(k=k):
            terms = refs[k]
            modes = terms.shape[0]
            out[:modes] = arrived[:modes] + terms[...]
            if out.shape[0] > modes:
                out[modes:] = arrived[modes:]

    @pl.when(slot_here < 0)
    def _():
        out[...] = arrived[: out.shape[0]]


def pick(numbers, *refs):
    out = refs[-1]
    choice = for_device(numbers)
    for k, ref in enumerate(refs[:-1]):

        @pl.when(choice == k)
        def _(ref=ref):
            out[...] = ref[...]


def add(one, *refs):
    out, first = refs[-1], 0
    for piece in refs[:-1]:
        rows = slice(first, first + piece.shape[0])
        out[rows] = one[rows] + piece[...]
        first += piece.shape[0]


def pass_on(value, out):
    out[...] = value[...]


def add_all(*refs):
    out, token = refs[-2:]
    total = refs[0][...]
    for ref in refs[1:-2]:
        total = total + ref[...]
    out[...] = total
    token[...] = jnp.zeros_like(token)


def take_off(scale, arrived, terms, base, out):
    modes = terms.shape[0]
    out[...] = base[...] - scale * (arrived[:modes] + terms[...])


def turn_sum(scale, arrived, base, out, strip):
    modes = base.shape[0]
    value = base[...] - scale * arrived[:modes]
    out[...] = value
    strip[...] = value.T[-HALO:]


def last_sum(scale, arrived, base, other, flux, out, flux_out, value, sems):
    cells = base.shape[1]
    copies = [
        pltpu.make_async_copy(other, out.at[:, pl.ds(cells, cells)], sems.at[0]),
        pltpu.make_async_copy(flux, flux_out, sems.at[1]),
    ]
    for copy in copies:
        copy.start()
    value[...] = base[...] - scale * arrived[...]
    copies.append(pltpu.make_async_copy(value, out.at[:, pl.ds(0, cells)], sems.at[2]))
    copies[-1].start()
    for copy in copies:
        copy.wait()


def strip_rows(distribution, leading, last):
    cells = distribution.shape[1]
    leading[...] = distribution[:, :LANES].T[:HALO]
    last[...] = distribution[:, cells - LANES :].T[-HALO:]


def strip_pairs(leading, last, out_even, out_odd):
    even = lax.axis_index("space") % 2 == 0

    @pl.when(even)
    def _():
        out_even[...] = last[...]
        out_odd[...] = leading[...]

    @pl.when(jnp.logical_not(even))
    def _():
        out_even[...] = leading[...]
        out_odd[...] = last[...]


def differences(cells):
    columns = cells // NY
    own, strip = np.zeros((cells, 4 * cells)), np.zeros((2 * HALO, 4 * cells))
    for x in range(columns):
        for y in range(NY):
            cell = x * NY + y
            for way in (-1, 1):
                for far, factor in enumerate((3.0, -4.0, 1.0)):
                    at_x, at_y = x + way * far, y + way * far
                    first = cell + (0 if way < 0 else cells)
                    factor = -way * factor
                    if at_x < 0:
                        strip[(at_x + 2) * NY + y, first] = factor
                    elif at_x >= columns:
                        strip[HALO + (at_x - columns) * NY + y, first] = factor
                    else:
                        own[at_x * NY + y, first] = factor
                    if 0 <= at_y < NY:
                        own[x * NY + at_y, first + 2 * cells] = factor
    return np.concatenate([own, own, strip, strip]).astype(jnp.bfloat16)


def strip_columns(came_even, came_odd, out):
    even = lax.axis_index("space") % 2 == 0
    before = jnp.where(even, came_odd[...], came_even[...])
    after = jnp.where(even, came_even[...], came_odd[...])
    parts = halves(jnp.concatenate([before, after], axis=0))
    rows = jnp.concatenate([p.astype(jnp.float32) for p in parts], axis=0)
    out[...] = rows.T.astype(jnp.bfloat16)


def still_rate(field, strip, operators, columns, kinds):
    cells = field.shape[1]
    left = jnp.concatenate([*halves(field), strip], axis=1)
    steps = jnp.dot(left, operators[...], preferred_element_type=jnp.float32)
    vx, vy, capacity = (columns[:, i : i + 1] for i in range(3))
    speeds = (jnp.maximum(vx, 0.0), jnp.minimum(vx, 0.0))
    speeds += (jnp.maximum(vy, 0.0), jnp.minimum(vy, 0.0))
    contact = jnp.where(kinds > 0, relax_rate, 0.0)
    source = jnp.where(kinds == 1, contact, -contact)
    rate = source * capacity - contact * field
    for k, speed in enumerate(speeds):
        rate = rate - (0.5 * speed) * steps[:, k * cells : (k + 1) * cells]
    return rate


def first_rest(field, strips, operators, table, kinds, base_a, base_b):
    modes, half = base_a.shape
    block = min(modes, BLOCK)

    def step(i, _):
        rows = pl.ds(pl.multiple_of(i * block, block), block)
        value = field[rows, :]
        rate = still_rate(value, strips[rows, :], operators, table[:, rows].T, kinds[...])
        base = value + time_step * rate
        base_a[rows, :] = base[:, :half]
        base_b[rows, :] = base[:, half:]
        return 0

    lax.fori_loop(0, modes // block, step, 0)


def second_rest(
    flux_scale,
    field,
    mid_a,
    mid_b,
    strips,
    operators,
    table,
    kinds,
    scattered,
    end_a,
    end_b,
    flux,
):
    modes, half = end_a.shape
    block = min(modes, BLOCK)
    step_size = 0.5 * time_step
    flux[...] = jnp.zeros_like(flux)

    def step(i, _):
        rows = pl.ds(pl.multiple_of(i * block, block), block)
        mid = jnp.concatenate([mid_a[rows, :], mid_b[rows, :]], axis=1)
        columns = table[:, rows].T
        taken = step_size * scattered[:, rows].T
        rate = still_rate(mid, strips[rows, :], operators, columns, kinds[...])
        end = 0.5 * (field[rows, :] + mid) + step_size * rate
        end_a[rows, :] = end[:, :half]
        end_b[rows, :] = end[:, half:]
        for d in range(2):
            terms = columns[:, 3 + d : 4 + d] * end - taken[:, d : d + 1] * mid
            flux[d : d + 1, :] += flux_scale * jnp.sum(terms, axis=0, keepdims=True)
        return 0

    lax.fori_loop(0, modes // block, step, 0)


def paired(to_even, to_odd):
    count = lax.axis_size("space")
    came = []
    for first, value in enumerate((to_even, to_odd)):
        pairs = [(i, i + 1) for i in range(first, count - 1, 2)]
        came.append(lax.ppermute(value, "space", pairs + [(j, i) for i, j in pairs]))
    return came


class Plan:
    def __init__(self, chips):
        self.chips = chips
        self.devices = range(2 * chips)
        sources = [self.sources(d) for d in self.devices]
        targets = [self.targets(d // 2) for d in self.devices]
        self.blocks = [
            [
                [2 * sources[e][slot][2] + e % 2 for e in (d ^ other for d in self.devices)]
                for other in (0, 1)
            ]
            for slot in range(chips)
        ]
        self.rows = [
            [[2 * targets[d][slot] + (d % 2 ^ other) for d in self.devices] for other in (0, 1)]
            for slot in range(chips)
        ]
        self.choices = [
            sorted({sources[d][slot][:2] for d in self.devices}) for slot in range(chips)
        ]
        self.picked = [
            [self.choices[slot].index(sources[d][slot][:2]) for d in self.devices]
            for slot in range(chips)
        ]
        self.sent = {}
        for stream in (0, 1):
            for step in range(1, chips):
                numbers = []
                for d in self.devices:
                    way = self.way(d, stream)
                    place = d // 2 if way > 0 else chips - 1 - d // 2
                    target = d // 2 + way * (chips - step)
                    numbers.append(targets[d].index(target) if place < step else -1)
                self.sent[stream, step] = numbers
        self.pairs = []
        for stream in (0, 1):
            up = [
                (d, d + 2) for d in self.devices[:-2] if self.way(d, stream) > 0
            ]
            self.pairs.append(up + [(j, i) for i, j in up])

    def way(self, device, stream):
        return 1 if (device // 2 + device % 2 + stream) % 2 == 0 else -1

    def sources(self, device):
        found = [(-1, -1, device // 2)]
        for step in range(self.chips - 1):
            for stream in (step % 2, 1 - step % 2):
                chip = device // 2 + self.way(device, stream) * (step + 1)
                if 0 <= chip < self.chips:
                    found.append((stream, step, chip))
        return found

    def targets(self, chip):
        found = []
        for step in range(1, self.chips):
            far = self.chips - step
            found += [t for t in (chip + far, chip - far) if 0 <= t < self.chips]
        return found + [chip]


def on_device(distribution, scatter_matrix, velocity, capacity, cell_type):
    modes, cells = distribution.shape
    total_modes = scatter_matrix.shape[0]
    half = cells // 2
    extra = -(-2 * modes // LANES // 8) * 8
    step_size = 0.5 * time_step
    part = (modes, half)
    devices = lax.axis_size("mode")
    chips = devices // 2
    plan = Plan(chips)
    call = Chain()
    across = [(i, i ^ 1) for i in range(devices)]
    cap = capacity[None, :]
    table = jnp.concatenate(
        [velocity, cap, cap * velocity, jnp.zeros((3, modes), jnp.float32)], axis=0
    )
    kinds = cell_type[None, :]

    def exchange(value, parts=1):
        cut = value.shape[0] // parts // 8 * 8
        ends = [cut * k for k in range(parts)] + [value.shape[0]]
        return [lax.ppermute(value[i:j], "mode", across) for i, j in zip(ends, ends[1:])]

    def along(stream, value):
        return lax.ppermute(value, "mode", plan.pairs[stream])

    class Round:
        def __init__(self, matrix, scale, rows):
            self.matrix, self.scale, self.rows = matrix, scale, rows
            self.terms, self.total = [], None

        def begin(self, own):
            self.own = own
            self.arrived = [[along(0, own)], [along(1, own)]]
            self.blocks = []

        def add_terms(self, field, column=0):
            kernel = functools.partial(slot_products, plan.rows[len(self.terms)], column)
            mine, other = call(kernel, [part] * 2, [self.matrix, field])
            self.terms.append((mine, *exchange(other)))

        def join_terms(self, *slots):
            for slot in slots:
                (self.terms[slot],) = call(add, [part], self.terms[slot])

        def take_own(self, later=False):
            own = call(pass_on, [self.own.shape], [self.own])[0] if later else self.own
            self.blocks.append((self.own, *exchange(own)))

        def send(self, step, between=None):
            sent = {}
            for stream in (step % 2, 1 - step % 2):
                if between is not None and sent:
                    between()
                numbers = plan.sent[stream, step]
                slots = sorted({n for n in numbers if n >= 0})
                for slot in slots:
                    if isinstance(self.terms[slot], tuple):
                        self.join_terms(slot)
                arrived = self.arrived[1 - stream][step - 1]
                kernel = functools.partial(payload, numbers, slots)
                arrays = [arrived] + [self.terms[s] for s in slots]
                shape = part if step == chips - 1 else arrived.shape
                (value,) = call(kernel, [shape], arrays)
                sent[stream] = along(stream, value)
            for stream in (0, 1):
                self.arrived[stream].append(sent[stream])

        def take(self, slot, parts=1):
            arrays = [self.arrived[stream][step] for stream, step in plan.choices[slot]]
            kernel = functools.partial(pick, plan.picked[slot])
            (here,) = call(kernel, [arrays[0].shape], arrays)
            self.blocks.append((here, *exchange(here, parts)))

        def hold(self, *slots):
            for slot in slots:
                here, there = self.blocks[slot]
                (there,) = call(pass_on, [there.shape], [there])
                self.blocks[slot] = (here, there)

        def multiply(self, slot, base=None, first=None):
            first, last = slot == 0 if first is None else first, base is not None
            blocks = self.blocks[slot]
            kernel = functools.partial(
                two_blocks, plan.blocks[slot], len(blocks) - 1, first, last, self.scale, self.rows
            )
            arrays = [self.matrix, *blocks]
            arrays += [] if first else [self.total]
            arrays += [base] if last else []
            outs = [(2 * half + (16 if self.rows else 0), modes)]
            if last:
                outs = [part, (HALO, modes), (8, modes)] if self.rows else [part]
            results = call(kernel, outs, arrays)
            self.total = results[0]
            return results

        def first_end(self, base):
            kernel = functools.partial(take_off, self.scale)
            arrived = self.arrived[(chips - 1) % 2][-1]
            (self.rest,) = call(kernel, [part], [arrived, self.terms[-1], base])

        def ends(self):
            return [self.arrived[chips % 2][-1], self.rest]

    own, _ = call(
        own_rows,
        [(modes + extra, half), (8, LANES)],
        [distribution, velocity, cap],
        places=[HBM] * 3,
        scratch=[
            pltpu.VMEM((2, modes), jnp.float32),
            pltpu.VMEM((1, modes), jnp.float32),
            pltpu.SemaphoreType.DMA((3,)),
        ],
        room=56,
    )
    one = Round(None, time_step, True)
    one.begin(own)
    *terms, matrix = call(
        functools.partial(load_and_products, plan.rows, half),
        [part] * (2 * chips - 2) + [jax.ShapeDtypeStruct(scatter_matrix.shape, jnp.bfloat16)],
        [scatter_matrix, distribution],
        places=[HBM] * 2,
        scratch=[
            pltpu.VMEM(part, jnp.float32),
            pltpu.SemaphoreType.DMA((2 * chips + 1,)),
        ],
        room=28,
    )
    one.matrix = matrix
    one.terms = [(terms[2 * s], *exchange(terms[2 * s + 1])) for s in range(chips - 1)]
    one.take_own()
    operators = jnp.asarray(differences(cells))
    strips = None

    def unpack():
        nonlocal strips
        shape = jax.ShapeDtypeStruct((modes, 4 * HALO), jnp.bfloat16)
        (strips,) = call(strip_columns, [shape], strips)

    for step in range(1, chips):
        if step == 1:
            one.take(1)
        one.send(step, unpack if step == 2 else None)
        if step == 1:
            one.join_terms(*(s for s in range(chips - 1) if isinstance(one.terms[s], tuple)))
            strips = call(strip_rows, [(HALO, modes)] * 2, [distribution])
            strips = paired(*call(strip_pairs, [(HALO, modes)] * 2, strips))
        else:
            one.take(step, 2 if step == chips - 1 else 1)
        if step == 2:
            one.add_terms(distribution, half)
        if step == chips - 1:
            one.join_terms(chips - 1)
        one.multiply(step - 1)
        if step == min(2, chips - 1):
            base_a, base_b = call(
                first_rest,
                [part] * 2,
                [distribution, strips, operators, table, kinds],
            )
    mid_a, leading, scattered = one.multiply(chips - 1, base_a)

    two = Round(matrix, step_size, False)
    two.add_terms(mid_a)
    one.first_end(base_b)
    mid_b, last = call(
        functools.partial(turn_sum, time_step), [part, (HALO, modes)], one.ends()
    )
    two.begin(mid_b)
    two.add_terms(mid_a)
    two.join_terms(0)
    strips = paired(*call(strip_pairs, [(HALO, modes)] * 2, [leading, last]))
    flux = None
    for step in range(1, chips):
        if step == 1:
            two.send(step, unpack)
            two.take_own()
            two.join_terms(1)
        elif step == 2:
            two.send(step, lambda: flux.over(1))
            two.join_terms(*range(2, chips))
        elif step == chips - 1:
            two.send(step, lambda: flux.over(*range(2, devices, 2)))
        else:
            two.send(step)
        two.take(step, 2 if step >= chips - 2 else 1)
        if step == 1:
            for slot in range(2, chips):
                two.add_terms(mid_a)
        if 1 < step < chips - 1:
            two.hold(*range(step) if step == 2 else (step - 1,))
        if step == chips - 2:
            two.multiply(step, first=True)
        if step == chips - 1:
            for slot in range(chips - 2):
                two.multiply(slot, first=False)
        if step == 1:
            end_a, end_b, part_flux = call(
                functools.partial(second_rest, 1.0 / math.sqrt(total_modes)),
                [part, part, (2, cells)],
                [distribution, mid_a, mid_b, strips, operators, table, kinds, scattered],
            )
            flux = Flux(call, part_flux, devices)
    (last_b,) = two.multiply(chips - 1, end_b)
    two.first_end(end_a)
    updated, heat_flux = call(
        functools.partial(last_sum, step_size),
        [(modes, cells), (2, cells)],
        [*two.ends(), last_b, flux.value],
        scratch=[pltpu.VMEM(part, jnp.float32), pltpu.SemaphoreType.DMA((3,))],
        out_specs=[HBM, HBM],
    )
    return (updated, heat_flux)


class Flux:
    def __init__(self, call, value, devices):
        self.call, self.value, self.devices = call, value, devices

    def over(self, *bits):
        came = [
            lax.ppermute(self.value, "mode", [(i, i ^ bit) for i in range(self.devices)])
            for bit in bits
        ]
        self.value, _ = self.call(add_all, [self.value.shape, (8, LANES)], [self.value, *came])


def solution(mesh):
    return jax.shard_map(
        on_device,
        mesh=mesh,
        in_specs=(P("mode", "space"), P(None, "mode"), P(None, "mode"), P("mode"), P("space")),
        out_specs=(P("mode", "space"), P(None, "space")),
        check_vma=False,
    )
```

```python
import functools
import math

import numpy as np

import jax
import jax.numpy as jnp
from jax import lax
from jax.experimental import pallas as pl
from jax.experimental.pallas import tpu as pltpu
from jax.sharding import PartitionSpec as P

NY = 16
HALO = 2 * NY
LANES = 128
BLOCK = 512


relax_rate = 0.5
time_step = 0.5

VMEM = pl.BlockSpec(memory_space=pltpu.VMEM)
ANY = pl.BlockSpec(memory_space=pl.ANY)
HBM = pl.BlockSpec(memory_space=pltpu.HBM)


class Chain:
    def __init__(self):
        self.last = None

    def __call__(self, kernel, outs, arrays, places=None, scratch=(), out_specs=None, room=16):
        extra = [] if self.last is None else [self.last]
        skip = len(extra)
        first = len(arrays)

        def body(*refs):
            kernel(*refs[:first], *refs[first + skip :])

        results = pl.pallas_call(
            body,
            out_shape=[
                jax.ShapeDtypeStruct(shape, jnp.float32) if isinstance(shape, tuple) else shape
                for shape in outs
            ],
            in_specs=list(places or [VMEM] * len(arrays)) + [ANY] * skip,
            out_specs=out_specs or [VMEM] * len(outs),
            scratch_shapes=list(scratch),
            compiler_params=pltpu.CompilerParams(vmem_limit_bytes=room * 1024 * 1024),
            cost_estimate=pl.CostEstimate(flops=1024, bytes_accessed=1024, transcendentals=0),
            name=getattr(kernel, "func", kernel).__name__,
        )(*arrays, *extra)
        self.last = results[-1]
        return results


def halves(value):
    high = value.astype(jnp.bfloat16)
    low = (value - high.astype(jnp.float32)).astype(jnp.bfloat16)
    return high, low


def for_device(numbers):
    if len(set(numbers)) == 1:
        return numbers[0]
    me = lax.axis_index("mode")
    chosen = jnp.int32(numbers[0])
    for device, number in enumerate(numbers[1:], 1):
        chosen = jnp.where(me == device, jnp.int32(number), chosen)
    return chosen


def rows_of(matrix, block):
    modes = matrix.shape[1]
    return pl.ds(pl.multiple_of(block * modes, modes), modes)


def one_slot(blocks, matrix, parts, mine, other):
    cells = mine.shape[1]
    for block, out in zip(blocks, (mine, other)):
        both = jnp.dot(matrix[rows_of(matrix, block), :], parts, preferred_element_type=jnp.float32)
        out[...] = both[:, :cells] + both[:, cells:]


def slot_products(blocks, column, matrix, field, mine, other):
    blocks = [for_device(numbers) for numbers in blocks]
    parts = jnp.concatenate(halves(field[:, column : column + mine.shape[1]]), axis=1)
    one_slot(blocks, matrix, parts, mine, other)


def load_and_products(blocks, column, matrix, distribution, *refs):
    slots = len(blocks) - 1
    outs, (held, field, sems) = refs[: 2 * slots], refs[2 * slots :]
    cells = field.shape[1]
    start = pltpu.make_async_copy(distribution.at[:, pl.ds(column, cells)], field, sems.at[0])
    start.start()
    blocks = [[for_device(numbers) for numbers in pair] for pair in blocks]
    copies = []
    for block in (block for pair in blocks for block in pair):
        rows = rows_of(held, block)
        copies.append(
            pltpu.make_async_copy(matrix.at[rows, :], held.at[rows, :], sems.at[1 + len(copies)])
        )
        copies[-1].start()
    start.wait()
    parts = jnp.concatenate(halves(field[...]), axis=1)
    for slot, pair in enumerate(blocks[:-1]):
        for copy in copies[2 * slot : 2 * slot + 2]:
            copy.wait()
        one_slot(pair, held, parts, outs[2 * slot], outs[2 * slot + 1])
    for copy in copies[2 * slots :]:
        copy.wait()


def two_blocks(numbers, parts, first, last, scale, rows, matrix, *refs):
    modes = matrix.shape[1]
    blocks, refs = [[refs[0]], refs[1 : 1 + parts]], refs[1 + parts :]
    if not first:
        before, refs = refs[0], refs[1:]
    if last:
        base, refs = refs[0], refs[1:]
    total = None if first else before[...]
    for k, pieces in enumerate(blocks):
        block = jnp.concatenate([piece[...] for piece in pieces], axis=0)
        pieces = list(halves(block[:modes].T))
        if rows:
            weights = [
                jnp.concatenate(
                    [
                        block[modes + i : modes + i + 1, :]
                        for i in range(d * modes // LANES, (d + 1) * modes // LANES)
                    ],
                    axis=1,
                )
                for d in range(2)
            ]
            weights.append(jnp.zeros((6, modes), jnp.float32))
            pieces += halves(jnp.concatenate(weights, axis=0))
        left = jnp.concatenate(pieces, axis=0)
        there = rows_of(matrix, for_device(numbers[k]))
        term = jnp.dot(left, matrix[there, :], preferred_element_type=jnp.float32)
        total = term if total is None else total + term
    if not last:
        refs[0][...] = total
        return
    cells = base.shape[1]
    value = base[...] - scale * (total[:cells] + total[cells : 2 * cells]).T
    refs[0][...] = value
    if rows:
        refs[1][...] = value.T[:HALO]
        refs[2][...] = total[2 * cells : 2 * cells + 8] + total[2 * cells + 8 :]


def own_rows(distribution, velocity, capacity, out, token, speeds, weight, sems):
    modes, cells = velocity.shape[1], out.shape[1]
    copies = [
        pltpu.make_async_copy(velocity, speeds, sems.at[0]),
        pltpu.make_async_copy(capacity, weight, sems.at[1]),
        pltpu.make_async_copy(
            distribution.at[:, pl.ds(0, cells)], out.at[pl.ds(0, modes), :], sems.at[2]
        ),
    ]
    for copy in copies:
        copy.start()
    token[...] = jnp.zeros_like(token)
    for copy in copies[:2]:
        copy.wait()
    per = modes // LANES
    out[modes:] = jnp.zeros((out.shape[0] - modes, LANES), jnp.float32)
    for d in range(2):
        for i in range(per):
            lanes = slice(i * LANES, (i + 1) * LANES)
            out[modes + d * per + i : modes + d * per + i + 1, :] = (
                speeds[d : d + 1, lanes] * weight[:, lanes]
            )
    copies[2].wait()


def payload(numbers, slots, arrived, *refs):
    out = refs[-1]
    slot_here = for_device(numbers)

    for k, slot in enumerate(slots):

        @pl.when(slot_here == slot)
        def _(k=k):
            terms = refs[k]
            modes = terms.shape[0]
            out[:modes] = arrived[:modes] + terms[...]
            if out.shape[0] > modes:
                out[modes:] = arrived[modes:]

    @pl.when(slot_here < 0)
    def _():
        out[...] = arrived[: out.shape[0]]


def pick(numbers, *refs):
    out = refs[-1]
    choice = for_device(numbers)
    for k, ref in enumerate(refs[:-1]):

        @pl.when(choice == k)
        def _(ref=ref):
            out[...] = ref[...]


def add(one, *refs):
    out, first = refs[-1], 0
    for piece in refs[:-1]:
        rows = slice(first, first + piece.shape[0])
        out[rows] = one[rows] + piece[...]
        first += piece.shape[0]


def pass_on(value, out):
    out[...] = value[...]


def add_all(*refs):
    out, token = refs[-2:]
    total = refs[0][...]
    for ref in refs[1:-2]:
        total = total + ref[...]
    out[...] = total
    token[...] = jnp.zeros_like(token)


def take_off(scale, arrived, terms, base, out):
    modes = terms.shape[0]
    out[...] = base[...] - scale * (arrived[:modes] + terms[...])


def turn_sum(scale, arrived, base, out):
    modes = base.shape[0]
    out[...] = base[...] - scale * arrived[:modes]


def last_strip(field, strip):
    strip[...] = field[:, field.shape[1] - LANES :].T[-HALO:]


def last_sum(scale, arrived, base, other, flux, out, flux_out, value, sems):
    cells = base.shape[1]
    copies = [
        pltpu.make_async_copy(other, out.at[:, pl.ds(cells, cells)], sems.at[0]),
        pltpu.make_async_copy(flux, flux_out, sems.at[1]),
    ]
    for copy in copies:
        copy.start()
    rows = base.shape[0] // 2
    for k in range(2):
        part = slice(k * rows, (k + 1) * rows)
        value[part] = base[part] - scale * arrived[part]
        at = pl.ds(k * rows, rows)
        copies.append(
            pltpu.make_async_copy(
                value.at[at, :], out.at[at, pl.ds(0, cells)], sems.at[2 + k]
            )
        )
        copies[-1].start()
    for copy in copies:
        copy.wait()


def strip_rows(distribution, leading, last):
    cells = distribution.shape[1]
    leading[...] = distribution[:, :LANES].T[:HALO]
    last[...] = distribution[:, cells - LANES :].T[-HALO:]


def strip_pairs(leading, last, out_even, out_odd):
    even = lax.axis_index("space") % 2 == 0

    @pl.when(even)
    def _():
        out_even[...] = last[...]
        out_odd[...] = leading[...]

    @pl.when(jnp.logical_not(even))
    def _():
        out_even[...] = leading[...]
        out_odd[...] = last[...]


def differences(cells):
    columns = cells // NY
    own, strip = np.zeros((cells, 4 * cells)), np.zeros((2 * HALO, 4 * cells))
    for x in range(columns):
        for y in range(NY):
            cell = x * NY + y
            for way in (-1, 1):
                for far, factor in enumerate((3.0, -4.0, 1.0)):
                    at_x, at_y = x + way * far, y + way * far
                    first = cell + (0 if way < 0 else cells)
                    factor = -way * factor
                    if at_x < 0:
                        strip[(at_x + 2) * NY + y, first] = factor
                    elif at_x >= columns:
                        strip[HALO + (at_x - columns) * NY + y, first] = factor
                    else:
                        own[at_x * NY + y, first] = factor
                    if 0 <= at_y < NY:
                        own[x * NY + at_y, first + 2 * cells] = factor
    return np.concatenate([own, own, strip, strip]).astype(jnp.bfloat16)


def strip_columns(came_even, came_odd, out):
    even = lax.axis_index("space") % 2 == 0
    before = jnp.where(even, came_odd[...], came_even[...])
    after = jnp.where(even, came_even[...], came_odd[...])
    parts = halves(jnp.concatenate([before, after], axis=0))
    rows = jnp.concatenate([p.astype(jnp.float32) for p in parts], axis=0)
    out[...] = rows.T.astype(jnp.bfloat16)


def still_rate(field, strip, operators, columns, kinds):
    cells = field.shape[1]
    left = jnp.concatenate([*halves(field), strip], axis=1)
    steps = jnp.dot(left, operators[...], preferred_element_type=jnp.float32)
    vx, vy, capacity = (columns[:, i : i + 1] for i in range(3))
    speeds = (jnp.maximum(vx, 0.0), jnp.minimum(vx, 0.0))
    speeds += (jnp.maximum(vy, 0.0), jnp.minimum(vy, 0.0))
    contact = jnp.where(kinds > 0, relax_rate, 0.0)
    source = jnp.where(kinds == 1, contact, -contact)
    rate = source * capacity - contact * field
    for k, speed in enumerate(speeds):
        rate = rate - (0.5 * speed) * steps[:, k * cells : (k + 1) * cells]
    return rate


def first_rest(field, strips, operators, table, kinds, base_a, base_b):
    modes, half = base_a.shape
    block = min(modes, BLOCK)

    def step(i, _):
        rows = pl.ds(pl.multiple_of(i * block, block), block)
        value = field[rows, :]
        rate = still_rate(value, strips[rows, :], operators, table[:, rows].T, kinds[...])
        base = value + time_step * rate
        base_a[rows, :] = base[:, :half]
        base_b[rows, :] = base[:, half:]
        return 0

    lax.fori_loop(0, modes // block, step, 0)


def second_rest(
    flux_scale,
    field,
    mid_a,
    mid_b,
    strips,
    operators,
    table,
    kinds,
    scattered,
    end_a,
    end_b,
    flux,
):
    modes, half = end_a.shape
    block = min(modes, BLOCK)
    step_size = 0.5 * time_step
    flux[...] = jnp.zeros_like(flux)

    def step(i, _):
        rows = pl.ds(pl.multiple_of(i * block, block), block)
        mid = jnp.concatenate([mid_a[rows, :], mid_b[rows, :]], axis=1)
        columns = table[:, rows].T
        taken = step_size * scattered[:, rows].T
        rate = still_rate(mid, strips[rows, :], operators, columns, kinds[...])
        end = 0.5 * (field[rows, :] + mid) + step_size * rate
        end_a[rows, :] = end[:, :half]
        end_b[rows, :] = end[:, half:]
        for d in range(2):
            terms = columns[:, 3 + d : 4 + d] * end - taken[:, d : d + 1] * mid
            flux[d : d + 1, :] += flux_scale * jnp.sum(terms, axis=0, keepdims=True)
        return 0

    lax.fori_loop(0, modes // block, step, 0)


def paired(to_even, to_odd):
    count = lax.axis_size("space")
    came = []
    for first, value in enumerate((to_even, to_odd)):
        pairs = [(i, i + 1) for i in range(first, count - 1, 2)]
        came.append(lax.ppermute(value, "space", pairs + [(j, i) for i, j in pairs]))
    return came


class Plan:
    def __init__(self, chips):
        self.chips = chips
        self.devices = range(2 * chips)
        sources = [self.sources(d) for d in self.devices]
        targets = [self.targets(d // 2) for d in self.devices]
        self.blocks = [
            [
                [2 * sources[e][slot][2] + e % 2 for e in (d ^ other for d in self.devices)]
                for other in (0, 1)
            ]
            for slot in range(chips)
        ]
        self.rows = [
            [[2 * targets[d][slot] + (d % 2 ^ other) for d in self.devices] for other in (0, 1)]
            for slot in range(chips)
        ]
        self.choices = [
            sorted({sources[d][slot][:2] for d in self.devices}) for slot in range(chips)
        ]
        self.picked = [
            [self.choices[slot].index(sources[d][slot][:2]) for d in self.devices]
            for slot in range(chips)
        ]
        self.sent = {}
        for stream in (0, 1):
            for step in range(1, chips):
                numbers = []
                for d in self.devices:
                    way = self.way(d, stream)
                    place = d // 2 if way > 0 else chips - 1 - d // 2
                    target = d // 2 + way * (chips - step)
                    numbers.append(targets[d].index(target) if place < step else -1)
                self.sent[stream, step] = numbers
        self.pairs = []
        for stream in (0, 1):
            up = [
                (d, d + 2) for d in self.devices[:-2] if self.way(d, stream) > 0
            ]
            self.pairs.append(up + [(j, i) for i, j in up])

    def way(self, device, stream):
        return 1 if (device // 2 + device % 2 + stream) % 2 == 0 else -1

    def sources(self, device):
        found = [(-1, -1, device // 2)]
        for step in range(self.chips - 1):
            for stream in (step % 2, 1 - step % 2):
                chip = device // 2 + self.way(device, stream) * (step + 1)
                if 0 <= chip < self.chips:
                    found.append((stream, step, chip))
        return found

    def targets(self, chip):
        found = []
        for step in range(1, self.chips):
            far = self.chips - step
            found += [t for t in (chip + far, chip - far) if 0 <= t < self.chips]
        return found + [chip]


def on_device(distribution, scatter_matrix, velocity, capacity, cell_type):
    modes, cells = distribution.shape
    total_modes = scatter_matrix.shape[0]
    half = cells // 2
    extra = -(-2 * modes // LANES // 8) * 8
    step_size = 0.5 * time_step
    part = (modes, half)
    devices = lax.axis_size("mode")
    chips = devices // 2
    plan = Plan(chips)
    call = Chain()
    across = [(i, i ^ 1) for i in range(devices)]
    cap = capacity[None, :]
    table = jnp.concatenate(
        [velocity, cap, cap * velocity, jnp.zeros((3, modes), jnp.float32)], axis=0
    )
    kinds = cell_type[None, :]

    def exchange(value, parts=1):
        cut = value.shape[0] // parts // 8 * 8
        ends = [cut * k for k in range(parts)] + [value.shape[0]]
        return [lax.ppermute(value[i:j], "mode", across) for i, j in zip(ends, ends[1:])]

    def along(stream, value):
        return lax.ppermute(value, "mode", plan.pairs[stream])

    class Round:
        def __init__(self, matrix, scale, rows):
            self.matrix, self.scale, self.rows = matrix, scale, rows
            self.terms, self.total = [], None

        def begin(self, own):
            self.own = own
            self.arrived = [[along(0, own)], [along(1, own)]]
            self.blocks = []

        def add_terms(self, field, column=0):
            kernel = functools.partial(slot_products, plan.rows[len(self.terms)], column)
            mine, other = call(kernel, [part] * 2, [self.matrix, field])
            self.terms.append((mine, *exchange(other)))

        def join_terms(self, *slots):
            for slot in slots:
                (self.terms[slot],) = call(add, [part], self.terms[slot])

        def take_own(self, later=False):
            own = call(pass_on, [self.own.shape], [self.own])[0] if later else self.own
            self.blocks.append((self.own, *exchange(own)))

        def send(self, step, between=None):
            sent = {}
            for stream in (step % 2, 1 - step % 2):
                if between is not None and sent:
                    between()
                numbers = plan.sent[stream, step]
                slots = sorted({n for n in numbers if n >= 0})
                for slot in slots:
                    if isinstance(self.terms[slot], tuple):
                        self.join_terms(slot)
                arrived = self.arrived[1 - stream][step - 1]
                kernel = functools.partial(payload, numbers, slots)
                arrays = [arrived] + [self.terms[s] for s in slots]
                shape = part if step == chips - 1 else arrived.shape
                (value,) = call(kernel, [shape], arrays)
                sent[stream] = along(stream, value)
            for stream in (0, 1):
                self.arrived[stream].append(sent[stream])

        def take(self, slot, parts=1):
            arrays = [self.arrived[stream][step] for stream, step in plan.choices[slot]]
            kernel = functools.partial(pick, plan.picked[slot])
            (here,) = call(kernel, [arrays[0].shape], arrays)
            self.blocks.append((here, *exchange(here, parts)))

        def hold(self, *slots):
            for slot in slots:
                here, there = self.blocks[slot]
                (there,) = call(pass_on, [there.shape], [there])
                self.blocks[slot] = (here, there)

        def multiply(self, slot, base=None, first=None):
            first, last = slot == 0 if first is None else first, base is not None
            blocks = self.blocks[slot]
            kernel = functools.partial(
                two_blocks, plan.blocks[slot], len(blocks) - 1, first, last, self.scale, self.rows
            )
            arrays = [self.matrix, *blocks]
            arrays += [] if first else [self.total]
            arrays += [base] if last else []
            outs = [(2 * half + (16 if self.rows else 0), modes)]
            if last:
                outs = [part, (HALO, modes), (8, modes)] if self.rows else [part]
            results = call(kernel, outs, arrays)
            self.total = results[0]
            return results

        def first_end(self, base):
            kernel = functools.partial(take_off, self.scale)
            arrived = self.arrived[(chips - 1) % 2][-1]
            (self.rest,) = call(kernel, [part], [arrived, self.terms[-1], base])

        def ends(self):
            return [self.arrived[chips % 2][-1], self.rest]

    own, _ = call(
        own_rows,
        [(modes + extra, half), (8, LANES)],
        [distribution, velocity, cap],
        places=[HBM] * 3,
        scratch=[
            pltpu.VMEM((2, modes), jnp.float32),
            pltpu.VMEM((1, modes), jnp.float32),
            pltpu.SemaphoreType.DMA((3,)),
        ],
        room=56,
    )
    one = Round(None, time_step, True)
    one.begin(own)
    *terms, matrix = call(
        functools.partial(load_and_products, plan.rows, half),
        [part] * (2 * chips - 2) + [jax.ShapeDtypeStruct(scatter_matrix.shape, jnp.bfloat16)],
        [scatter_matrix, distribution],
        places=[HBM] * 2,
        scratch=[
            pltpu.VMEM(part, jnp.float32),
            pltpu.SemaphoreType.DMA((2 * chips + 1,)),
        ],
        room=28,
    )
    one.matrix = matrix
    one.terms = [(terms[2 * s], *exchange(terms[2 * s + 1])) for s in range(chips - 1)]
    one.take_own()
    operators = jnp.asarray(differences(cells))
    strips = None

    def unpack():
        nonlocal strips
        shape = jax.ShapeDtypeStruct((modes, 4 * HALO), jnp.bfloat16)
        (strips,) = call(strip_columns, [shape], strips)

    for step in range(1, chips):
        if step == 1:
            one.take(1)
        one.send(step, unpack if step == 2 else None)
        if step == 1:
            one.join_terms(*(s for s in range(chips - 1) if isinstance(one.terms[s], tuple)))
            strips = call(strip_rows, [(HALO, modes)] * 2, [distribution])
            strips = paired(*call(strip_pairs, [(HALO, modes)] * 2, strips))
        else:
            one.take(step, 2 if step == chips - 1 else 1)
        if step == 2:
            one.add_terms(distribution, half)
        if step == chips - 1:
            one.join_terms(chips - 1)
        one.multiply(step - 1)
        if step == min(2, chips - 1):
            base_a, base_b = call(
                first_rest,
                [part] * 2,
                [distribution, strips, operators, table, kinds],
            )
    mid_a, leading, scattered = one.multiply(chips - 1, base_a)

    two = Round(matrix, step_size, False)
    two.add_terms(mid_a)
    two.add_terms(mid_a)
    one.first_end(base_b)
    (mid_b,) = call(functools.partial(turn_sum, time_step), [part], one.ends())
    two.begin(mid_b)
    two.join_terms(0)
    (last,) = call(last_strip, [(HALO, modes)], [mid_b])
    strips = paired(*call(strip_pairs, [(HALO, modes)] * 2, [leading, last]))
    flux = None
    for step in range(1, chips):
        if step == 1:
            two.send(step, unpack)
            two.take_own()
            two.join_terms(1)
        elif step == 2:
            two.send(step, lambda: flux.over(1))
            two.join_terms(*range(2, chips))
        elif step == chips - 1:
            two.send(step, lambda: flux.over(*range(2, devices, 2)))
        else:
            two.send(step)
        two.take(step, 2 if step >= chips - 2 else 1)
        if step == 1:
            for slot in range(2, chips):
                two.add_terms(mid_a)
        if 1 < step < chips - 1:
            two.hold(*range(step) if step == 2 else (step - 1,))
        if step == chips - 2:
            two.multiply(step, first=True)
        if step == chips - 1:
            for slot in range(chips - 2):
                two.multiply(slot, first=False)
        if step == 1:
            end_a, end_b, part_flux = call(
                functools.partial(second_rest, 1.0 / math.sqrt(total_modes)),
                [part, part, (2, cells)],
                [distribution, mid_a, mid_b, strips, operators, table, kinds, scattered],
            )
            flux = Flux(call, part_flux, devices)
    (last_b,) = two.multiply(chips - 1, end_b)
    two.first_end(end_a)
    updated, heat_flux = call(
        functools.partial(last_sum, step_size),
        [(modes, cells), (2, cells)],
        [*two.ends(), last_b, flux.value],
        scratch=[pltpu.VMEM(part, jnp.float32), pltpu.SemaphoreType.DMA((4,))],
        out_specs=[HBM, HBM],
    )
    return (updated, heat_flux)


class Flux:
    def __init__(self, call, value, devices):
        self.call, self.value, self.devices = call, value, devices

    def over(self, *bits):
        came = [
            lax.ppermute(self.value, "mode", [(i, i ^ bit) for i in range(self.devices)])
            for bit in bits
        ]
        self.value, _ = self.call(add_all, [self.value.shape, (8, LANES)], [self.value, *came])


def solution(mesh):
    return jax.shard_map(
        on_device,
        mesh=mesh,
        in_specs=(P("mode", "space"), P(None, "mode"), P(None, "mode"), P("mode"), P("space")),
        out_specs=(P("mode", "space"), P(None, "space")),
        check_vma=False,
    )
```

```python
import functools
import math

import numpy as np

import jax
import jax.numpy as jnp
from jax import lax
from jax.experimental import pallas as pl
from jax.experimental.pallas import tpu as pltpu
from jax.sharding import PartitionSpec as P

NY = 16
HALO = 2 * NY
LANES = 128
BLOCK = 1024


relax_rate = 0.5
time_step = 0.5

VMEM = pl.BlockSpec(memory_space=pltpu.VMEM)
ANY = pl.BlockSpec(memory_space=pl.ANY)
HBM = pl.BlockSpec(memory_space=pltpu.HBM)


class Chain:
    def __init__(self):
        self.last = None

    def __call__(self, kernel, outs, arrays, places=None, scratch=(), out_specs=None, room=16):
        extra = [] if self.last is None else [self.last]
        skip = len(extra)
        first = len(arrays)

        def body(*refs):
            kernel(*refs[:first], *refs[first + skip :])

        results = pl.pallas_call(
            body,
            out_shape=[
                jax.ShapeDtypeStruct(shape, jnp.float32) if isinstance(shape, tuple) else shape
                for shape in outs
            ],
            in_specs=list(places or [VMEM] * len(arrays)) + [ANY] * skip,
            out_specs=out_specs or [VMEM] * len(outs),
            scratch_shapes=list(scratch),
            compiler_params=pltpu.CompilerParams(vmem_limit_bytes=room * 1024 * 1024),
            cost_estimate=pl.CostEstimate(flops=1024, bytes_accessed=1024, transcendentals=0),
            name=getattr(kernel, "func", kernel).__name__,
        )(*arrays, *extra)
        self.last = results[-1]
        return results


def halves(value):
    high = value.astype(jnp.bfloat16)
    low = (value - high.astype(jnp.float32)).astype(jnp.bfloat16)
    return high, low


def for_device(numbers):
    if len(set(numbers)) == 1:
        return numbers[0]
    me = lax.axis_index("mode")
    chosen = jnp.int32(numbers[0])
    for device, number in enumerate(numbers[1:], 1):
        chosen = jnp.where(me == device, jnp.int32(number), chosen)
    return chosen


def rows_of(matrix, block):
    modes = matrix.shape[1]
    return pl.ds(pl.multiple_of(block * modes, modes), modes)


def one_slot(blocks, matrix, parts, mine, other):
    cells = mine.shape[1]
    for block, out in zip(blocks, (mine, other)):
        both = jnp.dot(matrix[rows_of(matrix, block), :], parts, preferred_element_type=jnp.float32)
        out[...] = both[:, :cells] + both[:, cells:]


def slot_products(blocks, column, matrix, field, mine, other):
    blocks = [for_device(numbers) for numbers in blocks]
    parts = jnp.concatenate(halves(field[:, column : column + mine.shape[1]]), axis=1)
    one_slot(blocks, matrix, parts, mine, other)


def load_and_products(blocks, column, matrix, distribution, *refs):
    slots = len(blocks) - 1
    outs, (held, field, sems) = refs[: 2 * slots], refs[2 * slots :]
    cells = field.shape[1]
    start = pltpu.make_async_copy(distribution.at[:, pl.ds(column, cells)], field, sems.at[0])
    start.start()
    blocks = [[for_device(numbers) for numbers in pair] for pair in blocks]
    copies = []
    for block in (block for pair in blocks for block in pair):
        rows = rows_of(held, block)
        copies.append(
            pltpu.make_async_copy(matrix.at[rows, :], held.at[rows, :], sems.at[1 + len(copies)])
        )
        copies[-1].start()
    start.wait()
    parts = jnp.concatenate(halves(field[...]), axis=1)
    for slot, pair in enumerate(blocks[:-1]):
        for copy in copies[2 * slot : 2 * slot + 2]:
            copy.wait()
        one_slot(pair, held, parts, outs[2 * slot], outs[2 * slot + 1])
    for copy in copies[2 * slots :]:
        copy.wait()


def two_blocks(numbers, parts, first, last, scale, rows, matrix, *refs):
    modes = matrix.shape[1]
    blocks, refs = [[refs[0]], refs[1 : 1 + parts]], refs[1 + parts :]
    if not first:
        before, refs = refs[0], refs[1:]
    if last:
        base, refs = refs[0], refs[1:]
    total = None if first else before[...]
    for k, pieces in enumerate(blocks):
        block = jnp.concatenate([piece[...] for piece in pieces], axis=0)
        pieces = list(halves(block[:modes].T))
        if rows:
            weights = [
                jnp.concatenate(
                    [
                        block[modes + i : modes + i + 1, :]
                        for i in range(d * modes // LANES, (d + 1) * modes // LANES)
                    ],
                    axis=1,
                )
                for d in range(2)
            ]
            weights.append(jnp.zeros((6, modes), jnp.float32))
            pieces += halves(jnp.concatenate(weights, axis=0))
        left = jnp.concatenate(pieces, axis=0)
        there = rows_of(matrix, for_device(numbers[k]))
        term = jnp.dot(left, matrix[there, :], preferred_element_type=jnp.float32)
        total = term if total is None else total + term
    if not last:
        refs[0][...] = total
        return
    cells = base.shape[1]
    value = base[...] - scale * (total[:cells] + total[cells : 2 * cells]).T
    refs[0][...] = value
    if rows:
        refs[1][...] = value.T[:HALO]
        refs[2][...] = total[2 * cells : 2 * cells + 8] + total[2 * cells + 8 :]


def own_rows(distribution, velocity, capacity, out, token, speeds, weight, sems):
    modes, cells = velocity.shape[1], out.shape[1]
    copies = [
        pltpu.make_async_copy(velocity, speeds, sems.at[0]),
        pltpu.make_async_copy(capacity, weight, sems.at[1]),
        pltpu.make_async_copy(
            distribution.at[:, pl.ds(0, cells)], out.at[pl.ds(0, modes), :], sems.at[2]
        ),
    ]
    for copy in copies:
        copy.start()
    token[...] = jnp.zeros_like(token)
    for copy in copies[:2]:
        copy.wait()
    per = modes // LANES
    out[modes:] = jnp.zeros((out.shape[0] - modes, LANES), jnp.float32)
    for d in range(2):
        for i in range(per):
            lanes = slice(i * LANES, (i + 1) * LANES)
            out[modes + d * per + i : modes + d * per + i + 1, :] = (
                speeds[d : d + 1, lanes] * weight[:, lanes]
            )
    copies[2].wait()


def payload(numbers, slots, arrived, *refs):
    out = refs[-1]
    slot_here = for_device(numbers)

    for k, slot in enumerate(slots):

        @pl.when(slot_here == slot)
        def _(k=k):
            terms = refs[k]
            modes = terms.shape[0]
            out[:modes] = arrived[:modes] + terms[...]
            if out.shape[0] > modes:
                out[modes:] = arrived[modes:]

    @pl.when(slot_here < 0)
    def _():
        out[...] = arrived[: out.shape[0]]


def pick(numbers, *refs):
    out = refs[-1]
    choice = for_device(numbers)
    for k, ref in enumerate(refs[:-1]):

        @pl.when(choice == k)
        def _(ref=ref):
            out[...] = ref[...]


def add(one, *refs):
    out, first = refs[-1], 0
    for piece in refs[:-1]:
        rows = slice(first, first + piece.shape[0])
        out[rows] = one[rows] + piece[...]
        first += piece.shape[0]


def pass_on(value, out):
    out[...] = value[...]


def add_all(*refs):
    out, token = refs[-2:]
    total = refs[0][...]
    for ref in refs[1:-2]:
        total = total + ref[...]
    out[...] = total
    token[...] = jnp.zeros_like(token)


def take_off(scale, arrived, terms, base, out):
    modes = terms.shape[0]
    out[...] = base[...] - scale * (arrived[:modes] + terms[...])


def turn_sum(scale, arrived, base, out):
    modes = base.shape[0]
    out[...] = base[...] - scale * arrived[:modes]


def last_strip(field, strip):
    strip[...] = field[:, field.shape[1] - LANES :].T[-HALO:]


def last_sum(scale, arrived, base, other, flux, out, flux_out, value, sems):
    cells = base.shape[1]
    copies = [
        pltpu.make_async_copy(other, out.at[:, pl.ds(cells, cells)], sems.at[0]),
        pltpu.make_async_copy(flux, flux_out, sems.at[1]),
    ]
    for copy in copies:
        copy.start()
    rows = base.shape[0] // 2
    for k in range(2):
        part = slice(k * rows, (k + 1) * rows)
        value[part] = base[part] - scale * arrived[part]
        at = pl.ds(k * rows, rows)
        copies.append(
            pltpu.make_async_copy(
                value.at[at, :], out.at[at, pl.ds(0, cells)], sems.at[2 + k]
            )
        )
        copies[-1].start()
    for copy in copies:
        copy.wait()


def strip_rows(distribution, leading, last):
    cells = distribution.shape[1]
    leading[...] = distribution[:, :LANES].T[:HALO]
    last[...] = distribution[:, cells - LANES :].T[-HALO:]


def strip_pairs(leading, last, out_even, out_odd):
    even = lax.axis_index("space") % 2 == 0

    @pl.when(even)
    def _():
        out_even[...] = last[...]
        out_odd[...] = leading[...]

    @pl.when(jnp.logical_not(even))
    def _():
        out_even[...] = leading[...]
        out_odd[...] = last[...]


def differences(cells):
    columns = cells // NY
    own, strip = np.zeros((cells, 4 * cells)), np.zeros((2 * HALO, 4 * cells))
    for x in range(columns):
        for y in range(NY):
            cell = x * NY + y
            for way in (-1, 1):
                for far, factor in enumerate((3.0, -4.0, 1.0)):
                    at_x, at_y = x + way * far, y + way * far
                    first = cell + (0 if way < 0 else cells)
                    factor = -way * factor
                    if at_x < 0:
                        strip[(at_x + 2) * NY + y, first] = factor
                    elif at_x >= columns:
                        strip[HALO + (at_x - columns) * NY + y, first] = factor
                    else:
                        own[at_x * NY + y, first] = factor
                    if 0 <= at_y < NY:
                        own[x * NY + at_y, first + 2 * cells] = factor
    return np.concatenate([own, own, strip, strip]).astype(jnp.bfloat16)


def strip_columns(came_even, came_odd, out):
    even = lax.axis_index("space") % 2 == 0
    before = jnp.where(even, came_odd[...], came_even[...])
    after = jnp.where(even, came_even[...], came_odd[...])
    parts = halves(jnp.concatenate([before, after], axis=0))
    rows = jnp.concatenate([p.astype(jnp.float32) for p in parts], axis=0)
    out[...] = rows.T.astype(jnp.bfloat16)


def still_rate(field, strip, operators, columns, kinds):
    cells = field.shape[1]
    left = jnp.concatenate([*halves(field), strip], axis=1)
    steps = jnp.dot(left, operators[...], preferred_element_type=jnp.float32)
    vx, vy, capacity = (columns[:, i : i + 1] for i in range(3))
    speeds = (jnp.maximum(vx, 0.0), jnp.minimum(vx, 0.0))
    speeds += (jnp.maximum(vy, 0.0), jnp.minimum(vy, 0.0))
    contact = jnp.where(kinds > 0, relax_rate, 0.0)
    source = jnp.where(kinds == 1, contact, -contact)
    rate = source * capacity - contact * field
    for k, speed in enumerate(speeds):
        rate = rate - (0.5 * speed) * steps[:, k * cells : (k + 1) * cells]
    return rate


def first_rest(field, strips, operators, table, kinds, base_a, base_b):
    modes, half = base_a.shape
    block = min(modes, BLOCK)

    def step(i, _):
        rows = pl.ds(pl.multiple_of(i * block, block), block)
        value = field[rows, :]
        rate = still_rate(value, strips[rows, :], operators, table[:, rows].T, kinds[...])
        base = value + time_step * rate
        base_a[rows, :] = base[:, :half]
        base_b[rows, :] = base[:, half:]
        return 0

    lax.fori_loop(0, modes // block, step, 0)


def second_rest(
    flux_scale,
    field,
    mid_a,
    mid_b,
    strips,
    operators,
    table,
    kinds,
    scattered,
    end_a,
    end_b,
    flux,
):
    modes, half = end_a.shape
    block = min(modes, BLOCK)
    step_size = 0.5 * time_step
    flux[...] = jnp.zeros_like(flux)

    def step(i, _):
        rows = pl.ds(pl.multiple_of(i * block, block), block)
        mid = jnp.concatenate([mid_a[rows, :], mid_b[rows, :]], axis=1)
        columns = table[:, rows].T
        taken = step_size * scattered[:, rows].T
        rate = still_rate(mid, strips[rows, :], operators, columns, kinds[...])
        end = 0.5 * (field[rows, :] + mid) + step_size * rate
        end_a[rows, :] = end[:, :half]
        end_b[rows, :] = end[:, half:]
        for d in range(2):
            terms = columns[:, 3 + d : 4 + d] * end - taken[:, d : d + 1] * mid
            flux[d : d + 1, :] += flux_scale * jnp.sum(terms, axis=0, keepdims=True)
        return 0

    lax.fori_loop(0, modes // block, step, 0)


def paired(to_even, to_odd):
    count = lax.axis_size("space")
    came = []
    for first, value in enumerate((to_even, to_odd)):
        pairs = [(i, i + 1) for i in range(first, count - 1, 2)]
        came.append(lax.ppermute(value, "space", pairs + [(j, i) for i, j in pairs]))
    return came


class Plan:
    def __init__(self, chips):
        self.chips = chips
        self.devices = range(2 * chips)
        sources = [self.sources(d) for d in self.devices]
        targets = [self.targets(d // 2) for d in self.devices]
        self.blocks = [
            [
                [2 * sources[e][slot][2] + e % 2 for e in (d ^ other for d in self.devices)]
                for other in (0, 1)
            ]
            for slot in range(chips)
        ]
        self.rows = [
            [[2 * targets[d][slot] + (d % 2 ^ other) for d in self.devices] for other in (0, 1)]
            for slot in range(chips)
        ]
        self.choices = [
            sorted({sources[d][slot][:2] for d in self.devices}) for slot in range(chips)
        ]
        self.picked = [
            [self.choices[slot].index(sources[d][slot][:2]) for d in self.devices]
            for slot in range(chips)
        ]
        self.sent = {}
        for stream in (0, 1):
            for step in range(1, chips):
                numbers = []
                for d in self.devices:
                    way = self.way(d, stream)
                    place = d // 2 if way > 0 else chips - 1 - d // 2
                    target = d // 2 + way * (chips - step)
                    numbers.append(targets[d].index(target) if place < step else -1)
                self.sent[stream, step] = numbers
        self.pairs = []
        for stream in (0, 1):
            up = [
                (d, d + 2) for d in self.devices[:-2] if self.way(d, stream) > 0
            ]
            self.pairs.append(up + [(j, i) for i, j in up])

    def way(self, device, stream):
        return 1 if (device // 2 + device % 2 + stream) % 2 == 0 else -1

    def sources(self, device):
        found = [(-1, -1, device // 2)]
        for step in range(self.chips - 1):
            for stream in (step % 2, 1 - step % 2):
                chip = device // 2 + self.way(device, stream) * (step + 1)
                if 0 <= chip < self.chips:
                    found.append((stream, step, chip))
        return found

    def targets(self, chip):
        found = []
        for step in range(1, self.chips):
            far = self.chips - step
            found += [t for t in (chip + far, chip - far) if 0 <= t < self.chips]
        return found + [chip]


def on_device(distribution, scatter_matrix, velocity, capacity, cell_type):
    modes, cells = distribution.shape
    total_modes = scatter_matrix.shape[0]
    half = cells // 2
    extra = -(-2 * modes // LANES // 8) * 8
    step_size = 0.5 * time_step
    part = (modes, half)
    devices = lax.axis_size("mode")
    chips = devices // 2
    plan = Plan(chips)
    call = Chain()
    across = [(i, i ^ 1) for i in range(devices)]
    cap = capacity[None, :]
    table = jnp.concatenate(
        [velocity, cap, cap * velocity, jnp.zeros((3, modes), jnp.float32)], axis=0
    )
    kinds = cell_type[None, :]

    def exchange(value, parts=1):
        cut = value.shape[0] // parts // 8 * 8
        ends = [cut * k for k in range(parts)] + [value.shape[0]]
        return [lax.ppermute(value[i:j], "mode", across) for i, j in zip(ends, ends[1:])]

    def along(stream, value):
        return lax.ppermute(value, "mode", plan.pairs[stream])

    class Round:
        def __init__(self, matrix, scale, rows):
            self.matrix, self.scale, self.rows = matrix, scale, rows
            self.terms, self.total = [], None

        def begin(self, own):
            self.own = own
            self.arrived = [[along(0, own)], [along(1, own)]]
            self.blocks = []

        def add_terms(self, field, column=0):
            kernel = functools.partial(slot_products, plan.rows[len(self.terms)], column)
            mine, other = call(kernel, [part] * 2, [self.matrix, field])
            self.terms.append((mine, *exchange(other)))

        def join_terms(self, *slots):
            for slot in slots:
                (self.terms[slot],) = call(add, [part], self.terms[slot])

        def take_own(self, later=False):
            own = call(pass_on, [self.own.shape], [self.own])[0] if later else self.own
            self.blocks.append((self.own, *exchange(own)))

        def send(self, step, between=None):
            sent = {}
            for stream in (step % 2, 1 - step % 2):
                if between is not None and sent:
                    between()
                numbers = plan.sent[stream, step]
                slots = sorted({n for n in numbers if n >= 0})
                for slot in slots:
                    if isinstance(self.terms[slot], tuple):
                        self.join_terms(slot)
                arrived = self.arrived[1 - stream][step - 1]
                kernel = functools.partial(payload, numbers, slots)
                arrays = [arrived] + [self.terms[s] for s in slots]
                shape = part if step == chips - 1 else arrived.shape
                (value,) = call(kernel, [shape], arrays)
                sent[stream] = along(stream, value)
            for stream in (0, 1):
                self.arrived[stream].append(sent[stream])

        def take(self, slot, parts=1):
            arrays = [self.arrived[stream][step] for stream, step in plan.choices[slot]]
            kernel = functools.partial(pick, plan.picked[slot])
            (here,) = call(kernel, [arrays[0].shape], arrays)
            self.blocks.append((here, *exchange(here, parts)))

        def hold(self, *slots):
            for slot in slots:
                here, there = self.blocks[slot]
                (there,) = call(pass_on, [there.shape], [there])
                self.blocks[slot] = (here, there)

        def multiply(self, slot, base=None, first=None):
            first, last = slot == 0 if first is None else first, base is not None
            blocks = self.blocks[slot]
            kernel = functools.partial(
                two_blocks, plan.blocks[slot], len(blocks) - 1, first, last, self.scale, self.rows
            )
            arrays = [self.matrix, *blocks]
            arrays += [] if first else [self.total]
            arrays += [base] if last else []
            outs = [(2 * half + (16 if self.rows else 0), modes)]
            if last:
                outs = [part, (HALO, modes), (8, modes)] if self.rows else [part]
            results = call(kernel, outs, arrays)
            self.total = results[0]
            return results

        def first_end(self, base):
            kernel = functools.partial(take_off, self.scale)
            arrived = self.arrived[(chips - 1) % 2][-1]
            (self.rest,) = call(kernel, [part], [arrived, self.terms[-1], base])

        def ends(self):
            return [self.arrived[chips % 2][-1], self.rest]

    own, _ = call(
        own_rows,
        [(modes + extra, half), (8, LANES)],
        [distribution, velocity, cap],
        places=[HBM] * 3,
        scratch=[
            pltpu.VMEM((2, modes), jnp.float32),
            pltpu.VMEM((1, modes), jnp.float32),
            pltpu.SemaphoreType.DMA((3,)),
        ],
        room=56,
    )
    one = Round(None, time_step, True)
    one.begin(own)
    *terms, matrix = call(
        functools.partial(load_and_products, plan.rows, half),
        [part] * (2 * chips - 2) + [jax.ShapeDtypeStruct(scatter_matrix.shape, jnp.bfloat16)],
        [scatter_matrix, distribution],
        places=[HBM] * 2,
        scratch=[
            pltpu.VMEM(part, jnp.float32),
            pltpu.SemaphoreType.DMA((2 * chips + 1,)),
        ],
        room=28,
    )
    one.matrix = matrix
    one.terms = [(terms[2 * s], *exchange(terms[2 * s + 1])) for s in range(chips - 1)]
    one.take_own()
    operators = jnp.asarray(differences(cells))
    strips = None

    def unpack():
        nonlocal strips
        shape = jax.ShapeDtypeStruct((modes, 4 * HALO), jnp.bfloat16)
        (strips,) = call(strip_columns, [shape], strips)

    for step in range(1, chips):
        if step == 1:
            one.take(1)
        one.send(step, unpack if step == 2 else None)
        if step == 1:
            one.join_terms(*(s for s in range(chips - 1) if isinstance(one.terms[s], tuple)))
            strips = call(strip_rows, [(HALO, modes)] * 2, [distribution])
            strips = paired(*call(strip_pairs, [(HALO, modes)] * 2, strips))
        else:
            one.take(step, 2 if step == chips - 1 else 1)
        if step == 2:
            one.add_terms(distribution, half)
        if step == chips - 1:
            one.join_terms(chips - 1)
        one.multiply(step - 1)
        if step == min(2, chips - 1):
            base_a, base_b = call(
                first_rest,
                [part] * 2,
                [distribution, strips, operators, table, kinds],
            )
    mid_a, leading, scattered = one.multiply(chips - 1, base_a)

    two = Round(matrix, step_size, False)
    two.add_terms(mid_a)
    two.add_terms(mid_a)
    one.first_end(base_b)
    (mid_b,) = call(functools.partial(turn_sum, time_step), [part], one.ends())
    two.begin(mid_b)
    two.join_terms(0)
    (last,) = call(last_strip, [(HALO, modes)], [mid_b])
    strips = paired(*call(strip_pairs, [(HALO, modes)] * 2, [leading, last]))
    flux = None
    for step in range(1, chips):
        if step == 1:
            two.send(step, unpack)
            two.take_own()
            two.join_terms(1)
        elif step == 2:
            two.send(step, lambda: flux.over(1))
            two.join_terms(*range(2, chips))
        elif step == chips - 1:
            two.send(step, lambda: flux.over(*range(2, devices, 2)))
        else:
            two.send(step)
        two.take(step, 2 if step >= chips - 2 else 1)
        if step == 1:
            for slot in range(2, chips):
                two.add_terms(mid_a)
        if 1 < step < chips - 1:
            two.hold(*range(step) if step == 2 else (step - 1,))
        if step == chips - 2:
            two.multiply(step, first=True)
        if step == chips - 1:
            for slot in range(chips - 2):
                two.multiply(slot, first=False)
        if step == 1:
            end_a, end_b, part_flux = call(
                functools.partial(second_rest, 1.0 / math.sqrt(total_modes)),
                [part, part, (2, cells)],
                [distribution, mid_a, mid_b, strips, operators, table, kinds, scattered],
            )
            flux = Flux(call, part_flux, devices)
    (last_b,) = two.multiply(chips - 1, end_b)
    two.first_end(end_a)
    updated, heat_flux = call(
        functools.partial(last_sum, step_size),
        [(modes, cells), (2, cells)],
        [*two.ends(), last_b, flux.value],
        scratch=[pltpu.VMEM(part, jnp.float32), pltpu.SemaphoreType.DMA((4,))],
        out_specs=[HBM, HBM],
    )
    return (updated, heat_flux)


class Flux:
    def __init__(self, call, value, devices):
        self.call, self.value, self.devices = call, value, devices

    def over(self, *bits):
        came = [
            lax.ppermute(self.value, "mode", [(i, i ^ bit) for i in range(self.devices)])
            for bit in bits
        ]
        self.value, _ = self.call(add_all, [self.value.shape, (8, LANES)], [self.value, *came])


def solution(mesh):
    return jax.shard_map(
        on_device,
        mesh=mesh,
        in_specs=(P("mode", "space"), P(None, "mode"), P(None, "mode"), P("mode"), P("space")),
        out_specs=(P("mode", "space"), P(None, "space")),
        check_vma=False,
    )
```
